32 devices in a mesh: shard: 4 (over y, core), replica: 8 (over z, x).
Axes of the slice: x: 2, y: 2, z: 4, core: 2. Of those that a mesh axis runs over, the one named last changes fastest.
Arguments:
- tokens: bfloat16 [256, 129, 1024], P(('shard', 'replica')), may hold values from -6 to 6
- norm1_gain: bfloat16 [1024], P('shard'), may hold values from 0.099609375 to 1.8984375
- norm1_shift: bfloat16 [1024], P('shard'), may hold values from -3 to 3
- w_qkv: bfloat16 [1024, 3072], P('shard'), may hold values from -0.1875 to 0.1875
- bias_qv: bfloat16 [2048], P('shard'), may hold values from -3 to 3
- w_out: bfloat16 [1024, 1024], P('shard'), may hold values from -0.75 to 0.75
- bias_out: bfloat16 [1024], P('shard'), may hold values from -3 to 3
- scale_one: bfloat16 [1024], P('shard'), may hold values from 0.5 to 1.5
- norm2_gain: bfloat16 [1024], P('shard'), may hold values from 0.099609375 to 1.8984375
- norm2_shift: bfloat16 [1024], P('shard'), may hold values from -3 to 3
- w_up: bfloat16 [1024, 4096], P(None, 'shard'), may hold values from -0.1875 to 0.1875
- bias_up: bfloat16 [4096], P('shard'), may hold values from -3 to 3
- w_down: bfloat16 [4096, 1024], P('shard'), may hold values from -0.09375 to 0.09375
- bias_down: bfloat16 [1024], P('shard'), may hold values from -3 to 3
- scale_two: bfloat16 [1024], P('shard'), may hold values from 0.5 to 1.5
- cotangent: bfloat16 [256, 129, 1024], P(('shard', 'replica')), may hold values from -6 to 6
Outputs:
- result: bfloat16 [256, 129, 1024], P(('shard', 'replica'))
- grad_tokens: bfloat16 [256, 129, 1024], P(('shard', 'replica'))
- grad_norm1_gain: float32 [1024], P('shard')
- grad_norm1_shift: float32 [1024], P('shard')
- grad_w_qkv: float32 [1024, 3072], P('shard')
- grad_bias_qv: float32 [2048], P('shard')
- grad_w_out: float32 [1024, 1024], P('shard')
- grad_bias_out: float32 [1024], P('shard')
- grad_scale_one: float32 [1024], P('shard')
- grad_norm2_gain: float32 [1024], P('shard')
- grad_norm2_shift: float32 [1024], P('shard')
- grad_w_up: float32 [1024, 4096], P(None, 'shard')
- grad_bias_up: float32 [4096], P('shard')
- grad_w_down: float32 [4096, 1024], P('shard')
- grad_bias_down: float32 [1024], P('shard')
- grad_scale_two: float32 [1024], P('shard')
The draws below stay inside these ranges and needn't reach their ends.
All inputs are finite; a program needn't handle non-finite values.
Results may differ from the reference program's by a relative error of at most 0.02.
Values may be sent and summed in bfloat16 or wider, within the bound.
A program may use at most 320 MiB of HBM per device.

```python
import jax
import jax.numpy as jnp
from jax import lax

D = 1024
FF = 4096
HEADS = 16
HEAD_DIM = 64
SEQ = 129
IMG_DEV = 8
IMAGES = 256
N_SHARD = 4


def steps_of(stream_key, dims, shards, low, high):
    def one(dim, shards_of):
        draws = jax.random.uniform(jax.random.fold_in(jax.random.fold_in(stream_key, 6), dim), (shards_of,), jnp.float32, low / len(shards), high / len(shards))
        return jnp.repeat(jnp.exp(draws), dims[dim] // shards_of).reshape((-1,) + (1,) * (len(dims) - dim - 1))

    level = one(*shards[0])
    for cut in shards[1:]:
        level = level * one(*cut)
    return level


def gaussian(own_key, dims, width, limit, split=(), kind=jnp.bfloat16):
    level = steps_of(own_key, dims, split, -0.22, 0.18) if split else 1.0
    result = jax.random.normal(own_key, dims, jnp.float32) * width * level
    return jnp.minimum(jnp.maximum(result, -limit), limit).astype(kind)


def setup_inputs(seed: int = 0) -> dict:
    streams_of = jax.random.split(jax.random.key(seed), 17)
    tokens = gaussian(streams_of[0], (IMAGES, SEQ, D), 1.0, 6.0, ((0, 32),))
    norm1_gain = jnp.clip(1.0 + 0.18 * jax.random.normal(streams_of[1], (D,), jnp.float32), 0.099609375, 1.8984375).astype(jnp.bfloat16)
    norm1_shift = gaussian(streams_of[2], (D,), 0.3, 3.0, ((0, 4),))
    w_qkv = gaussian(streams_of[3], (D, 3 * D), D ** -0.5, 0.1875, ((0, 4),))
    bias_qv = gaussian(streams_of[4], (2 * D,), 0.3, 3.0, ((0, 4),))
    w_out = gaussian(streams_of[5], (D, D), (D // 16) ** -0.5, 0.75, ((0, 4),))
    bias_out = gaussian(streams_of[6], (D,), 0.3, 3.0, ((0, 4),))
    scale_one = jnp.clip(0.5 + 1.0 * jax.random.uniform(streams_of[7], (D,), jnp.float32) ** steps_of(streams_of[7], (D,), ((0, 4),), -0.2, 0.2), 0.5, 1.5).astype(jnp.bfloat16)
    norm2_gain = jnp.clip(1.0 + 0.18 * jax.random.normal(streams_of[8], (D,), jnp.float32), 0.099609375, 1.8984375).astype(jnp.bfloat16)
    norm2_shift = gaussian(streams_of[9], (D,), 0.3, 3.0, ((0, 4),))
    w_up = gaussian(streams_of[10], (D, FF), D ** -0.5, 0.1875, ((1, 4),))
    bias_up = gaussian(streams_of[11], (FF,), 0.3, 3.0, ((0, 4),))
    w_down = gaussian(streams_of[12], (FF, D), FF ** -0.5, 0.09375, ((0, 4),))
    bias_down = gaussian(streams_of[13], (D,), 0.3, 3.0, ((0, 4),))
    scale_two = jnp.clip(0.5 + 1.0 * jax.random.uniform(streams_of[14], (D,), jnp.float32) ** steps_of(streams_of[14], (D,), ((0, 4),), -0.2, 0.2), 0.5, 1.5).astype(jnp.bfloat16)
    cotangent = gaussian(streams_of[15], (IMAGES, SEQ, D), 1.0, 6.0, ((0, 32),))
    return {"tokens": tokens, "norm1_gain": norm1_gain, "norm1_shift": norm1_shift, "w_qkv": w_qkv, "bias_qv": bias_qv, "w_out": w_out, "bias_out": bias_out, "scale_one": scale_one, "norm2_gain": norm2_gain, "norm2_shift": norm2_shift, "w_up": w_up, "bias_up": bias_up, "w_down": w_down, "bias_down": bias_down, "scale_two": scale_two, "cotangent": cotangent}


@jax.custom_vjp
def low(v):
    return lax.optimization_barrier(v.astype(jnp.bfloat16)).astype(jnp.float32)

@jax.custom_vjp
def low_back(v):
    return v

def low_keep(v):
    return (low(v), None)

def low_pass(kept, grad):
    return (grad,)

def back_keep(v):
    return (v, None)

def back_low(kept, grad):
    return (low(grad),)
low.defvjp(low_keep, low_pass)
low_back.defvjp(back_keep, back_low)

def matmul(left, right):
    return jnp.dot(left, right, precision=lax.Precision.HIGHEST)

def layer_norm(values, gain, shift):
    centered = values - lax.optimization_barrier(jnp.mean(values, axis=-1, keepdims=True))
    spread = lax.optimization_barrier(jnp.mean(centered * centered, axis=-1, keepdims=True))
    return centered * lax.rsqrt(spread + 1e-06) * gain + shift

def block(params, images):
    norm1_gain, norm1_shift, w_qkv, bias_qv, w_out, bias_out, scale_one, norm2_gain, norm2_shift, w_up, bias_up, w_down, bias_down, scale_two = params
    images_n, length, features = images.shape
    inputs = images.reshape(images_n * length, features)
    act_one = low(layer_norm(inputs, norm1_gain, norm1_shift))
    joined = low_back(matmul(act_one, w_qkv))
    queries = low(joined[:, :features] + bias_qv[:features]).reshape(images_n, length, HEADS, HEAD_DIM)
    keys_all = low(joined[:, features:2 * features]).reshape(images_n, length, HEADS, HEAD_DIM)
    values_all = low(joined[:, 2 * features:] + bias_qv[features:]).reshape(images_n, length, HEADS, HEAD_DIM)
    scores = low_back(jnp.einsum('bqhd,bkhd->bhqk', queries, keys_all, precision=lax.Precision.HIGHEST) * HEAD_DIM ** (-0.5))
    probs = jax.nn.softmax(scores, axis=-1)
    mixture = jnp.einsum('bhqk,bkhd->bqhd', low(probs), values_all, precision=lax.Precision.HIGHEST)
    attended = low(low_back(mixture.reshape(images_n * length, features)))
    branch = low_back(matmul(attended, w_out)) + bias_out
    middle = inputs + scale_one * branch
    act_two = low(layer_norm(middle, norm2_gain, norm2_shift))
    before = low_back(matmul(act_two, w_up)) + bias_up
    hidden = low(jax.nn.gelu(before, approximate=False))
    projected = low_back(matmul(hidden, w_down)) + bias_down
    return (middle + scale_two * projected).reshape(images_n, length, features)

def forward(images, params):
    stacked = images.reshape(IMAGES // (N_SHARD * IMG_DEV), N_SHARD * IMG_DEV, SEQ, D)
    checked = jax.checkpoint(block)

    def advance(carried, group_images):
        return (carried, checked(params, group_images))
    _, results = lax.scan(advance, jnp.float32(0.0), stacked)
    return results.reshape(IMAGES, SEQ, D)

def reference(tokens, norm1_gain, norm1_shift, w_qkv, bias_qv, w_out, bias_out, scale_one, norm2_gain, norm2_shift, w_up, bias_up, w_down, bias_down, scale_two, cotangent):
    params = tuple((piece.astype(jnp.float32) for piece in (norm1_gain, norm1_shift, w_qkv, bias_qv, w_out, bias_out, scale_one, norm2_gain, norm2_shift, w_up, bias_up, w_down, bias_down, scale_two)))
    widened = tokens.astype(jnp.float32)
    output, pullback = jax.vjp(forward, widened, params)
    grad_input, gradients = pullback(cotangent.astype(jnp.float32))
    return (output.astype(jnp.bfloat16), grad_input.astype(jnp.bfloat16), gradients[0], gradients[1], gradients[2], gradients[3], gradients[4], gradients[5], gradients[6], gradients[7], gradients[8], gradients[9], gradients[10], gradients[11], gradients[12], gradients[13])
```

```python
import jax
import jax.numpy as jnp
from jax import lax
from jax.sharding import PartitionSpec as P

HEADS = 16
HEAD_DIM = 64


def layer_norm(values, gain, shift):
    centered = values - jnp.mean(values, axis=-1, keepdims=True)
    inverse = lax.rsqrt(jnp.mean(centered * centered, axis=-1, keepdims=True) + 1e-06)
    normal_hat = centered * inverse
    return (normal_hat * gain + shift, normal_hat, inverse)


def norm_back(upstream, normal_hat, inverse, gain):
    scaled = upstream * gain
    back = inverse * (
        scaled
        - jnp.mean(scaled, axis=-1, keepdims=True)
        - normal_hat * jnp.mean(scaled * normal_hat, axis=-1, keepdims=True)
    )
    return (back, jnp.sum(upstream * normal_hat, axis=0), jnp.sum(upstream, axis=0))


def gelu_slope(before):
    return (
        0.5 * (1.0 + lax.erf(before * 0.7071067811865476))
        + before * jnp.exp(-0.5 * before * before) * 0.3989422804014327
    )


def matmul(left, right):
    return jnp.dot(left, right, preferred_element_type=jnp.float32)


def left_product(left, right):
    return lax.dot_general(
        left, right, (((0,), (0,)), ((), ())), preferred_element_type=jnp.float32
    )


def right_product(left, right):
    return lax.dot_general(
        left, right, (((1,), (1,)), ((), ())), preferred_element_type=jnp.float32
    )


def ring(axis_fn):
    shards, replicas = lax.axis_size("shard"), lax.axis_size("replica")
    pairs = []
    for s in range(shards):
        for r in range(replicas):
            t, q = axis_fn(s, r)
            pairs.append((s * replicas + r, t * replicas + q))
    return pairs


def swap_core(v):
    return lax.ppermute(v, ("shard", "replica"), ring(lambda s, r: (s ^ 1, r)))


def swap_y(v):
    return lax.ppermute(v, ("shard", "replica"), ring(lambda s, r: (s ^ 2, r)))


def swap_x(v):
    return lax.ppermute(v, ("shard", "replica"), ring(lambda s, r: (s, r ^ 1)))


def swap_z(v, step):
    return lax.ppermute(v, ("shard", "replica"), ring(lambda s, r: (s, r ^ (2 * step))))


def pick(v, index):
    return lax.dynamic_index_in_dim(v, index, 0, keepdims=False)


def put(out, v, index):
    return lax.dynamic_update_index_in_dim(out, v, index, 0)


def gather(piece):
    s = lax.axis_index("shard")
    x = lax.axis_index("replica") % 2
    rows, cols = piece.shape
    halves = piece.reshape(2, rows // 2, cols)
    from_core = swap_core(piece)
    from_y = swap_y(pick(halves, x))
    from_x = swap_x(from_y)
    far = jnp.zeros_like(halves)
    far = put(put(far, from_y, x), from_x, x ^ 1)
    far_core = swap_core(far)
    out = jnp.zeros((4, rows, cols), piece.dtype)
    out = put(out, piece, s)
    out = put(out, from_core, s ^ 1)
    out = put(out, far.reshape(rows, cols), s ^ 2)
    return put(out, far_core.reshape(rows, cols), s ^ 3)


def reduce_all(grad):
    s = lax.axis_index("shard")
    r = lax.axis_index("replica")
    x, z = r % 2, r // 2
    nz = lax.axis_size("replica") // 2
    low = jnp.bfloat16
    grad = grad.astype(low)
    rows, cols = grad.shape[1:]
    wide = lambda v: v.astype(jnp.float32)
    to_core = jnp.stack([pick(grad, s ^ 1), pick(grad, s ^ 3)])
    got = swap_core(to_core)
    mine = wide(pick(grad, s)) + wide(got[0])
    far = (wide(pick(grad, s ^ 2)) + wide(got[1])).astype(low)
    mine = (mine + wide(swap_y(far))).reshape(2, rows // 2, cols)
    got = swap_x(pick(mine, x ^ 1).astype(low))
    half = (pick(mine, x) + wide(got)).reshape(nz, rows // 2 // nz, cols)
    total = pick(half, z)
    for k in range(1, nz):
        total = total + wide(swap_z(pick(half, z ^ k).astype(low), k))
    total = total.astype(low)
    out = jnp.zeros((nz,) + total.shape, low)
    out = put(out, total, z)
    for k in range(1, nz):
        out = put(out, swap_z(total, k), z ^ k)
    both = jnp.zeros((2,) + out.shape, low)
    both = put(put(both, out, x), swap_x(out), x ^ 1)
    return both.reshape(rows, cols).astype(jnp.float32)


def on_device(
    tokens,
    norm1_gain,
    norm1_shift,
    w_qkv,
    bias_qv,
    w_out,
    bias_out,
    scale_one,
    norm2_gain,
    norm2_shift,
    w_up,
    bias_up,
    w_down,
    bias_down,
    scale_two,
    cotangent,
):
    images_n, length, features = tokens.shape
    rows_n = images_n * length
    factor = HEAD_DIM ** (-0.5)
    heads_shape = (images_n, length, HEADS, HEAD_DIM)
    vectors = jnp.concatenate([norm1_gain, norm1_shift, bias_out, scale_one, norm2_gain, norm2_shift, bias_down, scale_two, bias_qv, bias_up]).reshape(14, 256)
    vectors = lax.all_gather(vectors, "shard", axis=0)
    row = lambda first, count=1: vectors[:, first:first + count].reshape(-1)
    gain_one, shift_one, bias_branch, layer_one, gain_two, shift_two, bias_last, layer_two = (row(i) for i in range(8))
    bias_joint, bias_wide = row(8, 2), row(10, 4)
    qkv_full = gather(w_qkv).reshape(1024, 3072)
    out_full = gather(w_out).reshape(1024, 1024)
    up_full = jnp.moveaxis(gather(w_up), 0, 1).reshape(1024, 4096)
    down_full = gather(w_down).reshape(4096, 1024)
    gain_one = gain_one.astype(jnp.float32)
    shift_one = shift_one.astype(jnp.float32)
    bias_joint = bias_joint.astype(jnp.float32)
    bias_branch = bias_branch.astype(jnp.float32)
    layer_one = layer_one.astype(jnp.float32)
    gain_two = gain_two.astype(jnp.float32)
    shift_two = shift_two.astype(jnp.float32)
    bias_last = bias_last.astype(jnp.float32)
    layer_two = layer_two.astype(jnp.float32)
    bias_wide = bias_wide.astype(jnp.float32)
    inputs = tokens.reshape(rows_n, features).astype(jnp.float32)
    normed_one, hat_one, inverse_one = layer_norm(inputs, gain_one, shift_one)
    act_one = normed_one.astype(jnp.bfloat16)
    joined = matmul(act_one, qkv_full)
    queries = (
        (joined[:, :features] + bias_joint[:features]).astype(jnp.bfloat16).reshape(heads_shape)
    )
    keys_all = joined[:, features : 2 * features].astype(jnp.bfloat16).reshape(heads_shape)
    values_all = (
        (joined[:, 2 * features :] + bias_joint[features:])
        .astype(jnp.bfloat16)
        .reshape(heads_shape)
    )
    scores = (
        jnp.einsum("bqhd,bkhd->bhqk", queries, keys_all, preferred_element_type=jnp.float32)
        * factor
    )
    highest = jnp.max(scores, axis=-1, keepdims=True)
    log_total = highest + jnp.log(jnp.sum(jnp.exp(scores - highest), axis=-1, keepdims=True))
    probs = jnp.exp(scores - log_total)
    mixture = jnp.einsum(
        "bhqk,bkhd->bqhd",
        probs.astype(jnp.bfloat16),
        values_all,
        preferred_element_type=jnp.float32,
    )
    attended = mixture.reshape(rows_n, features).astype(jnp.bfloat16)
    branch = matmul(attended, out_full) + bias_branch
    middle = inputs + layer_one * branch
    normed_two, hat_two, inverse_two = layer_norm(middle, gain_two, shift_two)
    act_two = normed_two.astype(jnp.bfloat16)
    before = matmul(act_two, up_full) + bias_wide
    hidden = jax.nn.gelu(before, approximate=False).astype(jnp.bfloat16)
    projected = matmul(hidden, down_full) + bias_last
    result = (
        (middle + layer_two * projected).astype(jnp.bfloat16).reshape(images_n, length, features)
    )
    upstream = cotangent.reshape(rows_n, features).astype(jnp.float32)
    grad_layer_two = jnp.sum(upstream * projected, axis=0)
    grad_down_in = upstream * layer_two
    grad_bias_last = jnp.sum(grad_down_in, axis=0)
    down_round = grad_down_in.astype(jnp.bfloat16)
    grad_down_piece = left_product(hidden, down_round)
    grad_before = right_product(down_round, down_full) * gelu_slope(before)
    grad_bias_up = jnp.sum(grad_before, axis=0)
    before_round = grad_before.astype(jnp.bfloat16)
    grad_up_piece = left_product(act_two, before_round)
    grad_act_two = right_product(before_round, up_full)
    back_two, grad_gain_two, grad_shift_two = norm_back(
        grad_act_two, hat_two, inverse_two, gain_two
    )
    grad_middle = upstream + back_two
    grad_layer_one = jnp.sum(grad_middle * branch, axis=0)
    grad_branch = grad_middle * layer_one
    grad_bias_branch = jnp.sum(grad_branch, axis=0)
    branch_round = grad_branch.astype(jnp.bfloat16)
    grad_out_full = left_product(attended, branch_round)
    attended_round = right_product(branch_round, out_full).astype(jnp.bfloat16).reshape(heads_shape)
    scores_again = (
        jnp.einsum("bqhd,bkhd->bhqk", queries, keys_all, preferred_element_type=jnp.float32)
        * factor
    )
    probs_again = jnp.exp(scores_again - log_total)
    grad_values = jnp.einsum(
        "bhqk,bqhd->bkhd",
        probs_again.astype(jnp.bfloat16),
        attended_round,
        preferred_element_type=jnp.float32,
    )
    grad_probs = jnp.einsum(
        "bqhd,bkhd->bhqk", attended_round, values_all, preferred_element_type=jnp.float32
    )
    grad_scores = probs_again * (
        grad_probs - jnp.sum(probs_again * grad_probs, axis=-1, keepdims=True)
    )
    scores_round = grad_scores.astype(jnp.bfloat16)
    grad_queries = (
        jnp.einsum("bhqk,bkhd->bqhd", scores_round, keys_all, preferred_element_type=jnp.float32)
        * factor
    )
    grad_keys = (
        jnp.einsum("bhqk,bqhd->bkhd", scores_round, queries, preferred_element_type=jnp.float32)
        * factor
    )
    grad_queries = grad_queries.reshape(rows_n, features)
    grad_keys = grad_keys.reshape(rows_n, features)
    grad_values = grad_values.reshape(rows_n, features)
    grad_bias_joint = jnp.concatenate([jnp.sum(grad_queries, axis=0), jnp.sum(grad_values, axis=0)])
    joint_round = jnp.concatenate([grad_queries, grad_keys, grad_values], axis=1).astype(
        jnp.bfloat16
    )
    grad_qkv_full = left_product(act_one, joint_round)
    grad_act_one = right_product(joint_round, qkv_full)
    back_one, grad_gain_one, grad_shift_one = norm_back(
        grad_act_one, hat_one, inverse_one, gain_one
    )
    grad_input = (grad_middle + back_one).astype(jnp.bfloat16).reshape(images_n, length, features)
    small = jnp.concatenate([v.reshape(4, -1) for v in (grad_gain_one, grad_shift_one, grad_bias_branch, grad_layer_one, grad_gain_two, grad_shift_two, grad_bias_last, grad_layer_two, grad_bias_joint, grad_bias_up)], axis=1)
    small = lax.psum(small, ("shard", "replica"))
    small = pick(small, lax.axis_index("shard"))
    part = lambda first, count=1: small[256 * first:256 * (first + count)]
    sum_down = reduce_all(grad_down_piece.reshape(4, 1024, 1024))
    sum_up = reduce_all(jnp.moveaxis(grad_up_piece.reshape(1024, 4, 1024), 1, 0))
    sum_out = reduce_all(grad_out_full.reshape(4, 256, 1024))
    sum_qkv = reduce_all(grad_qkv_full.reshape(4, 256, 3072))
    totals = (part(0), part(1), sum_qkv, part(8, 2), sum_out, part(2), part(3), part(4), part(5), sum_up, part(10, 4), sum_down, part(6), part(7))
    return (result, grad_input) + tuple(totals)


def solution(mesh):
    placed = (
        P(("shard", "replica"), None, None),
        P("shard"),
        P("shard"),
        P("shard", None),
        P("shard"),
        P("shard", None),
        P("shard"),
        P("shard"),
        P("shard"),
        P("shard"),
        P(None, "shard"),
        P("shard"),
        P("shard", None),
        P("shard"),
        P("shard"),
        P(("shard", "replica"), None, None),
    )
    return jax.shard_map(
        on_device,
        mesh=mesh,
        in_specs=placed,
        out_specs=(
            P(("shard", "replica"), None, None),
            P(("shard", "replica"), None, None),
            P("shard"),
            P("shard"),
            P("shard", None),
            P("shard"),
            P("shard", None),
            P("shard"),
            P("shard"),
            P("shard"),
            P("shard"),
            P(None, "shard"),
            P("shard"),
            P("shard", None),
            P("shard"),
            P("shard"),
        ),
        check_vma=False,
    )
```

```python
import functools

import jax
import jax.numpy as jnp
from jax import lax
from jax.experimental import pallas as pl
from jax.experimental.pallas import tpu as pltpu
from jax.sharding import PartitionSpec as P

F32 = jnp.float32
BF16 = jnp.bfloat16
D = 1024
FF = 4096
HEADS = 16
PATCH = 128
CLS = 16
TILE = 512
FACTOR = 0.125
MESH = pl.DeviceIdType.MESH


def dot(a, b):
    return jnp.dot(a, b, preferred_element_type=F32)


def dot_nt(a, b):
    return lax.dot_general(a, b, (((1,), (1,)), ((), ())), preferred_element_type=F32)


def dot_tn(a, b):
    return lax.dot_general(a, b, (((0,), (0,)), ((), ())), preferred_element_type=F32)


def at(index, size):
    return pl.ds(pl.multiple_of(index * size, size), size)


def head_mask():
    lane = lax.shift_right_logical(lax.broadcasted_iota(jnp.int32, (HEADS, D), 1), 6)
    return lane == lax.broadcasted_iota(jnp.int32, (HEADS, D), 0)


def split_pair(v):
    low = lax.broadcasted_iota(jnp.int32, v.shape, 1) < 64
    zero = jnp.zeros_like(v)
    return jnp.concatenate([jnp.where(low, v, zero), jnp.where(low, zero, v)], 0)


def merge_pair(v):
    n = v.shape[0] // 2
    low = lax.broadcasted_iota(jnp.int32, (n, v.shape[1]), 1) < 64
    return jnp.where(low, v[:n], v[n:])


def place():
    s = lax.axis_index("shard")
    r = lax.axis_index("replica")
    x = lax.rem(r, 2)
    z = lax.div(r, 2)
    return s, r, x, z


def peers(s, r):
    sib = s + 1 - 2 * lax.rem(s, 2)
    across = lax.rem(s + 2, 4)
    side = r + 1 - 2 * lax.rem(r, 2)
    return sib, across, side


def rows_loop(n, step, body):
    lax.fori_loop(0, n // step, lambda k, c: (body(at(k, step)), c)[1], 0, unroll=5)


def unpack_vectors(vec, vecf, bias_qkv):
    for v in range(8):
        for s in range(4):
            vecf[v : v + 1, s * 256 : (s + 1) * 256] = vec[s, v : v + 1, :].astype(F32)
    bias_qkv[...] = jnp.zeros_like(bias_qkv)
    for s in range(4):
        for t in range(2):
            col = (s * 2 + t) * 256 + (D if s >= 2 else 0)
            bias_qkv[0:1, col : col + 256] = vec[s, 8 + t : 9 + t, :].astype(F32)


def layer_norm(v, gain, shift):
    c = v - jnp.mean(v, axis=-1, keepdims=True)
    inv = lax.rsqrt(jnp.mean(c * c, axis=-1, keepdims=True) + 1e-06)
    return c * inv * gain + shift


def to_images(src, dst, turn):
    images = (src.shape[0]) // (PATCH + 1)
    main = images * PATCH

    def lane_block(l, carry):
        cols = at(l, 128)
        slot = lax.rem(l, 2)
        turn[slot] = src[0:main, cols].astype(F32)
        for i in range(images):
            dst[i * PATCH : (i + 1) * PATCH, cols] = turn[slot, pl.ds(i, PATCH, stride=images), :].astype(BF16)
        return carry

    lax.fori_loop(0, D // 128, lane_block, 0)
    last = src[main : main + images, :].astype(F32)
    dst[main:, :] = jnp.concatenate([last, jnp.zeros((CLS - images, D), F32)], 0).astype(BF16)


def pack_vectors(vectors, dst):
    row = 0
    for v in vectors:
        count = v.shape[0] // 256
        wide = v[...].astype(F32)
        for k in range(count):
            dst[row : row + 1, :] = wide[k * 256 : (k + 1) * 256].reshape(1, 256)
            row += 1


def attend(i, qkv, qkv_cls, scores, probs, mix, probs_cls, att, att_cls, lse, lse_cls):
    rows = at(i, PATCH)
    mask = head_mask()
    own = qkv_cls[pl.ds(i, 1), :]
    q_c, k_c, v_c = own[:, :D] * FACTOR, own[:, D : 2 * D], own[:, 2 * D :]
    q_bd = jnp.where(mask, q_c, 0.0)
    k_bd = jnp.where(mask, k_c, 0.0).astype(BF16)
    v_bd = jnp.where(mask, v_c, 0.0).astype(BF16)
    to_cls = dot_nt(k_bd, qkv[rows, 0:D]) * FACTOR
    of_cls = dot_nt(q_bd.astype(BF16), qkv[rows, D : 2 * D])
    corner = jnp.sum(q_bd * k_c, axis=1, keepdims=True)
    top = jnp.maximum(jnp.max(of_cls, axis=1, keepdims=True), corner)
    e_row = jnp.exp(of_cls - top)
    e_cor = jnp.exp(corner - top)
    total = jnp.sum(e_row, axis=1, keepdims=True) + e_cor
    inv = 1.0 / total
    row = dot((e_row * inv).astype(BF16), qkv[rows, 2 * D : 3 * D])
    row = row + (e_cor * inv).astype(BF16).astype(F32) * v_c
    att_cls[pl.ds(i, 1), :] = jnp.sum(jnp.where(mask, row, 0.0), axis=0, keepdims=True)
    lse_cls[i] = jnp.broadcast_to(top + jnp.log(total), (HEADS, PATCH))
    for g in range(HEADS // 2):
        q2 = qkv[rows, g * 128 : g * 128 + 128] * jnp.asarray(FACTOR, BF16)
        scores[g] = dot_nt(split_pair(qkv[rows, g * 128 + D : g * 128 + D + 128]), q2)
    for g in range(HEADS // 2):
        for u in range(2):
            h = 2 * g + u
            part = scores[g, u * PATCH : (u + 1) * PATCH, :]
            extra = to_cls[h : h + 1, :]
            top = jnp.maximum(jnp.max(part, axis=0, keepdims=True), extra)
            e_part = jnp.exp(part - top)
            e_extra = jnp.exp(extra - top)
            total = jnp.sum(e_part, axis=0, keepdims=True) + e_extra
            inv = 1.0 / total
            probs[g, u * PATCH : (u + 1) * PATCH, :] = (e_part * inv).astype(BF16)
            probs_cls[h : h + 1, :] = e_extra * inv
            lse[i, h : h + 1, :] = top + jnp.log(total)
    for g in range(HEADS // 2):
        v2 = split_pair(qkv[rows, g * 128 + 2 * D : g * 128 + 2 * D + 128])
        mix[:, g * 128 : g * 128 + 128] = dot_tn(probs[g], v2)
    att[rows, :] = (mix[...] + dot_tn(probs_cls[...].astype(BF16), v_bd)).astype(BF16)


class Gather:
    def __init__(self, number, rows, coop, src, dst, sems, local):
        s, r, x, z = place()
        sib, across, side = peers(s, r)
        self.number, self.sems, self.rows, self.coop = number, sems, rows, coop
        mine = pl.multiple_of(x * coop, 16)
        other = pl.multiple_of((1 - x) * coop, 16)
        rest = rows - 2 * coop
        self.started = []
        self.kinds = {
            "own": (dst(s, 0, rows), dst(s, 0, rows), {"shard": sib}),
            "far": (dst(s, mine, coop), dst(s, mine, coop), {"shard": across}),
            "side": (dst(across, mine, coop), dst(across, mine, coop), {"replica": side}),
            "pass": (dst(across, mine, coop), dst(across, mine, coop), {"shard": sib}),
            "last": (dst(across, other, coop), dst(across, other, coop), {"shard": sib}),
        }
        if rest:
            self.kinds["rest"] = (dst(s, 2 * coop, rest), dst(s, 2 * coop, rest), {"shard": across})
            self.kinds["passrest"] = (dst(across, 2 * coop, rest), dst(across, 2 * coop, rest), {"shard": sib})
        self.names = ["own", "far", "side", "pass", "last", "rest", "passrest"]
        self.local = pltpu.make_async_copy(src(0, rows), dst(s, 0, rows), local.at[number])

    def copy(self, kind):
        a, b, to = self.kinds[kind]
        k = self.names.index(kind)
        return pltpu.make_async_remote_copy(
            a, b, self.sems.at[0, self.number, k], self.sems.at[1, self.number, k], device_id=to, device_id_type=MESH
        )

    def load(self):
        self.local.start()

    def begin(self):
        self.local.wait()
        for kind in ("far", "rest"):
            if kind in self.kinds:
                self.copy(kind).start()
        self.copy("own").start()

    def on_far(self):
        self.copy("far").wait_recv()
        self.copy("side").start()
        self.copy("pass").start()

    def on_rest(self):
        self.copy("rest").wait_recv()
        self.copy("passrest").start()

    def on_side(self):
        self.copy("side").wait_recv()
        self.copy("last").start()

    def ready(self):
        for kind in ("own", "pass", "last", "passrest"):
            if kind in self.kinds:
                self.copy(kind).wait_recv()

    def drain(self):
        for kind in self.kinds:
            self.copy(kind).wait_send()


def gather_kernel(
    tokens, v0, v1, v2, v3, v4, v5, v6, v7, v8, v9, w_qkv, w_out, w_up, w_down,
    qkv_w_o, out_w_o, up_w_o, down_w_o, vec_all, qkv_o, act_o, x_o, att_o, mid_o, branch_o, act2_o, lse_o, lsec_o,
    full_qkv, full_out, full_up, full_down, x_s, qkv, act, att, mid, branch, act2, lse, lsec,
    scores, probs, mix, probs_cls, cls, qkv_cls, turn, vec32, vec_own_s, vec, vecf, bias_qkv,
    sems, local, vsem, osem,
):
    s, r, x, z = place()
    sib, across, side = peers(s, r)
    n = x_s.shape[0]
    images = lse.shape[0]
    main = images * PATCH

    vec32[...] = jnp.zeros_like(vec32)
    pack_vectors((v0, v1, v2, v3, v4, v5, v6, v7, v8, v9), vec32)
    vec_own_s[...] = vec32[...].astype(BF16)
    barrier = pltpu.get_barrier_semaphore()
    for to in ({"shard": sib}, {"shard": across}, {"replica": side}):
        pl.semaphore_signal(barrier, inc=1, device_id=to, device_id_type=MESH)

    def unit(number, rows, coop, src, dst):
        return Gather(number, rows, coop, src, dst, sems, local)

    g_qkv = unit(0, 256, 96, lambda a, k: w_qkv.at[pl.ds(a, k), :],
                 lambda p, a, k: full_qkv.at[pl.ds(pl.multiple_of(p * 256 + a, 16), k), :])
    g_out = unit(1, 256, 128, lambda a, k: w_out.at[pl.ds(a, k), :],
                 lambda p, a, k: full_out.at[pl.ds(pl.multiple_of(p * 256 + a, 16), k), :])

    def up_unit(number, t):
        return unit(number, TILE, 256, lambda a, k: w_up.at[pl.ds(a + t * TILE, k), :],
                    lambda p, a, k: full_up.at[p, pl.ds(pl.multiple_of(a + t * TILE, 16), k), :])

    def down_unit(number, t):
        return unit(number, TILE, 256, lambda a, k: w_down.at[pl.ds(a + t * TILE, k), :],
                    lambda p, a, k: full_down.at[p, pl.ds(pl.multiple_of(a + t * TILE, 16), k), :])

    g_up0, g_down0, g_up1, g_down1 = up_unit(2, 0), down_unit(3, 0), up_unit(4, 1), down_unit(5, 1)

    for g in (g_qkv, g_out, g_up0, g_down0, g_up1, g_down1):
        g.load()
    pl.semaphore_wait(barrier, 3)

    def vec_copy(k, src, slot, to):
        return pltpu.make_async_remote_copy(src, vec.at[slot], vsem.at[0, k], vsem.at[1, k], device_id=to,
                                            device_id_type=MESH)

    vec_own = vec_copy(0, vec_own_s, s, {"shard": sib})
    vec_far = vec_copy(1, vec_own_s, s, {"shard": across})
    vec_pass = vec_copy(2, vec.at[across], across, {"shard": sib})
    vec_own.start()
    vec_far.start()
    g_qkv.begin()
    vec[s] = vec_own_s[...]

    to_images(tokens, x_s, turn)
    outs = []

    def send_out(k, src, dst):
        copy = pltpu.make_async_copy(src, dst, osem.at[k])
        copy.start()
        outs.append(copy)

    send_out(0, x_s, x_o)
    vec_far.wait_recv()
    vec_pass.start()
    vec_own.wait_recv()
    vec_pass.wait_recv()
    unpack_vectors(vec, vecf, bias_qkv)

    def first_norm(rows):
        act[rows, :] = layer_norm(x_s[rows, :].astype(F32), vecf[0:1, :], vecf[1:2, :]).astype(BF16)

    rows_loop(n, 16, first_norm)
    send_out(1, act, act_o)
    g_qkv.on_far()
    g_out.begin()
    g_up0.begin()
    g_qkv.on_rest()
    g_qkv.on_side()
    g_qkv.ready()

    send_out(4, full_qkv, qkv_w_o)

    def qkv_tile(j, carry):
        cols = at(j, TILE)
        low = (dot(act[...], full_qkv[:, cols]) + bias_qkv[0:1, cols]).astype(BF16)
        qkv[:, cols] = low
        qkv_cls[:, cols] = low[main:].astype(F32)
        return carry

    lax.fori_loop(0, 3 * D // TILE, qkv_tile, 0)
    send_out(2, qkv, qkv_o)
    send_out(3, vec, vec_all)
    cls[...] = jnp.zeros_like(cls)
    plan = {0: [g_out.on_far, g_down0.begin, g_out.on_side], 1: [g_up0.on_far, g_up1.begin], 5: [g_down0.on_far, g_down1.begin],
            6: [g_up0.on_side]}

    def image(i, carry):
        for k, steps in plan.items():
            @pl.when(i == k)
            def _(steps=steps):
                for step in steps:
                    step()

        attend(i, qkv, qkv_cls, scores, probs, mix, probs_cls, att, cls, lse, lsec)
        return carry

    lax.fori_loop(0, images, image, 0)
    att[main:, :] = cls[...].astype(BF16)
    send_out(8, att, att_o)
    send_out(9, lse, lse_o)
    send_out(10, lsec, lsec_o)
    g_out.ready()
    for j in range(D // TILE):
        cols = slice(j * TILE, (j + 1) * TILE)
        out = dot(att[...], full_out[:, cols]) + vecf[2:3, cols]
        branch[:, cols] = out.astype(BF16)
        mid[:, cols] = x_s[:, cols].astype(F32) + vecf[3:4, cols] * out
    send_out(11, mid, mid_o)
    send_out(12, branch, branch_o)
    g_down0.on_side()

    def second_norm(rows):
        act2[rows, :] = layer_norm(mid[rows, :], vecf[4:5, :], vecf[5:6, :]).astype(BF16)

    rows_loop(n, 16, second_norm)
    send_out(13, act2, act2_o)
    g_up1.on_far()
    g_up1.on_side()
    g_down1.on_far()
    g_down1.on_side()
    for g in (g_up0, g_down0, g_up1, g_down1):
        g.ready()
    send_out(5, full_out, out_w_o)
    send_out(6, full_up, up_w_o)
    send_out(7, full_down, down_w_o)
    for copy in outs:
        copy.wait()
    for g in (g_qkv, g_out, g_up0, g_down0, g_up1, g_down1):
        g.drain()
    for copy in (vec_own, vec_far, vec_pass):
        copy.wait_send()


class Chunk:
    def __init__(self, index, rows, mine, y_send, y_recv, x_recv, z_recv, far):
        self.index, self.rows, self.mine, self.y_send, self.far = index, rows, mine, y_send, far
        self.y_recv, self.x_recv, self.z_recv = y_recv, x_recv, z_recv


def chunk_layout(nz):
    last = 32 * nz
    sizes = [2048, 2048, 512, 1024, 512, last]
    y_base = 2048
    y_a = y_base
    y_b = y_a + 2048 + last
    mine_base = y_b + 2048
    chunks = []
    mine = mine_base
    late = 0
    xr = zr = 0
    for k, rows in enumerate(sizes):
        if k == 0:
            ys, yr = y_a, 0
        elif k == 1:
            ys, yr = y_b, 2048 + last
        else:
            ys, yr = y_a + late, late
            late += rows
        far = mine_base + sum(sizes) if k == 0 else ys
        chunks.append(Chunk(k, rows, mine, ys, yr, xr, zr, far))
        mine += rows
        xr += rows // 2
        zr += rows // 2 // nz
    return chunks, dict(buf=mine + sizes[0] // 2, total=sum(sizes), mine=mine_base, y_recv=2 * 2048 + last, x_recv=xr, z_recv=zr)


def add_rows(dst, d0, src, s0, rows):
    step = next(k for k in (128, 96, 64, 32, 16) if rows % k == 0)

    def body(k, carry):
        d = pl.ds(pl.multiple_of(d0 + k * step, 16), step)
        t = pl.ds(pl.multiple_of(s0 + k * step, 16), step)
        dst[d, :] = (dst[d, :].astype(F32) + src[t, :].astype(F32)).astype(BF16)
        return carry

    lax.fori_loop(0, rows // step, body, 0)


class Reduce:
    def __init__(self, nz, buf, core_recv, y_recv, x_recv, z_recv, sems, core_sems, credit):
        self.nz, self.buf, self.core_recv = nz, buf, core_recv
        self.y_recv, self.x_recv, self.z_recv = y_recv, x_recv, z_recv
        self.sems, self.core_sems, self.credit = sems, core_sems, credit
        self.s, self.r, self.x, self.z = place()
        self.sib, self.across, self.side = peers(self.s, self.r)

    def remote(self, src, dst, chunk, kind, to):
        return pltpu.make_async_remote_copy(
            src, dst, self.sems.at[0, chunk.index, kind], self.sems.at[1, chunk.index, kind], device_id=to,
            device_id_type=MESH)

    def peer(self, k):
        return {"replica": lax.rem(self.z + k, self.nz) * 2 + self.x}

    def core_copy(self, turn, rows):
        slot = turn % 2
        return pltpu.make_async_remote_copy(
            self.buf.at[pl.ds(0, rows), :], self.core_recv.at[slot, pl.ds(0, rows), :],
            self.core_sems.at[0, turn], self.core_sems.at[1, turn], device_id={"shard": self.sib}, device_id_type=MESH)

    def add_core(self, turn, first, dst, rows):
        add_rows(self.buf, dst, self.core_recv.at[turn % 2], first, rows)

    def y_copy(self, c):
        return self.remote(self.buf.at[pl.ds(c.y_send, c.rows), :], self.y_recv.at[pl.ds(c.y_recv, c.rows), :], c, 0,
                           {"shard": self.across})

    def x_copy(self, c):
        half = c.rows // 2
        return self.remote(self.buf.at[pl.ds(pl.multiple_of(c.mine + (1 - self.x) * half, 16), half), :],
                           self.x_recv.at[pl.ds(c.x_recv, half), :], c, 1, {"replica": self.side})

    def quarter(self, c, x, z):
        half = c.rows // 2
        size = half // self.nz
        return pl.ds(pl.multiple_of(c.mine + x * half + z * size, 16), size)

    def z_copy(self, c, k):
        size = c.rows // 2 // self.nz
        return self.remote(self.buf.at[self.quarter(c, self.x, lax.rem(self.z + k, self.nz)), :],
                           self.z_recv.at[k - 1, pl.ds(c.z_recv, size), :], c, 1 + k, self.peer(k))

    def done(self, first, c, z):
        size = c.rows // 2 // self.nz
        return pl.ds(pl.multiple_of(first + z * size, 16), size)

    def back_z(self, c, k):
        part = self.x_recv.at[self.done(c.x_recv, c, self.z), :]
        return self.remote(part, part, c, self.nz + k, self.peer(k))

    def back_x(self, c, k):
        z = lax.rem(self.z + self.nz - k, self.nz)
        return self.remote(self.x_recv.at[self.done(c.x_recv, c, z), :], self.buf.at[self.done(c.far, c, z), :], c,
                           2 * self.nz + k, {"replica": self.side})

    def on_y(self, c):
        self.y_copy(c).wait_recv()
        add_rows(self.buf, c.mine, self.y_recv, c.y_recv, c.rows)
        self.y_copy(c).wait_send()
        self.x_copy(c).start()

    def on_x(self, c):
        half = c.rows // 2
        self.x_copy(c).wait_recv()
        add_rows(self.buf, c.mine + self.x * half, self.x_recv, c.x_recv, half)
        for k in range(1, self.nz):
            self.z_copy(c, k).start()

    def on_z(self, c):
        size = c.rows // 2 // self.nz
        start = c.mine + self.x * (c.rows // 2) + self.z * size
        for k in range(1, self.nz):
            self.z_copy(c, k).wait_recv()
        step = next(k for k in (64, 48, 32, 16) if size % k == 0)

        def body(i, carry):
            d = pl.ds(pl.multiple_of(start + i * step, 16), step)
            total = self.buf[d, :].astype(F32)
            for k in range(1, self.nz):
                total = total + self.z_recv[k - 1, pl.ds(pl.multiple_of(c.z_recv + i * step, 16), step), :].astype(F32)
            to = pl.ds(pl.multiple_of(c.x_recv + self.z * size + i * step, 16), step)
            self.x_recv[to, :] = total.astype(BF16)
            return carry

        lax.fori_loop(0, size // step, body, 0)
        for k in range(1, self.nz):
            self.back_z(c, k).start()
        self.back_x(c, 0).start()

    def on_back(self, c):
        for k in range(1, self.nz):
            self.back_z(c, k).wait_recv()
            self.back_x(c, k).start()

    def finish(self, c):
        for k in range(self.nz):
            self.back_x(c, k).wait_recv()

    def drain(self, c):
        self.x_copy(c).wait_send()
        for k in range(1, self.nz):
            self.z_copy(c, k).wait_send()
            self.back_z(c, k).wait_send()
        for k in range(self.nz):
            self.back_x(c, k).wait_send()


def fold(v):
    return jnp.sum(v.reshape(v.shape[0] // 8, 8, v.shape[1]), axis=0)


def gelu_both(v):
    e = jnp.exp(-0.5 * v * v)
    t = 1.0 / (1.0 + 0.23164189 * jnp.abs(v))
    poly = ((((1.061405429 * t - 1.453152027) * t + 1.421413741) * t - 0.284496736) * t + 0.254829592) * t
    tail = 0.5 * poly * e
    phi = jnp.where(v >= 0.0, 1.0 - tail, tail)
    return v * phi, phi + v * e * 0.3989422804014327


def transpose_into(src, dst):
    for c in range(D // 128):
        dst[c * 128 : (c + 1) * 128, :] = src[:, c * 128 : (c + 1) * 128].T


def attend_back(i, qkv, qkv_cls, datt, datt_cls, lse, lsec, scores, dprobs, probs, dscores, cls_row, joint_cls, sum_q, sum_v):
    rows = at(i, PATCH)
    mask = head_mask()
    own = qkv_cls[pl.ds(i, 1), :]
    do_c = datt_cls[pl.ds(i, 1), :]
    q_c, k_c, v_c = own[:, :D] * FACTOR, own[:, D : 2 * D], own[:, 2 * D :]
    pick = lambda v: jnp.where(mask, v, 0.0)
    q_w, k_w, v_w, do_w = pick(q_c), pick(k_c), pick(v_c), pick(do_c)
    q_bd, k_bd, v_bd, do_bd = (v.astype(BF16) for v in (q_w, k_w, v_w, do_w))
    queries, keys, values = (qkv[rows, k * D : (k + 1) * D] for k in range(3))
    grads = datt[rows, :]
    low = lambda v: v.astype(BF16)
    top = lsec[i][:, 0:1]
    p_row = jnp.exp(dot_nt(q_bd, keys) - top)
    p_cor = jnp.exp(jnp.sum(q_w * k_c, axis=1, keepdims=True) - top)
    dp_row = dot_nt(do_bd, values)
    dp_cor = jnp.sum(do_w * v_c, axis=1, keepdims=True)
    delta = jnp.sum(p_row * dp_row, axis=1, keepdims=True) + p_cor * dp_cor
    ds_row = low(p_row * (dp_row - delta))
    ds_cor = low(p_cor * (dp_cor - delta)).astype(F32)
    p_col = jnp.exp(dot_nt(k_bd, queries) * FACTOR - lse[i])
    dp_col = dot_nt(v_bd, grads)
    for g in range(HEADS // 2):
        lanes = slice(g * 128, (g + 1) * 128)
        q2 = qkv[rows, lanes] * jnp.asarray(FACTOR, BF16)
        scores[g] = dot_nt(split_pair(qkv[rows, g * 128 + D : g * 128 + D + 128]), q2)
        dprobs[g] = dot_nt(split_pair(qkv[rows, g * 128 + 2 * D : g * 128 + 2 * D + 128]), datt[rows, lanes])
    for g in range(HEADS // 2):
        for u in range(2):
            h = 2 * g + u
            half = slice(u * PATCH, (u + 1) * PATCH)
            part = jnp.exp(scores[g, half, :] - lse[i, h : h + 1, :])
            dpart = dprobs[g, half, :]
            p_h, dp_h = p_col[h : h + 1, :], dp_col[h : h + 1, :]
            delta = jnp.sum(part * dpart, axis=0, keepdims=True) + p_h * dp_h
            probs[g, half, :] = low(part)
            dscores[g, half, :] = low(part * (dpart - delta))
            cls_row[h : h + 1, :] = p_h * (dp_h - delta)
    ds_col = low(cls_row[...])
    total = lambda v: jnp.sum(jnp.where(mask, v, 0.0), axis=0, keepdims=True)
    joint_cls[pl.ds(i, 1), 0:D] = FACTOR * (total(dot(ds_row, keys)) + jnp.sum(ds_cor * k_w, axis=0, keepdims=True))
    joint_cls[pl.ds(i, 1), D : 2 * D] = FACTOR * total(dot(ds_col, queries)) + jnp.sum(ds_cor * q_w, axis=0, keepdims=True)
    joint_cls[pl.ds(i, 1), 2 * D : 3 * D] = total(dot(low(p_col), grads)) + jnp.sum(
        low(p_cor).astype(F32) * do_w, axis=0, keepdims=True)
    p_row = low(p_row)
    for g in range(HEADS // 2):
        lanes = slice(g * 128, (g + 1) * 128)
        klanes = slice(g * 128 + D, g * 128 + D + 128)
        vlanes = slice(g * 128 + 2 * D, g * 128 + 2 * D + 128)
        q2 = qkv[rows, lanes] * jnp.asarray(FACTOR, BF16)
        dv = merge_pair(dot(probs[g], datt[rows, lanes])) + dot_tn(p_row, do_bd[:, lanes])
        dk = merge_pair(dot(dscores[g], q2)) + dot_tn(ds_row, q_bd[:, lanes])
        dq = (dot_tn(dscores[g], split_pair(qkv[rows, klanes])) + dot_tn(ds_col, k_bd[:, lanes])) * FACTOR
        qkv[rows, lanes] = low(dq)
        qkv[rows, klanes] = low(dk)
        qkv[rows, vlanes] = low(dv)
        sum_q[:, lanes] += fold(dq)
        sum_v[:, lanes] += fold(dv)


def to_tokens(src, dst, turn):
    images = dst.shape[0] // (PATCH + 1)
    main = images * PATCH

    def lane_block(l, carry):
        cols = at(l, 128)
        slot = lax.rem(l, 2)
        for i in range(images):
            turn[slot, pl.ds(i, PATCH, stride=images), :] = src[i * PATCH : (i + 1) * PATCH, cols].astype(F32)
        dst[0:main, cols] = turn[slot].astype(BF16)
        return carry

    lax.fori_loop(0, D // 128, lane_block, 0)
    dst[main : main + images, :] = src[main:, :].astype(F32)[0:images].astype(BF16)


def backward_kernel(
    nz, chunks, cot, vec, full_qkv, full_out, full_up, full_down, qkv_h, act_h, x_h, att_h, mid_h, branch_h, act2_h, lse_h,
    lsec_h,
    result_o, tokens_o, sums_o, hidden_o,
    buf, core_recv, y_recv, x_recv, z_recv, gmid, up_s, acc, sums_up, vecf, bias_qkv, bias_up, vrows,
    sems, core_sems, credit, dsem, wsem, hsem, osem, fsem,
):
    images = cot.shape[0] // (PATCH + 1)
    n = gmid.shape[0]
    main = images * PATCH
    red = Reduce(nz, buf, core_recv, y_recv, x_recv, z_recv, sems, core_sems, credit)
    s = red.s
    ca, cb, co, cq0, cq1, cv = chunks
    barrier = pltpu.get_barrier_semaphore()
    partners = [{"shard": red.sib}, {"shard": red.across}, {"replica": red.side}] + [red.peer(k) for k in range(1, nz)]
    for to in partners:
        pl.semaphore_signal(barrier, inc=1, device_id=to, device_id_type=MESH)
    pl.semaphore_wait(barrier, len(partners))

    unpack_vectors(vec, vecf, bias_qkv)
    for p in range(4):
        for t in range(2):
            for k in range(2):
                row = 10 + 2 * t + k
                bias_up[2 * p + t : 2 * p + t + 1, k * 256 : (k + 1) * 256] = vec[p, row : row + 1, :].astype(F32)
    acc[...] = jnp.zeros_like(acc)
    gmid[...] = jnp.zeros_like(gmid)
    for start in (0, cv.rows, cv.y_send, cv.mine):
        buf[pl.ds(start, cv.rows), :] = jnp.zeros((cv.rows, TILE), BF16)

    def load(k, src, dst):
        copy = pltpu.make_async_copy(src, dst, dsem.at[k])
        copy.start()
        return copy

    def relative(rel):
        low, high = lax.rem(rel, 2), lax.div(rel, 2)
        return s + low * (1 - 2 * lax.rem(s, 2)) + high * (2 - 4 * lax.div(s, 2))

    def target(rel, chunk):
        low, high = lax.rem(rel, 2), lax.div(rel, 2)
        return low * (1 - high) * chunk.rows + (1 - low) * (high * chunk.y_send + (1 - high) * chunk.mine)

    def ffn(dr, dr_t, act2, act2_t, w_up, w_down, hid, slope, br, turn):
        got = load(0, act2_h, act2)

        def fetch(j, slot):
            piece, t = relative(3 - 2 * lax.div(j, 4) - lax.rem(j, 2)), lax.rem(lax.div(j, 2), 2)
            return (
                pltpu.make_async_copy(full_up.at[piece, :, at(t, TILE)], w_up.at[slot], wsem.at[0, slot]),
                pltpu.make_async_copy(full_down.at[piece, at(t, TILE), :], w_down.at[slot], wsem.at[1, slot]),
            )

        def keep(j, slot):
            return pltpu.make_async_copy(hid.at[slot], hidden_o.at[j], hsem.at[slot])

        for copy in fetch(0, 0):
            copy.start()
        to_images(cot, up_s, turn)

        def down_rows(rows):
            g = up_s[rows, :].astype(F32) * vecf[7:8, :]
            acc[6] += fold(g)
            dr[rows, :] = g.astype(BF16)

        rows_loop(n, 16, down_rows)
        transpose_into(dr, dr_t)
        got.wait()
        transpose_into(act2, act2_t)

        def tile(j, carry):
            slot = lax.rem(j, 2)
            rel, t = 3 - 2 * lax.div(j, 4) - lax.rem(j, 2), lax.rem(lax.div(j, 2), 2)
            piece = relative(rel)
            low, high = lax.rem(rel, 2), lax.div(rel, 2)
            place_at = pl.multiple_of(
                (1 - low) * (high * (ca.y_send + t * (cb.y_send - ca.y_send)) + (1 - high) * (ca.mine + t * ca.rows)), 16)
            for copy in fetch(j, slot):
                copy.wait()

            @pl.when(j < 7)
            def _():
                for copy in fetch(j + 1, 1 - slot):
                    copy.start()

            @pl.when(j >= 2)
            def _():
                keep(j - 2, slot).wait()

            for k in (2, 4, 6):
                @pl.when(j == k)
                def _(k=k):
                    red.core_copy(k // 2 - 1, 2048).wait_send()

            before = dot(act2[...], w_up[slot]) + bias_up[pl.ds(2 * piece + t, 1), :]
            hidden, step = gelu_both(before)
            hid[slot] = hidden.astype(BF16)
            slope[...] = step
            keep(j, slot).start()
            buf[pl.ds(place_at, D), :] = dot(dr_t[...], hid[slot]).astype(BF16)
            grad = dot_nt(dr[...], w_down[slot]) * slope[...]
            sums_up[pl.ds(2 * piece + t, 1), :] = jnp.sum(grad, axis=0, keepdims=True)
            br[...] = grad.astype(BF16)
            buf[pl.ds(pl.multiple_of(place_at + D, 16), D), :] = dot(act2_t[...], br[...]).astype(BF16)
            gmid[...] += dot_nt(br[...], w_up[slot])
            for k in (0, 2, 4, 6):
                @pl.when(j == k)
                def _(k=k):
                    red.core_copy(k // 2, 2048).start()
            for k, chunk in ((1, ca), (3, cb)):
                @pl.when(j == k)
                def _(k=k, chunk=chunk):
                    red.core_copy(k // 2, 2048).wait_recv()
                    red.add_core(k // 2, 0, chunk.y_send, chunk.rows)
                    red.y_copy(chunk).start()
            for k, chunk in ((5, ca), (7, cb)):
                @pl.when(j == k)
                def _(k=k, chunk=chunk):
                    red.core_copy(k // 2, 2048).wait_recv()
                    red.add_core(k // 2, 0, chunk.mine, chunk.rows)
            return carry

        lax.fori_loop(0, 8, tile, 0)
        for j in (6, 7):
            keep(j, j % 2).wait()
        red.core_copy(3, 2048).wait_send()

    v = pltpu.VMEM
    pl.run_scoped(ffn, v((n, D), BF16), v((D, n), BF16), v((n, D), BF16), v((D, n), BF16), v((2, D, TILE), BF16),
                  v((2, TILE, D), BF16), v((2, n, TILE), BF16), v((n, TILE), F32), v((n, TILE), BF16),
                  v((2, main, 128), F32))

    def spread(out, chunk, tile_rows):
        for p in range(4):
            low = lax.rem(lax.rem(s, 2) + p % 2, 2)
            high = lax.rem(lax.div(s, 2) + p // 2, 2)
            start = pl.multiple_of(target(low + 2 * high, chunk) + tile_rows, 16)
            buf[pl.ds(start, 256), :] = out[p * 256 : (p + 1) * 256].astype(BF16)

    def on_core(turn, chunk):
        red.core_copy(turn, 2 * chunk.rows).wait_recv()
        red.add_core(turn, 0, chunk.y_send, chunk.rows)
        red.y_copy(chunk).start()
        red.add_core(turn, chunk.rows, chunk.mine, chunk.rows)

    def attention(qkv, datt, brr, lse, lsec, scores, dprobs, probs, dscores, cls_row, qkv_cls, datt_cls, joint_cls):
        got_qkv, got_lse, got_lsec = load(0, qkv_h, qkv), load(1, lse_h, lse), load(2, lsec_h, lsec)

        def middle(mid, branch, att, att_t, w_out):
            got_mid, got_branch = load(3, mid_h, mid), load(4, branch_h, branch)
            got_att, got_out = load(5, att_h, att), load(6, full_out, w_out)
            got_mid.wait()
            got_branch.wait()

            def norm_rows(rows):
                m = mid[rows, :]
                c = m - jnp.mean(m, axis=-1, keepdims=True)
                inv = lax.rsqrt(jnp.mean(c * c, axis=-1, keepdims=True) + 1e-06)
                hat = c * inv
                g = gmid[rows, :]
                acc[4] += fold(g * hat)
                acc[5] += fold(g)
                sc = g * vecf[4:5, :]
                back = inv * (sc - jnp.mean(sc, axis=-1, keepdims=True)
                              - hat * jnp.mean(sc * hat, axis=-1, keepdims=True))
                gm = up_s[rows, :].astype(F32) + back
                gmid[rows, :] = gm
                acc[3] += fold(gm * branch[rows, :].astype(F32))
                gb = gm * vecf[3:4, :]
                acc[2] += fold(gb)
                brr[rows, :] = gb.astype(BF16)

            rows_loop(n, 16, norm_rows)
            red.on_y(ca)
            pl.semaphore_signal(credit, inc=1, device_id={"shard": red.across}, device_id_type=MESH)
            got_att.wait()
            transpose_into(att, att_t)
            for q in range(2):
                spread(dot(att_t[...], brr[:, q * TILE : (q + 1) * TILE]), co, q * 256)
            red.core_copy(4, 2 * co.rows).start()
            got_out.wait()
            for q in range(2):
                datt[:, q * TILE : (q + 1) * TILE] = dot_nt(brr[...], w_out[q * TILE : (q + 1) * TILE, :]).astype(BF16)

        pl.run_scoped(middle, v((n, D), F32), v((n, D), BF16), v((n, D), BF16), v((D, n), BF16), v((D, D), BF16))
        got_qkv.wait()
        got_lse.wait()
        got_lsec.wait()
        qkv_cls[...] = qkv[main:, :].astype(F32)
        datt_cls[...] = datt[main:, :].astype(F32)
        joint_cls[...] = jnp.zeros_like(joint_cls)
        pl.semaphore_wait(credit, 1)
        on_core(4, co)
        plan = {5: [lambda: red.on_x(ca)]}

        def image(i, carry):
            for k, steps in plan.items():
                @pl.when(i == k)
                def _(steps=steps):
                    for step in steps:
                        step()

            attend_back(i, qkv, qkv_cls, datt, datt_cls, lse, lsec, scores, dprobs, probs, dscores, cls_row, joint_cls,
                        acc.at[8], acc.at[9])
            return carry

        lax.fori_loop(0, images, image, 0)
        qkv[main:, :] = joint_cls[...].astype(BF16)
        acc[8] += fold(joint_cls[:, 0:D])
        acc[9] += fold(joint_cls[:, 2 * D : 3 * D])

        def tail(act_t, gact, w_qkv, turn, flat):
            act, x_s = datt, brr
            got_act, got_x = load(3, act_h, act), load(4, x_h, x_s)

            def fetch(j):
                return pltpu.make_async_copy(full_qkv.at[pl.ds(j * 256, 256), :], w_qkv.at[j % 2], wsem.at[0, j % 2])

            fetch(0).start()
            fetch(1).start()
            got_act.wait()
            transpose_into(act, act_t)
            red.core_copy(4, 2 * co.rows).wait_send()
            for q in range(4):
                spread(dot(act_t[...], qkv[:, q * TILE : (q + 1) * TILE]), cq0, q * 256)
            red.core_copy(5, 2 * cq0.rows).start()
            red.on_z(ca)
            for j in range(4):
                fetch(j).wait()
                gact[:, j * 256 : (j + 1) * 256] = dot_nt(qkv[...], w_qkv[j % 2])
                if j < 2:
                    fetch(j + 2).start()
            red.on_y(cb)
            on_core(5, cq0)
            red.core_copy(5, 2 * cq0.rows).wait_send()
            for q in range(2):
                spread(dot(act_t[...], qkv[:, (q + 4) * TILE : (q + 5) * TILE]), cq1, q * 256)
            red.core_copy(6, 2 * cq1.rows).start()
            got_x.wait()

            def norm_rows(rows):
                m = x_s[rows, :].astype(F32)
                c = m - jnp.mean(m, axis=-1, keepdims=True)
                inv = lax.rsqrt(jnp.mean(c * c, axis=-1, keepdims=True) + 1e-06)
                hat = c * inv
                g = gact[rows, :]
                acc[0] += fold(g * hat)
                acc[1] += fold(g)
                sc = g * vecf[0:1, :]
                back = inv * (sc - jnp.mean(sc, axis=-1, keepdims=True)
                              - hat * jnp.mean(sc * hat, axis=-1, keepdims=True))
                x_s[rows, :] = (gmid[rows, :] + back).astype(BF16)

            rows_loop(n, 16, norm_rows)
            on_core(6, cq1)
            red.core_copy(6, 2 * cq1.rows).wait_send()
            to_tokens(x_s, flat, turn)
            copy = pltpu.make_async_copy(flat, tokens_o, osem.at[0])
            copy.start()
            red.on_back(ca)
            red.on_x(cb)
            copy.wait()

        pl.run_scoped(tail, v((D, n), BF16), v((n, D), F32), v((2, 256, 3 * D), BF16),
                      v((2, main, 128), F32), v((main + images, D), BF16))

    pl.run_scoped(attention, v((n, 3 * D), BF16), v((n, D), BF16), v((n, D), BF16), v((images, HEADS, PATCH), F32),
                  v((images, HEADS, PATCH), F32), v((8, 256, PATCH), F32), v((8, 256, PATCH), F32),
                  v((8, 256, PATCH), BF16), v((8, 256, PATCH), BF16), v((HEADS, PATCH), F32), v((CLS, 3 * D), F32),
                  v((CLS, D), F32), v((CLS, 3 * D), F32))

    def outcome(mid, hid, w_down, turn, flat, res):
        got_mid = load(3, mid_h, mid)

        def fetch(j, slot):
            piece, t = relative(3 - 2 * lax.div(j, 4) - lax.rem(j, 2)), lax.rem(lax.div(j, 2), 2)
            return (
                pltpu.make_async_copy(hidden_o.at[j], hid.at[slot], wsem.at[0, slot]),
                pltpu.make_async_copy(full_down.at[piece, at(t, TILE), :], w_down.at[slot], wsem.at[1, slot]),
            )

        for copy in fetch(0, 0):
            copy.start()
        gmid[...] = jnp.zeros_like(gmid)

        def tile(j, carry):
            slot = lax.rem(j, 2)
            for copy in fetch(j, slot):
                copy.wait()

            @pl.when(j < 7)
            def _():
                for copy in fetch(j + 1, 1 - slot):
                    copy.start()

            gmid[...] += dot(hid[slot], w_down[slot])
            return carry

        lax.fori_loop(0, 8, tile, 0)
        got_mid.wait()

        def rows_of(rows):
            projected = gmid[rows, :] + vecf[6:7, :]
            acc[7] += fold(up_s[rows, :].astype(F32) * projected)
            res[rows, :] = (mid[rows, :] + vecf[7:8, :] * projected).astype(BF16)

        rows_loop(n, 16, rows_of)
        for p in range(4):
            vrows[...] = jnp.zeros_like(vrows)
            for k in range(8):
                vrows[k : k + 1, 0:256] = jnp.sum(acc[k, :, p * 256 : (p + 1) * 256], axis=0, keepdims=True)
            joint = acc.at[8 + p // 2]
            for k in range(2):
                first = (p % 2) * TILE + k * 256
                vrows[8 + k : 9 + k, 0:256] = jnp.sum(joint[:, first : first + 256], axis=0, keepdims=True)
            for k in range(4):
                vrows[10 + k : 11 + k, 0:256] = sums_up[2 * p + k // 2 : 2 * p + k // 2 + 1, (k % 2) * 256 : (k % 2 + 1) * 256]
            low = lax.rem(lax.rem(s, 2) + p % 2, 2)
            high = lax.rem(lax.div(s, 2) + p // 2, 2)
            buf[pl.ds(pl.multiple_of(target(low + 2 * high, cv), 16), 16), :] = vrows[...].astype(BF16)
        red.core_copy(7, 2 * cv.rows).start()
        to_tokens(res, flat, turn)
        copy = pltpu.make_async_copy(flat, result_o, osem.at[0])
        copy.start()
        on_core(7, cv)
        red.on_z(cb)
        for c in (co, cq0):
            red.on_y(c)
        red.on_x(co)
        red.on_x(cq0)
        red.on_y(cq1)
        red.on_y(cv)
        red.on_z(co)
        red.on_z(cq0)
        red.on_back(cb)
        red.on_x(cq1)
        red.on_x(cv)
        red.on_back(co)
        red.on_back(cq0)
        red.on_z(cq1)
        red.on_z(cv)
        red.on_back(cq1)
        red.on_back(cv)
        copy.wait()

    pl.run_scoped(outcome, v((n, D), F32), v((2, n, TILE), BF16), v((2, TILE, D), BF16), v((2, main, 128), F32),
                  v((main + images, D), BF16), v((n, D), BF16))
    copies = []
    for c in chunks:
        red.finish(c)
        half = c.rows // 2
        for k, (src, first, where) in enumerate(((x_recv, c.x_recv, red.x), (buf, c.far, 1 - red.x))):
            copy = pltpu.make_async_copy(
                src.at[pl.ds(first, half), :],
                sums_o.at[pl.ds(pl.multiple_of(c.mine - ca.mine + where * half, 16), half), :], fsem.at[2 * c.index + k])
            copy.start()
            copies.append(copy)
    red.core_copy(7, 2 * cv.rows).wait_send()
    for c in chunks:
        red.drain(c)
    for copy in copies:
        copy.wait()


def low_shape(*shape):
    return jax.ShapeDtypeStruct(shape, BF16)


def wide_shape(*shape):
    return jax.ShapeDtypeStruct(shape, F32)


ANY = pl.BlockSpec(memory_space=pl.ANY)
VMEM = pl.BlockSpec(memory_space=pltpu.VMEM)
LIMIT = 62 * 2**20


def forward(flat, vectors, w_qkv, w_out, w_up, w_down):
    images = flat.shape[0] // (PATCH + 1)
    n = images * PATCH + CLS
    v = pltpu.VMEM
    outs = (
        low_shape(D, 3 * D), low_shape(D, D), low_shape(4, D, D), low_shape(4, D, D), low_shape(4, 16, 256),
        low_shape(n, 3 * D), low_shape(n, D), low_shape(n, D), low_shape(n, D), wide_shape(n, D), low_shape(n, D),
        low_shape(n, D), wide_shape(images, HEADS, PATCH), wide_shape(images, HEADS, PATCH),
    )
    return pl.pallas_call(
        gather_kernel,
        out_shape=outs,
        in_specs=[VMEM] * 11 + [ANY] * 4,
        out_specs=[ANY] * len(outs),
        scratch_shapes=[
            v((D, 3 * D), BF16), v((D, D), BF16), v((4, D, D), BF16), v((4, D, D), BF16),
            v((n, D), BF16), v((n, 3 * D), BF16), v((n, D), BF16), v((n, D), BF16), v((n, D), F32), v((n, D), BF16),
            v((n, D), BF16), v((images, HEADS, PATCH), F32), v((images, HEADS, PATCH), F32),
            v((8, 256, PATCH), F32), v((8, 256, PATCH), BF16), v((PATCH, D), F32), v((HEADS, PATCH), F32),
            v((CLS, D), F32), v((CLS, 3 * D), F32), v((2, images * PATCH, 128), F32), v((16, 256), F32),
            v((16, 256), BF16), v((4, 16, 256), BF16), v((16, D), F32), v((8, 3 * D), F32),
            pltpu.SemaphoreType.DMA((2, 6, 7)), pltpu.SemaphoreType.DMA((6,)), pltpu.SemaphoreType.DMA((2, 3)),
            pltpu.SemaphoreType.DMA((14,)),
        ],
        compiler_params=pltpu.CompilerParams(collective_id=0, has_side_effects=True, vmem_limit_bytes=LIMIT),
        cost_estimate=pl.CostEstimate(flops=18 * 2**30, bytes_accessed=64 * 2**20, transcendentals=3 * 2**20),
        name="gather_and_attention",
    )(flat, *vectors, w_qkv, w_out, w_up, w_down)


def backward(nz, cot, vec, *arrays):
    images = cot.shape[0] // (PATCH + 1)
    n = images * PATCH + CLS
    v = pltpu.VMEM
    chunks, sizes = chunk_layout(nz)
    outs = (low_shape(cot.shape[0], D), low_shape(cot.shape[0], D), low_shape(sizes["total"], TILE),
            low_shape(8, n, TILE))
    return pl.pallas_call(
        functools.partial(backward_kernel, nz, chunks),
        out_shape=outs,
        in_specs=[VMEM] * 2 + [ANY] * len(arrays),
        out_specs=[ANY] * len(outs),
        scratch_shapes=[
            v((sizes["buf"], TILE), BF16), v((2, 2048, TILE), BF16), v((sizes["y_recv"], TILE), BF16),
            v((sizes["x_recv"], TILE), BF16), v((nz - 1, sizes["z_recv"], TILE), BF16), v((n, D), F32), v((n, D), BF16),
            v((10, 8, D), F32), v((8, TILE), F32), v((16, D), F32), v((8, 3 * D), F32), v((8, TILE), F32),
            v((16, TILE), F32),
            pltpu.SemaphoreType.DMA((2, len(chunks), 3 * nz)), pltpu.SemaphoreType.DMA((2, 8)),
            pltpu.SemaphoreType.REGULAR, pltpu.SemaphoreType.DMA((7,)), pltpu.SemaphoreType.DMA((2, 2)),
            pltpu.SemaphoreType.DMA((2,)), pltpu.SemaphoreType.DMA((1,)), pltpu.SemaphoreType.DMA((2 * len(chunks),)),
        ],
        compiler_params=pltpu.CompilerParams(collective_id=1, has_side_effects=True, vmem_limit_bytes=LIMIT),
        cost_estimate=pl.CostEstimate(flops=66 * 2**30, bytes_accessed=128 * 2**20, transcendentals=8 * 2**20),
        name="layer_backward",
    )(cot, vec, *arrays), chunks


def on_device(
    tokens, norm1_gain, norm1_shift, w_qkv, bias_qv, w_out, bias_out, scale_one, norm2_gain, norm2_shift, w_up, bias_up,
    w_down, bias_down, scale_two, cotangent,
):
    images, length, _ = tokens.shape
    nz = lax.axis_size("replica") // 2
    flatten = lambda a: jnp.transpose(a, (1, 0, 2)).reshape(images * length, D)
    restore = lambda a: jnp.transpose(a.reshape(length, images, D), (1, 0, 2))
    vectors = (norm1_gain, norm1_shift, bias_out, scale_one, norm2_gain, norm2_shift, bias_down, scale_two, bias_qv, bias_up)
    full_qkv, full_out, full_up, full_down, vec, qkv, act, x_s, att, mid, branch, act2, lse, lsec = forward(
        flatten(tokens), vectors, w_qkv, w_out, w_up, w_down)
    (result, grad_tokens, sums, _), chunks = backward(
        nz, flatten(cotangent), vec, full_qkv, full_out, full_up, full_down, qkv, act, x_s, att, mid, branch, act2, lse, lsec)
    base = chunks[0].mine
    rows = lambda c, first, count: sums[c.mine - base + first : c.mine - base + first + count]
    ca, cb, co, cq0, cq1, cv = chunks
    grad_down = jnp.concatenate([rows(ca, 0, D), rows(cb, 0, D)], axis=1).T.astype(F32)
    grad_up = jnp.concatenate([rows(ca, D, D), rows(cb, D, D)], axis=1).astype(F32)
    grad_out = jnp.moveaxis(rows(co, 0, 512).reshape(2, 256, TILE), 0, 1).reshape(256, D).astype(F32)
    grad_qkv = jnp.moveaxis(sums[cq0.mine - base : cq0.mine - base + 1536].reshape(6, 256, TILE), 0, 1)
    grad_qkv = grad_qkv.reshape(256, 3 * D).astype(F32)
    small = rows(cv, 0, 16)[:, :256].astype(F32)
    part = lambda first, count=1: small[first : first + count].reshape(-1)
    return (
        restore(result), restore(grad_tokens), part(0), part(1), grad_qkv, part(8, 2), grad_out, part(2), part(3), part(4),
        part(5), grad_up, part(10, 4), grad_down, part(6), part(7),
    )


def solution(mesh):
    placed = (
        P(("shard", "replica"), None, None),
        P("shard"),
        P("shard"),
        P("shard", None),
        P("shard"),
        P("shard", None),
        P("shard"),
        P("shard"),
        P("shard"),
        P("shard"),
        P(None, "shard"),
        P("shard"),
        P("shard", None),
        P("shard"),
        P("shard"),
        P(("shard", "replica"), None, None),
    )
    return jax.shard_map(
        on_device,
        mesh=mesh,
        in_specs=placed,
        out_specs=(
            P(("shard", "replica"), None, None),
            P(("shard", "replica"), None, None),
            P("shard"),
            P("shard"),
            P("shard", None),
            P("shard"),
            P("shard", None),
            P("shard"),
            P("shard"),
            P("shard"),
            P("shard"),
            P(None, "shard"),
            P("shard"),
            P("shard", None),
            P("shard"),
            P("shard"),
        ),
        check_vma=False,
    )
```

```python
import functools

import jax
import jax.numpy as jnp
from jax import lax
from jax.experimental import pallas as pl
from jax.experimental.pallas import tpu as pltpu
from jax.sharding import PartitionSpec as P

F32 = jnp.float32
BF16 = jnp.bfloat16
D = 1024
FF = 4096
HEADS = 16
PATCH = 128
CLS = 16
TILE = 512
FACTOR = 0.125
MESH = pl.DeviceIdType.MESH


def dot(a, b):
    return jnp.dot(a, b, preferred_element_type=F32)


def dot_nt(a, b):
    return lax.dot_general(a, b, (((1,), (1,)), ((), ())), preferred_element_type=F32)


def dot_tn(a, b):
    return lax.dot_general(a, b, (((0,), (0,)), ((), ())), preferred_element_type=F32)


def at(index, size):
    return pl.ds(pl.multiple_of(index * size, size), size)


def head_mask():
    lane = lax.shift_right_logical(lax.broadcasted_iota(jnp.int32, (HEADS, D), 1), 6)
    return lane == lax.broadcasted_iota(jnp.int32, (HEADS, D), 0)


def split_pair(v):
    low = lax.broadcasted_iota(jnp.int32, v.shape, 1) < 64
    zero = jnp.zeros_like(v)
    return jnp.concatenate([jnp.where(low, v, zero), jnp.where(low, zero, v)], 0)


def merge_pair(v):
    n = v.shape[0] // 2
    low = lax.broadcasted_iota(jnp.int32, (n, v.shape[1]), 1) < 64
    return jnp.where(low, v[:n], v[n:])


def place():
    s = lax.axis_index("shard")
    r = lax.axis_index("replica")
    x = lax.rem(r, 2)
    z = lax.div(r, 2)
    return s, r, x, z


def peers(s, r):
    sib = s + 1 - 2 * lax.rem(s, 2)
    across = lax.rem(s + 2, 4)
    side = r + 1 - 2 * lax.rem(r, 2)
    return sib, across, side


def rows_loop(n, step, body):
    lax.fori_loop(0, n // step, lambda k, c: (body(at(k, step)), c)[1], 0, unroll=5)


def unpack_vectors(vec, vecf, bias_qkv):
    for v in range(8):
        for s in range(4):
            vecf[v : v + 1, s * 256 : (s + 1) * 256] = vec[s, v : v + 1, :].astype(F32)
    bias_qkv[...] = jnp.zeros_like(bias_qkv)
    for s in range(4):
        for t in range(2):
            col = (s * 2 + t) * 256 + (D if s >= 2 else 0)
            bias_qkv[0:1, col : col + 256] = vec[s, 8 + t : 9 + t, :].astype(F32)


def layer_norm(v, gain, shift):
    c = v - jnp.mean(v, axis=-1, keepdims=True)
    inv = lax.rsqrt(jnp.mean(c * c, axis=-1, keepdims=True) + 1e-06)
    return c * inv * gain + shift


def to_images(src, dst, turn):
    images = (src.shape[0]) // (PATCH + 1)
    main = images * PATCH

    def lane_block(l, carry):
        cols = at(l, 128)
        slot = lax.rem(l, 2)
        turn[slot] = src[0:main, cols].astype(F32)
        for i in range(images):
            dst[i * PATCH : (i + 1) * PATCH, cols] = turn[slot, pl.ds(i, PATCH, stride=images), :].astype(BF16)
        return carry

    lax.fori_loop(0, D // 128, lane_block, 0)
    last = src[main : main + images, :].astype(F32)
    dst[main:, :] = jnp.concatenate([last, jnp.zeros((CLS - images, D), F32)], 0).astype(BF16)


def pack_vectors(vectors, dst):
    row = 0
    for v in vectors:
        count = v.shape[0] // 256
        wide = v[...].astype(F32)
        for k in range(count):
            dst[row : row + 1, :] = wide[k * 256 : (k + 1) * 256].reshape(1, 256)
            row += 1


def attend(i, qkv, qkv_cls, scores, probs, mix, probs_cls, att, att_cls, lse, lse_cls):
    rows = at(i, PATCH)
    mask = head_mask()
    own = qkv_cls[pl.ds(i, 1), :]
    q_c, k_c, v_c = own[:, :D] * FACTOR, own[:, D : 2 * D], own[:, 2 * D :]
    q_bd = jnp.where(mask, q_c, 0.0)
    k_bd = jnp.where(mask, k_c, 0.0).astype(BF16)
    v_bd = jnp.where(mask, v_c, 0.0).astype(BF16)
    to_cls = dot_nt(k_bd, qkv[rows, 0:D]) * FACTOR
    of_cls = dot_nt(q_bd.astype(BF16), qkv[rows, D : 2 * D])
    corner = jnp.sum(q_bd * k_c, axis=1, keepdims=True)
    top = jnp.maximum(jnp.max(of_cls, axis=1, keepdims=True), corner)
    e_row = jnp.exp(of_cls - top)
    e_cor = jnp.exp(corner - top)
    total = jnp.sum(e_row, axis=1, keepdims=True) + e_cor
    inv = 1.0 / total
    row = dot((e_row * inv).astype(BF16), qkv[rows, 2 * D : 3 * D])
    row = row + (e_cor * inv).astype(BF16).astype(F32) * v_c
    att_cls[pl.ds(i, 1), :] = jnp.sum(jnp.where(mask, row, 0.0), axis=0, keepdims=True)
    lse_cls[i] = jnp.broadcast_to(top + jnp.log(total), (HEADS, PATCH))
    for g in range(HEADS // 2):
        q2 = qkv[rows, g * 128 : g * 128 + 128] * jnp.asarray(FACTOR, BF16)
        scores[g] = dot_nt(split_pair(qkv[rows, g * 128 + D : g * 128 + D + 128]), q2)
    for g in range(HEADS // 2):
        for u in range(2):
            h = 2 * g + u
            part = scores[g, u * PATCH : (u + 1) * PATCH, :]
            extra = to_cls[h : h + 1, :]
            top = jnp.maximum(jnp.max(part, axis=0, keepdims=True), extra)
            e_part = jnp.exp(part - top)
            e_extra = jnp.exp(extra - top)
            total = jnp.sum(e_part, axis=0, keepdims=True) + e_extra
            inv = 1.0 / total
            probs[g, u * PATCH : (u + 1) * PATCH, :] = (e_part * inv).astype(BF16)
            probs_cls[h : h + 1, :] = e_extra * inv
            lse[i, h : h + 1, :] = top + jnp.log(total)
    for g in range(HEADS // 2):
        v2 = split_pair(qkv[rows, g * 128 + 2 * D : g * 128 + 2 * D + 128])
        mix[:, g * 128 : g * 128 + 128] = dot_tn(probs[g], v2)
    att[rows, :] = (mix[...] + dot_tn(probs_cls[...].astype(BF16), v_bd)).astype(BF16)


class Gather:
    def __init__(self, number, rows, coop, src, dst, sems, local):
        s, r, x, z = place()
        sib, across, side = peers(s, r)
        self.number, self.sems, self.rows, self.coop = number, sems, rows, coop
        mine = pl.multiple_of(x * coop, 16)
        other = pl.multiple_of((1 - x) * coop, 16)
        rest = rows - 2 * coop
        self.started = []
        self.kinds = {
            "own": (dst(s, 0, rows), dst(s, 0, rows), {"shard": sib}),
            "far": (dst(s, mine, coop), dst(s, mine, coop), {"shard": across}),
            "side": (dst(across, mine, coop), dst(across, mine, coop), {"replica": side}),
            "pass": (dst(across, mine, coop), dst(across, mine, coop), {"shard": sib}),
            "last": (dst(across, other, coop), dst(across, other, coop), {"shard": sib}),
        }
        if rest:
            self.kinds["rest"] = (dst(s, 2 * coop, rest), dst(s, 2 * coop, rest), {"shard": across})
            self.kinds["passrest"] = (dst(across, 2 * coop, rest), dst(across, 2 * coop, rest), {"shard": sib})
        self.names = ["own", "far", "side", "pass", "last", "rest", "passrest"]
        self.local = pltpu.make_async_copy(src(0, rows), dst(s, 0, rows), local.at[number])

    def copy(self, kind):
        a, b, to = self.kinds[kind]
        k = self.names.index(kind)
        return pltpu.make_async_remote_copy(
            a, b, self.sems.at[0, self.number, k], self.sems.at[1, self.number, k], device_id=to, device_id_type=MESH
        )

    def load(self):
        self.local.start()

    def begin(self):
        self.local.wait()
        for kind in ("far", "rest"):
            if kind in self.kinds:
                self.copy(kind).start()
        self.copy("own").start()

    def on_far(self):
        self.copy("far").wait_recv()
        self.copy("side").start()
        self.copy("pass").start()

    def on_rest(self):
        self.copy("rest").wait_recv()
        self.copy("passrest").start()

    def on_side(self):
        self.copy("side").wait_recv()
        self.copy("last").start()

    def ready(self):
        for kind in ("own", "pass", "last", "passrest"):
            if kind in self.kinds:
                self.copy(kind).wait_recv()

    def drain(self):
        for kind in self.kinds:
            self.copy(kind).wait_send()


def gather_kernel(
    tokens, cot, v0, v1, v2, v3, v4, v5, v6, v7, v8, v9, w_qkv, w_out, w_up, w_down,
    qkv_w_o, out_w_o, up_w_o, down_w_o, vec_all, qkv_o, act_t_o, x_o, att_t_o, mid_o, branch_o, act2_o, act2_t_o, up_o,
    dr_o, dr_t_o, lse_o, lsec_o,
    full_qkv, full_out, full_up, full_down, x_s, qkv, act, att, mid, branch, act2, turned_a, turned_b, lse, lsec,
    scores, probs, mix, probs_cls, cls, qkv_cls, turn, vec32, vec_own_s, vec, vecf, bias_qkv,
    sems, local, vsem, osem,
):
    s, r, x, z = place()
    sib, across, side = peers(s, r)
    n = x_s.shape[0]
    images = lse.shape[0]
    main = images * PATCH

    vec32[...] = jnp.zeros_like(vec32)
    pack_vectors((v0, v1, v2, v3, v4, v5, v6, v7, v8, v9), vec32)
    vec_own_s[...] = vec32[...].astype(BF16)
    barrier = pltpu.get_barrier_semaphore()
    for to in ({"shard": sib}, {"shard": across}, {"replica": side}):
        pl.semaphore_signal(barrier, inc=1, device_id=to, device_id_type=MESH)

    def unit(number, rows, coop, src, dst):
        return Gather(number, rows, coop, src, dst, sems, local)

    g_qkv = unit(0, 256, 96, lambda a, k: w_qkv.at[pl.ds(a, k), :],
                 lambda p, a, k: full_qkv.at[pl.ds(pl.multiple_of(p * 256 + a, 16), k), :])
    g_out = unit(1, 256, 128, lambda a, k: w_out.at[pl.ds(a, k), :],
                 lambda p, a, k: full_out.at[pl.ds(pl.multiple_of(p * 256 + a, 16), k), :])

    def up_unit(number, t):
        return unit(number, TILE, 256, lambda a, k: w_up.at[pl.ds(a + t * TILE, k), :],
                    lambda p, a, k: full_up.at[p, pl.ds(pl.multiple_of(a + t * TILE, 16), k), :])

    def down_unit(number, t):
        return unit(number, TILE, 256, lambda a, k: w_down.at[pl.ds(a + t * TILE, k), :],
                    lambda p, a, k: full_down.at[p, pl.ds(pl.multiple_of(a + t * TILE, 16), k), :])

    g_up0, g_down0, g_up1, g_down1 = up_unit(2, 0), down_unit(3, 0), up_unit(4, 1), down_unit(5, 1)

    for g in (g_qkv, g_out, g_up0, g_down0, g_up1, g_down1):
        g.load()
    pl.semaphore_wait(barrier, 3)

    def vec_copy(k, src, slot, to):
        return pltpu.make_async_remote_copy(src, vec.at[slot], vsem.at[0, k], vsem.at[1, k], device_id=to,
                                            device_id_type=MESH)

    vec_own = vec_copy(0, vec_own_s, s, {"shard": sib})
    vec_far = vec_copy(1, vec_own_s, s, {"shard": across})
    vec_pass = vec_copy(2, vec.at[across], across, {"shard": sib})
    vec_own.start()
    vec_far.start()
    g_qkv.begin()
    vec[s] = vec_own_s[...]

    to_images(tokens, x_s, turn)
    outs = {}

    def send_out(k, src, dst):
        outs[k] = pltpu.make_async_copy(src, dst, osem.at[k])
        outs[k].start()

    send_out(0, x_s, x_o)
    vec_far.wait_recv()
    vec_pass.start()
    vec_own.wait_recv()
    vec_pass.wait_recv()
    unpack_vectors(vec, vecf, bias_qkv)

    def first_norm(rows):
        act[rows, :] = layer_norm(x_s[rows, :].astype(F32), vecf[0:1, :], vecf[1:2, :]).astype(BF16)

    rows_loop(n, 16, first_norm)
    transpose_into(act, turned_b)
    send_out(1, turned_b, act_t_o)
    g_qkv.on_far()
    g_out.begin()
    g_up0.begin()
    to_images(cot, branch, turn)

    def down_rows(rows):
        act2[rows, :] = (branch[rows, :].astype(F32) * vecf[7:8, :]).astype(BF16)

    rows_loop(n, 16, down_rows)
    g_qkv.on_rest()
    transpose_into(act2, turned_a)
    send_out(14, branch, up_o)
    send_out(15, act2, dr_o)
    send_out(16, turned_a, dr_t_o)
    g_qkv.on_side()
    g_qkv.ready()

    send_out(4, full_qkv, qkv_w_o)

    def qkv_tile(j, carry):
        cols = at(j, TILE)
        low = (dot(act[...], full_qkv[:, cols]) + bias_qkv[0:1, cols]).astype(BF16)
        qkv[:, cols] = low
        qkv_cls[:, cols] = low[main:].astype(F32)
        return carry

    lax.fori_loop(0, 3 * D // TILE, qkv_tile, 0)
    send_out(2, qkv, qkv_o)
    send_out(3, vec, vec_all)
    cls[...] = jnp.zeros_like(cls)
    plan = {0: [g_out.on_far, g_down0.begin, g_out.on_side], 1: [g_up0.on_far, g_up1.begin], 5: [g_down0.on_far, g_down1.begin],
            6: [g_up0.on_side]}

    def image(i, carry):
        for k, steps in plan.items():
            @pl.when(i == k)
            def _(steps=steps):
                for step in steps:
                    step()

        attend(i, qkv, qkv_cls, scores, probs, mix, probs_cls, att, cls, lse, lsec)
        return carry

    lax.fori_loop(0, images, image, 0)
    att[main:, :] = cls[...].astype(BF16)
    outs.pop(16).wait()
    transpose_into(att, turned_a)
    send_out(8, turned_a, att_t_o)
    send_out(9, lse, lse_o)
    send_out(10, lsec, lsec_o)
    g_out.ready()
    outs.pop(14).wait()
    for j in range(D // TILE):
        cols = slice(j * TILE, (j + 1) * TILE)
        out = dot(att[...], full_out[:, cols]) + vecf[2:3, cols]
        branch[:, cols] = out.astype(BF16)
        mid[:, cols] = x_s[:, cols].astype(F32) + vecf[3:4, cols] * out
    send_out(11, mid, mid_o)
    send_out(12, branch, branch_o)
    g_down0.on_side()

    def second_norm(rows):
        act2[rows, :] = layer_norm(mid[rows, :], vecf[4:5, :], vecf[5:6, :]).astype(BF16)

    outs.pop(15).wait()
    rows_loop(n, 16, second_norm)
    send_out(13, act2, act2_o)
    outs.pop(1).wait()
    transpose_into(act2, turned_b)
    send_out(17, turned_b, act2_t_o)
    g_up1.on_far()
    g_up1.on_side()
    g_down1.on_far()
    g_down1.on_side()
    for g in (g_up0, g_down0, g_up1, g_down1):
        g.ready()
    send_out(5, full_out, out_w_o)
    send_out(6, full_up, up_w_o)
    send_out(7, full_down, down_w_o)
    for copy in outs.values():
        copy.wait()
    for g in (g_qkv, g_out, g_up0, g_down0, g_up1, g_down1):
        g.drain()
    for copy in (vec_own, vec_far, vec_pass):
        copy.wait_send()


class Chunk:
    def __init__(self, index, rows, mine, y_send, y_recv, x_recv, z_recv, far):
        self.index, self.rows, self.mine, self.y_send, self.far = index, rows, mine, y_send, far
        self.y_recv, self.x_recv, self.z_recv = y_recv, x_recv, z_recv


def chunk_layout(nz):
    last = 32 * nz
    sizes = [1024, 1024, 1024, 1024, 512, 1024, 512, last]
    y_base = 2048
    y_a = y_base
    y_b = y_a + 2048 + last
    mine_base = y_b + 2048
    chunks = []
    mine = mine_base
    late = 0
    xr = zr = 0
    for k, rows in enumerate(sizes):
        if k < 2:
            ys, yr = y_a + 1024 * k, 1024 * k
        elif k < 4:
            ys, yr = y_b + 1024 * (k - 2), 2048 + last + 1024 * (k - 2)
        else:
            ys, yr = y_a + late, late
            late += rows
        far = mine_base + sum(sizes) + 512 * k if k < 2 else ys
        chunks.append(Chunk(k, rows, mine, ys, yr, xr, zr, far))
        mine += rows
        xr += rows // 2
        zr += rows // 2 // nz
    return chunks, dict(buf=mine + 1024, total=sum(sizes), mine=mine_base, y_recv=2 * 2048 + last, x_recv=xr, z_recv=zr)


def add_rows(dst, d0, src, s0, rows):
    step = next(k for k in (128, 96, 64, 32, 16) if rows % k == 0)

    def body(k, carry):
        d = pl.ds(pl.multiple_of(d0 + k * step, 16), step)
        t = pl.ds(pl.multiple_of(s0 + k * step, 16), step)
        dst[d, :] = (dst[d, :].astype(F32) + src[t, :].astype(F32)).astype(BF16)
        return carry

    lax.fori_loop(0, rows // step, body, 0)


class Reduce:
    def __init__(self, nz, buf, core_recv, y_recv, x_recv, z_recv, sems, core_sems, credit):
        self.nz, self.buf, self.core_recv = nz, buf, core_recv
        self.y_recv, self.x_recv, self.z_recv = y_recv, x_recv, z_recv
        self.sems, self.core_sems, self.credit = sems, core_sems, credit
        self.s, self.r, self.x, self.z = place()
        self.sib, self.across, self.side = peers(self.s, self.r)

    def remote(self, src, dst, chunk, kind, to):
        return pltpu.make_async_remote_copy(
            src, dst, self.sems.at[0, chunk.index, kind], self.sems.at[1, chunk.index, kind], device_id=to,
            device_id_type=MESH)

    def peer(self, k):
        return {"replica": lax.rem(self.z + k, self.nz) * 2 + self.x}

    def core_copy(self, turn, rows):
        slot = turn % 2
        return pltpu.make_async_remote_copy(
            self.buf.at[pl.ds(0, rows), :], self.core_recv.at[slot, pl.ds(0, rows), :],
            self.core_sems.at[0, turn], self.core_sems.at[1, turn], device_id={"shard": self.sib}, device_id_type=MESH)

    def add_core(self, turn, first, dst, rows):
        add_rows(self.buf, dst, self.core_recv.at[turn % 2], first, rows)

    def y_copy(self, c):
        return self.remote(self.buf.at[pl.ds(c.y_send, c.rows), :], self.y_recv.at[pl.ds(c.y_recv, c.rows), :], c, 0,
                           {"shard": self.across})

    def x_copy(self, c):
        half = c.rows // 2
        return self.remote(self.buf.at[pl.ds(pl.multiple_of(c.mine + (1 - self.x) * half, 16), half), :],
                           self.x_recv.at[pl.ds(c.x_recv, half), :], c, 1, {"replica": self.side})

    def quarter(self, c, x, z):
        half = c.rows // 2
        size = half // self.nz
        return pl.ds(pl.multiple_of(c.mine + x * half + z * size, 16), size)

    def z_copy(self, c, k):
        size = c.rows // 2 // self.nz
        return self.remote(self.buf.at[self.quarter(c, self.x, lax.rem(self.z + k, self.nz)), :],
                           self.z_recv.at[k - 1, pl.ds(c.z_recv, size), :], c, 1 + k, self.peer(k))

    def done(self, first, c, z):
        size = c.rows // 2 // self.nz
        return pl.ds(pl.multiple_of(first + z * size, 16), size)

    def back_z(self, c, k):
        part = self.x_recv.at[self.done(c.x_recv, c, self.z), :]
        return self.remote(part, part, c, self.nz + k, self.peer(k))

    def back_x(self, c, k):
        z = lax.rem(self.z + self.nz - k, self.nz)
        return self.remote(self.x_recv.at[self.done(c.x_recv, c, z), :], self.buf.at[self.done(c.far, c, z), :], c,
                           2 * self.nz + k, {"replica": self.side})

    def on_y(self, c):
        self.y_copy(c).wait_recv()
        add_rows(self.buf, c.mine, self.y_recv, c.y_recv, c.rows)
        self.y_copy(c).wait_send()
        self.x_copy(c).start()

    def on_x(self, c):
        half = c.rows // 2
        self.x_copy(c).wait_recv()
        add_rows(self.buf, c.mine + self.x * half, self.x_recv, c.x_recv, half)
        for k in range(1, self.nz):
            self.z_copy(c, k).start()

    def on_z(self, c):
        size = c.rows // 2 // self.nz
        start = c.mine + self.x * (c.rows // 2) + self.z * size
        for k in range(1, self.nz):
            self.z_copy(c, k).wait_recv()
        step = next(k for k in (64, 48, 32, 16) if size % k == 0)

        def body(i, carry):
            d = pl.ds(pl.multiple_of(start + i * step, 16), step)
            total = self.buf[d, :].astype(F32)
            for k in range(1, self.nz):
                total = total + self.z_recv[k - 1, pl.ds(pl.multiple_of(c.z_recv + i * step, 16), step), :].astype(F32)
            to = pl.ds(pl.multiple_of(c.x_recv + self.z * size + i * step, 16), step)
            self.x_recv[to, :] = total.astype(BF16)
            return carry

        lax.fori_loop(0, size // step, body, 0)
        for k in range(1, self.nz):
            self.back_z(c, k).start()
        self.back_x(c, 0).start()

    def on_back(self, c):
        for k in range(1, self.nz):
            self.back_z(c, k).wait_recv()
            self.back_x(c, k).start()

    def finish(self, c):
        for k in range(self.nz):
            self.back_x(c, k).wait_recv()

    def drain(self, c):
        self.x_copy(c).wait_send()
        for k in range(1, self.nz):
            self.z_copy(c, k).wait_send()
            self.back_z(c, k).wait_send()
        for k in range(self.nz):
            self.back_x(c, k).wait_send()


def fold(v):
    return jnp.sum(v.reshape(v.shape[0] // 8, 8, v.shape[1]), axis=0)


def gelu_both(v):
    e = jnp.exp(-0.5 * v * v)
    t = 1.0 / (1.0 + 0.23164189 * jnp.abs(v))
    poly = ((((1.061405429 * t - 1.453152027) * t + 1.421413741) * t - 0.284496736) * t + 0.254829592) * t
    tail = 0.5 * poly * e
    phi = jnp.where(v >= 0.0, 1.0 - tail, tail)
    return v * phi, phi + v * e * 0.3989422804014327


def transpose_into(src, dst):
    for c in range(D // 128):
        dst[c * 128 : (c + 1) * 128, :] = src[:, c * 128 : (c + 1) * 128].T


def attend_back(i, qkv, qkv_cls, datt, datt_cls, lse, lsec, scores, dprobs, probs, dscores, cls_row, joint_cls, sum_q, sum_v):
    rows = at(i, PATCH)
    mask = head_mask()
    own = qkv_cls[pl.ds(i, 1), :]
    do_c = datt_cls[pl.ds(i, 1), :]
    q_c, k_c, v_c = own[:, :D] * FACTOR, own[:, D : 2 * D], own[:, 2 * D :]
    pick = lambda v: jnp.where(mask, v, 0.0)
    q_w, k_w, v_w, do_w = pick(q_c), pick(k_c), pick(v_c), pick(do_c)
    q_bd, k_bd, v_bd, do_bd = (v.astype(BF16) for v in (q_w, k_w, v_w, do_w))
    queries, keys, values = (qkv[rows, k * D : (k + 1) * D] for k in range(3))
    grads = datt[rows, :]
    low = lambda v: v.astype(BF16)
    top = lsec[i][:, 0:1]
    p_row = jnp.exp(dot_nt(q_bd, keys) - top)
    p_cor = jnp.exp(jnp.sum(q_w * k_c, axis=1, keepdims=True) - top)
    dp_row = dot_nt(do_bd, values)
    dp_cor = jnp.sum(do_w * v_c, axis=1, keepdims=True)
    delta = jnp.sum(p_row * dp_row, axis=1, keepdims=True) + p_cor * dp_cor
    ds_row = low(p_row * (dp_row - delta))
    ds_cor = low(p_cor * (dp_cor - delta)).astype(F32)
    p_col = jnp.exp(dot_nt(k_bd, queries) * FACTOR - lse[i])
    dp_col = dot_nt(v_bd, grads)
    for g in range(HEADS // 2):
        lanes = slice(g * 128, (g + 1) * 128)
        q2 = qkv[rows, lanes] * jnp.asarray(FACTOR, BF16)
        scores[g] = dot_nt(split_pair(qkv[rows, g * 128 + D : g * 128 + D + 128]), q2)
        dprobs[g] = dot_nt(split_pair(qkv[rows, g * 128 + 2 * D : g * 128 + 2 * D + 128]), datt[rows, lanes])
    for g in range(HEADS // 2):
        for u in range(2):
            h = 2 * g + u
            half = slice(u * PATCH, (u + 1) * PATCH)
            part = jnp.exp(scores[g, half, :] - lse[i, h : h + 1, :])
            dpart = dprobs[g, half, :]
            p_h, dp_h = p_col[h : h + 1, :], dp_col[h : h + 1, :]
            delta = jnp.sum(part * dpart, axis=0, keepdims=True) + p_h * dp_h
            probs[g, half, :] = low(part)
            dscores[g, half, :] = low(part * (dpart - delta))
            cls_row[h : h + 1, :] = p_h * (dp_h - delta)
    ds_col = low(cls_row[...])
    total = lambda v: jnp.sum(jnp.where(mask, v, 0.0), axis=0, keepdims=True)
    joint_cls[pl.ds(i, 1), 0:D] = FACTOR * (total(dot(ds_row, keys)) + jnp.sum(ds_cor * k_w, axis=0, keepdims=True))
    joint_cls[pl.ds(i, 1), D : 2 * D] = FACTOR * total(dot(ds_col, queries)) + jnp.sum(ds_cor * q_w, axis=0, keepdims=True)
    joint_cls[pl.ds(i, 1), 2 * D : 3 * D] = total(dot(low(p_col), grads)) + jnp.sum(
        low(p_cor).astype(F32) * do_w, axis=0, keepdims=True)
    p_row = low(p_row)
    for g in range(HEADS // 2):
        lanes = slice(g * 128, (g + 1) * 128)
        klanes = slice(g * 128 + D, g * 128 + D + 128)
        vlanes = slice(g * 128 + 2 * D, g * 128 + 2 * D + 128)
        q2 = qkv[rows, lanes] * jnp.asarray(FACTOR, BF16)
        dv = merge_pair(dot(probs[g], datt[rows, lanes])) + dot_tn(p_row, do_bd[:, lanes])
        dk = merge_pair(dot(dscores[g], q2)) + dot_tn(ds_row, q_bd[:, lanes])
        dq = (dot_tn(dscores[g], split_pair(qkv[rows, klanes])) + dot_tn(ds_col, k_bd[:, lanes])) * FACTOR
        qkv[rows, lanes] = low(dq)
        qkv[rows, klanes] = low(dk)
        qkv[rows, vlanes] = low(dv)
        sum_q[:, lanes] += fold(dq)
        sum_v[:, lanes] += fold(dv)


def to_tokens(src, dst, turn):
    images = dst.shape[0] // (PATCH + 1)
    main = images * PATCH

    def lane_block(l, carry):
        cols = at(l, 128)
        slot = lax.rem(l, 2)
        for i in range(images):
            turn[slot, pl.ds(i, PATCH, stride=images), :] = src[i * PATCH : (i + 1) * PATCH, cols].astype(F32)
        dst[0:main, cols] = turn[slot].astype(BF16)
        return carry

    lax.fori_loop(0, D // 128, lane_block, 0)
    dst[main : main + images, :] = src[main:, :].astype(F32)[0:images].astype(BF16)


def backward_kernel(
    nz, chunks, vec, full_qkv, full_out, full_up, full_down, qkv_h, act_t_h, x_h, att_t_h, mid_h, branch_h, act2_h,
    act2_t_h, up_h, dr_h, dr_t_h, lse_h, lsec_h,
    result_o, tokens_o, sums_o, hidden_o,
    buf, core_recv, y_recv, x_recv, z_recv, gmid, up_s, acc, sums_up, vecf, bias_qkv, bias_up, vrows,
    sems, core_sems, credit, dsem, wsem, hsem, osem, fsem,
):
    images = lse_h.shape[0]
    n = gmid.shape[0]
    main = images * PATCH
    red = Reduce(nz, buf, core_recv, y_recv, x_recv, z_recv, sems, core_sems, credit)
    s = red.s
    cd0, cu0, cd1, cu1, co, cq0, cq1, cv = chunks

    def load(k, src, dst):
        copy = pltpu.make_async_copy(src, dst, dsem.at[k])
        copy.start()
        return copy

    def relative(rel):
        low, high = lax.rem(rel, 2), lax.div(rel, 2)
        return s + low * (1 - 2 * lax.rem(s, 2)) + high * (2 - 4 * lax.div(s, 2))

    def target(rel, chunk):
        low, high = lax.rem(rel, 2), lax.div(rel, 2)
        return low * (1 - high) * chunk.rows + (1 - low) * (high * chunk.y_send + (1 - high) * chunk.mine)

    got_up = load(7, up_h, up_s)

    def ffn(dr, dr_t, act2, act2_t, w_up, w_down, hid, br):
        gots = [load(0, act2_h, act2), load(1, dr_h, dr), load(2, dr_t_h, dr_t), load(3, act2_t_h, act2_t)]

        def fetch(j, slot):
            piece, t = relative(3 - lax.rem(j, 4)), lax.div(j, 4)
            return (
                pltpu.make_async_copy(full_up.at[piece, :, at(t, TILE)], w_up.at[slot], wsem.at[0, slot]),
                pltpu.make_async_copy(full_down.at[piece, at(t, TILE), :], w_down.at[slot], wsem.at[1, slot]),
            )

        def keep(j, slot):
            return pltpu.make_async_copy(hid.at[slot], hidden_o.at[j], hsem.at[slot])

        for copy in fetch(0, 0):
            copy.start()
        barrier = pltpu.get_barrier_semaphore()
        partners = [{"shard": red.sib}, {"shard": red.across}, {"replica": red.side}]
        partners += [red.peer(k) for k in range(1, nz)]
        for to in partners:
            pl.semaphore_signal(barrier, inc=1, device_id=to, device_id_type=MESH)
        pl.semaphore_wait(barrier, len(partners))
        unpack_vectors(vec, vecf, bias_qkv)
        for p in range(4):
            for t in range(2):
                for k in range(2):
                    row = 10 + 2 * t + k
                    bias_up[2 * p + t : 2 * p + t + 1, k * 256 : (k + 1) * 256] = vec[p, row : row + 1, :].astype(F32)
        acc[...] = jnp.zeros_like(acc)
        gmid[...] = jnp.zeros_like(gmid)
        for start in (0, cv.rows, cv.y_send, cv.mine):
            buf[pl.ds(start, cv.rows), :] = jnp.zeros((cv.rows, TILE), BF16)
        for copy in gots:
            copy.wait()
        cut = 16 * (n // 32)
        first, second = slice(0, cut), slice(cut, n)

        def tile(j, carry):
            slot = lax.rem(j, 2)
            rel, t = 3 - lax.rem(j, 4), lax.div(j, 4)
            piece = relative(rel)
            low, high = lax.rem(rel, 2), lax.div(rel, 2)
            place_at = pl.multiple_of(
                (1 - low) * (high * (cd0.y_send + t * (cd1.y_send - cd0.y_send)) + (1 - high) * (cd0.mine + t * 2048)), 16)
            for copy in fetch(j, slot):
                copy.wait()

            @pl.when(j < 7)
            def _():
                for copy in fetch(j + 1, 1 - slot):
                    copy.start()

            @pl.when(j >= 2)
            def _():
                keep(j - 2, slot).wait()

            for k in (2, 4, 6):
                @pl.when(j == k)
                def _(k=k):
                    red.core_copy(k // 2 - 1, 2048).wait_send()

            bias = bias_up[pl.ds(2 * piece + t, 1), :]

            def both(rows, before, grad):
                hidden, step = gelu_both(before)
                hid[slot, rows, :] = hidden.astype(BF16)
                grad = grad * step
                br[rows, :] = grad.astype(BF16)
                return jnp.sum(grad, axis=0, keepdims=True)

            before0 = dot(act2[first, :], w_up[slot]) + bias
            grad0 = dot_nt(dr[first, :], w_down[slot])
            before1 = dot(act2[second, :], w_up[slot]) + bias
            column = both(first, before0, grad0)
            grad1 = dot_nt(dr[second, :], w_down[slot])
            gmid[first, :] += dot_nt(br[first, :], w_up[slot])
            column = column + both(second, before1, grad1)
            sums_up[pl.ds(2 * piece + t, 1), :] = column
            gmid[second, :] += dot_nt(br[second, :], w_up[slot])
            keep(j, slot).start()
            buf[pl.ds(place_at, D), :] = dot(dr_t[...], hid[slot]).astype(BF16)
            buf[pl.ds(pl.multiple_of(place_at + D, 16), D), :] = dot(act2_t[...], br[...]).astype(BF16)

            def y_part(turn, chunk):
                red.core_copy(turn, 2048).wait_recv()
                for k, c in enumerate(chunk):
                    red.add_core(turn, k * 1024, c.y_send, c.rows)
                    red.y_copy(c).start()

            def own_part(turn, chunk):
                red.core_copy(turn, 2048).wait_recv()
                red.add_core(turn, 0, chunk[0].mine, 2048)

            steps = {
                0: [lambda: red.core_copy(0, 2048).start()],
                1: [lambda: y_part(0, (cd0, cu0))],
                2: [lambda: red.core_copy(1, 2048).start()],
                3: [lambda: own_part(1, (cd0, cu0))],
                4: [lambda: red.core_copy(2, 2048).start(), lambda: red.on_y(cd0)],
                5: [lambda: y_part(2, (cd1, cu1))],
                6: [lambda: red.core_copy(3, 2048).start(), lambda: red.on_y(cu0), lambda: red.on_x(cd0)],
                7: [lambda: own_part(3, (cd1, cu1))],
            }
            for k, todo in steps.items():
                @pl.when(j == k)
                def _(todo=todo):
                    for step in todo:
                        step()
            return carry

        lax.fori_loop(0, 8, tile, 0)
        pl.semaphore_signal(credit, inc=1, device_id={"shard": red.across}, device_id_type=MESH)
        for j in (6, 7):
            keep(j, j % 2).wait()
        red.core_copy(3, 2048).wait_send()

    v = pltpu.VMEM
    pl.run_scoped(ffn, v((n, D), BF16), v((D, n), BF16), v((n, D), BF16), v((D, n), BF16), v((2, D, TILE), BF16),
                  v((2, TILE, D), BF16), v((2, n, TILE), BF16), v((n, TILE), BF16))
    got_up.wait()

    def spread(out, chunk, tile_rows):
        for p in range(4):
            low = lax.rem(lax.rem(s, 2) + p % 2, 2)
            high = lax.rem(lax.div(s, 2) + p // 2, 2)
            start = pl.multiple_of(target(low + 2 * high, chunk) + tile_rows, 16)
            buf[pl.ds(start, 256), :] = out[p * 256 : (p + 1) * 256].astype(BF16)

    def on_core(turn, chunk):
        red.core_copy(turn, 2 * chunk.rows).wait_recv()
        red.add_core(turn, 0, chunk.y_send, chunk.rows)
        red.y_copy(chunk).start()
        red.add_core(turn, chunk.rows, chunk.mine, chunk.rows)

    def attention(qkv, datt, brr, lse, lsec, scores, dprobs, probs, dscores, cls_row, qkv_cls, datt_cls, joint_cls):
        got_qkv, got_lse, got_lsec = load(0, qkv_h, qkv), load(1, lse_h, lse), load(2, lsec_h, lsec)

        def middle(mid, branch, att_t, w_out):
            got_mid, got_branch = load(3, mid_h, mid), load(4, branch_h, branch)
            got_att, got_out = load(5, att_t_h, att_t), load(6, full_out, w_out)
            red.on_z(cd0)
            got_mid.wait()
            got_branch.wait()

            def norm_rows(rows):
                m = mid[rows, :]
                c = m - jnp.mean(m, axis=-1, keepdims=True)
                inv = lax.rsqrt(jnp.mean(c * c, axis=-1, keepdims=True) + 1e-06)
                hat = c * inv
                g = gmid[rows, :]
                acc[4] += fold(g * hat)
                acc[5] += fold(g)
                sc = g * vecf[4:5, :]
                back = inv * (sc - jnp.mean(sc, axis=-1, keepdims=True)
                              - hat * jnp.mean(sc * hat, axis=-1, keepdims=True))
                gm = up_s[rows, :].astype(F32) + back
                gmid[rows, :] = gm
                acc[3] += fold(gm * branch[rows, :].astype(F32))
                gb = gm * vecf[3:4, :]
                acc[2] += fold(gb)
                brr[rows, :] = gb.astype(BF16)

            rows_loop(n, 16, norm_rows)
            red.on_x(cu0)
            got_att.wait()
            for q in range(2):
                spread(dot(att_t[...], brr[:, q * TILE : (q + 1) * TILE]), co, q * 256)
            red.core_copy(4, 2 * co.rows).start()
            got_out.wait()
            for q in range(2):
                datt[:, q * TILE : (q + 1) * TILE] = dot_nt(brr[...], w_out[q * TILE : (q + 1) * TILE, :]).astype(BF16)

        pl.run_scoped(middle, v((n, D), F32), v((n, D), BF16), v((D, n), BF16), v((D, D), BF16))
        got_qkv.wait()
        got_lse.wait()
        got_lsec.wait()
        qkv_cls[...] = qkv[main:, :].astype(F32)
        datt_cls[...] = datt[main:, :].astype(F32)
        joint_cls[...] = jnp.zeros_like(joint_cls)
        pl.semaphore_wait(credit, 1)
        on_core(4, co)
        plan = {0: [lambda: red.on_y(cd1), lambda: red.on_back(cd0)], 2: [lambda: red.on_z(cu0)], 3: [lambda: red.on_x(cd1)],
                5: [lambda: red.on_back(cu0)], 6: [lambda: red.on_y(cu1), lambda: red.on_z(cd1)]}

        def image(i, carry):
            for k, steps in plan.items():
                @pl.when(i == k)
                def _(steps=steps):
                    for step in steps:
                        step()

            attend_back(i, qkv, qkv_cls, datt, datt_cls, lse, lsec, scores, dprobs, probs, dscores, cls_row, joint_cls,
                        acc.at[8], acc.at[9])
            return carry

        lax.fori_loop(0, images, image, 0)
        qkv[main:, :] = joint_cls[...].astype(BF16)
        acc[8] += fold(joint_cls[:, 0:D])
        acc[9] += fold(joint_cls[:, 2 * D : 3 * D])

        def tail(act_t, gact, w_qkv, turn, flat):
            x_s = brr
            got_act, got_x = load(3, act_t_h, act_t), load(4, x_h, x_s)

            def fetch(j):
                return pltpu.make_async_copy(full_qkv.at[pl.ds(j * 256, 256), :], w_qkv.at[j % 2], wsem.at[0, j % 2])

            fetch(0).start()
            fetch(1).start()
            got_act.wait()
            red.core_copy(4, 2 * co.rows).wait_send()
            for q in range(4):
                spread(dot(act_t[...], qkv[:, q * TILE : (q + 1) * TILE]), cq0, q * 256)
            red.core_copy(5, 2 * cq0.rows).start()
            red.on_y(co)
            red.on_x(cu1)

            def input_grad(j):
                fetch(j).wait()
                gact[:, j * 256 : (j + 1) * 256] = dot_nt(qkv[...], w_qkv[j % 2])
                if j < 2:
                    fetch(j + 2).start()

            for j in range(3):
                input_grad(j)
            on_core(5, cq0)
            red.on_back(cd1)
            red.core_copy(5, 2 * cq0.rows).wait_send()
            for q in range(2):
                spread(dot(act_t[...], qkv[:, (q + 4) * TILE : (q + 5) * TILE]), cq1, q * 256)
            red.core_copy(6, 2 * cq1.rows).start()
            input_grad(3)
            red.on_x(co)
            on_core(6, cq1)
            red.on_z(cu1)
            got_x.wait()

            def norm_rows(rows):
                m = x_s[rows, :].astype(F32)
                c = m - jnp.mean(m, axis=-1, keepdims=True)
                inv = lax.rsqrt(jnp.mean(c * c, axis=-1, keepdims=True) + 1e-06)
                hat = c * inv
                g = gact[rows, :]
                acc[0] += fold(g * hat)
                acc[1] += fold(g)
                sc = g * vecf[0:1, :]
                back = inv * (sc - jnp.mean(sc, axis=-1, keepdims=True)
                              - hat * jnp.mean(sc * hat, axis=-1, keepdims=True))
                x_s[rows, :] = (gmid[rows, :] + back).astype(BF16)

            rows_loop(n, 16, norm_rows)
            red.core_copy(6, 2 * cq1.rows).wait_send()
            red.on_z(co)
            to_tokens(x_s, flat, turn)
            copy = pltpu.make_async_copy(flat, tokens_o, osem.at[0])
            copy.start()
            red.on_back(cu1)
            red.on_back(co)
            copy.wait()

        pl.run_scoped(tail, v((D, n), BF16), v((n, D), F32), v((2, 256, 3 * D), BF16),
                      v((2, main, 128), F32), v((main + images, D), BF16))

    pl.run_scoped(attention, v((n, 3 * D), BF16), v((n, D), BF16), v((n, D), BF16), v((images, HEADS, PATCH), F32),
                  v((images, HEADS, PATCH), F32), v((8, 256, PATCH), F32), v((8, 256, PATCH), F32),
                  v((8, 256, PATCH), BF16), v((8, 256, PATCH), BF16), v((HEADS, PATCH), F32), v((CLS, 3 * D), F32),
                  v((CLS, D), F32), v((CLS, 3 * D), F32))

    def outcome(mid, hid, w_down, turn, flat, res):
        got_mid = load(3, mid_h, mid)

        def fetch(j, slot):
            piece, t = relative(3 - lax.rem(j, 4)), lax.div(j, 4)
            return (
                pltpu.make_async_copy(hidden_o.at[j], hid.at[slot], wsem.at[0, slot]),
                pltpu.make_async_copy(full_down.at[piece, at(t, TILE), :], w_down.at[slot], wsem.at[1, slot]),
            )

        for copy in fetch(0, 0):
            copy.start()
        gmid[...] = jnp.zeros_like(gmid)

        def tile(j, carry):
            slot = lax.rem(j, 2)
            for copy in fetch(j, slot):
                copy.wait()

            @pl.when(j < 7)
            def _():
                for copy in fetch(j + 1, 1 - slot):
                    copy.start()

            gmid[...] += dot(hid[slot], w_down[slot])
            return carry

        lax.fori_loop(0, 8, tile, 0)
        got_mid.wait()

        def rows_of(rows):
            projected = gmid[rows, :] + vecf[6:7, :]
            upstream = up_s[rows, :].astype(F32)
            acc[6] += fold(upstream * vecf[7:8, :])
            acc[7] += fold(upstream * projected)
            res[rows, :] = (mid[rows, :] + vecf[7:8, :] * projected).astype(BF16)

        rows_loop(n, 16, rows_of)
        for p in range(4):
            vrows[...] = jnp.zeros_like(vrows)
            for k in range(8):
                vrows[k : k + 1, 0:256] = jnp.sum(acc[k, :, p * 256 : (p + 1) * 256], axis=0, keepdims=True)
            joint = acc.at[8 + p // 2]
            for k in range(2):
                first = (p % 2) * TILE + k * 256
                vrows[8 + k : 9 + k, 0:256] = jnp.sum(joint[:, first : first + 256], axis=0, keepdims=True)
            for k in range(4):
                vrows[10 + k : 11 + k, 0:256] = sums_up[2 * p + k // 2 : 2 * p + k // 2 + 1, (k % 2) * 256 : (k % 2 + 1) * 256]
            low = lax.rem(lax.rem(s, 2) + p % 2, 2)
            high = lax.rem(lax.div(s, 2) + p // 2, 2)
            buf[pl.ds(pl.multiple_of(target(low + 2 * high, cv), 16), 16), :] = vrows[...].astype(BF16)
        red.core_copy(7, 2 * cv.rows).start()
        to_tokens(res, flat, turn)
        copy = pltpu.make_async_copy(flat, result_o, osem.at[0])
        copy.start()
        on_core(7, cv)
        red.on_y(cq0)
        red.on_y(cq1)
        red.on_x(cq0)
        red.on_y(cv)
        red.on_x(cq1)
        red.on_z(cq0)
        red.on_x(cv)
        red.on_z(cq1)
        red.on_back(cq0)
        red.on_z(cv)
        red.on_back(cq1)
        red.on_back(cv)
        copy.wait()

    pl.run_scoped(outcome, v((n, D), F32), v((2, n, TILE), BF16), v((2, TILE, D), BF16), v((2, main, 128), F32),
                  v((main + images, D), BF16), v((n, D), BF16))
    copies = []
    for c in chunks:
        red.finish(c)
        half = c.rows // 2
        for k, (src, first, where) in enumerate(((x_recv, c.x_recv, red.x), (buf, c.far, 1 - red.x))):
            copy = pltpu.make_async_copy(
                src.at[pl.ds(first, half), :],
                sums_o.at[pl.ds(pl.multiple_of(c.mine - cd0.mine + where * half, 16), half), :], fsem.at[2 * c.index + k])
            copy.start()
            copies.append(copy)
    red.core_copy(7, 2 * cv.rows).wait_send()
    for c in chunks:
        red.drain(c)
    for copy in copies:
        copy.wait()


def convert_kernel(
    chunks, sums, g1_o, s1_o, qkv_o, bqv_o, out_o, bo_o, l1_o, g2_o, s2_o, up_o, bup_o, down_o, bd_o, l2_o,
    low, small, qkv, out, up, down, dsem, osem,
):
    base = chunks[0].mine
    gots = []
    for c in chunks:
        rows = pl.ds(c.mine - base, c.rows)
        gots.append(pltpu.make_async_copy(sums.at[rows, :], low.at[rows, :], dsem.at[c.index]))
        gots[-1].start()
    outs = []

    def send_out(src, dst):
        copy = pltpu.make_async_copy(src, dst, osem.at[len(outs)])
        copy.start()
        outs.append(copy)

    def block(c, first, count):
        return low[c.mine - base + first : c.mine - base + first + count, :]

    for t in range(2):
        gots[2 * t].wait()
        for k in range(8):
            down[t * TILE : (t + 1) * TILE, k * 128 : (k + 1) * 128] = block(chunks[2 * t], k * 128, 128).T.astype(F32)
        send_out(down.at[pl.ds(t * TILE, TILE), :], down_o.at[pl.ds(t * TILE, TILE), :])
        gots[2 * t + 1].wait()
        up[t] = block(chunks[2 * t + 1], 0, D).astype(F32)
        send_out(up.at[t], up_o.at[:, pl.ds(t * TILE, TILE)])
    gots[4].wait()
    for k in range(2):
        out[:, k * TILE : (k + 1) * TILE] = block(chunks[4], k * 256, 256).astype(F32)
    send_out(out, out_o)
    gots[5].wait()
    gots[6].wait()
    for k in range(6):
        qkv[:, k * TILE : (k + 1) * TILE] = block(chunks[5], k * 256, 256).astype(F32)
    send_out(qkv, qkv_o)
    gots[7].wait()
    small[...] = block(chunks[7], 0, 16)[:, 0:256].astype(F32)
    vectors = (g1_o, s1_o, bo_o, l1_o, g2_o, s2_o, bd_o, l2_o, bqv_o, bup_o)
    row = 0
    for v in vectors:
        for k in range(v.shape[0] // 256):
            v[pl.ds(k * 256, 256)] = small[row : row + 1, :].reshape(256)
            row += 1
    for copy in outs:
        copy.wait()


def convert(chunks, sums):
    one = lambda k: jax.ShapeDtypeStruct((k,), F32)
    outs = (
        one(256), one(256), wide_shape(256, 3 * D), one(512), wide_shape(256, D), one(256), one(256), one(256), one(256),
        wide_shape(D, D), one(1024), wide_shape(D, D), one(256), one(256),
    )
    v = pltpu.VMEM
    return pl.pallas_call(
        functools.partial(convert_kernel, chunks),
        out_shape=outs,
        in_specs=[ANY],
        out_specs=[VMEM if len(o.shape) == 1 else ANY for o in outs],
        scratch_shapes=[v(sums.shape, BF16), v((16, 256), F32), v((256, 3 * D), F32), v((256, D), F32), v((2, D, TILE), F32),
                        v((D, D), F32), pltpu.SemaphoreType.DMA((8,)), pltpu.SemaphoreType.DMA((6,))],
        compiler_params=pltpu.CompilerParams(vmem_limit_bytes=LIMIT),
        name="gradients_to_float32",
    )(sums)


def low_shape(*shape):
    return jax.ShapeDtypeStruct(shape, BF16)


def wide_shape(*shape):
    return jax.ShapeDtypeStruct(shape, F32)


ANY = pl.BlockSpec(memory_space=pl.ANY)
VMEM = pl.BlockSpec(memory_space=pltpu.VMEM)
LIMIT = 62 * 2**20


def forward(flat, cot, vectors, w_qkv, w_out, w_up, w_down):
    images = flat.shape[0] // (PATCH + 1)
    n = images * PATCH + CLS
    v = pltpu.VMEM
    outs = (
        low_shape(D, 3 * D), low_shape(D, D), low_shape(4, D, D), low_shape(4, D, D), low_shape(4, 16, 256),
        low_shape(n, 3 * D), low_shape(D, n), low_shape(n, D), low_shape(D, n), wide_shape(n, D), low_shape(n, D),
        low_shape(n, D), low_shape(D, n), low_shape(n, D), low_shape(n, D), low_shape(D, n),
        wide_shape(images, HEADS, PATCH), wide_shape(images, HEADS, PATCH),
    )
    return pl.pallas_call(
        gather_kernel,
        out_shape=outs,
        in_specs=[VMEM] * 12 + [ANY] * 4,
        out_specs=[ANY] * len(outs),
        scratch_shapes=[
            v((D, 3 * D), BF16), v((D, D), BF16), v((4, D, D), BF16), v((4, D, D), BF16),
            v((n, D), BF16), v((n, 3 * D), BF16), v((n, D), BF16), v((n, D), BF16), v((n, D), F32), v((n, D), BF16),
            v((n, D), BF16), v((D, n), BF16), v((D, n), BF16),
            v((images, HEADS, PATCH), F32), v((images, HEADS, PATCH), F32),
            v((8, 256, PATCH), F32), v((8, 256, PATCH), BF16), v((PATCH, D), F32), v((HEADS, PATCH), F32),
            v((CLS, D), F32), v((CLS, 3 * D), F32), v((2, images * PATCH, 128), F32), v((16, 256), F32),
            v((16, 256), BF16), v((4, 16, 256), BF16), v((16, D), F32), v((8, 3 * D), F32),
            pltpu.SemaphoreType.DMA((2, 6, 7)), pltpu.SemaphoreType.DMA((6,)), pltpu.SemaphoreType.DMA((2, 3)),
            pltpu.SemaphoreType.DMA((18,)),
        ],
        compiler_params=pltpu.CompilerParams(collective_id=0, has_side_effects=True, vmem_limit_bytes=LIMIT),
        cost_estimate=pl.CostEstimate(flops=18 * 2**30, bytes_accessed=64 * 2**20, transcendentals=3 * 2**20),
        name="gather_and_attention",
    )(flat, cot, *vectors, w_qkv, w_out, w_up, w_down)


def backward(nz, images, vec, *arrays):
    n = images * PATCH + CLS
    tokens = images * (PATCH + 1)
    v = pltpu.VMEM
    chunks, sizes = chunk_layout(nz)
    outs = (low_shape(tokens, D), low_shape(tokens, D), low_shape(sizes["total"], TILE), low_shape(8, n, TILE))
    return pl.pallas_call(
        functools.partial(backward_kernel, nz, chunks),
        out_shape=outs,
        in_specs=[VMEM] + [ANY] * len(arrays),
        out_specs=[ANY] * len(outs),
        scratch_shapes=[
            v((sizes["buf"], TILE), BF16), v((2, 2048, TILE), BF16), v((sizes["y_recv"], TILE), BF16),
            v((sizes["x_recv"], TILE), BF16), v((nz - 1, sizes["z_recv"], TILE), BF16), v((n, D), F32), v((n, D), BF16),
            v((10, 8, D), F32), v((8, TILE), F32), v((16, D), F32), v((8, 3 * D), F32), v((8, TILE), F32),
            v((16, TILE), F32),
            pltpu.SemaphoreType.DMA((2, len(chunks), 3 * nz)), pltpu.SemaphoreType.DMA((2, 8)),
            pltpu.SemaphoreType.REGULAR, pltpu.SemaphoreType.DMA((8,)), pltpu.SemaphoreType.DMA((2, 2)),
            pltpu.SemaphoreType.DMA((2,)), pltpu.SemaphoreType.DMA((1,)), pltpu.SemaphoreType.DMA((2 * len(chunks),)),
        ],
        compiler_params=pltpu.CompilerParams(collective_id=1, has_side_effects=True, vmem_limit_bytes=LIMIT),
        cost_estimate=pl.CostEstimate(flops=66 * 2**30, bytes_accessed=128 * 2**20, transcendentals=8 * 2**20),
        name="layer_backward",
    )(vec, *arrays), chunks


def on_device(
    tokens, norm1_gain, norm1_shift, w_qkv, bias_qv, w_out, bias_out, scale_one, norm2_gain, norm2_shift, w_up, bias_up,
    w_down, bias_down, scale_two, cotangent,
):
    images, length, _ = tokens.shape
    nz = lax.axis_size("replica") // 2
    flatten = lambda a: jnp.transpose(a, (1, 0, 2)).reshape(images * length, D)
    restore = lambda a: jnp.transpose(a.reshape(length, images, D), (1, 0, 2))
    vectors = (norm1_gain, norm1_shift, bias_out, scale_one, norm2_gain, norm2_shift, bias_down, scale_two, bias_qv, bias_up)
    full_qkv, full_out, full_up, full_down, vec, *kept = forward(
        flatten(tokens), flatten(cotangent), vectors, w_qkv, w_out, w_up, w_down)
    (result, grad_tokens, sums, _), chunks = backward(nz, images, vec, full_qkv, full_out, full_up, full_down, *kept)
    return (restore(result), restore(grad_tokens)) + tuple(convert(chunks, sums))


def solution(mesh):
    placed = (
        P(("shard", "replica"), None, None),
        P("shard"),
        P("shard"),
        P("shard", None),
        P("shard"),
        P("shard", None),
        P("shard"),
        P("shard"),
        P("shard"),
        P("shard"),
        P(None, "shard"),
        P("shard"),
        P("shard", None),
        P("shard"),
        P("shard"),
        P(("shard", "replica"), None, None),
    )
    return jax.shard_map(
        on_device,
        mesh=mesh,
        in_specs=placed,
        out_specs=(
            P(("shard", "replica"), None, None),
            P(("shard", "replica"), None, None),
            P("shard"),
            P("shard"),
            P("shard", None),
            P("shard"),
            P("shard", None),
            P("shard"),
            P("shard"),
            P("shard"),
            P("shard"),
            P(None, "shard"),
            P("shard"),
            P("shard", None),
            P("shard"),
            P("shard"),
        ),
        check_vma=False,
    )
```

```python
import functools

import jax
import jax.numpy as jnp
from jax import lax
from jax.experimental import pallas as pl
from jax.experimental.pallas import tpu as pltpu
from jax.sharding import PartitionSpec as P

F32 = jnp.float32
BF16 = jnp.bfloat16
D = 1024
FF = 4096
HEADS = 16
PATCH = 128
CLS = 16
TILE = 512
FACTOR = 0.125
MESH = pl.DeviceIdType.MESH


def dot(a, b):
    return jnp.dot(a, b, preferred_element_type=F32)


def dot_nt(a, b):
    return lax.dot_general(a, b, (((1,), (1,)), ((), ())), preferred_element_type=F32)


def dot_tn(a, b):
    return lax.dot_general(a, b, (((0,), (0,)), ((), ())), preferred_element_type=F32)


def at(index, size):
    return pl.ds(pl.multiple_of(index * size, size), size)


def head_mask():
    lane = lax.shift_right_logical(lax.broadcasted_iota(jnp.int32, (HEADS, D), 1), 6)
    return lane == lax.broadcasted_iota(jnp.int32, (HEADS, D), 0)


def split_pair(v):
    low = lax.broadcasted_iota(jnp.int32, v.shape, 1) < 64
    zero = jnp.zeros_like(v)
    return jnp.concatenate([jnp.where(low, v, zero), jnp.where(low, zero, v)], 0)


def merge_pair(v):
    n = v.shape[0] // 2
    low = lax.broadcasted_iota(jnp.int32, (n, v.shape[1]), 1) < 64
    return jnp.where(low, v[:n], v[n:])


def place():
    s = lax.axis_index("shard")
    r = lax.axis_index("replica")
    x = lax.rem(r, 2)
    z = lax.div(r, 2)
    return s, r, x, z


def peers(s, r):
    sib = s + 1 - 2 * lax.rem(s, 2)
    across = lax.rem(s + 2, 4)
    side = r + 1 - 2 * lax.rem(r, 2)
    return sib, across, side


def rows_loop(n, step, body):
    lax.fori_loop(0, n // step, lambda k, c: (body(at(k, step)), c)[1], 0, unroll=5)


def unpack_vectors(vec, vecf, bias_qkv):
    for v in range(8):
        for s in range(4):
            vecf[v : v + 1, s * 256 : (s + 1) * 256] = vec[s, v : v + 1, :].astype(F32)
    bias_qkv[...] = jnp.zeros_like(bias_qkv)
    for s in range(4):
        for t in range(2):
            col = (s * 2 + t) * 256 + (D if s >= 2 else 0)
            bias_qkv[0:1, col : col + 256] = vec[s, 8 + t : 9 + t, :].astype(F32)


def layer_norm(v, gain, shift):
    c = v - jnp.mean(v, axis=-1, keepdims=True)
    inv = lax.rsqrt(jnp.mean(c * c, axis=-1, keepdims=True) + 1e-06)
    return c * inv * gain + shift


def to_images(src, dst, turn):
    images = (src.shape[0]) // (PATCH + 1)
    main = images * PATCH

    def lane_block(l, carry):
        cols = at(l, 128)
        slot = lax.rem(l, 2)
        turn[slot] = src[0:main, cols].astype(F32)
        for i in range(images):
            dst[i * PATCH : (i + 1) * PATCH, cols] = turn[slot, pl.ds(i, PATCH, stride=images), :].astype(BF16)
        return carry

    lax.fori_loop(0, D // 128, lane_block, 0)
    last = src[main : main + images, :].astype(F32)
    dst[main:, :] = jnp.concatenate([last, jnp.zeros((CLS - images, D), F32)], 0).astype(BF16)


def pack_vectors(vectors, dst):
    row = 0
    for v in vectors:
        count = v.shape[0] // 256
        wide = v[...].astype(F32)
        for k in range(count):
            dst[row : row + 1, :] = wide[k * 256 : (k + 1) * 256].reshape(1, 256)
            row += 1


def attend(i, qkv, qkv_cls, scores, probs, mix, probs_cls, att, att_cls, lse, lse_cls):
    rows = at(i, PATCH)
    mask = head_mask()
    own = qkv_cls[pl.ds(i, 1), :]
    q_c, k_c, v_c = own[:, :D] * FACTOR, own[:, D : 2 * D], own[:, 2 * D :]
    q_bd = jnp.where(mask, q_c, 0.0)
    k_bd = jnp.where(mask, k_c, 0.0).astype(BF16)
    v_bd = jnp.where(mask, v_c, 0.0).astype(BF16)
    to_cls = dot_nt(k_bd, qkv[rows, 0:D]) * FACTOR
    of_cls = dot_nt(q_bd.astype(BF16), qkv[rows, D : 2 * D])
    corner = jnp.sum(q_bd * k_c, axis=1, keepdims=True)
    top = jnp.maximum(jnp.max(of_cls, axis=1, keepdims=True), corner)
    e_row = jnp.exp(of_cls - top)
    e_cor = jnp.exp(corner - top)
    total = jnp.sum(e_row, axis=1, keepdims=True) + e_cor
    inv = 1.0 / total
    row = dot((e_row * inv).astype(BF16), qkv[rows, 2 * D : 3 * D])
    row = row + (e_cor * inv).astype(BF16).astype(F32) * v_c
    att_cls[pl.ds(i, 1), :] = jnp.sum(jnp.where(mask, row, 0.0), axis=0, keepdims=True)
    lse_cls[i] = jnp.broadcast_to(top + jnp.log(total), (HEADS, PATCH))
    for g in range(HEADS // 2):
        q2 = qkv[rows, g * 128 : g * 128 + 128] * jnp.asarray(FACTOR, BF16)
        scores[g] = dot_nt(split_pair(qkv[rows, g * 128 + D : g * 128 + D + 128]), q2)
    for g in range(HEADS // 2):
        for u in range(2):
            h = 2 * g + u
            part = scores[g, u * PATCH : (u + 1) * PATCH, :]
            extra = to_cls[h : h + 1, :]
            top = jnp.maximum(jnp.max(part, axis=0, keepdims=True), extra)
            e_part = jnp.exp(part - top)
            e_extra = jnp.exp(extra - top)
            total = jnp.sum(e_part, axis=0, keepdims=True) + e_extra
            inv = 1.0 / total
            probs[g, u * PATCH : (u + 1) * PATCH, :] = (e_part * inv).astype(BF16)
            probs_cls[h : h + 1, :] = e_extra * inv
            lse[i, h : h + 1, :] = top + jnp.log(total)
    for g in range(HEADS // 2):
        v2 = split_pair(qkv[rows, g * 128 + 2 * D : g * 128 + 2 * D + 128])
        mix[:, g * 128 : g * 128 + 128] = dot_tn(probs[g], v2)
    att[rows, :] = (mix[...] + dot_tn(probs_cls[...].astype(BF16), v_bd)).astype(BF16)


class Gather:
    KINDS = ("own", "far", "x1", "z1", "x2", "z2", "p0", "p1", "p2", "p3", "p4")

    def __init__(self, number, rows, src, dst, sems, local):
        s, r, x, z = place()
        sib, across, side = peers(s, r)
        self.number, self.sems = number, sems
        near = lax.rem(z, 2)
        level = {"replica": (z + 1 - 2 * near) * 2 + x}
        side, sib = {"replica": side}, {"shard": sib}
        size = rows // 4
        half = size // 2

        def start(zz, xx):
            return pl.multiple_of((2 * zz + xx) * size, 16)

        def same(first, count, to):
            ref = dst(across, pl.multiple_of(first, 16), count)
            return ref, ref, to

        mine, by_x, by_z, by_both = start(near, x), start(near, 1 - x), start(1 - near, x), start(1 - near, 1 - x)
        self.parts = {
            "own": (dst(s, 0, rows), dst(s, 0, rows), sib),
            "far": (dst(s, mine, size), dst(s, mine, size), {"shard": across}),
            "x1": same(mine, size, side),
            "z1": same(mine, size, level),
            "x2": same(by_z, half, side),
            "z2": same(by_x + half, half, level),
            "p0": same(mine, size, sib),
            "p1": same(by_x, size, sib),
            "p2": same(by_z, size, sib),
            "p3": same(by_both, half, sib),
            "p4": same(by_both + half, half, sib),
        }
        self.local = pltpu.make_async_copy(src(0, rows), dst(s, 0, rows), local.at[number])

    def copy(self, kind):
        a, b, to = self.parts[kind]
        k = self.KINDS.index(kind)
        return pltpu.make_async_remote_copy(
            a, b, self.sems.at[0, self.number, k], self.sems.at[1, self.number, k], device_id=to, device_id_type=MESH
        )

    def load(self):
        self.local.start()

    def begin(self):
        self.local.wait()
        self.copy("far").start()

    def share(self):
        self.copy("own").start()

    def on_far(self):
        self.copy("far").wait_recv()
        for kind in ("x1", "z1", "p0"):
            self.copy(kind).start()

    def on_near(self):
        self.copy("x1").wait_recv()
        self.copy("z2").start()
        self.copy("p1").start()
        self.copy("z1").wait_recv()
        self.copy("x2").start()
        self.copy("p2").start()

    def on_last(self):
        self.copy("x2").wait_recv()
        self.copy("p3").start()
        self.copy("z2").wait_recv()
        self.copy("p4").start()

    def ready(self):
        for kind in ("own", "p0", "p1", "p2", "p3", "p4"):
            self.copy(kind).wait_recv()

    def drain(self):
        for kind in self.KINDS:
            self.copy(kind).wait_send()


def gather_kernel(
    tokens, cot, v0, v1, v2, v3, v4, v5, v6, v7, v8, v9, w_qkv, w_out, w_up, w_down,
    qkv_w_o, out_w_o, up_w_o, down_w_o, vec_all, qkv_o, act_t_o, x_o, att_t_o, mid_o, branch_o, act2_o, act2_t_o, up_o,
    dr_o, dr_t_o, lse_o, lsec_o,
    full_qkv, full_out, full_up, full_down, x_s, qkv, act, att, mid, branch, act2, turned_a, turned_b, lse, lsec,
    scores, probs, mix, probs_cls, cls, qkv_cls, turn, vec32, vec_own_s, vec, vecf, bias_qkv,
    sems, local, vsem, osem,
):
    s, r, x, z = place()
    sib, across, side = peers(s, r)
    n = x_s.shape[0]
    images = lse.shape[0]
    main = images * PATCH

    vec32[...] = jnp.zeros_like(vec32)
    pack_vectors((v0, v1, v2, v3, v4, v5, v6, v7, v8, v9), vec32)
    vec_own_s[...] = vec32[...].astype(BF16)
    barrier = pltpu.get_barrier_semaphore()
    level = (z + 1 - 2 * lax.rem(z, 2)) * 2 + x
    for to in ({"shard": sib}, {"shard": across}, {"replica": side}, {"replica": level}):
        pl.semaphore_signal(barrier, inc=1, device_id=to, device_id_type=MESH)

    def unit(number, rows, src, dst):
        return Gather(number, rows, src, dst, sems, local)

    g_qkv = unit(0, 256, lambda a, k: w_qkv.at[pl.ds(a, k), :],
                 lambda p, a, k: full_qkv.at[pl.ds(pl.multiple_of(p * 256 + a, 16), k), :])
    g_out = unit(1, 256, lambda a, k: w_out.at[pl.ds(a, k), :],
                 lambda p, a, k: full_out.at[pl.ds(pl.multiple_of(p * 256 + a, 16), k), :])

    def up_unit(number, t):
        return unit(number, TILE, lambda a, k: w_up.at[pl.ds(a + t * TILE, k), :],
                    lambda p, a, k: full_up.at[p, pl.ds(pl.multiple_of(a + t * TILE, 16), k), :])

    def down_unit(number, t):
        return unit(number, TILE, lambda a, k: w_down.at[pl.ds(a + t * TILE, k), :],
                    lambda p, a, k: full_down.at[p, pl.ds(pl.multiple_of(a + t * TILE, 16), k), :])

    g_up0, g_down0, g_up1, g_down1 = up_unit(2, 0), down_unit(3, 0), up_unit(4, 1), down_unit(5, 1)

    for g in (g_qkv, g_out, g_up0, g_down0, g_up1, g_down1):
        g.load()
    pl.semaphore_wait(barrier, 4)

    def vec_copy(k, src, slot, to):
        return pltpu.make_async_remote_copy(src, vec.at[slot], vsem.at[0, k], vsem.at[1, k], device_id=to,
                                            device_id_type=MESH)

    vec_own = vec_copy(0, vec_own_s, s, {"shard": sib})
    vec_far = vec_copy(1, vec_own_s, s, {"shard": across})
    vec_pass = vec_copy(2, vec.at[across], across, {"shard": sib})
    vec_own.start()
    vec_far.start()
    g_qkv.begin()
    g_qkv.share()
    g_out.begin()
    vec[s] = vec_own_s[...]

    to_images(tokens, x_s, turn)
    outs = {}

    def send_out(k, src, dst):
        outs[k] = pltpu.make_async_copy(src, dst, osem.at[k])
        outs[k].start()

    send_out(0, x_s, x_o)
    vec_far.wait_recv()
    vec_pass.start()
    vec_own.wait_recv()
    vec_pass.wait_recv()
    unpack_vectors(vec, vecf, bias_qkv)

    def first_norm(rows):
        act[rows, :] = layer_norm(x_s[rows, :].astype(F32), vecf[0:1, :], vecf[1:2, :]).astype(BF16)

    rows_loop(n, 16, first_norm)
    g_qkv.on_far()
    for g in (g_up0, g_down0, g_up1, g_down1):
        g.begin()
    transpose_into(act, turned_b)
    send_out(1, turned_b, act_t_o)
    g_qkv.on_near()
    to_images(cot, branch, turn)

    def down_rows(rows):
        act2[rows, :] = (branch[rows, :].astype(F32) * vecf[7:8, :]).astype(BF16)

    rows_loop(n, 16, down_rows)
    g_qkv.on_last()
    g_out.on_far()
    send_out(14, branch, up_o)
    send_out(15, act2, dr_o)
    transpose_into(act2, turned_a)
    send_out(16, turned_a, dr_t_o)
    g_out.on_near()
    g_qkv.ready()
    send_out(4, full_qkv, qkv_w_o)
    for g in (g_out, g_up0, g_down0):
        g.share()

    def qkv_tile(j, carry):
        cols = at(j, TILE)
        low = (dot(act[...], full_qkv[:, cols]) + bias_qkv[0:1, cols]).astype(BF16)
        qkv[:, cols] = low
        qkv_cls[:, cols] = low[main:].astype(F32)
        return carry

    lax.fori_loop(0, 3 * D // TILE, qkv_tile, 0)
    send_out(2, qkv, qkv_o)
    send_out(3, vec, vec_all)
    cls[...] = jnp.zeros_like(cls)
    g_out.on_last()
    g_up0.on_far()
    plan = {1: [g_up0.on_near], 2: [g_down0.on_far], 3: [g_up0.on_last, g_up1.share], 4: [g_down0.on_near, g_up1.on_far],
            6: [g_down0.on_last, g_down1.share], 7: [g_up1.on_near, g_down1.on_far]}

    def image(i, carry):
        for k, steps in plan.items():
            @pl.when(i == k)
            def _(steps=steps):
                for step in steps:
                    step()

        attend(i, qkv, qkv_cls, scores, probs, mix, probs_cls, att, cls, lse, lsec)
        return carry

    lax.fori_loop(0, images, image, 0)
    att[main:, :] = cls[...].astype(BF16)
    outs.pop(16).wait()
    transpose_into(att, turned_a)
    send_out(8, turned_a, att_t_o)
    send_out(9, lse, lse_o)
    send_out(10, lsec, lsec_o)
    g_out.ready()
    outs.pop(14).wait()
    for j in range(D // TILE):
        cols = slice(j * TILE, (j + 1) * TILE)
        out = dot(att[...], full_out[:, cols]) + vecf[2:3, cols]
        branch[:, cols] = out.astype(BF16)
        mid[:, cols] = x_s[:, cols].astype(F32) + vecf[3:4, cols] * out
    send_out(11, mid, mid_o)
    send_out(12, branch, branch_o)
    g_up1.on_last()
    g_down1.on_near()

    def second_norm(rows):
        act2[rows, :] = layer_norm(mid[rows, :], vecf[4:5, :], vecf[5:6, :]).astype(BF16)

    outs.pop(15).wait()
    rows_loop(n, 16, second_norm)
    send_out(13, act2, act2_o)
    outs.pop(1).wait()
    transpose_into(act2, turned_b)
    send_out(17, turned_b, act2_t_o)
    g_down1.on_last()
    half = lambda t: pl.ds(t * TILE, TILE)
    send_out(5, full_out, out_w_o)
    for k, (g, src, dst, t) in enumerate(((g_up0, full_up, up_w_o, 0), (g_down0, full_down, down_w_o, 0),
                                          (g_up1, full_up, up_w_o, 1), (g_down1, full_down, down_w_o, 1))):
        g.ready()
        send_out(18 + k, src.at[:, half(t), :], dst.at[:, half(t), :])
    for copy in outs.values():
        copy.wait()
    for g in (g_qkv, g_out, g_up0, g_down0, g_up1, g_down1):
        g.drain()
    for copy in (vec_own, vec_far, vec_pass):
        copy.wait_send()


class Chunk:
    def __init__(self, index, rows, mine, y_send, y_recv, x_recv, z_recv, far):
        self.index, self.rows, self.mine, self.y_send, self.far = index, rows, mine, y_send, far
        self.y_recv, self.x_recv, self.z_recv = y_recv, x_recv, z_recv


def chunk_layout(nz):
    last = 32 * nz
    sizes = [1024, 1024, 1024, 1024, 512, 1024, 512, last]
    y_base = 2048
    y_a = y_base
    y_b = y_a + 2048 + last
    mine_base = y_b + 2048
    chunks = []
    mine = mine_base
    late = 0
    xr = zr = 0
    for k, rows in enumerate(sizes):
        if k < 2:
            ys, yr = y_a + 1024 * k, 1024 * k
        elif k < 4:
            ys, yr = y_b + 1024 * (k - 2), 2048 + last + 1024 * (k - 2)
        else:
            ys, yr = y_a + late, late
            late += rows
        far = mine_base + sum(sizes) + 512 * k if k < 2 else ys
        chunks.append(Chunk(k, rows, mine, ys, yr, xr, zr, far))
        mine += rows
        xr += rows // 2
        zr += rows // 2 // nz
    return chunks, dict(buf=mine + 1024, total=sum(sizes), mine=mine_base, y_recv=2 * 2048 + last, x_recv=xr, z_recv=zr)


def add_rows(dst, d0, src, s0, rows):
    step = next(k for k in (128, 96, 64, 32, 16) if rows % k == 0)

    def body(k, carry):
        d = pl.ds(pl.multiple_of(d0 + k * step, 16), step)
        t = pl.ds(pl.multiple_of(s0 + k * step, 16), step)
        dst[d, :] = (dst[d, :].astype(F32) + src[t, :].astype(F32)).astype(BF16)
        return carry

    lax.fori_loop(0, rows // step, body, 0)


class Reduce:
    def __init__(self, nz, buf, core_recv, y_recv, x_recv, z_recv, sems, core_sems, credit):
        self.nz, self.buf, self.core_recv = nz, buf, core_recv
        self.y_recv, self.x_recv, self.z_recv = y_recv, x_recv, z_recv
        self.sems, self.core_sems, self.credit = sems, core_sems, credit
        self.s, self.r, self.x, self.z = place()
        self.sib, self.across, self.side = peers(self.s, self.r)

    def remote(self, src, dst, chunk, kind, to):
        return pltpu.make_async_remote_copy(
            src, dst, self.sems.at[0, chunk.index, kind], self.sems.at[1, chunk.index, kind], device_id=to,
            device_id_type=MESH)

    def peer(self, k):
        return {"replica": lax.rem(self.z + k, self.nz) * 2 + self.x}

    def core_copy(self, turn, rows):
        slot = turn % 2
        return pltpu.make_async_remote_copy(
            self.buf.at[pl.ds(0, rows), :], self.core_recv.at[slot, pl.ds(0, rows), :],
            self.core_sems.at[0, turn], self.core_sems.at[1, turn], device_id={"shard": self.sib}, device_id_type=MESH)

    def add_core(self, turn, first, dst, rows):
        add_rows(self.buf, dst, self.core_recv.at[turn % 2], first, rows)

    def y_copy(self, c):
        return self.remote(self.buf.at[pl.ds(c.y_send, c.rows), :], self.y_recv.at[pl.ds(c.y_recv, c.rows), :], c, 0,
                           {"shard": self.across})

    def x_copy(self, c):
        half = c.rows // 2
        return self.remote(self.buf.at[pl.ds(pl.multiple_of(c.mine + (1 - self.x) * half, 16), half), :],
                           self.x_recv.at[pl.ds(c.x_recv, half), :], c, 1, {"replica": self.side})

    def quarter(self, c, x, z):
        half = c.rows // 2
        size = half // self.nz
        return pl.ds(pl.multiple_of(c.mine + x * half + z * size, 16), size)

    def z_copy(self, c, k):
        size = c.rows // 2 // self.nz
        return self.remote(self.buf.at[self.quarter(c, self.x, lax.rem(self.z + k, self.nz)), :],
                           self.z_recv.at[k - 1, pl.ds(c.z_recv, size), :], c, 1 + k, self.peer(k))

    def done(self, first, c, z):
        size = c.rows // 2 // self.nz
        return pl.ds(pl.multiple_of(first + z * size, 16), size)

    def back_z(self, c, k):
        part = self.x_recv.at[self.done(c.x_recv, c, self.z), :]
        return self.remote(part, part, c, self.nz + k, self.peer(k))

    def back_x(self, c, k):
        z = lax.rem(self.z + self.nz - k, self.nz)
        return self.remote(self.x_recv.at[self.done(c.x_recv, c, z), :], self.buf.at[self.done(c.far, c, z), :], c,
                           2 * self.nz + k, {"replica": self.side})

    def on_y(self, c):
        self.y_copy(c).wait_recv()
        add_rows(self.buf, c.mine, self.y_recv, c.y_recv, c.rows)
        self.y_copy(c).wait_send()
        self.x_copy(c).start()

    def on_x(self, c):
        half = c.rows // 2
        self.x_copy(c).wait_recv()
        add_rows(self.buf, c.mine + self.x * half, self.x_recv, c.x_recv, half)
        for k in range(1, self.nz):
            self.z_copy(c, k).start()

    def on_z(self, c):
        size = c.rows // 2 // self.nz
        start = c.mine + self.x * (c.rows // 2) + self.z * size
        for k in range(1, self.nz):
            self.z_copy(c, k).wait_recv()
        step = next(k for k in (64, 48, 32, 16) if size % k == 0)

        def body(i, carry):
            d = pl.ds(pl.multiple_of(start + i * step, 16), step)
            total = self.buf[d, :].astype(F32)
            for k in range(1, self.nz):
                total = total + self.z_recv[k - 1, pl.ds(pl.multiple_of(c.z_recv + i * step, 16), step), :].astype(F32)
            to = pl.ds(pl.multiple_of(c.x_recv + self.z * size + i * step, 16), step)
            self.x_recv[to, :] = total.astype(BF16)
            return carry

        lax.fori_loop(0, size // step, body, 0)
        for k in range(1, self.nz):
            self.back_z(c, k).start()
        self.back_x(c, 0).start()

    def on_back(self, c):
        for k in range(1, self.nz):
            self.back_z(c, k).wait_recv()
            self.back_x(c, k).start()

    def finish(self, c):
        for k in range(self.nz):
            self.back_x(c, k).wait_recv()

    def drain(self, c):
        self.x_copy(c).wait_send()
        for k in range(1, self.nz):
            self.z_copy(c, k).wait_send()
            self.back_z(c, k).wait_send()
        for k in range(self.nz):
            self.back_x(c, k).wait_send()


def fold(v):
    return jnp.sum(v.reshape(v.shape[0] // 8, 8, v.shape[1]), axis=0)


def gelu_both(v):
    e = jnp.exp(-0.5 * v * v)
    t = 1.0 / (1.0 + 0.23164189 * jnp.abs(v))
    poly = ((((1.061405429 * t - 1.453152027) * t + 1.421413741) * t - 0.284496736) * t + 0.254829592) * t
    tail = 0.5 * poly * e
    phi = jnp.where(v >= 0.0, 1.0 - tail, tail)
    return v * phi, phi + v * e * 0.3989422804014327


def transpose_into(src, dst):
    for c in range(D // 128):
        dst[c * 128 : (c + 1) * 128, :] = src[:, c * 128 : (c + 1) * 128].T


def attend_back(i, qkv, qkv_cls, datt, datt_cls, lse, lsec, scores, dprobs, probs, dscores, cls_row, joint_cls, sum_q, sum_v):
    rows = at(i, PATCH)
    mask = head_mask()
    own = qkv_cls[pl.ds(i, 1), :]
    do_c = datt_cls[pl.ds(i, 1), :]
    q_c, k_c, v_c = own[:, :D] * FACTOR, own[:, D : 2 * D], own[:, 2 * D :]
    pick = lambda v: jnp.where(mask, v, 0.0)
    q_w, k_w, v_w, do_w = pick(q_c), pick(k_c), pick(v_c), pick(do_c)
    q_bd, k_bd, v_bd, do_bd = (v.astype(BF16) for v in (q_w, k_w, v_w, do_w))
    queries, keys, values = (qkv[rows, k * D : (k + 1) * D] for k in range(3))
    grads = datt[rows, :]
    low = lambda v: v.astype(BF16)
    top = lsec[i][:, 0:1]
    p_row = jnp.exp(dot_nt(q_bd, keys) - top)
    p_cor = jnp.exp(jnp.sum(q_w * k_c, axis=1, keepdims=True) - top)
    dp_row = dot_nt(do_bd, values)
    dp_cor = jnp.sum(do_w * v_c, axis=1, keepdims=True)
    delta = jnp.sum(p_row * dp_row, axis=1, keepdims=True) + p_cor * dp_cor
    ds_row = low(p_row * (dp_row - delta))
    ds_cor = low(p_cor * (dp_cor - delta)).astype(F32)
    p_col = jnp.exp(dot_nt(k_bd, queries) * FACTOR - lse[i])
    dp_col = dot_nt(v_bd, grads)
    for g in range(HEADS // 2):
        lanes = slice(g * 128, (g + 1) * 128)
        q2 = qkv[rows, lanes] * jnp.asarray(FACTOR, BF16)
        scores[g] = dot_nt(split_pair(qkv[rows, g * 128 + D : g * 128 + D + 128]), q2)
        dprobs[g] = dot_nt(split_pair(qkv[rows, g * 128 + 2 * D : g * 128 + 2 * D + 128]), datt[rows, lanes])
    for g in range(HEADS // 2):
        for u in range(2):
            h = 2 * g + u
            half = slice(u * PATCH, (u + 1) * PATCH)
            part = jnp.exp(scores[g, half, :] - lse[i, h : h + 1, :])
            dpart = dprobs[g, half, :]
            p_h, dp_h = p_col[h : h + 1, :], dp_col[h : h + 1, :]
            delta = jnp.sum(part * dpart, axis=0, keepdims=True) + p_h * dp_h
            probs[g, half, :] = low(part)
            dscores[g, half, :] = low(part * (dpart - delta))
            cls_row[h : h + 1, :] = p_h * (dp_h - delta)
    ds_col = low(cls_row[...])
    total = lambda v: jnp.sum(jnp.where(mask, v, 0.0), axis=0, keepdims=True)
    joint_cls[pl.ds(i, 1), 0:D] = FACTOR * (total(dot(ds_row, keys)) + jnp.sum(ds_cor * k_w, axis=0, keepdims=True))
    joint_cls[pl.ds(i, 1), D : 2 * D] = FACTOR * total(dot(ds_col, queries)) + jnp.sum(ds_cor * q_w, axis=0, keepdims=True)
    joint_cls[pl.ds(i, 1), 2 * D : 3 * D] = total(dot(low(p_col), grads)) + jnp.sum(
        low(p_cor).astype(F32) * do_w, axis=0, keepdims=True)
    p_row = low(p_row)
    for g in range(HEADS // 2):
        lanes = slice(g * 128, (g + 1) * 128)
        klanes = slice(g * 128 + D, g * 128 + D + 128)
        vlanes = slice(g * 128 + 2 * D, g * 128 + 2 * D + 128)
        q2 = qkv[rows, lanes] * jnp.asarray(FACTOR, BF16)
        dv = merge_pair(dot(probs[g], datt[rows, lanes])) + dot_tn(p_row, do_bd[:, lanes])
        dk = merge_pair(dot(dscores[g], q2)) + dot_tn(ds_row, q_bd[:, lanes])
        dq = (dot_tn(dscores[g], split_pair(qkv[rows, klanes])) + dot_tn(ds_col, k_bd[:, lanes])) * FACTOR
        qkv[rows, lanes] = low(dq)
        qkv[rows, klanes] = low(dk)
        qkv[rows, vlanes] = low(dv)
        sum_q[:, lanes] += fold(dq)
        sum_v[:, lanes] += fold(dv)


def to_tokens(src, dst, turn):
    images = dst.shape[0] // (PATCH + 1)
    main = images * PATCH

    def lane_block(l, carry):
        cols = at(l, 128)
        slot = lax.rem(l, 2)
        for i in range(images):
            turn[slot, pl.ds(i, PATCH, stride=images), :] = src[i * PATCH : (i + 1) * PATCH, cols].astype(F32)
        dst[0:main, cols] = turn[slot].astype(BF16)
        return carry

    lax.fori_loop(0, D // 128, lane_block, 0)
    dst[main : main + images, :] = src[main:, :].astype(F32)[0:images].astype(BF16)


def backward_kernel(
    nz, chunks, vec, full_qkv, full_out, full_up, full_down, qkv_h, act_t_h, x_h, att_t_h, mid_h, branch_h, act2_h,
    act2_t_h, up_h, dr_h, dr_t_h, lse_h, lsec_h,
    result_o, tokens_o, sums_o, hidden_o,
    buf, core_recv, y_recv, x_recv, z_recv, gmid, up_s, acc, sums_up, vecf, bias_qkv, bias_up, vrows,
    sems, core_sems, credit, dsem, wsem, hsem, osem, fsem,
):
    images = lse_h.shape[0]
    n = gmid.shape[0]
    main = images * PATCH
    red = Reduce(nz, buf, core_recv, y_recv, x_recv, z_recv, sems, core_sems, credit)
    s = red.s
    cd0, cu0, cd1, cu1, co, cq0, cq1, cv = chunks

    def load(k, src, dst):
        copy = pltpu.make_async_copy(src, dst, dsem.at[k])
        copy.start()
        return copy

    def relative(rel):
        low, high = lax.rem(rel, 2), lax.div(rel, 2)
        return s + low * (1 - 2 * lax.rem(s, 2)) + high * (2 - 4 * lax.div(s, 2))

    def target(rel, chunk):
        low, high = lax.rem(rel, 2), lax.div(rel, 2)
        return low * (1 - high) * chunk.rows + (1 - low) * (high * chunk.y_send + (1 - high) * chunk.mine)

    got_up = load(7, up_h, up_s)

    def ffn(dr, dr_t, act2, act2_t, w_up, w_down, hid, br):
        gots = [load(0, act2_h, act2), load(1, dr_h, dr), load(2, dr_t_h, dr_t), load(3, act2_t_h, act2_t)]

        def fetch(j, slot):
            piece, t = relative(3 - lax.rem(j, 4)), lax.div(j, 4)
            return (
                pltpu.make_async_copy(full_up.at[piece, :, at(t, TILE)], w_up.at[slot], wsem.at[0, slot]),
                pltpu.make_async_copy(full_down.at[piece, at(t, TILE), :], w_down.at[slot], wsem.at[1, slot]),
            )

        def keep(j, slot):
            return pltpu.make_async_copy(hid.at[slot], hidden_o.at[j], hsem.at[slot])

        for copy in fetch(0, 0):
            copy.start()
        barrier = pltpu.get_barrier_semaphore()
        partners = [{"shard": red.sib}, {"shard": red.across}, {"replica": red.side}]
        partners += [red.peer(k) for k in range(1, nz)]
        for to in partners:
            pl.semaphore_signal(barrier, inc=1, device_id=to, device_id_type=MESH)
        pl.semaphore_wait(barrier, len(partners))
        unpack_vectors(vec, vecf, bias_qkv)
        for p in range(4):
            for t in range(2):
                for k in range(2):
                    row = 10 + 2 * t + k
                    bias_up[2 * p + t : 2 * p + t + 1, k * 256 : (k + 1) * 256] = vec[p, row : row + 1, :].astype(F32)
        acc[...] = jnp.zeros_like(acc)
        gmid[...] = jnp.zeros_like(gmid)
        for start in (0, cv.rows, cv.y_send, cv.mine):
            buf[pl.ds(start, cv.rows), :] = jnp.zeros((cv.rows, TILE), BF16)
        for copy in gots:
            copy.wait()
        cut = 16 * (n // 32)
        first, second = slice(0, cut), slice(cut, n)

        def tile(j, carry):
            slot = lax.rem(j, 2)
            rel, t = 3 - lax.rem(j, 4), lax.div(j, 4)
            piece = relative(rel)
            low, high = lax.rem(rel, 2), lax.div(rel, 2)
            place_at = pl.multiple_of(
                (1 - low) * (high * (cd0.y_send + t * (cd1.y_send - cd0.y_send)) + (1 - high) * (cd0.mine + t * 2048)), 16)
            for copy in fetch(j, slot):
                copy.wait()

            @pl.when(j < 7)
            def _():
                for copy in fetch(j + 1, 1 - slot):
                    copy.start()

            @pl.when(j >= 2)
            def _():
                keep(j - 2, slot).wait()

            for k in (2, 4, 6):
                @pl.when(j == k)
                def _(k=k):
                    red.core_copy(k // 2 - 1, 2048).wait_send()

            bias = bias_up[pl.ds(2 * piece + t, 1), :]

            def both(rows, before, grad):
                hidden, step = gelu_both(before)
                hid[slot, rows, :] = hidden.astype(BF16)
                grad = grad * step
                br[rows, :] = grad.astype(BF16)
                return jnp.sum(grad, axis=0, keepdims=True)

            before0 = dot(act2[first, :], w_up[slot]) + bias
            grad0 = dot_nt(dr[first, :], w_down[slot])
            before1 = dot(act2[second, :], w_up[slot]) + bias
            column = both(first, before0, grad0)
            grad1 = dot_nt(dr[second, :], w_down[slot])
            gmid[first, :] += dot_nt(br[first, :], w_up[slot])
            column = column + both(second, before1, grad1)
            sums_up[pl.ds(2 * piece + t, 1), :] = column
            gmid[second, :] += dot_nt(br[second, :], w_up[slot])
            keep(j, slot).start()
            buf[pl.ds(place_at, D), :] = dot(dr_t[...], hid[slot]).astype(BF16)
            buf[pl.ds(pl.multiple_of(place_at + D, 16), D), :] = dot(act2_t[...], br[...]).astype(BF16)

            def y_part(turn, chunk):
                red.core_copy(turn, 2048).wait_recv()
                for k, c in enumerate(chunk):
                    red.add_core(turn, k * 1024, c.y_send, c.rows)
                    red.y_copy(c).start()

            def own_part(turn, chunk):
                red.core_copy(turn, 2048).wait_recv()
                red.add_core(turn, 0, chunk[0].mine, 2048)

            steps = {
                0: [lambda: red.core_copy(0, 2048).start()],
                1: [lambda: y_part(0, (cd0, cu0))],
                2: [lambda: red.core_copy(1, 2048).start()],
                3: [lambda: own_part(1, (cd0, cu0))],
                4: [lambda: red.core_copy(2, 2048).start(), lambda: red.on_y(cd0)],
                5: [lambda: y_part(2, (cd1, cu1))],
                6: [lambda: red.core_copy(3, 2048).start(), lambda: red.on_y(cu0), lambda: red.on_x(cd0)],
                7: [lambda: own_part(3, (cd1, cu1))],
            }
            for k, todo in steps.items():
                @pl.when(j == k)
                def _(todo=todo):
                    for step in todo:
                        step()
            return carry

        lax.fori_loop(0, 8, tile, 0)
        pl.semaphore_signal(credit, inc=1, device_id={"shard": red.across}, device_id_type=MESH)
        for j in (6, 7):
            keep(j, j % 2).wait()
        red.core_copy(3, 2048).wait_send()

    v = pltpu.VMEM
    pl.run_scoped(ffn, v((n, D), BF16), v((D, n), BF16), v((n, D), BF16), v((D, n), BF16), v((2, D, TILE), BF16),
                  v((2, TILE, D), BF16), v((2, n, TILE), BF16), v((n, TILE), BF16))
    got_up.wait()

    def spread(out, chunk, tile_rows):
        for p in range(4):
            low = lax.rem(lax.rem(s, 2) + p % 2, 2)
            high = lax.rem(lax.div(s, 2) + p // 2, 2)
            start = pl.multiple_of(target(low + 2 * high, chunk) + tile_rows, 16)
            buf[pl.ds(start, 256), :] = out[p * 256 : (p + 1) * 256].astype(BF16)

    def on_core(turn, chunk):
        red.core_copy(turn, 2 * chunk.rows).wait_recv()
        red.add_core(turn, 0, chunk.y_send, chunk.rows)
        red.y_copy(chunk).start()
        red.add_core(turn, chunk.rows, chunk.mine, chunk.rows)

    def attention(qkv, datt, brr, lse, lsec, scores, dprobs, probs, dscores, cls_row, qkv_cls, datt_cls, joint_cls):
        got_qkv, got_lse, got_lsec = load(0, qkv_h, qkv), load(1, lse_h, lse), load(2, lsec_h, lsec)

        def middle(mid, branch, att_t, w_out):
            got_mid, got_branch = load(3, mid_h, mid), load(4, branch_h, branch)
            got_att, got_out = load(5, att_t_h, att_t), load(6, full_out, w_out)
            red.on_z(cd0)
            got_mid.wait()
            got_branch.wait()

            def norm_rows(rows):
                m = mid[rows, :]
                c = m - jnp.mean(m, axis=-1, keepdims=True)
                inv = lax.rsqrt(jnp.mean(c * c, axis=-1, keepdims=True) + 1e-06)
                hat = c * inv
                g = gmid[rows, :]
                acc[4] += fold(g * hat)
                acc[5] += fold(g)
                sc = g * vecf[4:5, :]
                back = inv * (sc - jnp.mean(sc, axis=-1, keepdims=True)
                              - hat * jnp.mean(sc * hat, axis=-1, keepdims=True))
                gm = up_s[rows, :].astype(F32) + back
                gmid[rows, :] = gm
                acc[3] += fold(gm * branch[rows, :].astype(F32))
                gb = gm * vecf[3:4, :]
                acc[2] += fold(gb)
                brr[rows, :] = gb.astype(BF16)

            rows_loop(n, 16, norm_rows)
            red.on_x(cu0)
            got_att.wait()
            for q in range(2):
                spread(dot(att_t[...], brr[:, q * TILE : (q + 1) * TILE]), co, q * 256)
            red.core_copy(4, 2 * co.rows).start()
            got_out.wait()
            for q in range(2):
                datt[:, q * TILE : (q + 1) * TILE] = dot_nt(brr[...], w_out[q * TILE : (q + 1) * TILE, :]).astype(BF16)

        pl.run_scoped(middle, v((n, D), F32), v((n, D), BF16), v((D, n), BF16), v((D, D), BF16))
        got_qkv.wait()
        got_lse.wait()
        got_lsec.wait()
        qkv_cls[...] = qkv[main:, :].astype(F32)
        datt_cls[...] = datt[main:, :].astype(F32)
        joint_cls[...] = jnp.zeros_like(joint_cls)
        pl.semaphore_wait(credit, 1)
        on_core(4, co)
        plan = {0: [lambda: red.on_y(cd1), lambda: red.on_back(cd0)], 2: [lambda: red.on_z(cu0)], 3: [lambda: red.on_x(cd1)],
                5: [lambda: red.on_back(cu0)], 6: [lambda: red.on_y(cu1), lambda: red.on_z(cd1)]}

        def image(i, carry):
            for k, steps in plan.items():
                @pl.when(i == k)
                def _(steps=steps):
                    for step in steps:
                        step()

            attend_back(i, qkv, qkv_cls, datt, datt_cls, lse, lsec, scores, dprobs, probs, dscores, cls_row, joint_cls,
                        acc.at[8], acc.at[9])
            return carry

        lax.fori_loop(0, images, image, 0)
        qkv[main:, :] = joint_cls[...].astype(BF16)
        acc[8] += fold(joint_cls[:, 0:D])
        acc[9] += fold(joint_cls[:, 2 * D : 3 * D])

        def tail(act_t, gact, w_qkv, turn, flat):
            x_s = brr
            got_act, got_x = load(3, act_t_h, act_t), load(4, x_h, x_s)

            def fetch(j):
                return pltpu.make_async_copy(full_qkv.at[pl.ds(j * 256, 256), :], w_qkv.at[j % 2], wsem.at[0, j % 2])

            fetch(0).start()
            fetch(1).start()
            got_act.wait()
            red.core_copy(4, 2 * co.rows).wait_send()
            for q in range(4):
                spread(dot(act_t[...], qkv[:, q * TILE : (q + 1) * TILE]), cq0, q * 256)
            red.core_copy(5, 2 * cq0.rows).start()
            red.on_y(co)
            red.on_x(cu1)

            def input_grad(j):
                fetch(j).wait()
                gact[:, j * 256 : (j + 1) * 256] = dot_nt(qkv[...], w_qkv[j % 2])
                if j < 2:
                    fetch(j + 2).start()

            input_grad(0)
            red.core_copy(5, 2 * cq0.rows).wait_send()
            for q in range(2):
                spread(dot(act_t[...], qkv[:, (q + 4) * TILE : (q + 5) * TILE]), cq1, q * 256)
            on_core(5, cq0)
            red.core_copy(6, 2 * cq1.rows).start()
            red.on_back(cd1)
            red.on_x(co)
            input_grad(1)
            input_grad(2)
            on_core(6, cq1)
            input_grad(3)
            red.on_z(cu1)
            got_x.wait()

            def norm_rows(rows):
                m = x_s[rows, :].astype(F32)
                c = m - jnp.mean(m, axis=-1, keepdims=True)
                inv = lax.rsqrt(jnp.mean(c * c, axis=-1, keepdims=True) + 1e-06)
                hat = c * inv
                g = gact[rows, :]
                acc[0] += fold(g * hat)
                acc[1] += fold(g)
                sc = g * vecf[0:1, :]
                back = inv * (sc - jnp.mean(sc, axis=-1, keepdims=True)
                              - hat * jnp.mean(sc * hat, axis=-1, keepdims=True))
                x_s[rows, :] = (gmid[rows, :] + back).astype(BF16)

            rows_loop(n, 16, norm_rows)
            red.core_copy(6, 2 * cq1.rows).wait_send()
            red.on_z(co)
            to_tokens(x_s, flat, turn)
            copy = pltpu.make_async_copy(flat, tokens_o, osem.at[0])
            copy.start()
            red.on_back(cu1)
            red.on_back(co)
            copy.wait()

        pl.run_scoped(tail, v((D, n), BF16), v((n, D), F32), v((2, 256, 3 * D), BF16),
                      v((2, main, 128), F32), v((main + images, D), BF16))

    pl.run_scoped(attention, v((n, 3 * D), BF16), v((n, D), BF16), v((n, D), BF16), v((images, HEADS, PATCH), F32),
                  v((images, HEADS, PATCH), F32), v((8, 256, PATCH), F32), v((8, 256, PATCH), F32),
                  v((8, 256, PATCH), BF16), v((8, 256, PATCH), BF16), v((HEADS, PATCH), F32), v((CLS, 3 * D), F32),
                  v((CLS, D), F32), v((CLS, 3 * D), F32))

    def outcome(mid, hid, w_down, turn, flat, res):
        got_mid = load(3, mid_h, mid)

        def fetch(j, slot):
            piece, t = relative(3 - lax.rem(j, 4)), lax.div(j, 4)
            return (
                pltpu.make_async_copy(hidden_o.at[j], hid.at[slot], wsem.at[0, slot]),
                pltpu.make_async_copy(full_down.at[piece, at(t, TILE), :], w_down.at[slot], wsem.at[1, slot]),
            )

        for copy in fetch(0, 0):
            copy.start()
        gmid[...] = jnp.zeros_like(gmid)

        def tile(j, carry):
            slot = lax.rem(j, 2)
            for copy in fetch(j, slot):
                copy.wait()

            @pl.when(j < 7)
            def _():
                for copy in fetch(j + 1, 1 - slot):
                    copy.start()

            gmid[...] += dot(hid[slot], w_down[slot])
            for k, todo in steps.items():
                @pl.when(j == k)
                def _(todo=todo):
                    for step in todo:
                        step()
            return carry

        steps = {0: [lambda: red.on_y(cq0)], 4: [lambda: red.on_y(cq1), lambda: red.on_x(cq0)], 6: [lambda: red.on_x(cq1)]}

        lax.fori_loop(0, 8, tile, 0)
        got_mid.wait()

        def rows_of(rows):
            projected = gmid[rows, :] + vecf[6:7, :]
            upstream = up_s[rows, :].astype(F32)
            acc[6] += fold(upstream * vecf[7:8, :])
            acc[7] += fold(upstream * projected)
            res[rows, :] = (mid[rows, :] + vecf[7:8, :] * projected).astype(BF16)

        rows_loop(n, 16, rows_of)
        for p in range(4):
            vrows[...] = jnp.zeros_like(vrows)
            for k in range(8):
                vrows[k : k + 1, 0:256] = jnp.sum(acc[k, :, p * 256 : (p + 1) * 256], axis=0, keepdims=True)
            joint = acc.at[8 + p // 2]
            for k in range(2):
                first = (p % 2) * TILE + k * 256
                vrows[8 + k : 9 + k, 0:256] = jnp.sum(joint[:, first : first + 256], axis=0, keepdims=True)
            for k in range(4):
                vrows[10 + k : 11 + k, 0:256] = sums_up[2 * p + k // 2 : 2 * p + k // 2 + 1, (k % 2) * 256 : (k % 2 + 1) * 256]
            low = lax.rem(lax.rem(s, 2) + p % 2, 2)
            high = lax.rem(lax.div(s, 2) + p // 2, 2)
            buf[pl.ds(pl.multiple_of(target(low + 2 * high, cv), 16), 16), :] = vrows[...].astype(BF16)
        red.core_copy(7, 2 * cv.rows).start()
        to_tokens(res, flat, turn)
        copy = pltpu.make_async_copy(flat, result_o, osem.at[0])
        copy.start()
        on_core(7, cv)
        red.on_z(cq0)
        red.on_y(cv)
        red.on_z(cq1)
        red.on_x(cv)
        red.on_back(cq0)
        red.on_z(cv)
        red.on_back(cq1)
        red.on_back(cv)
        copy.wait()

    pl.run_scoped(outcome, v((n, D), F32), v((2, n, TILE), BF16), v((2, TILE, D), BF16), v((2, main, 128), F32),
                  v((main + images, D), BF16), v((n, D), BF16))
    copies = []
    for c in chunks:
        red.finish(c)
        half = c.rows // 2
        for k, (src, first, where) in enumerate(((x_recv, c.x_recv, red.x), (buf, c.far, 1 - red.x))):
            copy = pltpu.make_async_copy(
                src.at[pl.ds(first, half), :],
                sums_o.at[pl.ds(pl.multiple_of(c.mine - cd0.mine + where * half, 16), half), :], fsem.at[2 * c.index + k])
            copy.start()
            copies.append(copy)
    red.core_copy(7, 2 * cv.rows).wait_send()
    for c in chunks:
        red.drain(c)
    for copy in copies:
        copy.wait()


def convert_kernel(
    chunks, sums, result, tokens, result_o, tokens_o, g1_o, s1_o, qkv_o, bqv_o, out_o, bo_o, l1_o, g2_o, s2_o, up_o, bup_o, down_o, bd_o, l2_o,
    low, small, qkv, out, up, down, moved, dsem, osem, msem,
):
    base = chunks[0].mine
    moves = [pltpu.make_async_copy(src, moved.at[k], msem.at[0, k]) for k, src in enumerate((result, tokens))]
    stores = [pltpu.make_async_copy(moved.at[k], dst, msem.at[1, k]) for k, dst in enumerate((result_o, tokens_o))]
    gots = []
    for c in chunks:
        rows = pl.ds(c.mine - base, c.rows)
        gots.append(pltpu.make_async_copy(sums.at[rows, :], low.at[rows, :], dsem.at[c.index]))
        gots[-1].start()
    for copy in moves:
        copy.start()
    outs = []

    def send_out(src, dst):
        copy = pltpu.make_async_copy(src, dst, osem.at[len(outs)])
        copy.start()
        outs.append(copy)

    def block(c, first, count):
        return low[c.mine - base + first : c.mine - base + first + count, :]

    for t in range(2):
        gots[2 * t].wait()
        for k in range(8):
            down[t * TILE : (t + 1) * TILE, k * 128 : (k + 1) * 128] = block(chunks[2 * t], k * 128, 128).T.astype(F32)
        send_out(down.at[pl.ds(t * TILE, TILE), :], down_o.at[pl.ds(t * TILE, TILE), :])
        gots[2 * t + 1].wait()
        up[t] = block(chunks[2 * t + 1], 0, D).astype(F32)
        send_out(up.at[t], up_o.at[:, pl.ds(t * TILE, TILE)])
    for k in range(2):
        moves[k].wait()
        stores[k].start()
    gots[4].wait()
    for k in range(2):
        out[:, k * TILE : (k + 1) * TILE] = block(chunks[4], k * 256, 256).astype(F32)
    send_out(out, out_o)
    gots[5].wait()
    gots[6].wait()
    for k in range(6):
        qkv[:, k * TILE : (k + 1) * TILE] = block(chunks[5], k * 256, 256).astype(F32)
    send_out(qkv, qkv_o)
    gots[7].wait()
    small[...] = block(chunks[7], 0, 16)[:, 0:256].astype(F32)
    vectors = (g1_o, s1_o, bo_o, l1_o, g2_o, s2_o, bd_o, l2_o, bqv_o, bup_o)
    row = 0
    for v in vectors:
        for k in range(v.shape[0] // 256):
            v[pl.ds(k * 256, 256)] = small[row : row + 1, :].reshape(256)
            row += 1
    for copy in outs + stores:
        copy.wait()


def convert(chunks, sums, result, tokens):
    one = lambda k: jax.ShapeDtypeStruct((k,), F32)
    outs = (
        low_shape(*result.shape), low_shape(*tokens.shape), one(256), one(256), wide_shape(256, 3 * D), one(512), wide_shape(256, D), one(256), one(256), one(256), one(256),
        wide_shape(D, D), one(1024), wide_shape(D, D), one(256), one(256),
    )
    v = pltpu.VMEM
    return pl.pallas_call(
        functools.partial(convert_kernel, chunks),
        out_shape=outs,
        in_specs=[ANY] * 3,
        out_specs=[VMEM if len(o.shape) == 1 else ANY for o in outs],
        scratch_shapes=[v(sums.shape, BF16), v((16, 256), F32), v((256, 3 * D), F32), v((256, D), F32), v((2, D, TILE), F32),
                        v((D, D), F32), v((2,) + result.shape, BF16), pltpu.SemaphoreType.DMA((8,)),
                        pltpu.SemaphoreType.DMA((6,)), pltpu.SemaphoreType.DMA((2, 2))],
        compiler_params=pltpu.CompilerParams(vmem_limit_bytes=LIMIT),
        name="gradients_to_float32",
    )(sums, result, tokens)


def low_shape(*shape):
    return jax.ShapeDtypeStruct(shape, BF16)


def wide_shape(*shape):
    return jax.ShapeDtypeStruct(shape, F32)


ANY = pl.BlockSpec(memory_space=pl.ANY)
VMEM = pl.BlockSpec(memory_space=pltpu.VMEM)
LIMIT = 62 * 2**20


def forward(flat, cot, vectors, w_qkv, w_out, w_up, w_down):
    images = flat.shape[0] // (PATCH + 1)
    n = images * PATCH + CLS
    v = pltpu.VMEM
    outs = (
        low_shape(D, 3 * D), low_shape(D, D), low_shape(4, D, D), low_shape(4, D, D), low_shape(4, 16, 256),
        low_shape(n, 3 * D), low_shape(D, n), low_shape(n, D), low_shape(D, n), wide_shape(n, D), low_shape(n, D),
        low_shape(n, D), low_shape(D, n), low_shape(n, D), low_shape(n, D), low_shape(D, n),
        wide_shape(images, HEADS, PATCH), wide_shape(images, HEADS, PATCH),
    )
    return pl.pallas_call(
        gather_kernel,
        out_shape=outs,
        in_specs=[VMEM] * 12 + [ANY] * 4,
        out_specs=[ANY] * len(outs),
        scratch_shapes=[
            v((D, 3 * D), BF16), v((D, D), BF16), v((4, D, D), BF16), v((4, D, D), BF16),
            v((n, D), BF16), v((n, 3 * D), BF16), v((n, D), BF16), v((n, D), BF16), v((n, D), F32), v((n, D), BF16),
            v((n, D), BF16), v((D, n), BF16), v((D, n), BF16),
            v((images, HEADS, PATCH), F32), v((images, HEADS, PATCH), F32),
            v((8, 256, PATCH), F32), v((8, 256, PATCH), BF16), v((PATCH, D), F32), v((HEADS, PATCH), F32),
            v((CLS, D), F32), v((CLS, 3 * D), F32), v((2, images * PATCH, 128), F32), v((16, 256), F32),
            v((16, 256), BF16), v((4, 16, 256), BF16), v((16, D), F32), v((8, 3 * D), F32),
            pltpu.SemaphoreType.DMA((2, 6, 11)), pltpu.SemaphoreType.DMA((6,)), pltpu.SemaphoreType.DMA((2, 3)),
            pltpu.SemaphoreType.DMA((22,)),
        ],
        compiler_params=pltpu.CompilerParams(collective_id=0, has_side_effects=True, vmem_limit_bytes=LIMIT),
        cost_estimate=pl.CostEstimate(flops=18 * 2**30, bytes_accessed=64 * 2**20, transcendentals=3 * 2**20),
        name="gather_and_attention",
    )(flat, cot, *vectors, w_qkv, w_out, w_up, w_down)


def backward(nz, images, vec, *arrays):
    n = images * PATCH + CLS
    tokens = images * (PATCH + 1)
    v = pltpu.VMEM
    chunks, sizes = chunk_layout(nz)
    outs = (low_shape(tokens, D), low_shape(tokens, D), low_shape(sizes["total"], TILE), low_shape(8, n, TILE))
    return pl.pallas_call(
        functools.partial(backward_kernel, nz, chunks),
        out_shape=outs,
        in_specs=[VMEM] + [ANY] * len(arrays),
        out_specs=[ANY] * len(outs),
        scratch_shapes=[
            v((sizes["buf"], TILE), BF16), v((2, 2048, TILE), BF16), v((sizes["y_recv"], TILE), BF16),
            v((sizes["x_recv"], TILE), BF16), v((nz - 1, sizes["z_recv"], TILE), BF16), v((n, D), F32), v((n, D), BF16),
            v((10, 8, D), F32), v((8, TILE), F32), v((16, D), F32), v((8, 3 * D), F32), v((8, TILE), F32),
            v((16, TILE), F32),
            pltpu.SemaphoreType.DMA((2, len(chunks), 3 * nz)), pltpu.SemaphoreType.DMA((2, 8)),
            pltpu.SemaphoreType.REGULAR, pltpu.SemaphoreType.DMA((8,)), pltpu.SemaphoreType.DMA((2, 2)),
            pltpu.SemaphoreType.DMA((2,)), pltpu.SemaphoreType.DMA((1,)), pltpu.SemaphoreType.DMA((2 * len(chunks),)),
        ],
        compiler_params=pltpu.CompilerParams(collective_id=1, has_side_effects=True, vmem_limit_bytes=LIMIT),
        cost_estimate=pl.CostEstimate(flops=66 * 2**30, bytes_accessed=128 * 2**20, transcendentals=8 * 2**20),
        name="layer_backward",
    )(vec, *arrays), chunks


def on_device(
    tokens, norm1_gain, norm1_shift, w_qkv, bias_qv, w_out, bias_out, scale_one, norm2_gain, norm2_shift, w_up, bias_up,
    w_down, bias_down, scale_two, cotangent,
):
    images, length, _ = tokens.shape
    nz = lax.axis_size("replica") // 2
    flatten = lambda a: jnp.transpose(a, (1, 0, 2)).reshape(images * length, D)
    restore = lambda a: jnp.transpose(a.reshape(length, images, D), (1, 0, 2))
    vectors = (norm1_gain, norm1_shift, bias_out, scale_one, norm2_gain, norm2_shift, bias_down, scale_two, bias_qv, bias_up)
    full_qkv, full_out, full_up, full_down, vec, *kept = forward(
        flatten(tokens), flatten(cotangent), vectors, w_qkv, w_out, w_up, w_down)
    (result, grad_tokens, sums, _), chunks = backward(nz, images, vec, full_qkv, full_out, full_up, full_down, *kept)
    result, grad_tokens, *gradients = convert(chunks, sums, result, grad_tokens)
    return (restore(result), restore(grad_tokens)) + tuple(gradients)


def solution(mesh):
    placed = (
        P(("shard", "replica"), None, None),
        P("shard"),
        P("shard"),
        P("shard", None),
        P("shard"),
        P("shard", None),
        P("shard"),
        P("shard"),
        P("shard"),
        P("shard"),
        P(None, "shard"),
        P("shard"),
        P("shard", None),
        P("shard"),
        P("shard"),
        P(("shard", "replica"), None, None),
    )
    return jax.shard_map(
        on_device,
        mesh=mesh,
        in_specs=placed,
        out_specs=(
            P(("shard", "replica"), None, None),
            P(("shard", "replica"), None, None),
            P("shard"),
            P("shard"),
            P("shard", None),
            P("shard"),
            P("shard", None),
            P("shard"),
            P("shard"),
            P("shard"),
            P("shard"),
            P(None, "shard"),
            P("shard"),
            P("shard", None),
            P("shard"),
            P("shard"),
        ),
        check_vma=False,
    )
```

```python
import functools

import jax
import jax.numpy as jnp
from jax import lax
from jax.experimental import pallas as pl
from jax.experimental.pallas import tpu as pltpu
from jax.sharding import PartitionSpec as P

F32 = jnp.float32
BF16 = jnp.bfloat16
D = 1024
FF = 4096
HEADS = 16
PATCH = 128
CLS = 16
TILE = 512
FACTOR = 0.125
MESH = pl.DeviceIdType.MESH


def dot(a, b):
    return jnp.dot(a, b, preferred_element_type=F32)


def dot_nt(a, b):
    return lax.dot_general(a, b, (((1,), (1,)), ((), ())), preferred_element_type=F32)


def dot_tn(a, b):
    return lax.dot_general(a, b, (((0,), (0,)), ((), ())), preferred_element_type=F32)


def at(index, size):
    return pl.ds(pl.multiple_of(index * size, size), size)


def head_mask():
    lane = lax.shift_right_logical(lax.broadcasted_iota(jnp.int32, (HEADS, D), 1), 6)
    return lane == lax.broadcasted_iota(jnp.int32, (HEADS, D), 0)


def split_pair(v):
    low = lax.broadcasted_iota(jnp.int32, v.shape, 1) < 64
    zero = jnp.zeros_like(v)
    return jnp.concatenate([jnp.where(low, v, zero), jnp.where(low, zero, v)], 0)


def merge_pair(v):
    n = v.shape[0] // 2
    low = lax.broadcasted_iota(jnp.int32, (n, v.shape[1]), 1) < 64
    return jnp.where(low, v[:n], v[n:])


def place():
    s = lax.axis_index("shard")
    r = lax.axis_index("replica")
    x = lax.rem(r, 2)
    z = lax.div(r, 2)
    return s, r, x, z


def peers(s, r):
    sib = s + 1 - 2 * lax.rem(s, 2)
    across = lax.rem(s + 2, 4)
    side = r + 1 - 2 * lax.rem(r, 2)
    return sib, across, side


def rows_loop(n, step, body):
    lax.fori_loop(0, n // step, lambda k, c: (body(at(k, step)), c)[1], 0, unroll=5)


def unpack_vectors(vec, vecf, bias_qkv):
    for v in range(8):
        for s in range(4):
            vecf[v : v + 1, s * 256 : (s + 1) * 256] = vec[s, v : v + 1, :].astype(F32)
    bias_qkv[...] = jnp.zeros_like(bias_qkv)
    for s in range(4):
        for t in range(2):
            col = (s * 2 + t) * 256 + (D if s >= 2 else 0)
            bias_qkv[0:1, col : col + 256] = vec[s, 8 + t : 9 + t, :].astype(F32)


def layer_norm(v, gain, shift):
    c = v - jnp.mean(v, axis=-1, keepdims=True)
    inv = lax.rsqrt(jnp.mean(c * c, axis=-1, keepdims=True) + 1e-06)
    return c * inv * gain + shift


def to_images(src, dst, turn):
    images = (src.shape[0]) // (PATCH + 1)
    main = images * PATCH

    def lane_block(l, carry):
        cols = at(l, 128)
        slot = lax.rem(l, 2)
        turn[slot] = src[0:main, cols].astype(F32)
        for i in range(images):
            dst[i * PATCH : (i + 1) * PATCH, cols] = turn[slot, pl.ds(i, PATCH, stride=images), :].astype(BF16)
        return carry

    lax.fori_loop(0, D // 128, lane_block, 0)
    last = src[main : main + images, :].astype(F32)
    dst[main:, :] = jnp.concatenate([last, jnp.zeros((CLS - images, D), F32)], 0).astype(BF16)


def pack_vectors(vectors, dst):
    row = 0
    for v in vectors:
        count = v.shape[0] // 256
        wide = v[...].astype(F32)
        for k in range(count):
            dst[row : row + 1, :] = wide[k * 256 : (k + 1) * 256].reshape(1, 256)
            row += 1


def attend(i, qkv, qkv_cls, scores, probs, mix, probs_cls, att, att_cls, lse, lse_cls):
    rows = at(i, PATCH)
    mask = head_mask()
    own = qkv_cls[pl.ds(i, 1), :]
    q_c, k_c, v_c = own[:, :D] * FACTOR, own[:, D : 2 * D], own[:, 2 * D :]
    q_bd = jnp.where(mask, q_c, 0.0)
    k_bd = jnp.where(mask, k_c, 0.0).astype(BF16)
    v_bd = jnp.where(mask, v_c, 0.0).astype(BF16)
    to_cls = dot_nt(k_bd, qkv[rows, 0:D]) * FACTOR
    of_cls = dot_nt(q_bd.astype(BF16), qkv[rows, D : 2 * D])
    corner = jnp.sum(q_bd * k_c, axis=1, keepdims=True)
    top = jnp.maximum(jnp.max(of_cls, axis=1, keepdims=True), corner)
    e_row = jnp.exp(of_cls - top)
    e_cor = jnp.exp(corner - top)
    total = jnp.sum(e_row, axis=1, keepdims=True) + e_cor
    inv = 1.0 / total
    row = dot((e_row * inv).astype(BF16), qkv[rows, 2 * D : 3 * D])
    row = row + (e_cor * inv).astype(BF16).astype(F32) * v_c
    att_cls[pl.ds(i, 1), :] = jnp.sum(jnp.where(mask, row, 0.0), axis=0, keepdims=True)
    lse_cls[i] = jnp.broadcast_to(top + jnp.log(total), (HEADS, PATCH))
    for g in range(HEADS // 2):
        q2 = qkv[rows, g * 128 : g * 128 + 128] * jnp.asarray(FACTOR, BF16)
        scores[g] = dot_nt(split_pair(qkv[rows, g * 128 + D : g * 128 + D + 128]), q2)
    for g in range(HEADS // 2):
        for u in range(2):
            h = 2 * g + u
            part = scores[g, u * PATCH : (u + 1) * PATCH, :]
            extra = to_cls[h : h + 1, :]
            top = jnp.maximum(jnp.max(part, axis=0, keepdims=True), extra)
            e_part = jnp.exp(part - top)
            e_extra = jnp.exp(extra - top)
            total = jnp.sum(e_part, axis=0, keepdims=True) + e_extra
            inv = 1.0 / total
            probs[g, u * PATCH : (u + 1) * PATCH, :] = (e_part * inv).astype(BF16)
            probs_cls[h : h + 1, :] = e_extra * inv
            lse[i, h : h + 1, :] = top + jnp.log(total)
    for g in range(HEADS // 2):
        v2 = split_pair(qkv[rows, g * 128 + 2 * D : g * 128 + 2 * D + 128])
        mix[:, g * 128 : g * 128 + 128] = dot_tn(probs[g], v2)
    att[rows, :] = (mix[...] + dot_tn(probs_cls[...].astype(BF16), v_bd)).astype(BF16)


class Gather:
    KINDS = ("own", "far", "x1", "z1", "x2", "z2", "p0", "p1", "p2", "p3", "p4")

    def __init__(self, number, rows, src, dst, sems, local):
        s, r, x, z = place()
        sib, across, side = peers(s, r)
        self.number, self.sems = number, sems
        near = lax.rem(z, 2)
        level = {"replica": (z + 1 - 2 * near) * 2 + x}
        side, sib = {"replica": side}, {"shard": sib}
        size = rows // 4
        half = size // 2

        def start(zz, xx):
            return pl.multiple_of((2 * zz + xx) * size, 16)

        def same(first, count, to):
            ref = dst(across, pl.multiple_of(first, 16), count)
            return ref, ref, to

        mine, by_x, by_z, by_both = start(near, x), start(near, 1 - x), start(1 - near, x), start(1 - near, 1 - x)
        self.parts = {
            "own": (dst(s, 0, rows), dst(s, 0, rows), sib),
            "far": (dst(s, mine, size), dst(s, mine, size), {"shard": across}),
            "x1": same(mine, size, side),
            "z1": same(mine, size, level),
            "x2": same(by_z, half, side),
            "z2": same(by_x + half, half, level),
            "p0": same(mine, size, sib),
            "p1": same(by_x, size, sib),
            "p2": same(by_z, size, sib),
            "p3": same(by_both, half, sib),
            "p4": same(by_both + half, half, sib),
        }
        self.local = pltpu.make_async_copy(src(0, rows), dst(s, 0, rows), local.at[number])

    def copy(self, kind):
        a, b, to = self.parts[kind]
        k = self.KINDS.index(kind)
        return pltpu.make_async_remote_copy(
            a, b, self.sems.at[0, self.number, k], self.sems.at[1, self.number, k], device_id=to, device_id_type=MESH
        )

    def load(self):
        self.local.start()

    def begin(self):
        self.local.wait()
        self.copy("far").start()

    def share(self):
        self.copy("own").start()

    def on_far(self):
        self.copy("far").wait_recv()
        for kind in ("x1", "z1", "p0"):
            self.copy(kind).start()

    def on_near(self):
        self.copy("x1").wait_recv()
        self.copy("z2").start()
        self.copy("p1").start()
        self.copy("z1").wait_recv()
        self.copy("x2").start()
        self.copy("p2").start()

    def on_last(self):
        self.copy("x2").wait_recv()
        self.copy("p3").start()
        self.copy("z2").wait_recv()
        self.copy("p4").start()

    def ready(self):
        for kind in ("own", "p0", "p1", "p2", "p3", "p4"):
            self.copy(kind).wait_recv()

    def drain(self):
        for kind in self.KINDS:
            self.copy(kind).wait_send()


def relative_piece(s, rel):
    low, high = lax.rem(rel, 2), lax.div(rel, 2)
    return s + low * (1 - 2 * lax.rem(s, 2)) + high * (2 - 4 * lax.div(s, 2))


def unpack_bias_up(vec, bias_up):
    for p in range(4):
        for t in range(2):
            for k in range(2):
                row = 10 + 2 * t + k
                bias_up[2 * p + t : 2 * p + t + 1, k * 256 : (k + 1) * 256] = vec[p, row : row + 1, :].astype(F32)


def ffn_tile(act2, dr, dr_t, act2_t, w_up, w_down, bias, hid, br, gmid, fresh, on_hidden, put):
    n = act2.shape[0]
    cut = 16 * (n // 32)
    first, second = slice(0, cut), slice(cut, n)

    def both(rows, before, grad):
        hidden, step = gelu_both(before)
        hid[rows, :] = hidden.astype(BF16)
        grad = grad * step
        br[rows, :] = grad.astype(BF16)
        return jnp.sum(grad, axis=0, keepdims=True)

    def back(rows):
        out = dot_nt(br[rows, :], w_up())
        if fresh:
            gmid[rows, :] = out
        else:
            gmid[rows, :] += out

    before0 = dot(act2[first, :], w_up()) + bias
    grad0 = dot_nt(dr[first, :], w_down())
    before1 = dot(act2[second, :], w_up()) + bias
    column = both(first, before0, grad0)
    grad1 = dot_nt(dr[second, :], w_down())
    back(first)
    column = column + both(second, before1, grad1)
    back(second)
    on_hidden()
    put(0, dot(dr_t[...], hid[...]).astype(BF16))
    put(1, dot(act2_t[...], br[...]).astype(BF16))
    return column


def gather_kernel(
    tokens, cot, v0, v1, v2, v3, v4, v5, v6, v7, v8, v9, w_qkv, w_out, w_up, w_down,
    qkv_w_o, out_w_o, up_w_o, down_w_o, vec_all, qkv_o, act_t_o, x_o, att_t_o, mid_o, branch_o, act2_o, act2_t_o, up_o,
    dr_o, dr_t_o, lse_o, lsec_o, parts_o, hid_o, gact_o, column_o,
    full_qkv, full_out, full_up, full_down, x_s, qkv, act, att, mid, branch, act2, turned_a, turned_b, lse, lsec,
    scores, probs, mix, probs_cls, cls, qkv_cls, turn, vec32, vec_own_s, vec, vecf, bias_qkv,
    bias_up, column,
    sems, local, vsem, osem,
):
    s, r, x, z = place()
    sib, across, side = peers(s, r)
    n = x_s.shape[0]
    images = lse.shape[0]
    main = images * PATCH

    vec32[...] = jnp.zeros_like(vec32)
    pack_vectors((v0, v1, v2, v3, v4, v5, v6, v7, v8, v9), vec32)
    vec_own_s[...] = vec32[...].astype(BF16)
    barrier = pltpu.get_barrier_semaphore()
    level = (z + 1 - 2 * lax.rem(z, 2)) * 2 + x
    for to in ({"shard": sib}, {"shard": across}, {"replica": side}, {"replica": level}):
        pl.semaphore_signal(barrier, inc=1, device_id=to, device_id_type=MESH)

    def unit(number, rows, src, dst):
        return Gather(number, rows, src, dst, sems, local)

    g_qkv = unit(0, 256, lambda a, k: w_qkv.at[pl.ds(a, k), :],
                 lambda p, a, k: full_qkv.at[pl.ds(pl.multiple_of(p * 256 + a, 16), k), :])
    g_out = unit(1, 256, lambda a, k: w_out.at[pl.ds(a, k), :],
                 lambda p, a, k: full_out.at[pl.ds(pl.multiple_of(p * 256 + a, 16), k), :])

    def up_unit(number, t):
        cols = pl.ds(t * TILE, TILE)
        return unit(number, D, lambda a, k: w_up.at[pl.ds(a, k), cols],
                    lambda p, a, k: full_up.at[p, pl.ds(pl.multiple_of(a, 16), k), cols])

    def down_unit(number, t):
        return unit(number, TILE, lambda a, k: w_down.at[pl.ds(a + t * TILE, k), :],
                    lambda p, a, k: full_down.at[p, pl.ds(pl.multiple_of(a + t * TILE, 16), k), :])

    g_up0, g_down0, g_up1, g_down1 = up_unit(2, 0), down_unit(3, 0), up_unit(4, 1), down_unit(5, 1)

    for g in (g_qkv, g_out, g_up0, g_down0, g_up1, g_down1):
        g.load()
    pl.semaphore_wait(barrier, 4)

    def vec_copy(k, src, slot, to):
        return pltpu.make_async_remote_copy(src, vec.at[slot], vsem.at[0, k], vsem.at[1, k], device_id=to,
                                            device_id_type=MESH)

    vec_own = vec_copy(0, vec_own_s, s, {"shard": sib})
    vec_far = vec_copy(1, vec_own_s, s, {"shard": across})
    vec_pass = vec_copy(2, vec.at[across], across, {"shard": sib})
    vec_own.start()
    vec_far.start()
    g_qkv.begin()
    g_qkv.share()
    g_out.begin()
    vec[s] = vec_own_s[...]

    to_images(tokens, x_s, turn)
    outs = {}

    def send_out(k, src, dst):
        outs[k] = pltpu.make_async_copy(src, dst, osem.at[k])
        outs[k].start()

    send_out(0, x_s, x_o)
    vec_far.wait_recv()
    vec_pass.start()
    vec_own.wait_recv()
    vec_pass.wait_recv()
    unpack_vectors(vec, vecf, bias_qkv)

    def first_norm(rows):
        act[rows, :] = layer_norm(x_s[rows, :].astype(F32), vecf[0:1, :], vecf[1:2, :]).astype(BF16)

    rows_loop(n, 16, first_norm)
    g_qkv.on_far()
    for g in (g_up0, g_down0, g_up1, g_down1):
        g.begin()
    transpose_into(act, turned_b)
    send_out(1, turned_b, act_t_o)
    g_qkv.on_near()
    to_images(cot, branch, turn)

    def down_rows(rows):
        act2[rows, :] = (branch[rows, :].astype(F32) * vecf[7:8, :]).astype(BF16)

    rows_loop(n, 16, down_rows)
    g_qkv.on_last()
    g_out.on_far()
    send_out(14, branch, up_o)
    send_out(15, act2, dr_o)
    transpose_into(act2, turned_a)
    send_out(16, turned_a, dr_t_o)
    g_out.on_near()
    g_qkv.ready()
    send_out(4, full_qkv, qkv_w_o)
    for g in (g_out, g_up0, g_down0):
        g.share()

    def qkv_tile(j, carry):
        cols = at(j, TILE)
        low = (dot(act[...], full_qkv[:, cols]) + bias_qkv[0:1, cols]).astype(BF16)
        qkv[:, cols] = low
        qkv_cls[:, cols] = low[main:].astype(F32)
        return carry

    lax.fori_loop(0, 3 * D // TILE, qkv_tile, 0)
    send_out(2, qkv, qkv_o)
    act[...] = act2[...]
    unpack_bias_up(vec, bias_up)
    column[...] = jnp.zeros_like(column)
    send_out(3, vec, vec_all)
    cls[...] = jnp.zeros_like(cls)
    g_out.on_last()
    g_up0.on_far()
    plan = {1: [g_up0.on_near], 2: [g_down0.on_far], 3: [g_up0.on_last, g_up1.share], 4: [g_down0.on_near, g_up1.on_far],
            6: [g_down0.on_last, g_down1.share], 7: [g_up1.on_near, g_down1.on_far]}

    def image(i, carry):
        for k, steps in plan.items():
            @pl.when(i == k)
            def _(steps=steps):
                for step in steps:
                    step()

        attend(i, qkv, qkv_cls, scores, probs, mix, probs_cls, att, cls, lse, lsec)
        return carry

    lax.fori_loop(0, images, image, 0)
    att[main:, :] = cls[...].astype(BF16)
    outs.pop(1).wait()
    transpose_into(att, turned_b)
    send_out(8, turned_b, att_t_o)
    send_out(9, lse, lse_o)
    send_out(10, lsec, lsec_o)
    g_out.ready()
    outs.pop(14).wait()
    for j in range(D // TILE):
        cols = slice(j * TILE, (j + 1) * TILE)
        out = dot(att[...], full_out[:, cols]) + vecf[2:3, cols]
        branch[:, cols] = out.astype(BF16)
        mid[:, cols] = x_s[:, cols].astype(F32) + vecf[3:4, cols] * out
    send_out(11, mid, mid_o)
    send_out(12, branch, branch_o)
    g_up1.on_last()
    g_down1.on_near()

    def second_norm(rows):
        act2[rows, :] = layer_norm(mid[rows, :], vecf[4:5, :], vecf[5:6, :]).astype(BF16)

    outs.pop(15).wait()
    rows_loop(n, 16, second_norm)
    send_out(13, act2, act2_o)
    outs.pop(8).wait()
    transpose_into(act2, turned_b)
    send_out(17, turned_b, act2_t_o)
    half = pl.ds(0, TILE)
    rest = pl.ds(TILE, TILE)
    send_out(5, full_out, out_w_o)
    g_up0.ready()
    send_out(18, full_up.at[:, :, half], up_w_o.at[:, :, half])
    g_down0.ready()
    send_out(19, full_down.at[:, half, :], down_w_o.at[:, half, :])
    for k in (2, 11):
        outs.pop(k).wait()
    hid, br = qkv.at[:, pl.ds(0, TILE)], qkv.at[:, pl.ds(TILE, TILE)]
    for k, rel in enumerate((3, 2)):
        piece = relative_piece(s, rel)

        def put(half_k, value, k=k):
            qkv[0:D, (2 + 2 * k + half_k) * TILE : (3 + 2 * k + half_k) * TILE] = value

        if k:
            outs.pop(22).wait()
        column[pl.ds(2 * piece, 1), :] = ffn_tile(
            act2, act, turned_a, turned_b, lambda: full_up[piece, :, 0:TILE], lambda: full_down[piece, 0:TILE, :],
            bias_up[pl.ds(2 * piece, 1), :], hid, br, mid, k == 0, lambda: send_out(22 + k, hid, hid_o.at[k]), put)
        for half_k in range(2):
            send_out(24 + 2 * k + half_k, qkv.at[pl.ds(0, D), pl.ds((2 + 2 * k + half_k) * TILE, TILE)],
                     parts_o.at[k, pl.ds(half_k * D, D), :])
        if k == 0:
            g_down1.on_last()
            g_up1.ready()
            send_out(20, full_up.at[:, :, rest], up_w_o.at[:, :, rest])
    send_out(28, mid, gact_o)
    send_out(29, column, column_o)
    g_down1.ready()
    send_out(21, full_down.at[:, rest, :], down_w_o.at[:, rest, :])
    for copy in outs.values():
        copy.wait()
    for g in (g_qkv, g_out, g_up0, g_down0, g_up1, g_down1):
        g.drain()
    for copy in (vec_own, vec_far, vec_pass):
        copy.wait_send()


class Chunk:
    def __init__(self, index, rows, mine, y_send, y_recv, x_recv, z_recv, far):
        self.index, self.rows, self.mine, self.y_send, self.far = index, rows, mine, y_send, far
        self.y_recv, self.x_recv, self.z_recv = y_recv, x_recv, z_recv


def chunk_layout(nz):
    sizes = [1024, 1024, 1024, 1024, 512, 1024, 512]
    y_base = 2048
    y_a = y_base
    y_b = y_a + 2048
    mine_base = y_b + 2048
    chunks = []
    mine = mine_base
    late = 0
    xr = zr = 0
    for k, rows in enumerate(sizes):
        if k < 2:
            ys, yr = y_a + 1024 * k, 1024 * k
        elif k < 4:
            ys, yr = y_b + 1024 * (k - 2), 2048 + 1024 * (k - 2)
        else:
            ys, yr = y_a + late, late
            late += rows
        far = mine_base + sum(sizes) + 512 * k if k < 2 else ys
        chunks.append(Chunk(k, rows, mine, ys, yr, xr, zr, far))
        mine += rows
        xr += rows // 2
        zr += rows // 2 // nz
    return chunks, dict(buf=mine + 1024, total=sum(sizes), mine=mine_base, y_recv=2 * 2048, x_recv=xr, z_recv=zr)


def add_rows(dst, d0, src, s0, rows):
    step = next(k for k in (128, 96, 64, 32, 16) if rows % k == 0)

    def body(k, carry):
        d = pl.ds(pl.multiple_of(d0 + k * step, 16), step)
        t = pl.ds(pl.multiple_of(s0 + k * step, 16), step)
        dst[d, :] = (dst[d, :].astype(F32) + src[t, :].astype(F32)).astype(BF16)
        return carry

    lax.fori_loop(0, rows // step, body, 0)


class Reduce:
    def __init__(self, nz, buf, core_recv, y_recv, x_recv, z_recv, sems, core_sems, credit):
        self.nz, self.buf, self.core_recv = nz, buf, core_recv
        self.y_recv, self.x_recv, self.z_recv = y_recv, x_recv, z_recv
        self.sems, self.core_sems, self.credit = sems, core_sems, credit
        self.s, self.r, self.x, self.z = place()
        self.sib, self.across, self.side = peers(self.s, self.r)

    def remote(self, src, dst, chunk, kind, to):
        return pltpu.make_async_remote_copy(
            src, dst, self.sems.at[0, chunk.index, kind], self.sems.at[1, chunk.index, kind], device_id=to,
            device_id_type=MESH)

    def peer(self, k):
        return {"replica": lax.rem(self.z + k, self.nz) * 2 + self.x}

    def core_copy(self, turn, rows):
        slot = turn % 2
        return pltpu.make_async_remote_copy(
            self.buf.at[pl.ds(0, rows), :], self.core_recv.at[slot, pl.ds(0, rows), :],
            self.core_sems.at[0, turn], self.core_sems.at[1, turn], device_id={"shard": self.sib}, device_id_type=MESH)

    def add_core(self, turn, first, dst, rows):
        add_rows(self.buf, dst, self.core_recv.at[turn % 2], first, rows)

    def y_copy(self, c):
        return self.remote(self.buf.at[pl.ds(c.y_send, c.rows), :], self.y_recv.at[pl.ds(c.y_recv, c.rows), :], c, 0,
                           {"shard": self.across})

    def x_copy(self, c):
        half = c.rows // 2
        return self.remote(self.buf.at[pl.ds(pl.multiple_of(c.mine + (1 - self.x) * half, 16), half), :],
                           self.x_recv.at[pl.ds(c.x_recv, half), :], c, 1, {"replica": self.side})

    def quarter(self, c, x, z):
        half = c.rows // 2
        size = half // self.nz
        return pl.ds(pl.multiple_of(c.mine + x * half + z * size, 16), size)

    def z_copy(self, c, k):
        size = c.rows // 2 // self.nz
        return self.remote(self.buf.at[self.quarter(c, self.x, lax.rem(self.z + k, self.nz)), :],
                           self.z_recv.at[k - 1, pl.ds(c.z_recv, size), :], c, 1 + k, self.peer(k))

    def done(self, first, c, z):
        size = c.rows // 2 // self.nz
        return pl.ds(pl.multiple_of(first + z * size, 16), size)

    def back_z(self, c, k):
        part = self.x_recv.at[self.done(c.x_recv, c, self.z), :]
        return self.remote(part, part, c, self.nz + k, self.peer(k))

    def back_x(self, c, k):
        z = lax.rem(self.z + self.nz - k, self.nz)
        return self.remote(self.x_recv.at[self.done(c.x_recv, c, z), :], self.buf.at[self.done(c.far, c, z), :], c,
                           2 * self.nz + k, {"replica": self.side})

    def on_y(self, c):
        self.y_copy(c).wait_recv()
        add_rows(self.buf, c.mine, self.y_recv, c.y_recv, c.rows)
        self.y_copy(c).wait_send()
        self.x_copy(c).start()

    def on_x(self, c):
        half = c.rows // 2
        self.x_copy(c).wait_recv()
        add_rows(self.buf, c.mine + self.x * half, self.x_recv, c.x_recv, half)
        for k in range(1, self.nz):
            self.z_copy(c, k).start()

    def on_z(self, c):
        size = c.rows // 2 // self.nz
        start = c.mine + self.x * (c.rows // 2) + self.z * size
        for k in range(1, self.nz):
            self.z_copy(c, k).wait_recv()
        step = next(k for k in (64, 48, 32, 16) if size % k == 0)

        def body(i, carry):
            d = pl.ds(pl.multiple_of(start + i * step, 16), step)
            total = self.buf[d, :].astype(F32)
            for k in range(1, self.nz):
                total = total + self.z_recv[k - 1, pl.ds(pl.multiple_of(c.z_recv + i * step, 16), step), :].astype(F32)
            to = pl.ds(pl.multiple_of(c.x_recv + self.z * size + i * step, 16), step)
            self.x_recv[to, :] = total.astype(BF16)
            return carry

        lax.fori_loop(0, size // step, body, 0)
        for k in range(1, self.nz):
            self.back_z(c, k).start()
        self.back_x(c, 0).start()

    def on_back(self, c):
        for k in range(1, self.nz):
            self.back_z(c, k).wait_recv()
            self.back_x(c, k).start()

    def finish(self, c):
        for k in range(self.nz):
            self.back_x(c, k).wait_recv()

    def drain(self, c):
        self.x_copy(c).wait_send()
        for k in range(1, self.nz):
            self.z_copy(c, k).wait_send()
            self.back_z(c, k).wait_send()
        for k in range(self.nz):
            self.back_x(c, k).wait_send()


def fold(v):
    return jnp.sum(v.reshape(v.shape[0] // 8, 8, v.shape[1]), axis=0)


def gelu_both(v):
    e = jnp.exp(-0.5 * v * v)
    t = 1.0 / (1.0 + 0.23164189 * jnp.abs(v))
    poly = ((((1.061405429 * t - 1.453152027) * t + 1.421413741) * t - 0.284496736) * t + 0.254829592) * t
    tail = 0.5 * poly * e
    phi = jnp.where(v >= 0.0, 1.0 - tail, tail)
    return v * phi, phi + v * e * 0.3989422804014327


def transpose_into(src, dst):
    for c in range(D // 128):
        dst[c * 128 : (c + 1) * 128, :] = src[:, c * 128 : (c + 1) * 128].T


def attend_back(i, qkv, qkv_cls, datt, datt_cls, lse, lsec, scores, dprobs, probs, dscores, cls_row, joint_cls, sum_q, sum_v):
    rows = at(i, PATCH)
    mask = head_mask()
    own = qkv_cls[pl.ds(i, 1), :]
    do_c = datt_cls[pl.ds(i, 1), :]
    q_c, k_c, v_c = own[:, :D] * FACTOR, own[:, D : 2 * D], own[:, 2 * D :]
    pick = lambda v: jnp.where(mask, v, 0.0)
    q_w, k_w, v_w, do_w = pick(q_c), pick(k_c), pick(v_c), pick(do_c)
    q_bd, k_bd, v_bd, do_bd = (v.astype(BF16) for v in (q_w, k_w, v_w, do_w))
    queries, keys, values = (qkv[rows, k * D : (k + 1) * D] for k in range(3))
    grads = datt[rows, :]
    low = lambda v: v.astype(BF16)
    top = lsec[i][:, 0:1]
    p_row = jnp.exp(dot_nt(q_bd, keys) - top)
    p_cor = jnp.exp(jnp.sum(q_w * k_c, axis=1, keepdims=True) - top)
    dp_row = dot_nt(do_bd, values)
    dp_cor = jnp.sum(do_w * v_c, axis=1, keepdims=True)
    delta = jnp.sum(p_row * dp_row, axis=1, keepdims=True) + p_cor * dp_cor
    ds_row = low(p_row * (dp_row - delta))
    ds_cor = low(p_cor * (dp_cor - delta)).astype(F32)
    p_col = jnp.exp(dot_nt(k_bd, queries) * FACTOR - lse[i])
    dp_col = dot_nt(v_bd, grads)
    for g in range(HEADS // 2):
        lanes = slice(g * 128, (g + 1) * 128)
        q2 = qkv[rows, lanes] * jnp.asarray(FACTOR, BF16)
        scores[g] = dot_nt(split_pair(qkv[rows, g * 128 + D : g * 128 + D + 128]), q2)
        dprobs[g] = dot_nt(split_pair(qkv[rows, g * 128 + 2 * D : g * 128 + 2 * D + 128]), datt[rows, lanes])
    for g in range(HEADS // 2):
        for u in range(2):
            h = 2 * g + u
            half = slice(u * PATCH, (u + 1) * PATCH)
            part = jnp.exp(scores[g, half, :] - lse[i, h : h + 1, :])
            dpart = dprobs[g, half, :]
            p_h, dp_h = p_col[h : h + 1, :], dp_col[h : h + 1, :]
            delta = jnp.sum(part * dpart, axis=0, keepdims=True) + p_h * dp_h
            probs[g, half, :] = low(part)
            dscores[g, half, :] = low(part * (dpart - delta))
            cls_row[h : h + 1, :] = p_h * (dp_h - delta)
    ds_col = low(cls_row[...])
    total = lambda v: jnp.sum(jnp.where(mask, v, 0.0), axis=0, keepdims=True)
    joint_cls[pl.ds(i, 1), 0:D] = FACTOR * (total(dot(ds_row, keys)) + jnp.sum(ds_cor * k_w, axis=0, keepdims=True))
    joint_cls[pl.ds(i, 1), D : 2 * D] = FACTOR * total(dot(ds_col, queries)) + jnp.sum(ds_cor * q_w, axis=0, keepdims=True)
    joint_cls[pl.ds(i, 1), 2 * D : 3 * D] = total(dot(low(p_col), grads)) + jnp.sum(
        low(p_cor).astype(F32) * do_w, axis=0, keepdims=True)
    p_row = low(p_row)
    for g in range(HEADS // 2):
        lanes = slice(g * 128, (g + 1) * 128)
        klanes = slice(g * 128 + D, g * 128 + D + 128)
        vlanes = slice(g * 128 + 2 * D, g * 128 + 2 * D + 128)
        q2 = qkv[rows, lanes] * jnp.asarray(FACTOR, BF16)
        dv = merge_pair(dot(probs[g], datt[rows, lanes])) + dot_tn(p_row, do_bd[:, lanes])
        dk = merge_pair(dot(dscores[g], q2)) + dot_tn(ds_row, q_bd[:, lanes])
        dq = (dot_tn(dscores[g], split_pair(qkv[rows, klanes])) + dot_tn(ds_col, k_bd[:, lanes])) * FACTOR
        qkv[rows, lanes] = low(dq)
        qkv[rows, klanes] = low(dk)
        qkv[rows, vlanes] = low(dv)
        sum_q[:, lanes] += fold(dq)
        sum_v[:, lanes] += fold(dv)


def to_tokens(src, dst, turn):
    images = dst.shape[0] // (PATCH + 1)
    main = images * PATCH

    def lane_block(l, carry):
        cols = at(l, 128)
        slot = lax.rem(l, 2)
        for i in range(images):
            turn[slot, pl.ds(i, PATCH, stride=images), :] = src[i * PATCH : (i + 1) * PATCH, cols].astype(F32)
        dst[0:main, cols] = turn[slot].astype(BF16)
        return carry

    lax.fori_loop(0, D // 128, lane_block, 0)
    dst[main : main + images, :] = src[main:, :].astype(F32)[0:images].astype(BF16)


def backward_kernel(
    nz, chunks, vec, full_qkv, full_out, full_up, full_down, qkv_h, act_t_h, x_h, att_t_h, mid_h, branch_h, act2_h,
    act2_t_h, up_h, dr_h, dr_t_h, lse_h, lsec_h, parts_h, hid_h, gact_h, column_h,
    result_o, tokens_o, sums_o, small_o, hidden_o,
    buf, core_recv, y_recv, x_recv, z_recv, gmid, up_s, acc, sums_up, vecf, bias_qkv, bias_up, v_part, v_group, v_sum, v_all,
    sems, core_sems, group_sems, all_sems, credit, dsem, wsem, hsem, osem, fsem,
):
    images = lse_h.shape[0]
    n = gmid.shape[0]
    main = images * PATCH
    red = Reduce(nz, buf, core_recv, y_recv, x_recv, z_recv, sems, core_sems, credit)
    s = red.s
    cd0, cu0, cd1, cu1, co, cq0, cq1 = chunks

    def load(k, src, dst):
        copy = pltpu.make_async_copy(src, dst, dsem.at[k])
        copy.start()
        return copy

    def relative(rel):
        return relative_piece(s, rel)

    def target(rel, chunk):
        low, high = lax.rem(rel, 2), lax.div(rel, 2)
        return low * (1 - high) * chunk.rows + (1 - low) * (high * chunk.y_send + (1 - high) * chunk.mine)

    def group_peer(k):
        return {"shard": lax.rem(s + k, 4)}

    def replica_peer(k):
        return {"replica": lax.rem(red.r + k, 2 * nz)}

    def group_copy(k):
        return pltpu.make_async_remote_copy(
            v_part.at[lax.rem(s + k, 4)], v_group.at[k - 1], group_sems.at[0, k - 1], group_sems.at[1, k - 1],
            device_id=group_peer(k), device_id_type=MESH)

    def all_copy(k):
        return pltpu.make_async_remote_copy(
            v_sum, v_all.at[red.r], all_sems.at[0, k - 1], all_sems.at[1, k - 1], device_id=replica_peer(k),
            device_id_type=MESH)

    got_up = load(7, up_h, up_s)

    def ffn(dr, dr_t, act2, act2_t, w_up, w_down, hid, br):
        gots = [load(8, parts_h.at[0], buf.at[pl.ds(0, 2048), :]),
                load(9, parts_h.at[1], buf.at[pl.ds(cd0.y_send, 2048), :]), load(0, act2_h, act2), load(1, dr_h, dr),
                load(2, dr_t_h, dr_t), load(3, act2_t_h, act2_t), load(10, gact_h, gmid), load(11, column_h, sums_up)]

        def fetch(j, slot):
            piece, t = relative(3 - lax.rem(j, 4)), lax.div(j, 4)
            return (
                pltpu.make_async_copy(full_up.at[piece, :, at(t, TILE)], w_up.at[slot], wsem.at[0, slot]),
                pltpu.make_async_copy(full_down.at[piece, at(t, TILE), :], w_down.at[slot], wsem.at[1, slot]),
            )

        def keep(j, slot):
            return pltpu.make_async_copy(hid.at[slot], hidden_o.at[j - 2], hsem.at[slot])

        barrier = pltpu.get_barrier_semaphore()
        partners = [group_peer(k) for k in range(1, 4)] + [replica_peer(k) for k in range(1, 2 * nz)]
        for to in partners:
            pl.semaphore_signal(barrier, inc=1, device_id=to, device_id_type=MESH)
        pl.semaphore_wait(barrier, len(partners))
        unpack_vectors(vec, vecf, bias_qkv)
        unpack_bias_up(vec, bias_up)
        acc[...] = jnp.zeros_like(acc)
        gots[0].wait()
        red.core_copy(0, 2048).start()
        for copy in fetch(2, 0):
            copy.start()
        for copy in gots[1:]:
            copy.wait()

        def tile(j, carry):
            slot = lax.rem(j, 2)
            rel, t = 3 - lax.rem(j, 4), lax.div(j, 4)
            piece = relative(rel)
            low, high = lax.rem(rel, 2), lax.div(rel, 2)
            place_at = pl.multiple_of(
                (1 - low) * (high * (cd0.y_send + t * (cd1.y_send - cd0.y_send)) + (1 - high) * (cd0.mine + t * 2048)), 16)
            for copy in fetch(j, slot):
                copy.wait()

            @pl.when(j < 7)
            def _():
                for copy in fetch(j + 1, 1 - slot):
                    copy.start()

            @pl.when(j >= 4)
            def _():
                keep(j - 2, slot).wait()

            for k in (2, 4, 6):
                @pl.when(j == k)
                def _(k=k):
                    red.core_copy(k // 2 - 1, 2048).wait_send()

            def put(half, value):
                buf[pl.ds(pl.multiple_of(place_at + half * D, 16), D), :] = value

            sums_up[pl.ds(2 * piece + t, 1), :] = ffn_tile(
                act2, dr, dr_t, act2_t, lambda: w_up[slot], lambda: w_down[slot], bias_up[pl.ds(2 * piece + t, 1), :],
                hid.at[slot], br, gmid, False, lambda: keep(j, slot).start(), put)

            def y_part(turn, chunk):
                red.core_copy(turn, 2048).wait_recv()
                for k, c in enumerate(chunk):
                    red.add_core(turn, k * 1024, c.y_send, c.rows)
                    red.y_copy(c).start()

            def own_part(turn, chunk):
                red.core_copy(turn, 2048).wait_recv()
                red.add_core(turn, 0, chunk[0].mine, 2048)

            steps = {
                2: [lambda: y_part(0, (cd0, cu0)), lambda: red.core_copy(1, 2048).start()],
                3: [lambda: own_part(1, (cd0, cu0))],
                4: [lambda: red.core_copy(2, 2048).start()],
                5: [lambda: y_part(2, (cd1, cu1)), lambda: red.on_y(cd0)],
                6: [lambda: red.core_copy(3, 2048).start(), lambda: red.on_x(cd0)],
                7: [lambda: own_part(3, (cd1, cu1)), lambda: red.on_y(cu0)],
            }
            for k, todo in steps.items():
                @pl.when(j == k)
                def _(todo=todo):
                    for step in todo:
                        step()
            return carry

        lax.fori_loop(2, 8, tile, 0)
        pl.semaphore_signal(credit, inc=1, device_id={"shard": red.across}, device_id_type=MESH)
        for j in (6, 7):
            keep(j, j % 2).wait()
        red.core_copy(3, 2048).wait_send()

    v = pltpu.VMEM
    pl.run_scoped(ffn, v((n, D), BF16), v((D, n), BF16), v((n, D), BF16), v((D, n), BF16), v((2, D, TILE), BF16),
                  v((2, TILE, D), BF16), v((2, n, TILE), BF16), v((n, TILE), BF16))
    got_up.wait()

    def spread(out, chunk, tile_rows):
        for p in range(4):
            low = lax.rem(lax.rem(s, 2) + p % 2, 2)
            high = lax.rem(lax.div(s, 2) + p // 2, 2)
            start = pl.multiple_of(target(low + 2 * high, chunk) + tile_rows, 16)
            buf[pl.ds(start, 256), :] = out[p * 256 : (p + 1) * 256].astype(BF16)

    def on_core(turn, chunk):
        red.core_copy(turn, 2 * chunk.rows).wait_recv()
        red.add_core(turn, 0, chunk.y_send, chunk.rows)
        red.y_copy(chunk).start()
        red.add_core(turn, chunk.rows, chunk.mine, chunk.rows)

    def attention(qkv, datt, brr, lse, lsec, scores, dprobs, probs, dscores, cls_row, qkv_cls, datt_cls, joint_cls):
        got_qkv, got_lse, got_lsec = load(0, qkv_h, qkv), load(1, lse_h, lse), load(2, lsec_h, lsec)

        def middle(mid, branch, att_t, w_out):
            got_mid, got_branch = load(3, mid_h, mid), load(4, branch_h, branch)
            got_att, got_out = load(5, att_t_h, att_t), load(6, full_out, w_out)
            red.on_z(cd0)
            got_mid.wait()
            got_branch.wait()

            def norm_rows(rows):
                m = mid[rows, :]
                c = m - jnp.mean(m, axis=-1, keepdims=True)
                inv = lax.rsqrt(jnp.mean(c * c, axis=-1, keepdims=True) + 1e-06)
                hat = c * inv
                g = gmid[rows, :]
                acc[4] += fold(g * hat)
                acc[5] += fold(g)
                sc = g * vecf[4:5, :]
                back = inv * (sc - jnp.mean(sc, axis=-1, keepdims=True)
                              - hat * jnp.mean(sc * hat, axis=-1, keepdims=True))
                gm = up_s[rows, :].astype(F32) + back
                gmid[rows, :] = gm
                acc[3] += fold(gm * branch[rows, :].astype(F32))
                gb = gm * vecf[3:4, :]
                acc[2] += fold(gb)
                brr[rows, :] = gb.astype(BF16)

            rows_loop(n, 16, norm_rows)
            got_att.wait()
            for q in range(2):
                spread(dot(att_t[...], brr[:, q * TILE : (q + 1) * TILE]), co, q * 256)
            red.core_copy(4, 2 * co.rows).start()
            got_out.wait()
            for q in range(2):
                datt[:, q * TILE : (q + 1) * TILE] = dot_nt(brr[...], w_out[q * TILE : (q + 1) * TILE, :]).astype(BF16)
            red.on_x(cu0)

        pl.run_scoped(middle, v((n, D), F32), v((n, D), BF16), v((D, n), BF16), v((D, D), BF16))
        got_qkv.wait()
        got_lse.wait()
        got_lsec.wait()
        qkv_cls[...] = qkv[main:, :].astype(F32)
        datt_cls[...] = datt[main:, :].astype(F32)
        joint_cls[...] = jnp.zeros_like(joint_cls)
        pl.semaphore_wait(credit, 1)
        on_core(4, co)
        plan = {0: [lambda: red.on_y(cd1), lambda: red.on_back(cd0)], 3: [lambda: red.on_z(cu0)], 5: [lambda: red.on_x(cd1)],
                6: [lambda: red.on_y(cu1), lambda: red.on_back(cu0)]}

        def image(i, carry):
            for k, steps in plan.items():
                @pl.when(i == k)
                def _(steps=steps):
                    for step in steps:
                        step()

            attend_back(i, qkv, qkv_cls, datt, datt_cls, lse, lsec, scores, dprobs, probs, dscores, cls_row, joint_cls,
                        acc.at[8], acc.at[9])
            return carry

        lax.fori_loop(0, images, image, 0)
        qkv[main:, :] = joint_cls[...].astype(BF16)
        acc[8] += fold(joint_cls[:, 0:D])
        acc[9] += fold(joint_cls[:, 2 * D : 3 * D])

        def tail(act_t, gact, w_qkv, turn, flat):
            x_s = brr
            got_act, got_x = load(3, act_t_h, act_t), load(4, x_h, x_s)

            def fetch(j):
                return pltpu.make_async_copy(full_qkv.at[pl.ds(j * 256, 256), :], w_qkv.at[j % 2], wsem.at[0, j % 2])

            fetch(0).start()
            fetch(1).start()
            got_act.wait()
            red.on_z(cd1)
            red.core_copy(4, 2 * co.rows).wait_send()
            for q in range(4):
                spread(dot(act_t[...], qkv[:, q * TILE : (q + 1) * TILE]), cq0, q * 256)
            red.core_copy(5, 2 * cq0.rows).start()
            red.on_y(co)
            red.on_x(cu1)

            def input_grad(j):
                fetch(j).wait()
                gact[:, j * 256 : (j + 1) * 256] = dot_nt(qkv[...], w_qkv[j % 2])
                if j < 2:
                    fetch(j + 2).start()

            input_grad(0)
            red.core_copy(5, 2 * cq0.rows).wait_send()
            for q in range(2):
                spread(dot(act_t[...], qkv[:, (q + 4) * TILE : (q + 5) * TILE]), cq1, q * 256)
            on_core(5, cq0)
            red.core_copy(6, 2 * cq1.rows).start()
            red.on_back(cd1)
            red.on_x(co)
            input_grad(1)
            input_grad(2)
            on_core(6, cq1)
            input_grad(3)
            red.on_z(cu1)
            got_x.wait()

            def norm_rows(rows):
                m = x_s[rows, :].astype(F32)
                c = m - jnp.mean(m, axis=-1, keepdims=True)
                inv = lax.rsqrt(jnp.mean(c * c, axis=-1, keepdims=True) + 1e-06)
                hat = c * inv
                g = gact[rows, :]
                acc[0] += fold(g * hat)
                acc[1] += fold(g)
                sc = g * vecf[0:1, :]
                back = inv * (sc - jnp.mean(sc, axis=-1, keepdims=True)
                              - hat * jnp.mean(sc * hat, axis=-1, keepdims=True))
                x_s[rows, :] = (gmid[rows, :] + back).astype(BF16)

            rows_loop(n, 16, norm_rows)
            red.on_z(co)
            to_tokens(x_s, flat, turn)
            copy = pltpu.make_async_copy(flat, tokens_o, osem.at[0])
            copy.start()
            red.on_back(cu1)
            red.on_back(co)
            copy.wait()

        pl.run_scoped(tail, v((D, n), BF16), v((n, D), F32), v((2, 256, 3 * D), BF16),
                      v((2, main, 128), F32), v((main + images, D), BF16))

    pl.run_scoped(attention, v((n, 3 * D), BF16), v((n, D), BF16), v((n, D), BF16), v((images, HEADS, PATCH), F32),
                  v((images, HEADS, PATCH), F32), v((8, 256, PATCH), F32), v((8, 256, PATCH), F32),
                  v((8, 256, PATCH), BF16), v((8, 256, PATCH), BF16), v((HEADS, PATCH), F32), v((CLS, 3 * D), F32),
                  v((CLS, D), F32), v((CLS, 3 * D), F32))

    def outcome(mid, hid, w_down, turn, flat, res):
        got_mid = load(3, mid_h, mid)

        def fetch(pair):
            copies = []
            for k in range(2):
                j = 2 * pair + k
                slot = pair % 2
                piece, t = relative(3 - j % 4), j // 4
                src = hid_h.at[k] if pair == 0 else hidden_o.at[j - 2]
                copies.append(pltpu.make_async_copy(src, hid.at[slot, :, pl.ds(k * TILE, TILE)], wsem.at[0, 2 * slot + k]))
                copies.append(pltpu.make_async_copy(full_down.at[piece, pl.ds(t * TILE, TILE), :],
                                                    w_down.at[slot, pl.ds(k * TILE, TILE), :], wsem.at[1, 2 * slot + k]))
            return copies

        for copy in fetch(0):
            copy.start()
        steps = {0: [lambda: red.on_y(cq0)], 2: [lambda: red.on_y(cq1), lambda: red.on_x(cq0)]}
        for pair in range(4):
            if pair < 3:
                for copy in fetch(pair + 1):
                    copy.start()
            for copy in fetch(pair):
                copy.wait()
            for q in range(2):
                cols = slice(q * TILE, (q + 1) * TILE)
                out = dot(hid[pair % 2], w_down[pair % 2, :, cols])
                if pair:
                    gmid[:, cols] += out
                else:
                    gmid[:, cols] = out
            for step in steps.get(pair, []):
                step()
        got_mid.wait()

        def rows_of(rows):
            projected = gmid[rows, :] + vecf[6:7, :]
            upstream = up_s[rows, :].astype(F32)
            acc[6] += fold(upstream * vecf[7:8, :])
            acc[7] += fold(upstream * projected)
            res[rows, :] = (mid[rows, :] + vecf[7:8, :] * projected).astype(BF16)

        rows_loop(n, 16, rows_of)
        for p in range(4):
            for k in range(8):
                v_part[p, k : k + 1, :] = jnp.sum(acc[k, :, p * 256 : (p + 1) * 256], axis=0, keepdims=True)
            joint = acc.at[8 + p // 2]
            for k in range(2):
                start = (p % 2) * TILE + k * 256
                v_part[p, 8 + k : 9 + k, :] = jnp.sum(joint[:, start : start + 256], axis=0, keepdims=True)
            for k in range(4):
                v_part[p, 10 + k : 11 + k, :] = sums_up[2 * p + k // 2 : 2 * p + k // 2 + 1, (k % 2) * 256 : (k % 2 + 1) * 256]
            v_part[p, 14:16, :] = jnp.zeros((2, 256), F32)
        for k in range(1, 4):
            group_copy(k).start()
        red.on_x(cq1)
        red.on_z(cq0)
        total = v_part[s]
        for k in range(1, 4):
            group_copy(k).wait_recv()
            total = total + v_group[k - 1]
        v_sum[...] = total
        v_all[red.r] = total
        for k in range(1, 2 * nz):
            all_copy(k).start()
        to_tokens(res, flat, turn)
        copy = pltpu.make_async_copy(flat, result_o, osem.at[0])
        copy.start()
        red.on_z(cq1)
        red.on_back(cq0)
        for k in range(1, 2 * nz):
            all_copy(k).wait_recv()
        total = v_all[0]
        for k in range(1, 2 * nz):
            total = total + v_all[k]
        v_group[0] = total
        small = pltpu.make_async_copy(v_group.at[0], small_o, osem.at[1])
        small.start()
        red.on_back(cq1)
        copy.wait()
        small.wait()

    pl.run_scoped(outcome, v((n, D), F32), v((2, n, D), BF16), v((2, D, D), BF16), v((2, main, 128), F32),
                  v((main + images, D), BF16), v((n, D), BF16))
    copies = []
    for c in chunks:
        red.finish(c)
        half = c.rows // 2
        for k, (src, first, where) in enumerate(((x_recv, c.x_recv, red.x), (buf, c.far, 1 - red.x))):
            copy = pltpu.make_async_copy(
                src.at[pl.ds(first, half), :],
                sums_o.at[pl.ds(pl.multiple_of(c.mine - cd0.mine + where * half, 16), half), :], fsem.at[2 * c.index + k])
            copy.start()
            copies.append(copy)
    red.core_copy(6, 2 * cq1.rows).wait_send()
    for k in range(1, 4):
        group_copy(k).wait_send()
    for k in range(1, 2 * nz):
        all_copy(k).wait_send()
    for c in chunks:
        red.drain(c)
    for copy in copies:
        copy.wait()


def convert_kernel(
    chunks, sums, small, result, tokens, result_o, tokens_o, g1_o, s1_o, qkv_o, bqv_o, out_o, bo_o, l1_o, g2_o, s2_o, up_o, bup_o, down_o, bd_o, l2_o,
    low, qkv, out, up, down, moved, dsem, osem, msem,
):
    base = chunks[0].mine
    moves = [pltpu.make_async_copy(src, moved.at[k], msem.at[0, k]) for k, src in enumerate((result, tokens))]
    stores = [pltpu.make_async_copy(moved.at[k], dst, msem.at[1, k]) for k, dst in enumerate((result_o, tokens_o))]
    gots = []
    for c in chunks:
        rows = pl.ds(c.mine - base, c.rows)
        gots.append(pltpu.make_async_copy(sums.at[rows, :], low.at[rows, :], dsem.at[c.index]))
        gots[-1].start()
    for copy in moves:
        copy.start()
    outs = []

    def send_out(src, dst):
        copy = pltpu.make_async_copy(src, dst, osem.at[len(outs)])
        copy.start()
        outs.append(copy)

    def block(c, first, count):
        return low[c.mine - base + first : c.mine - base + first + count, :]

    for t in range(2):
        gots[2 * t].wait()
        for k in range(8):
            down[t * TILE : (t + 1) * TILE, k * 128 : (k + 1) * 128] = block(chunks[2 * t], k * 128, 128).T.astype(F32)
        send_out(down.at[pl.ds(t * TILE, TILE), :], down_o.at[pl.ds(t * TILE, TILE), :])
        gots[2 * t + 1].wait()
        up[t] = block(chunks[2 * t + 1], 0, D).astype(F32)
        send_out(up.at[t], up_o.at[:, pl.ds(t * TILE, TILE)])
    for k in range(2):
        moves[k].wait()
        stores[k].start()
    gots[4].wait()
    for k in range(2):
        out[:, k * TILE : (k + 1) * TILE] = block(chunks[4], k * 256, 256).astype(F32)
    send_out(out, out_o)
    gots[5].wait()
    gots[6].wait()
    for k in range(6):
        qkv[:, k * TILE : (k + 1) * TILE] = block(chunks[5], k * 256, 256).astype(F32)
    send_out(qkv, qkv_o)
    vectors = (g1_o, s1_o, bo_o, l1_o, g2_o, s2_o, bd_o, l2_o, bqv_o, bup_o)
    row = 0
    for v in vectors:
        for k in range(v.shape[0] // 256):
            v[pl.ds(k * 256, 256)] = small[row : row + 1, :].reshape(256)
            row += 1
    for copy in outs + stores:
        copy.wait()


def convert(chunks, sums, small, result, tokens):
    one = lambda k: jax.ShapeDtypeStruct((k,), F32)
    outs = (
        low_shape(*result.shape), low_shape(*tokens.shape), one(256), one(256), wide_shape(256, 3 * D), one(512), wide_shape(256, D), one(256), one(256), one(256), one(256),
        wide_shape(D, D), one(1024), wide_shape(D, D), one(256), one(256),
    )
    v = pltpu.VMEM
    return pl.pallas_call(
        functools.partial(convert_kernel, chunks),
        out_shape=outs,
        in_specs=[ANY, VMEM, ANY, ANY],
        out_specs=[VMEM if len(o.shape) == 1 else ANY for o in outs],
        scratch_shapes=[v(sums.shape, BF16), v((256, 3 * D), F32), v((256, D), F32), v((2, D, TILE), F32),
                        v((D, D), F32), v((2,) + result.shape, BF16), pltpu.SemaphoreType.DMA((8,)),
                        pltpu.SemaphoreType.DMA((6,)), pltpu.SemaphoreType.DMA((2, 2))],
        compiler_params=pltpu.CompilerParams(vmem_limit_bytes=LIMIT),
        name="gradients_to_float32",
    )(sums, small, result, tokens)


def low_shape(*shape):
    return jax.ShapeDtypeStruct(shape, BF16)


def wide_shape(*shape):
    return jax.ShapeDtypeStruct(shape, F32)


ANY = pl.BlockSpec(memory_space=pl.ANY)
VMEM = pl.BlockSpec(memory_space=pltpu.VMEM)
LIMIT = 62 * 2**20


def forward(flat, cot, vectors, w_qkv, w_out, w_up, w_down):
    images = flat.shape[0] // (PATCH + 1)
    n = images * PATCH + CLS
    v = pltpu.VMEM
    outs = (
        low_shape(D, 3 * D), low_shape(D, D), low_shape(4, D, D), low_shape(4, D, D), low_shape(4, 16, 256),
        low_shape(n, 3 * D), low_shape(D, n), low_shape(n, D), low_shape(D, n), wide_shape(n, D), low_shape(n, D),
        low_shape(n, D), low_shape(D, n), low_shape(n, D), low_shape(n, D), low_shape(D, n),
        wide_shape(images, HEADS, PATCH), wide_shape(images, HEADS, PATCH),
        low_shape(2, 2048, TILE), low_shape(2, n, TILE), wide_shape(n, D), wide_shape(8, TILE),
    )
    return pl.pallas_call(
        gather_kernel,
        out_shape=outs,
        in_specs=[VMEM] * 12 + [ANY] * 4,
        out_specs=[ANY] * len(outs),
        scratch_shapes=[
            v((D, 3 * D), BF16), v((D, D), BF16), v((4, D, D), BF16), v((4, D, D), BF16),
            v((n, D), BF16), v((n, 3 * D), BF16), v((n, D), BF16), v((n, D), BF16), v((n, D), F32), v((n, D), BF16),
            v((n, D), BF16), v((D, n), BF16), v((D, n), BF16),
            v((images, HEADS, PATCH), F32), v((images, HEADS, PATCH), F32),
            v((8, 256, PATCH), F32), v((8, 256, PATCH), BF16), v((PATCH, D), F32), v((HEADS, PATCH), F32),
            v((CLS, D), F32), v((CLS, 3 * D), F32), v((2, images * PATCH, 128), F32), v((16, 256), F32),
            v((16, 256), BF16), v((4, 16, 256), BF16), v((16, D), F32), v((8, 3 * D), F32), v((8, TILE), F32),
            v((8, TILE), F32), pltpu.SemaphoreType.DMA((2, 6, 11)), pltpu.SemaphoreType.DMA((6,)), pltpu.SemaphoreType.DMA((2, 3)),
            pltpu.SemaphoreType.DMA((30,)),
        ],
        compiler_params=pltpu.CompilerParams(collective_id=0, has_side_effects=True, vmem_limit_bytes=LIMIT),
        cost_estimate=pl.CostEstimate(flops=18 * 2**30, bytes_accessed=64 * 2**20, transcendentals=3 * 2**20),
        name="gather_and_attention",
    )(flat, cot, *vectors, w_qkv, w_out, w_up, w_down)


def backward(nz, images, vec, *arrays):
    n = images * PATCH + CLS
    tokens = images * (PATCH + 1)
    v = pltpu.VMEM
    chunks, sizes = chunk_layout(nz)
    outs = (low_shape(tokens, D), low_shape(tokens, D), low_shape(sizes["total"], TILE), wide_shape(16, 256),
            low_shape(6, n, TILE))
    return pl.pallas_call(
        functools.partial(backward_kernel, nz, chunks),
        out_shape=outs,
        in_specs=[VMEM] + [ANY] * len(arrays),
        out_specs=[ANY] * len(outs),
        scratch_shapes=[
            v((sizes["buf"], TILE), BF16), v((2, 2048, TILE), BF16), v((sizes["y_recv"], TILE), BF16),
            v((sizes["x_recv"], TILE), BF16), v((nz - 1, sizes["z_recv"], TILE), BF16), v((n, D), F32), v((n, D), BF16),
            v((10, 8, D), F32), v((8, TILE), F32), v((16, D), F32), v((8, 3 * D), F32), v((8, TILE), F32),
            v((4, 16, 256), F32), v((3, 16, 256), F32), v((16, 256), F32), v((2 * nz, 16, 256), F32),
            pltpu.SemaphoreType.DMA((2, len(chunks), 3 * nz)), pltpu.SemaphoreType.DMA((2, 7)),
            pltpu.SemaphoreType.DMA((2, 3)), pltpu.SemaphoreType.DMA((2, 2 * nz - 1)),
            pltpu.SemaphoreType.REGULAR, pltpu.SemaphoreType.DMA((12,)), pltpu.SemaphoreType.DMA((2, 4)),
            pltpu.SemaphoreType.DMA((2,)), pltpu.SemaphoreType.DMA((2,)), pltpu.SemaphoreType.DMA((2 * len(chunks),)),
        ],
        compiler_params=pltpu.CompilerParams(collective_id=1, has_side_effects=True, vmem_limit_bytes=LIMIT),
        cost_estimate=pl.CostEstimate(flops=66 * 2**30, bytes_accessed=128 * 2**20, transcendentals=8 * 2**20),
        name="layer_backward",
    )(vec, *arrays), chunks


def on_device(
    tokens, norm1_gain, norm1_shift, w_qkv, bias_qv, w_out, bias_out, scale_one, norm2_gain, norm2_shift, w_up, bias_up,
    w_down, bias_down, scale_two, cotangent,
):
    images, length, _ = tokens.shape
    nz = lax.axis_size("replica") // 2
    flatten = lambda a: jnp.transpose(a, (1, 0, 2)).reshape(images * length, D)
    restore = lambda a: jnp.transpose(a.reshape(length, images, D), (1, 0, 2))
    vectors = (norm1_gain, norm1_shift, bias_out, scale_one, norm2_gain, norm2_shift, bias_down, scale_two, bias_qv, bias_up)
    full_qkv, full_out, full_up, full_down, vec, *kept = forward(
        flatten(tokens), flatten(cotangent), vectors, w_qkv, w_out, w_up, w_down)
    (result, grad_tokens, sums, small, _), chunks = backward(nz, images, vec, full_qkv, full_out, full_up, full_down, *kept)
    result, grad_tokens, *gradients = convert(chunks, sums, small, result, grad_tokens)
    return (restore(result), restore(grad_tokens)) + tuple(gradients)


def solution(mesh):
    placed = (
        P(("shard", "replica"), None, None),
        P("shard"),
        P("shard"),
        P("shard", None),
        P("shard"),
        P("shard", None),
        P("shard"),
        P("shard"),
        P("shard"),
        P("shard"),
        P(None, "shard"),
        P("shard"),
        P("shard", None),
        P("shard"),
        P("shard"),
        P(("shard", "replica"), None, None),
    )
    return jax.shard_map(
        on_device,
        mesh=mesh,
        in_specs=placed,
        out_specs=(
            P(("shard", "replica"), None, None),
            P(("shard", "replica"), None, None),
            P("shard"),
            P("shard"),
            P("shard", None),
            P("shard"),
            P("shard", None),
            P("shard"),
            P("shard"),
            P("shard"),
            P("shard"),
            P(None, "shard"),
            P("shard"),
            P("shard", None),
            P("shard"),
            P("shard"),
        ),
        check_vma=False,
    )
```

```python
import functools

import jax
import jax.numpy as jnp
from jax import lax
from jax.experimental import pallas as pl
from jax.experimental.pallas import tpu as pltpu
from jax.sharding import PartitionSpec as P

F32 = jnp.float32
BF16 = jnp.bfloat16
D = 1024
FF = 4096
HEADS = 16
PATCH = 128
CLS = 16
TILE = 512
FACTOR = 0.125
MESH = pl.DeviceIdType.MESH


def dot(a, b):
    return jnp.dot(a, b, preferred_element_type=F32)


def dot_nt(a, b):
    return lax.dot_general(a, b, (((1,), (1,)), ((), ())), preferred_element_type=F32)


def dot_tn(a, b):
    return lax.dot_general(a, b, (((0,), (0,)), ((), ())), preferred_element_type=F32)


def at(index, size):
    return pl.ds(pl.multiple_of(index * size, size), size)


def head_mask():
    lane = lax.shift_right_logical(lax.broadcasted_iota(jnp.int32, (HEADS, D), 1), 6)
    return lane == lax.broadcasted_iota(jnp.int32, (HEADS, D), 0)


def split_pair(v):
    low = lax.broadcasted_iota(jnp.int32, v.shape, 1) < 64
    zero = jnp.zeros_like(v)
    return jnp.concatenate([jnp.where(low, v, zero), jnp.where(low, zero, v)], 0)


def merge_pair(v):
    n = v.shape[0] // 2
    low = lax.broadcasted_iota(jnp.int32, (n, v.shape[1]), 1) < 64
    return jnp.where(low, v[:n], v[n:])


def place():
    s = lax.axis_index("shard")
    r = lax.axis_index("replica")
    x = lax.rem(r, 2)
    z = lax.div(r, 2)
    return s, r, x, z


def peers(s, r):
    sib = s + 1 - 2 * lax.rem(s, 2)
    across = lax.rem(s + 2, 4)
    side = r + 1 - 2 * lax.rem(r, 2)
    return sib, across, side


def rows_loop(n, step, body):
    lax.fori_loop(0, n // step, lambda k, c: (body(at(k, step)), c)[1], 0, unroll=5)


def unpack_vectors(vec, vecf, bias_qkv):
    for v in range(8):
        for s in range(4):
            vecf[v : v + 1, s * 256 : (s + 1) * 256] = vec[s, v : v + 1, :].astype(F32)
    bias_qkv[...] = jnp.zeros_like(bias_qkv)
    for s in range(4):
        for t in range(2):
            col = (s * 2 + t) * 256 + (D if s >= 2 else 0)
            bias_qkv[0:1, col : col + 256] = vec[s, 8 + t : 9 + t, :].astype(F32)


def layer_norm(v, gain, shift):
    c = v - jnp.mean(v, axis=-1, keepdims=True)
    inv = lax.rsqrt(jnp.mean(c * c, axis=-1, keepdims=True) + 1e-06)
    return c * inv * gain + shift


def to_images(src, dst, turn):
    images = (src.shape[0]) // (PATCH + 1)
    main = images * PATCH

    def lane_block(l, carry):
        cols = at(l, 128)
        slot = lax.rem(l, 2)
        turn[slot] = src[0:main, cols].astype(F32)
        for i in range(images):
            dst[i * PATCH : (i + 1) * PATCH, cols] = turn[slot, pl.ds(i, PATCH, stride=images), :].astype(BF16)
        return carry

    lax.fori_loop(0, D // 128, lane_block, 0)
    last = src[main : main + images, :].astype(F32)
    dst[main:, :] = jnp.concatenate([last, jnp.zeros((CLS - images, D), F32)], 0).astype(BF16)


def pack_vectors(vectors, dst):
    row = 0
    for v in vectors:
        count = v.shape[0] // 256
        wide = v[...].astype(F32)
        for k in range(count):
            dst[row : row + 1, :] = wide[k * 256 : (k + 1) * 256].reshape(1, 256)
            row += 1


def attend(i, qkv, qkv_cls, scores, probs, mix, probs_cls, att, att_cls, lse, lse_cls):
    rows = at(i, PATCH)
    mask = head_mask()
    own = qkv_cls[pl.ds(i, 1), :]
    q_c, k_c, v_c = own[:, :D] * FACTOR, own[:, D : 2 * D], own[:, 2 * D :]
    q_bd = jnp.where(mask, q_c, 0.0)
    k_bd = jnp.where(mask, k_c, 0.0).astype(BF16)
    v_bd = jnp.where(mask, v_c, 0.0).astype(BF16)
    to_cls = dot_nt(k_bd, qkv[rows, 0:D]) * FACTOR
    of_cls = dot_nt(q_bd.astype(BF16), qkv[rows, D : 2 * D])
    corner = jnp.sum(q_bd * k_c, axis=1, keepdims=True)
    top = jnp.maximum(jnp.max(of_cls, axis=1, keepdims=True), corner)
    e_row = jnp.exp(of_cls - top)
    e_cor = jnp.exp(corner - top)
    total = jnp.sum(e_row, axis=1, keepdims=True) + e_cor
    inv = 1.0 / total
    row = dot((e_row * inv).astype(BF16), qkv[rows, 2 * D : 3 * D])
    row = row + (e_cor * inv).astype(BF16).astype(F32) * v_c
    att_cls[pl.ds(i, 1), :] = jnp.sum(jnp.where(mask, row, 0.0), axis=0, keepdims=True)
    lse_cls[i] = jnp.broadcast_to(top + jnp.log(total), (HEADS, PATCH))
    for g in range(HEADS // 2):
        q2 = qkv[rows, g * 128 : g * 128 + 128] * jnp.asarray(FACTOR, BF16)
        scores[g] = dot_nt(split_pair(qkv[rows, g * 128 + D : g * 128 + D + 128]), q2)
    for g in range(HEADS // 2):
        for u in range(2):
            h = 2 * g + u
            part = scores[g, u * PATCH : (u + 1) * PATCH, :]
            extra = to_cls[h : h + 1, :]
            top = jnp.maximum(jnp.max(part, axis=0, keepdims=True), extra)
            e_part = jnp.exp(part - top)
            e_extra = jnp.exp(extra - top)
            total = jnp.sum(e_part, axis=0, keepdims=True) + e_extra
            inv = 1.0 / total
            probs[g, u * PATCH : (u + 1) * PATCH, :] = (e_part * inv).astype(BF16)
            probs_cls[h : h + 1, :] = e_extra * inv
            lse[i, h : h + 1, :] = top + jnp.log(total)
    for g in range(HEADS // 2):
        v2 = split_pair(qkv[rows, g * 128 + 2 * D : g * 128 + 2 * D + 128])
        mix[:, g * 128 : g * 128 + 128] = dot_tn(probs[g], v2)
    att[rows, :] = (mix[...] + dot_tn(probs_cls[...].astype(BF16), v_bd)).astype(BF16)


class Gather:
    KINDS = ("own", "far", "x1", "z1", "x2", "z2", "p0", "p1", "p2", "p3", "p4")

    def __init__(self, number, rows, src, dst, sems, local):
        s, r, x, z = place()
        sib, across, side = peers(s, r)
        self.number, self.sems = number, sems
        near = lax.rem(z, 2)
        level = {"replica": (z + 1 - 2 * near) * 2 + x}
        side, sib = {"replica": side}, {"shard": sib}
        size = rows // 4
        half = size // 2

        def start(zz, xx):
            return pl.multiple_of((2 * zz + xx) * size, 16)

        def same(first, count, to):
            ref = dst(across, pl.multiple_of(first, 16), count)
            return ref, ref, to

        mine, by_x, by_z, by_both = start(near, x), start(near, 1 - x), start(1 - near, x), start(1 - near, 1 - x)
        self.parts = {
            "own": (dst(s, 0, rows), dst(s, 0, rows), sib),
            "far": (dst(s, mine, size), dst(s, mine, size), {"shard": across}),
            "x1": same(mine, size, side),
            "z1": same(mine, size, level),
            "x2": same(by_z, half, side),
            "z2": same(by_x + half, half, level),
            "p0": same(mine, size, sib),
            "p1": same(by_x, size, sib),
            "p2": same(by_z, size, sib),
            "p3": same(by_both, half, sib),
            "p4": same(by_both + half, half, sib),
        }
        self.local = pltpu.make_async_copy(src(0, rows), dst(s, 0, rows), local.at[number])

    def copy(self, kind):
        a, b, to = self.parts[kind]
        k = self.KINDS.index(kind)
        return pltpu.make_async_remote_copy(
            a, b, self.sems.at[0, self.number, k], self.sems.at[1, self.number, k], device_id=to, device_id_type=MESH
        )

    def load(self):
        self.local.start()

    def begin(self):
        self.local.wait()
        self.copy("far").start()

    def share(self):
        self.copy("own").start()

    def on_far(self):
        self.copy("far").wait_recv()
        for kind in ("x1", "z1", "p0"):
            self.copy(kind).start()

    def on_near(self):
        self.copy("x1").wait_recv()
        self.copy("z2").start()
        self.copy("p1").start()
        self.copy("z1").wait_recv()
        self.copy("x2").start()
        self.copy("p2").start()

    def on_last(self):
        self.copy("x2").wait_recv()
        self.copy("p3").start()
        self.copy("z2").wait_recv()
        self.copy("p4").start()

    def ready(self):
        for kind in ("own", "p0", "p1", "p2", "p3", "p4"):
            self.copy(kind).wait_recv()

    def drain(self):
        for kind in self.KINDS:
            self.copy(kind).wait_send()


def relative_piece(s, rel):
    low, high = lax.rem(rel, 2), lax.div(rel, 2)
    return s + low * (1 - 2 * lax.rem(s, 2)) + high * (2 - 4 * lax.div(s, 2))


def unpack_bias_up(vec, bias_up):
    for p in range(4):
        for t in range(2):
            for k in range(2):
                row = 10 + 2 * t + k
                bias_up[2 * p + t : 2 * p + t + 1, k * 256 : (k + 1) * 256] = vec[p, row : row + 1, :].astype(F32)


def ffn_tile(act2, dr, dr_t, act2_t, w_up, w_down, bias, hid, br, gmid, fresh, on_hidden, put):
    n = act2.shape[0]
    cut = 16 * (n // 32)
    first, second = slice(0, cut), slice(cut, n)

    def both(rows, before, grad):
        hidden, step = gelu_both(before)
        hid[rows, :] = hidden.astype(BF16)
        grad = grad * step
        br[rows, :] = grad.astype(BF16)
        return jnp.sum(grad, axis=0, keepdims=True)

    def back(rows):
        out = dot_nt(br[rows, :], w_up())
        if fresh:
            gmid[rows, :] = out
        else:
            gmid[rows, :] += out

    before0 = dot(act2[first, :], w_up()) + bias
    grad0 = dot_nt(dr[first, :], w_down())
    before1 = dot(act2[second, :], w_up()) + bias
    column = both(first, before0, grad0)
    grad1 = dot_nt(dr[second, :], w_down())
    back(first)
    column = column + both(second, before1, grad1)
    back(second)
    on_hidden()
    put(0, dot(dr_t[...], hid[...]).astype(BF16))
    put(1, dot(act2_t[...], br[...]).astype(BF16))
    return column


def gather_kernel(
    tokens, cot, v0, v1, v2, v3, v4, v5, v6, v7, v8, v9, w_qkv, w_out, w_up, w_down,
    qkv_w_o, out_w_o, up_w_o, down_w_o, vec_all, qkv_o, act_t_o, x_o, att_t_o, mid_o, branch_o, act2_o, act2_t_o, up_o,
    dr_o, dr_t_o, lse_o, lsec_o, parts_o, hid_o, gact_o, column_o,
    full_qkv, full_out, full_up, full_down, x_s, qkv, act, att, mid, branch, act2, turned_a, turned_b, lse, lsec,
    scores, probs, mix, probs_cls, cls, qkv_cls, turn, vec32, vec_own_s, vec, vecf, bias_qkv,
    bias_up, column,
    sems, local, vsem, osem,
):
    s, r, x, z = place()
    sib, across, side = peers(s, r)
    n = x_s.shape[0]
    images = lse.shape[0]
    main = images * PATCH

    vec32[...] = jnp.zeros_like(vec32)
    pack_vectors((v0, v1, v2, v3, v4, v5, v6, v7, v8, v9), vec32)
    vec_own_s[...] = vec32[...].astype(BF16)
    barrier = pltpu.get_barrier_semaphore()
    level = (z + 1 - 2 * lax.rem(z, 2)) * 2 + x
    for to in ({"shard": sib}, {"shard": across}, {"replica": side}, {"replica": level}):
        pl.semaphore_signal(barrier, inc=1, device_id=to, device_id_type=MESH)

    def unit(number, rows, src, dst):
        return Gather(number, rows, src, dst, sems, local)

    g_qkv = unit(0, 256, lambda a, k: w_qkv.at[pl.ds(a, k), :],
                 lambda p, a, k: full_qkv.at[pl.ds(pl.multiple_of(p * 256 + a, 16), k), :])
    g_out = unit(1, 256, lambda a, k: w_out.at[pl.ds(a, k), :],
                 lambda p, a, k: full_out.at[pl.ds(pl.multiple_of(p * 256 + a, 16), k), :])

    def up_unit(number, t):
        cols = pl.ds(t * TILE, TILE)
        return unit(number, D, lambda a, k: w_up.at[pl.ds(a, k), cols],
                    lambda p, a, k: full_up.at[p, pl.ds(pl.multiple_of(a, 16), k), cols])

    def down_unit(number, t):
        return unit(number, TILE, lambda a, k: w_down.at[pl.ds(a + t * TILE, k), :],
                    lambda p, a, k: full_down.at[p, pl.ds(pl.multiple_of(a + t * TILE, 16), k), :])

    g_up0, g_down0, g_up1, g_down1 = up_unit(2, 0), down_unit(3, 0), up_unit(4, 1), down_unit(5, 1)

    for g in (g_qkv, g_out, g_up0, g_down0, g_up1, g_down1):
        g.load()
    pl.semaphore_wait(barrier, 4)

    def vec_copy(k, src, slot, to):
        return pltpu.make_async_remote_copy(src, vec.at[slot], vsem.at[0, k], vsem.at[1, k], device_id=to,
                                            device_id_type=MESH)

    vec_own = vec_copy(0, vec_own_s, s, {"shard": sib})
    vec_far = vec_copy(1, vec_own_s, s, {"shard": across})
    vec_pass = vec_copy(2, vec.at[across], across, {"shard": sib})
    vec_own.start()
    vec_far.start()
    g_qkv.begin()
    g_qkv.share()
    g_out.begin()
    vec[s] = vec_own_s[...]

    to_images(tokens, x_s, turn)
    outs = {}

    def send_out(k, src, dst):
        outs[k] = pltpu.make_async_copy(src, dst, osem.at[k])
        outs[k].start()

    send_out(0, x_s, x_o)
    vec_far.wait_recv()
    vec_pass.start()
    vec_own.wait_recv()
    vec_pass.wait_recv()
    unpack_vectors(vec, vecf, bias_qkv)

    def first_norm(rows):
        act[rows, :] = layer_norm(x_s[rows, :].astype(F32), vecf[0:1, :], vecf[1:2, :]).astype(BF16)

    rows_loop(n, 16, first_norm)
    g_qkv.on_far()
    for g in (g_up0, g_down0, g_up1, g_down1):
        g.begin()
    transpose_into(act, turned_b)
    send_out(1, turned_b, act_t_o)
    g_qkv.on_near()
    to_images(cot, branch, turn)

    def down_rows(rows):
        act2[rows, :] = (branch[rows, :].astype(F32) * vecf[7:8, :]).astype(BF16)

    rows_loop(n, 16, down_rows)
    g_qkv.on_last()
    g_out.on_far()
    send_out(14, branch, up_o)
    send_out(15, act2, dr_o)
    transpose_into(act2, turned_a)
    send_out(16, turned_a, dr_t_o)
    g_out.on_near()
    g_qkv.ready()
    send_out(4, full_qkv, qkv_w_o)
    for g in (g_out, g_up0, g_down0):
        g.share()

    def qkv_tile(j, carry):
        cols = at(j, TILE)
        low = (dot(act[...], full_qkv[:, cols]) + bias_qkv[0:1, cols]).astype(BF16)
        qkv[:, cols] = low
        qkv_cls[:, cols] = low[main:].astype(F32)
        return carry

    lax.fori_loop(0, 3 * D // TILE, qkv_tile, 0)
    send_out(2, qkv, qkv_o)
    act[...] = act2[...]
    unpack_bias_up(vec, bias_up)
    column[...] = jnp.zeros_like(column)
    send_out(3, vec, vec_all)
    cls[...] = jnp.zeros_like(cls)
    g_out.on_last()
    g_up0.on_far()
    plan = {1: [g_up0.on_near], 2: [g_down0.on_far], 3: [g_up0.on_last, g_up1.share], 4: [g_down0.on_near, g_up1.on_far],
            6: [g_down0.on_last, g_down1.share], 7: [g_up1.on_near, g_down1.on_far]}

    def image(i, carry):
        for k, steps in plan.items():
            @pl.when(i == k)
            def _(steps=steps):
                for step in steps:
                    step()

        attend(i, qkv, qkv_cls, scores, probs, mix, probs_cls, att, cls, lse, lsec)
        return carry

    lax.fori_loop(0, images, image, 0)
    att[main:, :] = cls[...].astype(BF16)
    outs.pop(1).wait()
    transpose_into(att, turned_b)
    send_out(8, turned_b, att_t_o)
    send_out(9, lse, lse_o)
    send_out(10, lsec, lsec_o)
    g_out.ready()
    outs.pop(14).wait()
    for j in range(D // TILE):
        cols = slice(j * TILE, (j + 1) * TILE)
        out = dot(att[...], full_out[:, cols]) + vecf[2:3, cols]
        branch[:, cols] = out.astype(BF16)
        mid[:, cols] = x_s[:, cols].astype(F32) + vecf[3:4, cols] * out
    send_out(11, mid, mid_o)
    send_out(12, branch, branch_o)
    g_up1.on_last()
    g_down1.on_near()

    def second_norm(rows):
        act2[rows, :] = layer_norm(mid[rows, :], vecf[4:5, :], vecf[5:6, :]).astype(BF16)

    outs.pop(15).wait()
    rows_loop(n, 16, second_norm)
    send_out(13, act2, act2_o)
    outs.pop(8).wait()
    transpose_into(act2, turned_b)
    send_out(17, turned_b, act2_t_o)
    half = pl.ds(0, TILE)
    rest = pl.ds(TILE, TILE)
    send_out(5, full_out, out_w_o)
    g_up0.ready()
    send_out(18, full_up.at[:, :, half], up_w_o.at[:, :, half])
    g_down0.ready()
    send_out(19, full_down.at[:, half, :], down_w_o.at[:, half, :])
    for k in (2, 11):
        outs.pop(k).wait()
    hid, br = qkv.at[:, pl.ds(0, TILE)], qkv.at[:, pl.ds(TILE, TILE)]
    for k, rel in enumerate((3, 2)):
        piece = relative_piece(s, rel)

        def put(half_k, value, k=k):
            qkv[0:D, (2 + 2 * k + half_k) * TILE : (3 + 2 * k + half_k) * TILE] = value

        if k:
            outs.pop(22).wait()
        column[pl.ds(2 * piece, 1), :] = ffn_tile(
            act2, act, turned_a, turned_b, lambda: full_up[piece, :, 0:TILE], lambda: full_down[piece, 0:TILE, :],
            bias_up[pl.ds(2 * piece, 1), :], hid, br, mid, k == 0, lambda: send_out(22 + k, hid, hid_o.at[k]), put)
        for half_k in range(2):
            send_out(24 + 2 * k + half_k, qkv.at[pl.ds(0, D), pl.ds((2 + 2 * k + half_k) * TILE, TILE)],
                     parts_o.at[k, pl.ds(half_k * D, D), :])
        if k == 0:
            g_down1.on_last()
            g_up1.ready()
            send_out(20, full_up.at[:, :, rest], up_w_o.at[:, :, rest])
    send_out(28, mid, gact_o)
    send_out(29, column, column_o)
    g_down1.ready()
    send_out(21, full_down.at[:, rest, :], down_w_o.at[:, rest, :])
    for copy in outs.values():
        copy.wait()
    for g in (g_qkv, g_out, g_up0, g_down0, g_up1, g_down1):
        g.drain()
    for copy in (vec_own, vec_far, vec_pass):
        copy.wait_send()


class Chunk:
    def __init__(self, index, rows, mine, y_send, y_recv, x_recv, z_recv, far):
        self.index, self.rows, self.mine, self.y_send, self.far = index, rows, mine, y_send, far
        self.y_recv, self.x_recv, self.z_recv = y_recv, x_recv, z_recv


def chunk_layout(nz):
    sizes = [1024, 1024, 1024, 1024, 512, 1024, 512]
    y_base = 2048
    y_a = y_base
    y_b = y_a + 2048
    mine_base = y_b + 2048
    chunks = []
    mine = mine_base
    late = 0
    xr = zr = 0
    for k, rows in enumerate(sizes):
        if k < 2:
            ys, yr = y_a + 1024 * k, 1024 * k
        elif k < 4:
            ys, yr = y_b + 1024 * (k - 2), 2048 + 1024 * (k - 2)
        else:
            ys, yr = y_a + late, late
            late += rows
        far = mine_base + sum(sizes) + 512 * k if k < 2 else ys
        chunks.append(Chunk(k, rows, mine, ys, yr, xr, zr, far))
        mine += rows
        xr += rows // 2
        zr += rows // 2 // nz
    return chunks, dict(buf=mine + 1024, total=sum(sizes), mine=mine_base, y_recv=2 * 2048, x_recv=xr, z_recv=zr)


def add_rows(dst, d0, src, s0, rows):
    step = next(k for k in (128, 96, 64, 32, 16) if rows % k == 0)

    def body(k, carry):
        d = pl.ds(pl.multiple_of(d0 + k * step, 16), step)
        t = pl.ds(pl.multiple_of(s0 + k * step, 16), step)
        dst[d, :] = (dst[d, :].astype(F32) + src[t, :].astype(F32)).astype(BF16)
        return carry

    lax.fori_loop(0, rows // step, body, 0)


class Reduce:
    def __init__(self, nz, buf, core_recv, y_recv, x_recv, z_recv, sems, core_sems, credit):
        self.nz, self.buf, self.core_recv = nz, buf, core_recv
        self.y_recv, self.x_recv, self.z_recv = y_recv, x_recv, z_recv
        self.sems, self.core_sems, self.credit = sems, core_sems, credit
        self.s, self.r, self.x, self.z = place()
        self.sib, self.across, self.side = peers(self.s, self.r)

    def remote(self, src, dst, chunk, kind, to):
        return pltpu.make_async_remote_copy(
            src, dst, self.sems.at[0, chunk.index, kind], self.sems.at[1, chunk.index, kind], device_id=to,
            device_id_type=MESH)

    def peer(self, k):
        return {"replica": lax.rem(self.z + k, self.nz) * 2 + self.x}

    def core_copy(self, turn, rows):
        slot = turn % 2
        return pltpu.make_async_remote_copy(
            self.buf.at[pl.ds(0, rows), :], self.core_recv.at[slot, pl.ds(0, rows), :],
            self.core_sems.at[0, turn], self.core_sems.at[1, turn], device_id={"shard": self.sib}, device_id_type=MESH)

    def add_core(self, turn, first, dst, rows):
        add_rows(self.buf, dst, self.core_recv.at[turn % 2], first, rows)

    def y_copy(self, c):
        return self.remote(self.buf.at[pl.ds(c.y_send, c.rows), :], self.y_recv.at[pl.ds(c.y_recv, c.rows), :], c, 0,
                           {"shard": self.across})

    def x_copy(self, c):
        half = c.rows // 2
        return self.remote(self.buf.at[pl.ds(pl.multiple_of(c.mine + (1 - self.x) * half, 16), half), :],
                           self.x_recv.at[pl.ds(c.x_recv, half), :], c, 1, {"replica": self.side})

    def quarter(self, c, x, z):
        half = c.rows // 2
        size = half // self.nz
        return pl.ds(pl.multiple_of(c.mine + x * half + z * size, 16), size)

    def z_copy(self, c, k):
        size = c.rows // 2 // self.nz
        return self.remote(self.buf.at[self.quarter(c, self.x, lax.rem(self.z + k, self.nz)), :],
                           self.z_recv.at[k - 1, pl.ds(c.z_recv, size), :], c, 1 + k, self.peer(k))

    def done(self, first, c, z):
        size = c.rows // 2 // self.nz
        return pl.ds(pl.multiple_of(first + z * size, 16), size)

    def back_z(self, c, k):
        part = self.x_recv.at[self.done(c.x_recv, c, self.z), :]
        return self.remote(part, part, c, self.nz + k, self.peer(k))

    def back_x(self, c, k):
        z = lax.rem(self.z + self.nz - k, self.nz)
        return self.remote(self.x_recv.at[self.done(c.x_recv, c, z), :], self.buf.at[self.done(c.far, c, z), :], c,
                           2 * self.nz + k, {"replica": self.side})

    def on_y(self, c):
        self.y_copy(c).wait_recv()
        add_rows(self.buf, c.mine, self.y_recv, c.y_recv, c.rows)
        self.y_copy(c).wait_send()
        self.x_copy(c).start()

    def on_x(self, c):
        half = c.rows // 2
        self.x_copy(c).wait_recv()
        add_rows(self.buf, c.mine + self.x * half, self.x_recv, c.x_recv, half)
        for k in range(1, self.nz):
            self.z_copy(c, k).start()

    def on_z(self, c):
        size = c.rows // 2 // self.nz
        start = c.mine + self.x * (c.rows // 2) + self.z * size
        for k in range(1, self.nz):
            self.z_copy(c, k).wait_recv()
        step = next(k for k in (64, 48, 32, 16) if size % k == 0)

        def body(i, carry):
            d = pl.ds(pl.multiple_of(start + i * step, 16), step)
            total = self.buf[d, :].astype(F32)
            for k in range(1, self.nz):
                total = total + self.z_recv[k - 1, pl.ds(pl.multiple_of(c.z_recv + i * step, 16), step), :].astype(F32)
            to = pl.ds(pl.multiple_of(c.x_recv + self.z * size + i * step, 16), step)
            self.x_recv[to, :] = total.astype(BF16)
            return carry

        lax.fori_loop(0, size // step, body, 0)
        for k in range(1, self.nz):
            self.back_z(c, k).start()
        self.back_x(c, 0).start()

    def on_back(self, c):
        for k in range(1, self.nz):
            self.back_z(c, k).wait_recv()
            self.back_x(c, k).start()

    def finish(self, c):
        for k in range(self.nz):
            self.back_x(c, k).wait_recv()

    def drain(self, c):
        self.x_copy(c).wait_send()
        for k in range(1, self.nz):
            self.z_copy(c, k).wait_send()
            self.back_z(c, k).wait_send()
        for k in range(self.nz):
            self.back_x(c, k).wait_send()


def fold(v):
    return jnp.sum(v.reshape(v.shape[0] // 8, 8, v.shape[1]), axis=0)


def gelu_both(v):
    e = jnp.exp(-0.5 * v * v)
    t = 1.0 / (1.0 + 0.23164189 * jnp.abs(v))
    poly = ((((1.061405429 * t - 1.453152027) * t + 1.421413741) * t - 0.284496736) * t + 0.254829592) * t
    tail = 0.5 * poly * e
    phi = jnp.where(v >= 0.0, 1.0 - tail, tail)
    return v * phi, phi + v * e * 0.3989422804014327


def transpose_into(src, dst):
    for c in range(D // 128):
        dst[c * 128 : (c + 1) * 128, :] = src[:, c * 128 : (c + 1) * 128].T


def attend_back(
    i, qkv, qkv_cls, datt, datt_cls, lse, lsec, scores, dprobs, probs, dscores, cls_row, joint_cls, joint, extra, sum_q, sum_v
):
    rows = at(i, PATCH)
    mask = head_mask()
    own = qkv_cls[pl.ds(i, 1), :]
    do_c = datt_cls[pl.ds(i, 1), :]
    q_c, k_c, v_c = own[:, :D] * FACTOR, own[:, D : 2 * D], own[:, 2 * D :]
    pick = lambda v: jnp.where(mask, v, 0.0)
    q_w, k_w, v_w, do_w = pick(q_c), pick(k_c), pick(v_c), pick(do_c)
    q_bd, k_bd, v_bd, do_bd = (v.astype(BF16) for v in (q_w, k_w, v_w, do_w))
    queries, keys, values = (qkv[rows, k * D : (k + 1) * D] for k in range(3))
    grads = datt[rows, :]
    low = lambda v: v.astype(BF16)
    top = lsec[i][:, 0:1]
    p_row = jnp.exp(dot_nt(q_bd, keys) - top)
    p_cor = jnp.exp(jnp.sum(q_w * k_c, axis=1, keepdims=True) - top)
    dp_row = dot_nt(do_bd, values)
    dp_cor = jnp.sum(do_w * v_c, axis=1, keepdims=True)
    delta = jnp.sum(p_row * dp_row, axis=1, keepdims=True) + p_cor * dp_cor
    ds_row = low(p_row * (dp_row - delta))
    ds_cor = low(p_cor * (dp_cor - delta)).astype(F32)
    p_col = jnp.exp(dot_nt(k_bd, queries) * FACTOR - lse[i])
    dp_col = dot_nt(v_bd, grads)
    for g in range(HEADS // 2):
        lanes = slice(g * 128, (g + 1) * 128)
        q2 = qkv[rows, lanes] * jnp.asarray(FACTOR, BF16)
        scores[g] = dot_nt(split_pair(qkv[rows, g * 128 + D : g * 128 + D + 128]), q2)
        dprobs[g] = dot_nt(split_pair(qkv[rows, g * 128 + 2 * D : g * 128 + 2 * D + 128]), datt[rows, lanes])
    for g in range(HEADS // 2):
        for u in range(2):
            h = 2 * g + u
            half = slice(u * PATCH, (u + 1) * PATCH)
            part = jnp.exp(scores[g, half, :] - lse[i, h : h + 1, :])
            dpart = dprobs[g, half, :]
            p_h, dp_h = p_col[h : h + 1, :], dp_col[h : h + 1, :]
            delta = jnp.sum(part * dpart, axis=0, keepdims=True) + p_h * dp_h
            probs[g, half, :] = low(part)
            dscores[g, half, :] = low(part * (dpart - delta))
            cls_row[h : h + 1, :] = p_h * (dp_h - delta)
    ds_col = low(cls_row[...])
    total = lambda v: jnp.sum(jnp.where(mask, v, 0.0), axis=0, keepdims=True)
    joint_cls[pl.ds(i, 1), 0:D] = FACTOR * (total(dot(ds_row, keys)) + jnp.sum(ds_cor * k_w, axis=0, keepdims=True))
    joint_cls[pl.ds(i, 1), D : 2 * D] = FACTOR * total(dot(ds_col, queries)) + jnp.sum(ds_cor * q_w, axis=0, keepdims=True)
    joint_cls[pl.ds(i, 1), 2 * D : 3 * D] = total(dot(low(p_col), grads)) + jnp.sum(
        low(p_cor).astype(F32) * do_w, axis=0, keepdims=True)
    extra[0] = dot_tn(ds_col, k_bd) * FACTOR
    extra[1] = dot_tn(ds_row, q_bd)
    extra[2] = dot_tn(low(p_row), do_bd)
    for g in range(HEADS // 2):
        lanes = slice(g * 128, (g + 1) * 128)
        klanes = slice(g * 128 + D, g * 128 + D + 128)
        vlanes = slice(g * 128 + 2 * D, g * 128 + 2 * D + 128)
        q2 = qkv[rows, lanes] * jnp.asarray(FACTOR, BF16)
        dv = merge_pair(dot(probs[g], datt[rows, lanes])) + extra[2, :, lanes]
        dk = merge_pair(dot(dscores[g], q2)) + extra[1, :, lanes]
        dq = dot_tn(dscores[g], split_pair(qkv[rows, klanes])) * FACTOR + extra[0, :, lanes]
        joint[:, lanes] = low(dq)
        joint[:, klanes] = low(dk)
        joint[:, vlanes] = low(dv)
        sum_q[:, lanes] += fold(dq)
        sum_v[:, lanes] += fold(dv)
    qkv[rows, :] = joint[...]


def to_tokens(src, dst, turn):
    images = dst.shape[0] // (PATCH + 1)
    main = images * PATCH

    def lane_block(l, carry):
        cols = at(l, 128)
        slot = lax.rem(l, 2)
        for i in range(images):
            turn[slot, pl.ds(i, PATCH, stride=images), :] = src[i * PATCH : (i + 1) * PATCH, cols].astype(F32)
        dst[0:main, cols] = turn[slot].astype(BF16)
        return carry

    lax.fori_loop(0, D // 128, lane_block, 0)
    dst[main : main + images, :] = src[main:, :].astype(F32)[0:images].astype(BF16)


def backward_kernel(
    nz, chunks, vec, full_qkv, full_out, full_up, full_down, qkv_h, act_t_h, x_h, att_t_h, mid_h, branch_h, act2_h,
    act2_t_h, up_h, dr_h, dr_t_h, lse_h, lsec_h, parts_h, hid_h, gact_h, column_h,
    result_o, tokens_o, sums_o, small_o, hidden_o,
    buf, core_recv, y_recv, x_recv, z_recv, gmid, grad_mid, up_s, acc, sums_up, vecf, bias_qkv, bias_up, v_part, v_group, v_sum, v_all,
    sems, core_sems, group_sems, all_sems, credit, dsem, wsem, hsem, osem, fsem,
):
    images = lse_h.shape[0]
    n = gmid.shape[0]
    main = images * PATCH
    red = Reduce(nz, buf, core_recv, y_recv, x_recv, z_recv, sems, core_sems, credit)
    s = red.s
    cd0, cu0, cd1, cu1, co, cq0, cq1 = chunks

    def load(k, src, dst):
        copy = pltpu.make_async_copy(src, dst, dsem.at[k])
        copy.start()
        return copy

    def relative(rel):
        return relative_piece(s, rel)

    def target(rel, chunk):
        low, high = lax.rem(rel, 2), lax.div(rel, 2)
        return low * (1 - high) * chunk.rows + (1 - low) * (high * chunk.y_send + (1 - high) * chunk.mine)

    def group_peer(k):
        return {"shard": lax.rem(s + k, 4)}

    def replica_peer(k):
        return {"replica": lax.rem(red.r + k, 2 * nz)}

    def group_copy(k):
        return pltpu.make_async_remote_copy(
            v_part.at[lax.rem(s + k, 4)], v_group.at[k - 1], group_sems.at[0, k - 1], group_sems.at[1, k - 1],
            device_id=group_peer(k), device_id_type=MESH)

    def all_copy(k):
        return pltpu.make_async_remote_copy(
            v_sum, v_all.at[red.r], all_sems.at[0, k - 1], all_sems.at[1, k - 1], device_id=replica_peer(k),
            device_id_type=MESH)

    got_up = load(7, up_h, up_s)

    def ffn(dr, dr_t, act2, act2_t, w_up, w_down, hid, br):
        gots = [load(8, parts_h.at[0], buf.at[pl.ds(0, 2048), :]),
                load(9, parts_h.at[1], buf.at[pl.ds(cd0.y_send, 2048), :]), load(0, act2_h, act2), load(1, dr_h, dr),
                load(2, dr_t_h, dr_t), load(3, act2_t_h, act2_t), load(10, gact_h, gmid), load(11, column_h, sums_up)]

        def fetch(j, slot):
            piece, t = relative(3 - lax.rem(j, 4)), lax.div(j, 4)
            return (
                pltpu.make_async_copy(full_up.at[piece, :, at(t, TILE)], w_up.at[slot], wsem.at[0, slot]),
                pltpu.make_async_copy(full_down.at[piece, at(t, TILE), :], w_down.at[slot], wsem.at[1, slot]),
            )

        def keep(j, slot):
            return pltpu.make_async_copy(hid.at[slot], hidden_o.at[j - 2], hsem.at[slot])

        barrier = pltpu.get_barrier_semaphore()
        partners = [group_peer(k) for k in range(1, 4)] + [replica_peer(k) for k in range(1, 2 * nz)]
        for to in partners:
            pl.semaphore_signal(barrier, inc=1, device_id=to, device_id_type=MESH)
        pl.semaphore_wait(barrier, len(partners))
        unpack_vectors(vec, vecf, bias_qkv)
        unpack_bias_up(vec, bias_up)
        acc[...] = jnp.zeros_like(acc)
        gots[0].wait()
        red.core_copy(0, 2048).start()
        for copy in fetch(2, 0):
            copy.start()
        for copy in gots[1:]:
            copy.wait()

        def tile(j, carry):
            slot = lax.rem(j, 2)
            rel, t = 3 - lax.rem(j, 4), lax.div(j, 4)
            piece = relative(rel)
            low, high = lax.rem(rel, 2), lax.div(rel, 2)
            place_at = pl.multiple_of(
                (1 - low) * (high * (cd0.y_send + t * (cd1.y_send - cd0.y_send)) + (1 - high) * (cd0.mine + t * 2048)), 16)
            for copy in fetch(j, slot):
                copy.wait()

            @pl.when(j < 7)
            def _():
                for copy in fetch(j + 1, 1 - slot):
                    copy.start()

            @pl.when(j >= 4)
            def _():
                keep(j - 2, slot).wait()

            for k in (2, 4, 6):
                @pl.when(j == k)
                def _(k=k):
                    red.core_copy(k // 2 - 1, 2048).wait_send()

            def put(half, value):
                buf[pl.ds(pl.multiple_of(place_at + half * D, 16), D), :] = value

            sums_up[pl.ds(2 * piece + t, 1), :] = ffn_tile(
                act2, dr, dr_t, act2_t, lambda: w_up[slot], lambda: w_down[slot], bias_up[pl.ds(2 * piece + t, 1), :],
                hid.at[slot], br, gmid, False, lambda: keep(j, slot).start(), put)

            def y_part(turn, chunk):
                red.core_copy(turn, 2048).wait_recv()
                for k, c in enumerate(chunk):
                    red.add_core(turn, k * 1024, c.y_send, c.rows)
                    red.y_copy(c).start()

            def own_part(turn, chunk):
                red.core_copy(turn, 2048).wait_recv()
                red.add_core(turn, 0, chunk[0].mine, 2048)

            steps = {
                2: [lambda: y_part(0, (cd0, cu0)), lambda: red.core_copy(1, 2048).start()],
                3: [lambda: own_part(1, (cd0, cu0))],
                4: [lambda: red.core_copy(2, 2048).start()],
                5: [lambda: y_part(2, (cd1, cu1)), lambda: red.on_y(cd0)],
                6: [lambda: red.core_copy(3, 2048).start(), lambda: red.on_x(cd0)],
                7: [lambda: own_part(3, (cd1, cu1)), lambda: red.on_y(cu0)],
            }
            for k, todo in steps.items():
                @pl.when(j == k)
                def _(todo=todo):
                    for step in todo:
                        step()
            return carry

        lax.fori_loop(2, 8, tile, 0)
        pl.semaphore_signal(credit, inc=1, device_id={"shard": red.across}, device_id_type=MESH)
        for j in (6, 7):
            keep(j, j % 2).wait()
        red.core_copy(3, 2048).wait_send()

    v = pltpu.VMEM
    pl.run_scoped(ffn, v((n, D), BF16), v((D, n), BF16), v((n, D), BF16), v((D, n), BF16), v((2, D, TILE), BF16),
                  v((2, TILE, D), BF16), v((2, n, TILE), BF16), v((n, TILE), BF16))
    got_up.wait()

    def spread(out, chunk, tile_rows):
        for p in range(4):
            low = lax.rem(lax.rem(s, 2) + p % 2, 2)
            high = lax.rem(lax.div(s, 2) + p // 2, 2)
            start = pl.multiple_of(target(low + 2 * high, chunk) + tile_rows, 16)
            buf[pl.ds(start, 256), :] = out[p * 256 : (p + 1) * 256].astype(BF16)

    def on_core(turn, chunk):
        red.core_copy(turn, 2 * chunk.rows).wait_recv()
        red.add_core(turn, 0, chunk.y_send, chunk.rows)
        red.y_copy(chunk).start()
        red.add_core(turn, chunk.rows, chunk.mine, chunk.rows)

    def attention(
        qkv, datt, brr, lse, lsec, scores, dprobs, probs, dscores, cls_row, qkv_cls, datt_cls, joint_cls, joint, extra
    ):
        got_qkv, got_lse, got_lsec = load(0, qkv_h, qkv), load(1, lse_h, lse), load(2, lsec_h, lsec)

        def middle(mid, branch, att_t, w_out):
            got_mid, got_branch = load(3, mid_h, mid), load(4, branch_h, branch)
            got_att, got_out = load(5, att_t_h, att_t), load(6, full_out, w_out)
            red.on_z(cd0)
            got_mid.wait()
            got_branch.wait()

            def norm_rows(rows):
                m = mid[rows, :]
                c = m - jnp.mean(m, axis=-1, keepdims=True)
                inv = lax.rsqrt(jnp.mean(c * c, axis=-1, keepdims=True) + 1e-06)
                hat = c * inv
                g = gmid[rows, :]
                acc[4] += fold(g * hat)
                acc[5] += fold(g)
                sc = g * vecf[4:5, :]
                back = inv * (sc - jnp.mean(sc, axis=-1, keepdims=True)
                              - hat * jnp.mean(sc * hat, axis=-1, keepdims=True))
                gm = up_s[rows, :].astype(F32) + back
                grad_mid[rows, :] = gm
                acc[3] += fold(gm * branch[rows, :].astype(F32))
                gb = gm * vecf[3:4, :]
                acc[2] += fold(gb)
                brr[rows, :] = gb.astype(BF16)

            rows_loop(n, 16, norm_rows)
            got_att.wait()
            for q in range(2):
                spread(dot(att_t[...], brr[:, q * TILE : (q + 1) * TILE]), co, q * 256)
            red.core_copy(4, 2 * co.rows).start()
            got_out.wait()
            for q in range(2):
                datt[:, q * TILE : (q + 1) * TILE] = dot_nt(brr[...], w_out[q * TILE : (q + 1) * TILE, :]).astype(BF16)
            red.on_x(cu0)

        pl.run_scoped(middle, v((n, D), F32), v((n, D), BF16), v((D, n), BF16), v((D, D), BF16))
        got_qkv.wait()
        got_lse.wait()
        got_lsec.wait()
        qkv_cls[...] = qkv[main:, :].astype(F32)
        datt_cls[...] = datt[main:, :].astype(F32)
        joint_cls[...] = jnp.zeros_like(joint_cls)
        pl.semaphore_wait(credit, 1)
        on_core(4, co)
        plan = {0: [lambda: red.on_y(cd1), lambda: red.on_back(cd0)], 3: [lambda: red.on_z(cu0)], 5: [lambda: red.on_x(cd1)],
                6: [lambda: red.on_y(cu1), lambda: red.on_back(cu0)]}

        def image(i, carry):
            for k, steps in plan.items():
                @pl.when(i == k)
                def _(steps=steps):
                    for step in steps:
                        step()

            attend_back(i, qkv, qkv_cls, datt, datt_cls, lse, lsec, scores, dprobs, probs, dscores, cls_row, joint_cls,
                        joint, extra, acc.at[8], acc.at[9])
            return carry

        lax.fori_loop(0, images, image, 0)
        qkv[main:, :] = joint_cls[...].astype(BF16)
        acc[8] += fold(joint_cls[:, 0:D])
        acc[9] += fold(joint_cls[:, 2 * D : 3 * D])

        def tail(act_t, w_qkv, turn, flat):
            x_s, gact, new = brr, gmid, datt
            got_act, got_x = load(3, act_t_h, act_t), load(4, x_h, x_s)

            def fetch(j):
                return pltpu.make_async_copy(full_qkv.at[pl.ds(j * 256, 256), :], w_qkv.at[j % 2], wsem.at[0, j % 2])

            fetch(0).start()
            fetch(1).start()
            got_act.wait()
            red.on_z(cd1)
            red.core_copy(4, 2 * co.rows).wait_send()
            for q in range(4):
                spread(dot(act_t[...], qkv[:, q * TILE : (q + 1) * TILE]), cq0, q * 256)
            red.core_copy(5, 2 * cq0.rows).start()
            red.on_y(co)
            red.on_x(cu1)

            def input_grad(j):
                fetch(j).wait()
                gact[:, j * 256 : (j + 1) * 256] = dot_nt(qkv[...], w_qkv[j % 2])
                if j < 2:
                    fetch(j + 2).start()

            input_grad(0)
            red.core_copy(5, 2 * cq0.rows).wait_send()
            for q in range(2):
                spread(dot(act_t[...], qkv[:, (q + 4) * TILE : (q + 5) * TILE]), cq1, q * 256)
            on_core(5, cq0)
            red.core_copy(6, 2 * cq1.rows).start()
            red.on_back(cd1)
            red.on_x(co)
            input_grad(1)
            input_grad(2)
            on_core(6, cq1)
            input_grad(3)
            red.on_z(cu1)
            got_x.wait()

            def norm_rows(rows):
                m = x_s[rows, :].astype(F32)
                c = m - jnp.mean(m, axis=-1, keepdims=True)
                inv = lax.rsqrt(jnp.mean(c * c, axis=-1, keepdims=True) + 1e-06)
                hat = c * inv
                g = gact[rows, :]
                acc[0] += fold(g * hat)
                acc[1] += fold(g)
                sc = g * vecf[0:1, :]
                back = inv * (sc - jnp.mean(sc, axis=-1, keepdims=True)
                              - hat * jnp.mean(sc * hat, axis=-1, keepdims=True))
                new[rows, :] = (grad_mid[rows, :] + back).astype(BF16)

            rows_loop(n, 16, norm_rows)
            red.on_z(co)
            to_tokens(new, flat, turn)
            copy = pltpu.make_async_copy(flat, tokens_o, osem.at[0])
            copy.start()
            red.on_back(cu1)
            red.on_back(co)
            copy.wait()

        pl.run_scoped(tail, v((D, n), BF16), v((2, 256, 3 * D), BF16),
                      v((2, main, 128), F32), v((main + images, D), BF16))

    pl.run_scoped(attention, v((n, 3 * D), BF16), v((n, D), BF16), v((n, D), BF16), v((images, HEADS, PATCH), F32),
                  v((images, HEADS, PATCH), F32), v((8, 256, PATCH), F32), v((8, 256, PATCH), F32),
                  v((8, 256, PATCH), BF16), v((8, 256, PATCH), BF16), v((HEADS, PATCH), F32), v((CLS, 3 * D), F32),
                  v((CLS, D), F32), v((CLS, 3 * D), F32), v((PATCH, 3 * D), BF16), v((3, PATCH, D), F32))

    def outcome(mid, hid, w_down, turn, flat, res):
        got_mid = load(3, mid_h, mid)

        def fetch(pair):
            copies = []
            for k in range(2):
                j = 2 * pair + k
                slot = pair % 2
                piece, t = relative(3 - j % 4), j // 4
                src = hid_h.at[k] if pair == 0 else hidden_o.at[j - 2]
                copies.append(pltpu.make_async_copy(src, hid.at[slot, :, pl.ds(k * TILE, TILE)], wsem.at[0, 2 * slot + k]))
                copies.append(pltpu.make_async_copy(full_down.at[piece, pl.ds(t * TILE, TILE), :],
                                                    w_down.at[slot, pl.ds(k * TILE, TILE), :], wsem.at[1, 2 * slot + k]))
            return copies

        for copy in fetch(0):
            copy.start()
        steps = {0: [lambda: red.on_y(cq0)], 2: [lambda: red.on_y(cq1), lambda: red.on_x(cq0)]}
        for pair in range(4):
            if pair < 3:
                for copy in fetch(pair + 1):
                    copy.start()
            for copy in fetch(pair):
                copy.wait()
            for q in range(2):
                cols = slice(q * TILE, (q + 1) * TILE)
                out = dot(hid[pair % 2], w_down[pair % 2, :, cols])
                if pair:
                    gmid[:, cols] += out
                else:
                    gmid[:, cols] = out
            for step in steps.get(pair, []):
                step()
        got_mid.wait()

        def rows_of(rows):
            projected = gmid[rows, :] + vecf[6:7, :]
            upstream = up_s[rows, :].astype(F32)
            acc[6] += fold(upstream * vecf[7:8, :])
            acc[7] += fold(upstream * projected)
            res[rows, :] = (mid[rows, :] + vecf[7:8, :] * projected).astype(BF16)

        rows_loop(n, 16, rows_of)
        for p in range(4):
            for k in range(8):
                v_part[p, k : k + 1, :] = jnp.sum(acc[k, :, p * 256 : (p + 1) * 256], axis=0, keepdims=True)
            joint = acc.at[8 + p // 2]
            for k in range(2):
                start = (p % 2) * TILE + k * 256
                v_part[p, 8 + k : 9 + k, :] = jnp.sum(joint[:, start : start + 256], axis=0, keepdims=True)
            for k in range(4):
                v_part[p, 10 + k : 11 + k, :] = sums_up[2 * p + k // 2 : 2 * p + k // 2 + 1, (k % 2) * 256 : (k % 2 + 1) * 256]
            v_part[p, 14:16, :] = jnp.zeros((2, 256), F32)
        for k in range(1, 4):
            group_copy(k).start()
        red.on_x(cq1)
        red.on_z(cq0)
        total = v_part[s]
        for k in range(1, 4):
            group_copy(k).wait_recv()
            total = total + v_group[k - 1]
        v_sum[...] = total
        v_all[red.r] = total
        for k in range(1, 2 * nz):
            all_copy(k).start()
        to_tokens(res, flat, turn)
        copy = pltpu.make_async_copy(flat, result_o, osem.at[0])
        copy.start()
        red.on_z(cq1)
        red.on_back(cq0)
        for k in range(1, 2 * nz):
            all_copy(k).wait_recv()
        total = v_all[0]
        for k in range(1, 2 * nz):
            total = total + v_all[k]
        v_group[0] = total
        small = pltpu.make_async_copy(v_group.at[0], small_o, osem.at[1])
        small.start()
        red.on_back(cq1)
        copy.wait()
        small.wait()

    pl.run_scoped(outcome, v((n, D), F32), v((2, n, D), BF16), v((2, D, D), BF16), v((2, main, 128), F32),
                  v((main + images, D), BF16), v((n, D), BF16))
    copies = []
    for c in chunks:
        red.finish(c)
        half = c.rows // 2
        for k, (src, first, where) in enumerate(((x_recv, c.x_recv, red.x), (buf, c.far, 1 - red.x))):
            copy = pltpu.make_async_copy(
                src.at[pl.ds(first, half), :],
                sums_o.at[pl.ds(pl.multiple_of(c.mine - cd0.mine + where * half, 16), half), :], fsem.at[2 * c.index + k])
            copy.start()
            copies.append(copy)
    red.core_copy(6, 2 * cq1.rows).wait_send()
    for k in range(1, 4):
        group_copy(k).wait_send()
    for k in range(1, 2 * nz):
        all_copy(k).wait_send()
    for c in chunks:
        red.drain(c)
    for copy in copies:
        copy.wait()


def convert_kernel(
    chunks, sums, small, result, tokens, result_o, tokens_o, g1_o, s1_o, qkv_o, bqv_o, out_o, bo_o, l1_o, g2_o, s2_o, up_o, bup_o, down_o, bd_o, l2_o,
    low, qkv, out, up, down, moved, dsem, osem, msem,
):
    base = chunks[0].mine
    moves = [pltpu.make_async_copy(src, moved.at[k], msem.at[0, k]) for k, src in enumerate((result, tokens))]
    stores = [pltpu.make_async_copy(moved.at[k], dst, msem.at[1, k]) for k, dst in enumerate((result_o, tokens_o))]
    gots = []
    for c in chunks:
        rows = pl.ds(c.mine - base, c.rows)
        gots.append(pltpu.make_async_copy(sums.at[rows, :], low.at[rows, :], dsem.at[c.index]))
        gots[-1].start()
    for copy in moves:
        copy.start()
    outs = []

    def send_out(src, dst):
        copy = pltpu.make_async_copy(src, dst, osem.at[len(outs)])
        copy.start()
        outs.append(copy)

    def block(c, first, count):
        return low[c.mine - base + first : c.mine - base + first + count, :]

    for t in range(2):
        gots[2 * t].wait()
        for k in range(8):
            down[t * TILE : (t + 1) * TILE, k * 128 : (k + 1) * 128] = block(chunks[2 * t], k * 128, 128).T.astype(F32)
        send_out(down.at[pl.ds(t * TILE, TILE), :], down_o.at[pl.ds(t * TILE, TILE), :])
        gots[2 * t + 1].wait()
        up[t] = block(chunks[2 * t + 1], 0, D).astype(F32)
        send_out(up.at[t], up_o.at[:, pl.ds(t * TILE, TILE)])
    for k in range(2):
        moves[k].wait()
        stores[k].start()
    gots[4].wait()
    for k in range(2):
        out[:, k * TILE : (k + 1) * TILE] = block(chunks[4], k * 256, 256).astype(F32)
    send_out(out, out_o)
    gots[5].wait()
    gots[6].wait()
    for k in range(6):
        qkv[:, k * TILE : (k + 1) * TILE] = block(chunks[5], k * 256, 256).astype(F32)
    send_out(qkv, qkv_o)
    vectors = (g1_o, s1_o, bo_o, l1_o, g2_o, s2_o, bd_o, l2_o, bqv_o, bup_o)
    row = 0
    for v in vectors:
        for k in range(v.shape[0] // 256):
            v[pl.ds(k * 256, 256)] = small[row : row + 1, :].reshape(256)
            row += 1
    for copy in outs + stores:
        copy.wait()


def convert(chunks, sums, small, result, tokens):
    one = lambda k: jax.ShapeDtypeStruct((k,), F32)
    outs = (
        low_shape(*result.shape), low_shape(*tokens.shape), one(256), one(256), wide_shape(256, 3 * D), one(512), wide_shape(256, D), one(256), one(256), one(256), one(256),
        wide_shape(D, D), one(1024), wide_shape(D, D), one(256), one(256),
    )
    v = pltpu.VMEM
    return pl.pallas_call(
        functools.partial(convert_kernel, chunks),
        out_shape=outs,
        in_specs=[ANY, VMEM, ANY, ANY],
        out_specs=[VMEM if len(o.shape) == 1 else ANY for o in outs],
        scratch_shapes=[v(sums.shape, BF16), v((256, 3 * D), F32), v((256, D), F32), v((2, D, TILE), F32),
                        v((D, D), F32), v((2,) + result.shape, BF16), pltpu.SemaphoreType.DMA((8,)),
                        pltpu.SemaphoreType.DMA((6,)), pltpu.SemaphoreType.DMA((2, 2))],
        compiler_params=pltpu.CompilerParams(vmem_limit_bytes=LIMIT),
        name="gradients_to_float32",
    )(sums, small, result, tokens)


def low_shape(*shape):
    return jax.ShapeDtypeStruct(shape, BF16)


def wide_shape(*shape):
    return jax.ShapeDtypeStruct(shape, F32)


ANY = pl.BlockSpec(memory_space=pl.ANY)
VMEM = pl.BlockSpec(memory_space=pltpu.VMEM)
LIMIT = 62 * 2**20


def forward(flat, cot, vectors, w_qkv, w_out, w_up, w_down):
    images = flat.shape[0] // (PATCH + 1)
    n = images * PATCH + CLS
    v = pltpu.VMEM
    outs = (
        low_shape(D, 3 * D), low_shape(D, D), low_shape(4, D, D), low_shape(4, D, D), low_shape(4, 16, 256),
        low_shape(n, 3 * D), low_shape(D, n), low_shape(n, D), low_shape(D, n), wide_shape(n, D), low_shape(n, D),
        low_shape(n, D), low_shape(D, n), low_shape(n, D), low_shape(n, D), low_shape(D, n),
        wide_shape(images, HEADS, PATCH), wide_shape(images, HEADS, PATCH),
        low_shape(2, 2048, TILE), low_shape(2, n, TILE), wide_shape(n, D), wide_shape(8, TILE),
    )
    return pl.pallas_call(
        gather_kernel,
        out_shape=outs,
        in_specs=[VMEM] * 12 + [ANY] * 4,
        out_specs=[ANY] * len(outs),
        scratch_shapes=[
            v((D, 3 * D), BF16), v((D, D), BF16), v((4, D, D), BF16), v((4, D, D), BF16),
            v((n, D), BF16), v((n, 3 * D), BF16), v((n, D), BF16), v((n, D), BF16), v((n, D), F32), v((n, D), BF16),
            v((n, D), BF16), v((D, n), BF16), v((D, n), BF16),
            v((images, HEADS, PATCH), F32), v((images, HEADS, PATCH), F32),
            v((8, 256, PATCH), F32), v((8, 256, PATCH), BF16), v((PATCH, D), F32), v((HEADS, PATCH), F32),
            v((CLS, D), F32), v((CLS, 3 * D), F32), v((2, images * PATCH, 128), F32), v((16, 256), F32),
            v((16, 256), BF16), v((4, 16, 256), BF16), v((16, D), F32), v((8, 3 * D), F32), v((8, TILE), F32),
            v((8, TILE), F32), pltpu.SemaphoreType.DMA((2, 6, 11)), pltpu.SemaphoreType.DMA((6,)), pltpu.SemaphoreType.DMA((2, 3)),
            pltpu.SemaphoreType.DMA((30,)),
        ],
        compiler_params=pltpu.CompilerParams(collective_id=0, has_side_effects=True, vmem_limit_bytes=LIMIT),
        cost_estimate=pl.CostEstimate(flops=18 * 2**30, bytes_accessed=64 * 2**20, transcendentals=3 * 2**20),
        name="gather_and_attention",
    )(flat, cot, *vectors, w_qkv, w_out, w_up, w_down)


def backward(nz, images, vec, *arrays):
    n = images * PATCH + CLS
    tokens = images * (PATCH + 1)
    v = pltpu.VMEM
    chunks, sizes = chunk_layout(nz)
    outs = (low_shape(tokens, D), low_shape(tokens, D), low_shape(sizes["total"], TILE), wide_shape(16, 256),
            low_shape(6, n, TILE))
    return pl.pallas_call(
        functools.partial(backward_kernel, nz, chunks),
        out_shape=outs,
        in_specs=[VMEM] + [ANY] * len(arrays),
        out_specs=[ANY] * len(outs),
        scratch_shapes=[
            v((sizes["buf"], TILE), BF16), v((2, 2048, TILE), BF16), v((sizes["y_recv"], TILE), BF16),
            v((sizes["x_recv"], TILE), BF16), v((nz - 1, sizes["z_recv"], TILE), BF16), v((n, D), F32), v((n, D), F32), v((n, D), BF16),
            v((10, 8, D), F32), v((8, TILE), F32), v((16, D), F32), v((8, 3 * D), F32), v((8, TILE), F32),
            v((4, 16, 256), F32), v((3, 16, 256), F32), v((16, 256), F32), v((2 * nz, 16, 256), F32),
            pltpu.SemaphoreType.DMA((2, len(chunks), 3 * nz)), pltpu.SemaphoreType.DMA((2, 7)),
            pltpu.SemaphoreType.DMA((2, 3)), pltpu.SemaphoreType.DMA((2, 2 * nz - 1)),
            pltpu.SemaphoreType.REGULAR, pltpu.SemaphoreType.DMA((12,)), pltpu.SemaphoreType.DMA((2, 4)),
            pltpu.SemaphoreType.DMA((2,)), pltpu.SemaphoreType.DMA((2,)), pltpu.SemaphoreType.DMA((2 * len(chunks),)),
        ],
        compiler_params=pltpu.CompilerParams(collective_id=1, has_side_effects=True, vmem_limit_bytes=LIMIT),
        cost_estimate=pl.CostEstimate(flops=66 * 2**30, bytes_accessed=128 * 2**20, transcendentals=8 * 2**20),
        name="layer_backward",
    )(vec, *arrays), chunks


def on_device(
    tokens, norm1_gain, norm1_shift, w_qkv, bias_qv, w_out, bias_out, scale_one, norm2_gain, norm2_shift, w_up, bias_up,
    w_down, bias_down, scale_two, cotangent,
):
    images, length, _ = tokens.shape
    nz = lax.axis_size("replica") // 2
    flatten = lambda a: jnp.transpose(a, (1, 0, 2)).reshape(images * length, D)
    restore = lambda a: jnp.transpose(a.reshape(length, images, D), (1, 0, 2))
    vectors = (norm1_gain, norm1_shift, bias_out, scale_one, norm2_gain, norm2_shift, bias_down, scale_two, bias_qv, bias_up)
    full_qkv, full_out, full_up, full_down, vec, *kept = forward(
        flatten(tokens), flatten(cotangent), vectors, w_qkv, w_out, w_up, w_down)
    (result, grad_tokens, sums, small, _), chunks = backward(nz, images, vec, full_qkv, full_out, full_up, full_down, *kept)
    result, grad_tokens, *gradients = convert(chunks, sums, small, result, grad_tokens)
    return (restore(result), restore(grad_tokens)) + tuple(gradients)


def solution(mesh):
    placed = (
        P(("shard", "replica"), None, None),
        P("shard"),
        P("shard"),
        P("shard", None),
        P("shard"),
        P("shard", None),
        P("shard"),
        P("shard"),
        P("shard"),
        P("shard"),
        P(None, "shard"),
        P("shard"),
        P("shard", None),
        P("shard"),
        P("shard"),
        P(("shard", "replica"), None, None),
    )
    return jax.shard_map(
        on_device,
        mesh=mesh,
        in_specs=placed,
        out_specs=(
            P(("shard", "replica"), None, None),
            P(("shard", "replica"), None, None),
            P("shard"),
            P("shard"),
            P("shard", None),
            P("shard"),
            P("shard", None),
            P("shard"),
            P("shard"),
            P("shard"),
            P("shard"),
            P(None, "shard"),
            P("shard"),
            P("shard", None),
            P("shard"),
            P("shard"),
        ),
        check_vma=False,
    )
```

```python
import functools

import jax
import jax.numpy as jnp
from jax import lax
from jax.experimental import pallas as pl
from jax.experimental.pallas import tpu as pltpu
from jax.sharding import PartitionSpec as P

F32 = jnp.float32
BF16 = jnp.bfloat16
D = 1024
FF = 4096
HEADS = 16
PATCH = 128
CLS = 16
TILE = 512
FACTOR = 0.125
MESH = pl.DeviceIdType.MESH


def dot(a, b):
    return jnp.dot(a, b, preferred_element_type=F32)


def dot_nt(a, b):
    return lax.dot_general(a, b, (((1,), (1,)), ((), ())), preferred_element_type=F32)


def dot_tn(a, b):
    return lax.dot_general(a, b, (((0,), (0,)), ((), ())), preferred_element_type=F32)


def at(index, size):
    return pl.ds(pl.multiple_of(index * size, size), size)


def head_mask():
    lane = lax.shift_right_logical(lax.broadcasted_iota(jnp.int32, (HEADS, D), 1), 6)
    return lane == lax.broadcasted_iota(jnp.int32, (HEADS, D), 0)


def split_pair(v):
    low = lax.broadcasted_iota(jnp.int32, v.shape, 1) < 64
    zero = jnp.zeros_like(v)
    return jnp.concatenate([jnp.where(low, v, zero), jnp.where(low, zero, v)], 0)


def merge_pair(v):
    n = v.shape[0] // 2
    low = lax.broadcasted_iota(jnp.int32, (n, v.shape[1]), 1) < 64
    return jnp.where(low, v[:n], v[n:])


def place():
    s = lax.axis_index("shard")
    r = lax.axis_index("replica")
    x = lax.rem(r, 2)
    z = lax.div(r, 2)
    return s, r, x, z


def peers(s, r):
    sib = s + 1 - 2 * lax.rem(s, 2)
    across = lax.rem(s + 2, 4)
    side = r + 1 - 2 * lax.rem(r, 2)
    return sib, across, side


def rows_loop(n, step, body):
    lax.fori_loop(0, n // step, lambda k, c: (body(at(k, step)), c)[1], 0, unroll=5)


def unpack_vectors(vec, vecf, bias_qkv):
    for v in range(8):
        for s in range(4):
            vecf[v : v + 1, s * 256 : (s + 1) * 256] = vec[s, v : v + 1, :].astype(F32)
    bias_qkv[...] = jnp.zeros_like(bias_qkv)
    for s in range(4):
        for t in range(2):
            col = (s * 2 + t) * 256 + (D if s >= 2 else 0)
            bias_qkv[0:1, col : col + 256] = vec[s, 8 + t : 9 + t, :].astype(F32)


def layer_norm(v, gain, shift):
    c = v - jnp.mean(v, axis=-1, keepdims=True)
    inv = lax.rsqrt(jnp.mean(c * c, axis=-1, keepdims=True) + 1e-06)
    return c * inv * gain + shift


def to_images(src, dst, turn):
    images = (src.shape[0]) // (PATCH + 1)
    main = images * PATCH

    def lane_block(l, carry):
        cols = at(l, 128)
        slot = lax.rem(l, 2)
        turn[slot] = src[0:main, cols].astype(F32)
        for i in range(images):
            dst[i * PATCH : (i + 1) * PATCH, cols] = turn[slot, pl.ds(i, PATCH, stride=images), :].astype(BF16)
        return carry

    lax.fori_loop(0, D // 128, lane_block, 0)
    last = src[main : main + images, :].astype(F32)
    dst[main:, :] = jnp.concatenate([last, jnp.zeros((CLS - images, D), F32)], 0).astype(BF16)


def pack_vectors(vectors, dst):
    row = 0
    for v in vectors:
        count = v.shape[0] // 256
        wide = v[...].astype(F32)
        for k in range(count):
            dst[row : row + 1, :] = wide[k * 256 : (k + 1) * 256].reshape(1, 256)
            row += 1


def attend(i, qkv, qkv_cls, scores, probs, mix, probs_cls, att, att_cls, lse, lse_cls):
    rows = at(i, PATCH)
    mask = head_mask()
    own = qkv_cls[pl.ds(i, 1), :]
    q_c, k_c, v_c = own[:, :D] * FACTOR, own[:, D : 2 * D], own[:, 2 * D :]
    q_bd = jnp.where(mask, q_c, 0.0)
    k_bd = jnp.where(mask, k_c, 0.0).astype(BF16)
    v_bd = jnp.where(mask, v_c, 0.0).astype(BF16)
    to_cls = dot_nt(k_bd, qkv[rows, 0:D]) * FACTOR
    of_cls = dot_nt(q_bd.astype(BF16), qkv[rows, D : 2 * D])
    corner = jnp.sum(q_bd * k_c, axis=1, keepdims=True)
    top = jnp.maximum(jnp.max(of_cls, axis=1, keepdims=True), corner)
    e_row = jnp.exp(of_cls - top)
    e_cor = jnp.exp(corner - top)
    total = jnp.sum(e_row, axis=1, keepdims=True) + e_cor
    inv = 1.0 / total
    row = dot((e_row * inv).astype(BF16), qkv[rows, 2 * D : 3 * D])
    row = row + (e_cor * inv).astype(BF16).astype(F32) * v_c
    att_cls[pl.ds(i, 1), :] = jnp.sum(jnp.where(mask, row, 0.0), axis=0, keepdims=True)
    lse_cls[i] = jnp.broadcast_to(top + jnp.log(total), (HEADS, PATCH))
    for g in range(HEADS // 2):
        q2 = qkv[rows, g * 128 : g * 128 + 128] * jnp.asarray(FACTOR, BF16)
        scores[g] = dot_nt(split_pair(qkv[rows, g * 128 + D : g * 128 + D + 128]), q2)
    for g in range(HEADS // 2):
        for u in range(2):
            h = 2 * g + u
            part = scores[g, u * PATCH : (u + 1) * PATCH, :]
            extra = to_cls[h : h + 1, :]
            top = jnp.maximum(jnp.max(part, axis=0, keepdims=True), extra)
            e_part = jnp.exp(part - top)
            e_extra = jnp.exp(extra - top)
            total = jnp.sum(e_part, axis=0, keepdims=True) + e_extra
            inv = 1.0 / total
            probs[g, u * PATCH : (u + 1) * PATCH, :] = (e_part * inv).astype(BF16)
            probs_cls[h : h + 1, :] = e_extra * inv
            lse[i, h : h + 1, :] = top + jnp.log(total)
    for g in range(HEADS // 2):
        v2 = split_pair(qkv[rows, g * 128 + 2 * D : g * 128 + 2 * D + 128])
        mix[:, g * 128 : g * 128 + 128] = dot_tn(probs[g], v2)
    att[rows, :] = (mix[...] + dot_tn(probs_cls[...].astype(BF16), v_bd)).astype(BF16)


class Gather:
    KINDS = ("own", "far", "x1", "z1", "x2", "z2", "p0", "p1", "p2", "p3", "p4")

    def __init__(self, number, rows, src, dst, sems, local):
        s, r, x, z = place()
        sib, across, side = peers(s, r)
        self.number, self.sems = number, sems
        near = lax.rem(z, 2)
        level = {"replica": (z + 1 - 2 * near) * 2 + x}
        side, sib = {"replica": side}, {"shard": sib}
        size = rows // 4
        half = size // 2

        def start(zz, xx):
            return pl.multiple_of((2 * zz + xx) * size, 16)

        def same(first, count, to):
            ref = dst(across, pl.multiple_of(first, 16), count)
            return ref, ref, to

        mine, by_x, by_z, by_both = start(near, x), start(near, 1 - x), start(1 - near, x), start(1 - near, 1 - x)
        self.parts = {
            "own": (dst(s, 0, rows), dst(s, 0, rows), sib),
            "far": (dst(s, mine, size), dst(s, mine, size), {"shard": across}),
            "x1": same(mine, size, side),
            "z1": same(mine, size, level),
            "x2": same(by_z, half, side),
            "z2": same(by_x + half, half, level),
            "p0": same(mine, size, sib),
            "p1": same(by_x, size, sib),
            "p2": same(by_z, size, sib),
            "p3": same(by_both, half, sib),
            "p4": same(by_both + half, half, sib),
        }
        self.local = pltpu.make_async_copy(src(0, rows), dst(s, 0, rows), local.at[number])

    def copy(self, kind):
        a, b, to = self.parts[kind]
        k = self.KINDS.index(kind)
        return pltpu.make_async_remote_copy(
            a, b, self.sems.at[0, self.number, k], self.sems.at[1, self.number, k], device_id=to, device_id_type=MESH
        )

    def load(self):
        self.local.start()

    def begin(self):
        self.local.wait()
        self.copy("far").start()

    def share(self):
        self.copy("own").start()

    def on_far(self):
        self.copy("far").wait_recv()
        for kind in ("x1", "z1", "p0"):
            self.copy(kind).start()

    def on_near(self):
        self.copy("x1").wait_recv()
        self.copy("z2").start()
        self.copy("p1").start()
        self.copy("z1").wait_recv()
        self.copy("x2").start()
        self.copy("p2").start()

    def on_last(self):
        self.copy("x2").wait_recv()
        self.copy("p3").start()
        self.copy("z2").wait_recv()
        self.copy("p4").start()

    def ready(self):
        for kind in ("own", "p0", "p1", "p2", "p3", "p4"):
            self.copy(kind).wait_recv()

    def drain(self):
        for kind in self.KINDS:
            self.copy(kind).wait_send()


def relative_piece(s, rel):
    low, high = lax.rem(rel, 2), lax.div(rel, 2)
    return s + low * (1 - 2 * lax.rem(s, 2)) + high * (2 - 4 * lax.div(s, 2))


def unpack_bias_up(vec, bias_up):
    for p in range(4):
        for t in range(2):
            for k in range(2):
                row = 10 + 2 * t + k
                bias_up[2 * p + t : 2 * p + t + 1, k * 256 : (k + 1) * 256] = vec[p, row : row + 1, :].astype(F32)


def ffn_tile(act2, dr, dr_t, act2_t, w_up, w_down, bias, hid, br, gmid, fresh, on_hidden, put):
    n = act2.shape[0]
    cut = 16 * (n // 32)
    first, second = slice(0, cut), slice(cut, n)

    def both(rows, before, grad):
        hidden, step = gelu_both(before)
        hid[rows, :] = hidden.astype(BF16)
        grad = grad * step
        br[rows, :] = grad.astype(BF16)
        return jnp.sum(grad, axis=0, keepdims=True)

    def back(rows):
        out = dot_nt(br[rows, :], w_up())
        if fresh:
            gmid[rows, :] = out
        else:
            gmid[rows, :] += out

    before0 = dot(act2[first, :], w_up()) + bias
    grad0 = dot_nt(dr[first, :], w_down())
    before1 = dot(act2[second, :], w_up()) + bias
    column = both(first, before0, grad0)
    grad1 = dot_nt(dr[second, :], w_down())
    back(first)
    column = column + both(second, before1, grad1)
    back(second)
    on_hidden()
    put(0, dot(dr_t[...], hid[...]).astype(BF16))
    put(1, dot(act2_t[...], br[...]).astype(BF16))
    return column


def gather_kernel(
    tokens, cot, v0, v1, v2, v3, v4, v5, v6, v7, v8, v9, w_qkv, w_out, w_up, w_down,
    qkv_w_o, out_w_o, up_w_o, down_w_o, vec_all, qkv_o, act_t_o, x_o, att_t_o, mid_o, branch_o, act2_o, act2_t_o, up_o,
    dr_o, dr_t_o, lse_o, lsec_o, parts_o, hid_o, gact_o, column_o,
    full_qkv, full_out, full_up, full_down, x_s, qkv, act, att, mid, branch, act2, turned_a, turned_b, lse, lsec,
    scores, probs, mix, probs_cls, cls, qkv_cls, turn, vec32, vec_own_s, vec, vecf, bias_qkv,
    bias_up, column,
    sems, local, vsem, osem,
):
    s, r, x, z = place()
    sib, across, side = peers(s, r)
    n = x_s.shape[0]
    images = lse.shape[0]
    main = images * PATCH

    vec32[...] = jnp.zeros_like(vec32)
    pack_vectors((v0, v1, v2, v3, v4, v5, v6, v7, v8, v9), vec32)
    vec_own_s[...] = vec32[...].astype(BF16)
    barrier = pltpu.get_barrier_semaphore()
    level = (z + 1 - 2 * lax.rem(z, 2)) * 2 + x
    for to in ({"shard": sib}, {"shard": across}, {"replica": side}, {"replica": level}):
        pl.semaphore_signal(barrier, inc=1, device_id=to, device_id_type=MESH)

    def unit(number, rows, src, dst):
        return Gather(number, rows, src, dst, sems, local)

    g_qkv = unit(0, 256, lambda a, k: w_qkv.at[pl.ds(a, k), :],
                 lambda p, a, k: full_qkv.at[pl.ds(pl.multiple_of(p * 256 + a, 16), k), :])
    g_out = unit(1, 256, lambda a, k: w_out.at[pl.ds(a, k), :],
                 lambda p, a, k: full_out.at[pl.ds(pl.multiple_of(p * 256 + a, 16), k), :])

    def up_unit(number, t):
        cols = pl.ds(t * TILE, TILE)
        return unit(number, D, lambda a, k: w_up.at[pl.ds(a, k), cols],
                    lambda p, a, k: full_up.at[p, pl.ds(pl.multiple_of(a, 16), k), cols])

    def down_unit(number, t):
        return unit(number, TILE, lambda a, k: w_down.at[pl.ds(a + t * TILE, k), :],
                    lambda p, a, k: full_down.at[p, pl.ds(pl.multiple_of(a + t * TILE, 16), k), :])

    g_up0, g_down0, g_up1, g_down1 = up_unit(2, 0), down_unit(3, 0), up_unit(4, 1), down_unit(5, 1)

    for g in (g_qkv, g_out, g_up0, g_down0, g_up1, g_down1):
        g.load()
    pl.semaphore_wait(barrier, 4)

    def vec_copy(k, src, slot, to):
        return pltpu.make_async_remote_copy(src, vec.at[slot], vsem.at[0, k], vsem.at[1, k], device_id=to,
                                            device_id_type=MESH)

    vec_own = vec_copy(0, vec_own_s, s, {"shard": sib})
    vec_far = vec_copy(1, vec_own_s, s, {"shard": across})
    vec_pass = vec_copy(2, vec.at[across], across, {"shard": sib})
    vec_own.start()
    vec_far.start()
    g_qkv.begin()
    g_qkv.share()
    g_out.begin()
    vec[s] = vec_own_s[...]

    to_images(tokens, x_s, turn)
    outs = {}

    def send_out(k, src, dst):
        outs[k] = pltpu.make_async_copy(src, dst, osem.at[k])
        outs[k].start()

    send_out(0, x_s, x_o)
    vec_far.wait_recv()
    vec_pass.start()
    vec_own.wait_recv()
    vec_pass.wait_recv()
    unpack_vectors(vec, vecf, bias_qkv)

    def first_norm(rows):
        act[rows, :] = layer_norm(x_s[rows, :].astype(F32), vecf[0:1, :], vecf[1:2, :]).astype(BF16)

    rows_loop(n, 16, first_norm)
    g_qkv.on_far()
    for g in (g_up0, g_down0, g_up1, g_down1):
        g.begin()
    transpose_into(act, turned_b)
    send_out(1, turned_b, act_t_o)
    g_qkv.on_near()
    to_images(cot, branch, turn)

    def down_rows(rows):
        act2[rows, :] = (branch[rows, :].astype(F32) * vecf[7:8, :]).astype(BF16)

    rows_loop(n, 16, down_rows)
    g_qkv.on_last()
    g_out.on_far()
    send_out(14, branch, up_o)
    send_out(15, act2, dr_o)
    transpose_into(act2, turned_a)
    send_out(16, turned_a, dr_t_o)
    g_out.on_near()
    g_qkv.ready()
    send_out(4, full_qkv, qkv_w_o)
    for g in (g_out, g_up0, g_down0):
        g.share()

    def qkv_tile(j, carry):
        cols = at(j, TILE)
        low = (dot(act[...], full_qkv[:, cols]) + bias_qkv[0:1, cols]).astype(BF16)
        qkv[:, cols] = low
        qkv_cls[:, cols] = low[main:].astype(F32)
        return carry

    lax.fori_loop(0, 3 * D // TILE, qkv_tile, 0)
    send_out(2, qkv, qkv_o)
    act[...] = act2[...]
    unpack_bias_up(vec, bias_up)
    column[...] = jnp.zeros_like(column)
    send_out(3, vec, vec_all)
    cls[...] = jnp.zeros_like(cls)
    g_out.on_last()
    g_up0.on_far()
    plan = {1: [g_up0.on_near], 2: [g_down0.on_far], 3: [g_up0.on_last, g_up1.share], 4: [g_down0.on_near, g_up1.on_far],
            6: [g_down0.on_last, g_down1.share], 7: [g_up1.on_near, g_down1.on_far]}

    def image(i, carry):
        for k, steps in plan.items():
            @pl.when(i == k)
            def _(steps=steps):
                for step in steps:
                    step()

        attend(i, qkv, qkv_cls, scores, probs, mix, probs_cls, att, cls, lse, lsec)
        return carry

    lax.fori_loop(0, images, image, 0)
    att[main:, :] = cls[...].astype(BF16)
    outs.pop(1).wait()
    transpose_into(att, turned_b)
    send_out(8, turned_b, att_t_o)
    send_out(9, lse, lse_o)
    send_out(10, lsec, lsec_o)
    g_out.ready()
    outs.pop(14).wait()
    for j in range(D // TILE):
        cols = slice(j * TILE, (j + 1) * TILE)
        out = dot(att[...], full_out[:, cols]) + vecf[2:3, cols]
        branch[:, cols] = out.astype(BF16)
        mid[:, cols] = x_s[:, cols].astype(F32) + vecf[3:4, cols] * out
    send_out(11, mid, mid_o)
    send_out(12, branch, branch_o)
    g_up1.on_last()
    g_down1.on_near()

    def second_norm(rows):
        act2[rows, :] = layer_norm(mid[rows, :], vecf[4:5, :], vecf[5:6, :]).astype(BF16)

    outs.pop(15).wait()
    rows_loop(n, 16, second_norm)
    send_out(13, act2, act2_o)
    outs.pop(8).wait()
    transpose_into(act2, turned_b)
    send_out(17, turned_b, act2_t_o)
    half = pl.ds(0, TILE)
    rest = pl.ds(TILE, TILE)
    send_out(5, full_out, out_w_o)
    g_up0.ready()
    send_out(18, full_up.at[:, :, half], up_w_o.at[:, :, half])
    g_down0.ready()
    send_out(19, full_down.at[:, half, :], down_w_o.at[:, half, :])
    for k in (2, 11):
        outs.pop(k).wait()
    hid, br = qkv.at[:, pl.ds(0, TILE)], qkv.at[:, pl.ds(TILE, TILE)]
    for k, rel in enumerate((3, 2)):
        piece = relative_piece(s, rel)

        def put(half_k, value, k=k):
            qkv[0:D, (2 + 2 * k + half_k) * TILE : (3 + 2 * k + half_k) * TILE] = value

        if k:
            outs.pop(22).wait()
        column[pl.ds(2 * piece, 1), :] = ffn_tile(
            act2, act, turned_a, turned_b, lambda: full_up[piece, :, 0:TILE], lambda: full_down[piece, 0:TILE, :],
            bias_up[pl.ds(2 * piece, 1), :], hid, br, mid, k == 0, lambda: send_out(22 + k, hid, hid_o.at[k]), put)
        for half_k in range(2):
            send_out(24 + 2 * k + half_k, qkv.at[pl.ds(0, D), pl.ds((2 + 2 * k + half_k) * TILE, TILE)],
                     parts_o.at[k, pl.ds(half_k * D, D), :])
        if k == 0:
            g_down1.on_last()
            g_up1.ready()
            send_out(20, full_up.at[:, :, rest], up_w_o.at[:, :, rest])
    send_out(28, mid, gact_o)
    send_out(29, column, column_o)
    g_down1.ready()
    send_out(21, full_down.at[:, rest, :], down_w_o.at[:, rest, :])
    for copy in outs.values():
        copy.wait()
    for g in (g_qkv, g_out, g_up0, g_down0, g_up1, g_down1):
        g.drain()
    for copy in (vec_own, vec_far, vec_pass):
        copy.wait_send()


class Chunk:
    def __init__(self, index, rows, mine, y_send, y_recv, x_recv, z_recv, far):
        self.index, self.rows, self.mine, self.y_send, self.far = index, rows, mine, y_send, far
        self.y_recv, self.x_recv, self.z_recv = y_recv, x_recv, z_recv


def chunk_layout(nz):
    sizes = [1024, 1024, 1024, 1024, 512, 512, 512, 512]
    y_base = 2048
    y_a = y_base
    y_b = y_a + 2048
    mine_base = y_b + 2048
    chunks = []
    mine = mine_base
    late = 0
    xr = zr = 0
    for k, rows in enumerate(sizes):
        if k < 2:
            ys, yr = y_a + 1024 * k, 1024 * k
        elif k < 4:
            ys, yr = y_b + 1024 * (k - 2), 2048 + 1024 * (k - 2)
        else:
            ys, yr = y_a + late, late
            late += rows
        far = mine_base + sum(sizes) + 512 * k if k < 2 else ys
        chunks.append(Chunk(k, rows, mine, ys, yr, xr, zr, far))
        mine += rows
        xr += rows // 2
        zr += rows // 2 // nz
    return chunks, dict(buf=mine + 1024, total=sum(sizes), mine=mine_base, y_recv=2 * 2048, x_recv=xr, z_recv=zr)


def add_rows(dst, d0, src, s0, rows):
    step = next(k for k in (128, 96, 64, 32, 16) if rows % k == 0)

    def body(k, carry):
        d = pl.ds(pl.multiple_of(d0 + k * step, 16), step)
        t = pl.ds(pl.multiple_of(s0 + k * step, 16), step)
        dst[d, :] = (dst[d, :].astype(F32) + src[t, :].astype(F32)).astype(BF16)
        return carry

    lax.fori_loop(0, rows // step, body, 0)


class Reduce:
    def __init__(self, nz, buf, core_recv, y_recv, x_recv, z_recv, sems, core_sems, credit):
        self.nz, self.buf, self.core_recv = nz, buf, core_recv
        self.y_recv, self.x_recv, self.z_recv = y_recv, x_recv, z_recv
        self.sems, self.core_sems, self.credit = sems, core_sems, credit
        self.s, self.r, self.x, self.z = place()
        self.sib, self.across, self.side = peers(self.s, self.r)

    def remote(self, src, dst, chunk, kind, to):
        return pltpu.make_async_remote_copy(
            src, dst, self.sems.at[0, chunk.index, kind], self.sems.at[1, chunk.index, kind], device_id=to,
            device_id_type=MESH)

    def peer(self, k):
        return {"replica": lax.rem(self.z + k, self.nz) * 2 + self.x}

    def core_copy(self, turn, rows):
        slot = turn % 2
        return pltpu.make_async_remote_copy(
            self.buf.at[pl.ds(slot * 1024 if turn > 3 else 0, rows), :], self.core_recv.at[slot, pl.ds(0, rows), :],
            self.core_sems.at[0, turn], self.core_sems.at[1, turn], device_id={"shard": self.sib}, device_id_type=MESH)

    def add_core(self, turn, first, dst, rows):
        add_rows(self.buf, dst, self.core_recv.at[turn % 2], first, rows)

    def y_copy(self, c):
        return self.remote(self.buf.at[pl.ds(c.y_send, c.rows), :], self.y_recv.at[pl.ds(c.y_recv, c.rows), :], c, 0,
                           {"shard": self.across})

    def x_copy(self, c):
        half = c.rows // 2
        return self.remote(self.buf.at[pl.ds(pl.multiple_of(c.mine + (1 - self.x) * half, 16), half), :],
                           self.x_recv.at[pl.ds(c.x_recv, half), :], c, 1, {"replica": self.side})

    def quarter(self, c, x, z):
        half = c.rows // 2
        size = half // self.nz
        return pl.ds(pl.multiple_of(c.mine + x * half + z * size, 16), size)

    def z_copy(self, c, k):
        size = c.rows // 2 // self.nz
        return self.remote(self.buf.at[self.quarter(c, self.x, lax.rem(self.z + k, self.nz)), :],
                           self.z_recv.at[k - 1, pl.ds(c.z_recv, size), :], c, 1 + k, self.peer(k))

    def done(self, first, c, z):
        size = c.rows // 2 // self.nz
        return pl.ds(pl.multiple_of(first + z * size, 16), size)

    def back_z(self, c, k):
        part = self.x_recv.at[self.done(c.x_recv, c, self.z), :]
        return self.remote(part, part, c, self.nz + k, self.peer(k))

    def back_x(self, c, k):
        z = lax.rem(self.z + self.nz - k, self.nz)
        return self.remote(self.x_recv.at[self.done(c.x_recv, c, z), :], self.buf.at[self.done(c.far, c, z), :], c,
                           2 * self.nz + k, {"replica": self.side})

    def on_y(self, c):
        self.y_copy(c).wait_recv()
        add_rows(self.buf, c.mine, self.y_recv, c.y_recv, c.rows)
        self.y_copy(c).wait_send()
        self.x_copy(c).start()

    def on_x(self, c):
        half = c.rows // 2
        self.x_copy(c).wait_recv()
        add_rows(self.buf, c.mine + self.x * half, self.x_recv, c.x_recv, half)
        for k in range(1, self.nz):
            self.z_copy(c, k).start()

    def on_z(self, c):
        size = c.rows // 2 // self.nz
        start = c.mine + self.x * (c.rows // 2) + self.z * size
        for k in range(1, self.nz):
            self.z_copy(c, k).wait_recv()
        step = next(k for k in (64, 48, 32, 16) if size % k == 0)

        def body(i, carry):
            d = pl.ds(pl.multiple_of(start + i * step, 16), step)
            total = self.buf[d, :].astype(F32)
            for k in range(1, self.nz):
                total = total + self.z_recv[k - 1, pl.ds(pl.multiple_of(c.z_recv + i * step, 16), step), :].astype(F32)
            to = pl.ds(pl.multiple_of(c.x_recv + self.z * size + i * step, 16), step)
            self.x_recv[to, :] = total.astype(BF16)
            return carry

        lax.fori_loop(0, size // step, body, 0)
        for k in range(1, self.nz):
            self.back_z(c, k).start()
        self.back_x(c, 0).start()

    def on_back(self, c):
        for k in range(1, self.nz):
            self.back_z(c, k).wait_recv()
            self.back_x(c, k).start()

    def finish(self, c):
        for k in range(self.nz):
            self.back_x(c, k).wait_recv()

    def drain(self, c):
        self.x_copy(c).wait_send()
        for k in range(1, self.nz):
            self.z_copy(c, k).wait_send()
            self.back_z(c, k).wait_send()
        for k in range(self.nz):
            self.back_x(c, k).wait_send()


def fold(v):
    return jnp.sum(v.reshape(v.shape[0] // 8, 8, v.shape[1]), axis=0)


def gelu_both(v):
    e = jnp.exp(-0.5 * v * v)
    t = 1.0 / (1.0 + 0.23164189 * jnp.abs(v))
    poly = ((((1.061405429 * t - 1.453152027) * t + 1.421413741) * t - 0.284496736) * t + 0.254829592) * t
    tail = 0.5 * poly * e
    phi = jnp.where(v >= 0.0, 1.0 - tail, tail)
    return v * phi, phi + v * e * 0.3989422804014327


def transpose_into(src, dst):
    for c in range(D // 128):
        dst[c * 128 : (c + 1) * 128, :] = src[:, c * 128 : (c + 1) * 128].T


def attend_back(
    i, qkv, qkv_cls, datt, datt_cls, lse, lsec, scores, dprobs, probs, dscores, cls_row, joint_cls, joint, extra, sum_q, sum_v
):
    rows = at(i, PATCH)
    mask = head_mask()
    own = qkv_cls[pl.ds(i, 1), :]
    do_c = datt_cls[pl.ds(i, 1), :]
    q_c, k_c, v_c = own[:, :D] * FACTOR, own[:, D : 2 * D], own[:, 2 * D :]
    pick = lambda v: jnp.where(mask, v, 0.0)
    q_w, k_w, v_w, do_w = pick(q_c), pick(k_c), pick(v_c), pick(do_c)
    q_bd, k_bd, v_bd, do_bd = (v.astype(BF16) for v in (q_w, k_w, v_w, do_w))
    queries, keys, values = (qkv[rows, k * D : (k + 1) * D] for k in range(3))
    grads = datt[rows, :]
    low = lambda v: v.astype(BF16)
    top = lsec[i][:, 0:1]
    p_row = jnp.exp(dot_nt(q_bd, keys) - top)
    p_cor = jnp.exp(jnp.sum(q_w * k_c, axis=1, keepdims=True) - top)
    dp_row = dot_nt(do_bd, values)
    dp_cor = jnp.sum(do_w * v_c, axis=1, keepdims=True)
    delta = jnp.sum(p_row * dp_row, axis=1, keepdims=True) + p_cor * dp_cor
    ds_row = low(p_row * (dp_row - delta))
    ds_cor = low(p_cor * (dp_cor - delta)).astype(F32)
    p_col = jnp.exp(dot_nt(k_bd, queries) * FACTOR - lse[i])
    dp_col = dot_nt(v_bd, grads)
    for g in range(HEADS // 2):
        lanes = slice(g * 128, (g + 1) * 128)
        q2 = qkv[rows, lanes] * jnp.asarray(FACTOR, BF16)
        scores[g] = dot_nt(split_pair(qkv[rows, g * 128 + D : g * 128 + D + 128]), q2)
        dprobs[g] = dot_nt(split_pair(qkv[rows, g * 128 + 2 * D : g * 128 + 2 * D + 128]), datt[rows, lanes])
    for g in range(HEADS // 2):
        for u in range(2):
            h = 2 * g + u
            half = slice(u * PATCH, (u + 1) * PATCH)
            part = jnp.exp(scores[g, half, :] - lse[i, h : h + 1, :])
            dpart = dprobs[g, half, :]
            p_h, dp_h = p_col[h : h + 1, :], dp_col[h : h + 1, :]
            delta = jnp.sum(part * dpart, axis=0, keepdims=True) + p_h * dp_h
            probs[g, half, :] = low(part)
            dscores[g, half, :] = low(part * (dpart - delta))
            cls_row[h : h + 1, :] = p_h * (dp_h - delta)
    ds_col = low(cls_row[...])
    total = lambda v: jnp.sum(jnp.where(mask, v, 0.0), axis=0, keepdims=True)
    joint_cls[pl.ds(i, 1), 0:D] = FACTOR * (total(dot(ds_row, keys)) + jnp.sum(ds_cor * k_w, axis=0, keepdims=True))
    joint_cls[pl.ds(i, 1), D : 2 * D] = FACTOR * total(dot(ds_col, queries)) + jnp.sum(ds_cor * q_w, axis=0, keepdims=True)
    joint_cls[pl.ds(i, 1), 2 * D : 3 * D] = total(dot(low(p_col), grads)) + jnp.sum(
        low(p_cor).astype(F32) * do_w, axis=0, keepdims=True)
    extra[0] = dot_tn(ds_col, k_bd) * FACTOR
    extra[1] = dot_tn(ds_row, q_bd)
    extra[2] = dot_tn(low(p_row), do_bd)
    for g in range(HEADS // 2):
        lanes = slice(g * 128, (g + 1) * 128)
        klanes = slice(g * 128 + D, g * 128 + D + 128)
        vlanes = slice(g * 128 + 2 * D, g * 128 + 2 * D + 128)
        q2 = qkv[rows, lanes] * jnp.asarray(FACTOR, BF16)
        dv = merge_pair(dot(probs[g], datt[rows, lanes])) + extra[2, :, lanes]
        dk = merge_pair(dot(dscores[g], q2)) + extra[1, :, lanes]
        dq = dot_tn(dscores[g], split_pair(qkv[rows, klanes])) * FACTOR + extra[0, :, lanes]
        joint[:, lanes] = low(dq)
        joint[:, klanes] = low(dk)
        joint[:, vlanes] = low(dv)
        sum_q[:, lanes] += fold(dq)
        sum_v[:, lanes] += fold(dv)
    qkv[rows, :] = joint[...]


def to_tokens(src, dst, turn):
    images = dst.shape[0] // (PATCH + 1)
    main = images * PATCH

    def lane_block(l, carry):
        cols = at(l, 128)
        slot = lax.rem(l, 2)
        for i in range(images):
            turn[slot, pl.ds(i, PATCH, stride=images), :] = src[i * PATCH : (i + 1) * PATCH, cols].astype(F32)
        dst[0:main, cols] = turn[slot].astype(BF16)
        return carry

    lax.fori_loop(0, D // 128, lane_block, 0)
    dst[main : main + images, :] = src[main:, :].astype(F32)[0:images].astype(BF16)


def backward_kernel(
    nz, chunks, vec, full_qkv, full_out, full_up, full_down, qkv_h, act_t_h, x_h, att_t_h, mid_h, branch_h, act2_h,
    act2_t_h, up_h, dr_h, dr_t_h, lse_h, lsec_h, parts_h, hid_h, gact_h, column_h,
    result_o, tokens_o, sums_o, small_o, hidden_o,
    buf, core_recv, y_recv, x_recv, z_recv, gmid, grad_mid, up_s, acc, sums_up, vecf, bias_qkv, bias_up, v_part, v_group, v_sum, v_all,
    sems, core_sems, group_sems, all_sems, credit, dsem, wsem, hsem, osem, fsem,
):
    images = lse_h.shape[0]
    n = gmid.shape[0]
    main = images * PATCH
    red = Reduce(nz, buf, core_recv, y_recv, x_recv, z_recv, sems, core_sems, credit)
    s = red.s
    cd0, cu0, cd1, cu1, co, *cq = chunks

    def load(k, src, dst):
        copy = pltpu.make_async_copy(src, dst, dsem.at[k])
        copy.start()
        return copy

    def relative(rel):
        return relative_piece(s, rel)

    def target(rel, chunk, base):
        low, high = lax.rem(rel, 2), lax.div(rel, 2)
        return low * (base + (1 - high) * chunk.rows) + (1 - low) * (high * chunk.y_send + (1 - high) * chunk.mine)

    def group_peer(k):
        return {"shard": lax.rem(s + k, 4)}

    def replica_peer(k):
        return {"replica": lax.rem(red.r + k, 2 * nz)}

    def group_copy(k):
        return pltpu.make_async_remote_copy(
            v_part.at[lax.rem(s + k, 4)], v_group.at[k - 1], group_sems.at[0, k - 1], group_sems.at[1, k - 1],
            device_id=group_peer(k), device_id_type=MESH)

    def all_copy(k):
        return pltpu.make_async_remote_copy(
            v_sum, v_all.at[red.r], all_sems.at[0, k - 1], all_sems.at[1, k - 1], device_id=replica_peer(k),
            device_id_type=MESH)

    got_up = load(7, up_h, up_s)

    def ffn(dr, dr_t, act2, act2_t, w_up, w_down, hid, br):
        gots = [load(8, parts_h.at[0], buf.at[pl.ds(0, 2048), :]),
                load(9, parts_h.at[1], buf.at[pl.ds(cd0.y_send, 2048), :]), load(0, act2_h, act2), load(1, dr_h, dr),
                load(2, dr_t_h, dr_t), load(3, act2_t_h, act2_t), load(10, gact_h, gmid), load(11, column_h, sums_up)]

        def fetch(j, slot):
            piece, t = relative(3 - lax.rem(j, 4)), lax.div(j, 4)
            return (
                pltpu.make_async_copy(full_up.at[piece, :, at(t, TILE)], w_up.at[slot], wsem.at[0, slot]),
                pltpu.make_async_copy(full_down.at[piece, at(t, TILE), :], w_down.at[slot], wsem.at[1, slot]),
            )

        def keep(j, slot):
            return pltpu.make_async_copy(hid.at[slot], hidden_o.at[j - 2], hsem.at[slot])

        barrier = pltpu.get_barrier_semaphore()
        partners = [group_peer(k) for k in range(1, 4)] + [replica_peer(k) for k in range(1, 2 * nz)]
        for to in partners:
            pl.semaphore_signal(barrier, inc=1, device_id=to, device_id_type=MESH)
        pl.semaphore_wait(barrier, len(partners))
        unpack_vectors(vec, vecf, bias_qkv)
        unpack_bias_up(vec, bias_up)
        acc[...] = jnp.zeros_like(acc)
        gots[0].wait()
        red.core_copy(0, 2048).start()
        for copy in fetch(2, 0):
            copy.start()
        late = gots[4:6]
        for copy in gots[1:4] + gots[6:]:
            copy.wait()

        def tile(j, carry):
            slot = lax.rem(j, 2)
            rel, t = 3 - lax.rem(j, 4), lax.div(j, 4)
            piece = relative(rel)
            low, high = lax.rem(rel, 2), lax.div(rel, 2)
            place_at = pl.multiple_of(
                (1 - low) * (high * (cd0.y_send + t * (cd1.y_send - cd0.y_send)) + (1 - high) * (cd0.mine + t * 2048)), 16)
            for copy in fetch(j, slot):
                copy.wait()

            @pl.when(j < 7)
            def _():
                for copy in fetch(j + 1, 1 - slot):
                    copy.start()

            @pl.when(j >= 4)
            def _():
                keep(j - 2, slot).wait()

            for k in (2, 4, 6):
                @pl.when(j == k)
                def _(k=k):
                    red.core_copy(k // 2 - 1, 2048).wait_send()

            def on_hidden():
                keep(j, slot).start()

                @pl.when(j == 2)
                def _():
                    for copy in late:
                        copy.wait()

            def put(half, value):
                buf[pl.ds(pl.multiple_of(place_at + half * D, 16), D), :] = value

            sums_up[pl.ds(2 * piece + t, 1), :] = ffn_tile(
                act2, dr, dr_t, act2_t, lambda: w_up[slot], lambda: w_down[slot], bias_up[pl.ds(2 * piece + t, 1), :],
                hid.at[slot], br, gmid, False, on_hidden, put)

            def y_part(turn, chunk):
                red.core_copy(turn, 2048).wait_recv()
                for k, c in enumerate(chunk):
                    red.add_core(turn, k * 1024, c.y_send, c.rows)
                    red.y_copy(c).start()

            def own_part(turn, chunk):
                red.core_copy(turn, 2048).wait_recv()
                red.add_core(turn, 0, chunk[0].mine, 2048)

            steps = {
                2: [lambda: y_part(0, (cd0, cu0)), lambda: red.core_copy(1, 2048).start()],
                3: [lambda: own_part(1, (cd0, cu0))],
                4: [lambda: red.core_copy(2, 2048).start()],
                5: [lambda: y_part(2, (cd1, cu1)), lambda: red.on_y(cd0)],
                6: [lambda: red.core_copy(3, 2048).start(), lambda: red.on_x(cd0)],
                7: [lambda: own_part(3, (cd1, cu1)), lambda: red.on_y(cu0)],
            }
            for k, todo in steps.items():
                @pl.when(j == k)
                def _(todo=todo):
                    for step in todo:
                        step()
            return carry

        lax.fori_loop(2, 8, tile, 0)
        pl.semaphore_signal(credit, inc=1, device_id={"shard": red.across}, device_id_type=MESH)
        for j in (6, 7):
            keep(j, j % 2).wait()
        red.core_copy(3, 2048).wait_send()

    v = pltpu.VMEM
    pl.run_scoped(ffn, v((n, D), BF16), v((D, n), BF16), v((n, D), BF16), v((D, n), BF16), v((2, D, TILE), BF16),
                  v((2, TILE, D), BF16), v((2, n, TILE), BF16), v((n, TILE), BF16))
    got_up.wait()

    def spread(out, chunk, tile_rows, turn):
        for p in range(4):
            low = lax.rem(lax.rem(s, 2) + p % 2, 2)
            high = lax.rem(lax.div(s, 2) + p // 2, 2)
            start = pl.multiple_of(target(low + 2 * high, chunk, 1024 * (turn % 2)) + tile_rows, 16)
            buf[pl.ds(start, 256), :] = out[p * 256 : (p + 1) * 256].astype(BF16)

    def on_core(turn, chunk):
        red.core_copy(turn, 2 * chunk.rows).wait_recv()
        red.add_core(turn, 0, chunk.y_send, chunk.rows)
        red.y_copy(chunk).start()
        red.add_core(turn, chunk.rows, chunk.mine, chunk.rows)

    def attention(
        qkv, datt, brr, lse, lsec, scores, dprobs, probs, dscores, cls_row, qkv_cls, datt_cls, joint_cls, joint, extra
    ):
        got_qkv, got_lse, got_lsec = load(0, qkv_h, qkv), load(1, lse_h, lse), load(2, lsec_h, lsec)

        def middle(mid, branch, att_t, w_out):
            got_mid, got_branch = load(3, mid_h, mid), load(4, branch_h, branch)
            got_att, got_out = load(5, att_t_h, att_t), load(6, full_out, w_out)
            red.on_z(cd0)
            got_mid.wait()
            got_branch.wait()

            def norm_rows(rows):
                m = mid[rows, :]
                c = m - jnp.mean(m, axis=-1, keepdims=True)
                inv = lax.rsqrt(jnp.mean(c * c, axis=-1, keepdims=True) + 1e-06)
                hat = c * inv
                g = gmid[rows, :]
                acc[4] += fold(g * hat)
                acc[5] += fold(g)
                sc = g * vecf[4:5, :]
                back = inv * (sc - jnp.mean(sc, axis=-1, keepdims=True)
                              - hat * jnp.mean(sc * hat, axis=-1, keepdims=True))
                gm = up_s[rows, :].astype(F32) + back
                grad_mid[rows, :] = gm
                acc[3] += fold(gm * branch[rows, :].astype(F32))
                gb = gm * vecf[3:4, :]
                acc[2] += fold(gb)
                brr[rows, :] = gb.astype(BF16)

            rows_loop(n, 16, norm_rows)
            got_att.wait()
            for q in range(2):
                spread(dot(att_t[...], brr[:, q * TILE : (q + 1) * TILE]), co, q * 256, 4)
            red.core_copy(4, 2 * co.rows).start()
            got_out.wait()
            for q in range(2):
                datt[:, q * TILE : (q + 1) * TILE] = dot_nt(brr[...], w_out[q * TILE : (q + 1) * TILE, :]).astype(BF16)
            red.on_x(cu0)

        pl.run_scoped(middle, v((n, D), F32), v((n, D), BF16), v((D, n), BF16), v((D, D), BF16))
        got_qkv.wait()
        got_lse.wait()
        got_lsec.wait()
        qkv_cls[...] = qkv[main:, :].astype(F32)
        datt_cls[...] = datt[main:, :].astype(F32)
        joint_cls[...] = jnp.zeros_like(joint_cls)
        pl.semaphore_wait(credit, 1)
        on_core(4, co)
        plan = {0: [lambda: red.on_y(cd1), lambda: red.on_back(cd0)], 3: [lambda: red.on_z(cu0)], 5: [lambda: red.on_x(cd1)],
                6: [lambda: red.on_y(cu1), lambda: red.on_back(cu0)]}

        def image(i, carry):
            for k, steps in plan.items():
                @pl.when(i == k)
                def _(steps=steps):
                    for step in steps:
                        step()

            attend_back(i, qkv, qkv_cls, datt, datt_cls, lse, lsec, scores, dprobs, probs, dscores, cls_row, joint_cls,
                        joint, extra, acc.at[8], acc.at[9])
            return carry

        lax.fori_loop(0, images, image, 0)
        qkv[main:, :] = joint_cls[...].astype(BF16)
        acc[8] += fold(joint_cls[:, 0:D])
        acc[9] += fold(joint_cls[:, 2 * D : 3 * D])

        def tail(act_t, w_qkv, turn, flat):
            x_s, gact, new = brr, gmid, datt
            got_act, got_x = load(3, act_t_h, act_t), load(4, x_h, x_s)

            def fetch(j):
                return pltpu.make_async_copy(full_qkv.at[pl.ds(j * 256, 256), :], w_qkv.at[j % 2], wsem.at[0, j % 2])

            fetch(0).start()
            fetch(1).start()
            def weight_grad(k):
                for q in range(2):
                    cols = slice((2 * k + q) * TILE, (2 * k + q + 1) * TILE)
                    spread(dot(act_t[...], qkv[:, cols]), cq[k], q * 256, 5 + k)

            def input_grad(j):
                fetch(j).wait()
                gact[:, j * 256 : (j + 1) * 256] = dot_nt(qkv[...], w_qkv[j % 2])
                if j < 2:
                    fetch(j + 2).start()

            got_act.wait()
            weight_grad(0)
            red.core_copy(5, 1024).start()
            red.on_z(cd1)
            red.core_copy(4, 1024).wait_send()
            weight_grad(1)
            on_core(5, cq[0])
            red.core_copy(6, 1024).start()
            red.on_y(co)
            red.core_copy(5, 1024).wait_send()
            weight_grad(2)
            on_core(6, cq[1])
            red.core_copy(7, 1024).start()
            red.on_x(cu1)
            red.on_back(cd1)
            input_grad(0)
            input_grad(1)
            on_core(7, cq[2])
            red.on_x(co)
            input_grad(2)
            red.on_y(cq[0])
            input_grad(3)
            red.on_z(cu1)
            got_x.wait()

            def norm_rows(rows):
                m = x_s[rows, :].astype(F32)
                c = m - jnp.mean(m, axis=-1, keepdims=True)
                inv = lax.rsqrt(jnp.mean(c * c, axis=-1, keepdims=True) + 1e-06)
                hat = c * inv
                g = gact[rows, :]
                acc[0] += fold(g * hat)
                acc[1] += fold(g)
                sc = g * vecf[0:1, :]
                back = inv * (sc - jnp.mean(sc, axis=-1, keepdims=True)
                              - hat * jnp.mean(sc * hat, axis=-1, keepdims=True))
                new[rows, :] = (grad_mid[rows, :] + back).astype(BF16)

            rows_loop(n, 16, norm_rows)
            red.on_z(co)
            red.on_x(cq[0])
            to_tokens(new, flat, turn)
            copy = pltpu.make_async_copy(flat, tokens_o, osem.at[0])
            copy.start()
            red.on_back(cu1)
            red.on_back(co)
            red.on_y(cq[1])
            copy.wait()

        pl.run_scoped(tail, v((D, n), BF16), v((2, 256, 3 * D), BF16),
                      v((2, main, 128), F32), v((main + images, D), BF16))

    pl.run_scoped(attention, v((n, 3 * D), BF16), v((n, D), BF16), v((n, D), BF16), v((images, HEADS, PATCH), F32),
                  v((images, HEADS, PATCH), F32), v((8, 256, PATCH), F32), v((8, 256, PATCH), F32),
                  v((8, 256, PATCH), BF16), v((8, 256, PATCH), BF16), v((HEADS, PATCH), F32), v((CLS, 3 * D), F32),
                  v((CLS, D), F32), v((CLS, 3 * D), F32), v((PATCH, 3 * D), BF16), v((3, PATCH, D), F32))

    def outcome(mid, hid, w_down, turn, flat, res):
        got_mid = load(3, mid_h, mid)

        def fetch(pair):
            copies = []
            for k in range(2):
                j = 2 * pair + k
                slot = pair % 2
                piece, t = relative(3 - j % 4), j // 4
                src = hid_h.at[k] if pair == 0 else hidden_o.at[j - 2]
                copies.append(pltpu.make_async_copy(src, hid.at[slot, :, pl.ds(k * TILE, TILE)], wsem.at[0, 2 * slot + k]))
                copies.append(pltpu.make_async_copy(full_down.at[piece, pl.ds(t * TILE, TILE), :],
                                                    w_down.at[slot, pl.ds(k * TILE, TILE), :], wsem.at[1, 2 * slot + k]))
            return copies

        for copy in fetch(0):
            copy.start()
        steps = {0: [lambda: red.on_z(cq[0]), lambda: red.on_x(cq[1])], 1: [lambda: red.on_back(cq[0])],
                 2: [lambda: red.on_y(cq[2]), lambda: red.on_z(cq[1])], 3: [lambda: red.on_back(cq[1])]}
        for pair in range(4):
            if pair < 3:
                for copy in fetch(pair + 1):
                    copy.start()
            for copy in fetch(pair):
                copy.wait()
            for q in range(2):
                cols = slice(q * TILE, (q + 1) * TILE)
                out = dot(hid[pair % 2], w_down[pair % 2, :, cols])
                if pair:
                    gmid[:, cols] += out
                else:
                    gmid[:, cols] = out
            for step in steps.get(pair, []):
                step()
        got_mid.wait()

        def rows_of(rows):
            projected = gmid[rows, :] + vecf[6:7, :]
            upstream = up_s[rows, :].astype(F32)
            acc[6] += fold(upstream * vecf[7:8, :])
            acc[7] += fold(upstream * projected)
            res[rows, :] = (mid[rows, :] + vecf[7:8, :] * projected).astype(BF16)

        rows_loop(n, 16, rows_of)
        for p in range(4):
            for k in range(8):
                v_part[p, k : k + 1, :] = jnp.sum(acc[k, :, p * 256 : (p + 1) * 256], axis=0, keepdims=True)
            joint = acc.at[8 + p // 2]
            for k in range(2):
                start = (p % 2) * TILE + k * 256
                v_part[p, 8 + k : 9 + k, :] = jnp.sum(joint[:, start : start + 256], axis=0, keepdims=True)
            for k in range(4):
                v_part[p, 10 + k : 11 + k, :] = sums_up[2 * p + k // 2 : 2 * p + k // 2 + 1, (k % 2) * 256 : (k % 2 + 1) * 256]
            v_part[p, 14:16, :] = jnp.zeros((2, 256), F32)
        for k in range(1, 4):
            group_copy(k).start()
        red.on_x(cq[2])
        total = v_part[s]
        for k in range(1, 4):
            group_copy(k).wait_recv()
            total = total + v_group[k - 1]
        v_sum[...] = total
        v_all[red.r] = total
        for k in range(1, 2 * nz):
            all_copy(k).start()
        to_tokens(res, flat, turn)
        copy = pltpu.make_async_copy(flat, result_o, osem.at[0])
        copy.start()
        red.on_z(cq[2])
        for k in range(1, 2 * nz):
            all_copy(k).wait_recv()
        total = v_all[0]
        for k in range(1, 2 * nz):
            total = total + v_all[k]
        v_group[0] = total
        small = pltpu.make_async_copy(v_group.at[0], small_o, osem.at[1])
        small.start()
        red.on_back(cq[2])
        copy.wait()
        small.wait()

    pl.run_scoped(outcome, v((n, D), F32), v((2, n, D), BF16), v((2, D, D), BF16), v((2, main, 128), F32),
                  v((main + images, D), BF16), v((n, D), BF16))
    copies = []
    for c in chunks:
        red.finish(c)
        half = c.rows // 2
        for k, (src, first, where) in enumerate(((x_recv, c.x_recv, red.x), (buf, c.far, 1 - red.x))):
            copy = pltpu.make_async_copy(
                src.at[pl.ds(first, half), :],
                sums_o.at[pl.ds(pl.multiple_of(c.mine - cd0.mine + where * half, 16), half), :], fsem.at[2 * c.index + k])
            copy.start()
            copies.append(copy)
    red.core_copy(6, 1024).wait_send()
    red.core_copy(7, 1024).wait_send()
    for k in range(1, 4):
        group_copy(k).wait_send()
    for k in range(1, 2 * nz):
        all_copy(k).wait_send()
    for c in chunks:
        red.drain(c)
    for copy in copies:
        copy.wait()


def convert_kernel(
    chunks, sums, small, result, tokens, result_o, tokens_o, g1_o, s1_o, qkv_o, bqv_o, out_o, bo_o, l1_o, g2_o, s2_o, up_o, bup_o, down_o, bd_o, l2_o,
    low, qkv, out, up, down, moved, dsem, osem, msem,
):
    base = chunks[0].mine
    moves = [pltpu.make_async_copy(src, moved.at[k], msem.at[0, k]) for k, src in enumerate((result, tokens))]
    stores = [pltpu.make_async_copy(moved.at[k], dst, msem.at[1, k]) for k, dst in enumerate((result_o, tokens_o))]
    gots = []
    for c in chunks:
        rows = pl.ds(c.mine - base, c.rows)
        gots.append(pltpu.make_async_copy(sums.at[rows, :], low.at[rows, :], dsem.at[c.index]))
        gots[-1].start()
    for copy in moves:
        copy.start()
    outs = []

    def send_out(src, dst):
        copy = pltpu.make_async_copy(src, dst, osem.at[len(outs)])
        copy.start()
        outs.append(copy)

    def block(c, first, count):
        return low[c.mine - base + first : c.mine - base + first + count, :]

    for t in range(2):
        gots[2 * t].wait()
        for k in range(8):
            down[t * TILE : (t + 1) * TILE, k * 128 : (k + 1) * 128] = block(chunks[2 * t], k * 128, 128).T.astype(F32)
        send_out(down.at[pl.ds(t * TILE, TILE), :], down_o.at[pl.ds(t * TILE, TILE), :])
        gots[2 * t + 1].wait()
        up[t] = block(chunks[2 * t + 1], 0, D).astype(F32)
        send_out(up.at[t], up_o.at[:, pl.ds(t * TILE, TILE)])
    for k in range(2):
        moves[k].wait()
        stores[k].start()
    gots[4].wait()
    for k in range(2):
        out[:, k * TILE : (k + 1) * TILE] = block(chunks[4], k * 256, 256).astype(F32)
    send_out(out, out_o)
    for k in range(5, 8):
        gots[k].wait()
    for k in range(6):
        qkv[:, k * TILE : (k + 1) * TILE] = block(chunks[5], k * 256, 256).astype(F32)
    send_out(qkv, qkv_o)
    vectors = (g1_o, s1_o, bo_o, l1_o, g2_o, s2_o, bd_o, l2_o, bqv_o, bup_o)
    row = 0
    for v in vectors:
        for k in range(v.shape[0] // 256):
            v[pl.ds(k * 256, 256)] = small[row : row + 1, :].reshape(256)
            row += 1
    for copy in outs + stores:
        copy.wait()


def convert(chunks, sums, small, result, tokens):
    one = lambda k: jax.ShapeDtypeStruct((k,), F32)
    outs = (
        low_shape(*result.shape), low_shape(*tokens.shape), one(256), one(256), wide_shape(256, 3 * D), one(512), wide_shape(256, D), one(256), one(256), one(256), one(256),
        wide_shape(D, D), one(1024), wide_shape(D, D), one(256), one(256),
    )
    v = pltpu.VMEM
    return pl.pallas_call(
        functools.partial(convert_kernel, chunks),
        out_shape=outs,
        in_specs=[ANY, VMEM, ANY, ANY],
        out_specs=[VMEM if len(o.shape) == 1 else ANY for o in outs],
        scratch_shapes=[v(sums.shape, BF16), v((256, 3 * D), F32), v((256, D), F32), v((2, D, TILE), F32),
                        v((D, D), F32), v((2,) + result.shape, BF16), pltpu.SemaphoreType.DMA((8,)),
                        pltpu.SemaphoreType.DMA((6,)), pltpu.SemaphoreType.DMA((2, 2))],
        compiler_params=pltpu.CompilerParams(vmem_limit_bytes=LIMIT),
        name="gradients_to_float32",
    )(sums, small, result, tokens)


def low_shape(*shape):
    return jax.ShapeDtypeStruct(shape, BF16)


def wide_shape(*shape):
    return jax.ShapeDtypeStruct(shape, F32)


ANY = pl.BlockSpec(memory_space=pl.ANY)
VMEM = pl.BlockSpec(memory_space=pltpu.VMEM)
LIMIT = 62 * 2**20


def forward(flat, cot, vectors, w_qkv, w_out, w_up, w_down):
    images = flat.shape[0] // (PATCH + 1)
    n = images * PATCH + CLS
    v = pltpu.VMEM
    outs = (
        low_shape(D, 3 * D), low_shape(D, D), low_shape(4, D, D), low_shape(4, D, D), low_shape(4, 16, 256),
        low_shape(n, 3 * D), low_shape(D, n), low_shape(n, D), low_shape(D, n), wide_shape(n, D), low_shape(n, D),
        low_shape(n, D), low_shape(D, n), low_shape(n, D), low_shape(n, D), low_shape(D, n),
        wide_shape(images, HEADS, PATCH), wide_shape(images, HEADS, PATCH),
        low_shape(2, 2048, TILE), low_shape(2, n, TILE), wide_shape(n, D), wide_shape(8, TILE),
    )
    return pl.pallas_call(
        gather_kernel,
        out_shape=outs,
        in_specs=[VMEM] * 12 + [ANY] * 4,
        out_specs=[ANY] * len(outs),
        scratch_shapes=[
            v((D, 3 * D), BF16), v((D, D), BF16), v((4, D, D), BF16), v((4, D, D), BF16),
            v((n, D), BF16), v((n, 3 * D), BF16), v((n, D), BF16), v((n, D), BF16), v((n, D), F32), v((n, D), BF16),
            v((n, D), BF16), v((D, n), BF16), v((D, n), BF16),
            v((images, HEADS, PATCH), F32), v((images, HEADS, PATCH), F32),
            v((8, 256, PATCH), F32), v((8, 256, PATCH), BF16), v((PATCH, D), F32), v((HEADS, PATCH), F32),
            v((CLS, D), F32), v((CLS, 3 * D), F32), v((2, images * PATCH, 128), F32), v((16, 256), F32),
            v((16, 256), BF16), v((4, 16, 256), BF16), v((16, D), F32), v((8, 3 * D), F32), v((8, TILE), F32),
            v((8, TILE), F32), pltpu.SemaphoreType.DMA((2, 6, 11)), pltpu.SemaphoreType.DMA((6,)), pltpu.SemaphoreType.DMA((2, 3)),
            pltpu.SemaphoreType.DMA((30,)),
        ],
        compiler_params=pltpu.CompilerParams(collective_id=0, has_side_effects=True, vmem_limit_bytes=LIMIT),
        cost_estimate=pl.CostEstimate(flops=18 * 2**30, bytes_accessed=64 * 2**20, transcendentals=3 * 2**20),
        name="gather_and_attention",
    )(flat, cot, *vectors, w_qkv, w_out, w_up, w_down)


def backward(nz, images, vec, *arrays):
    n = images * PATCH + CLS
    tokens = images * (PATCH + 1)
    v = pltpu.VMEM
    chunks, sizes = chunk_layout(nz)
    outs = (low_shape(tokens, D), low_shape(tokens, D), low_shape(sizes["total"], TILE), wide_shape(16, 256),
            low_shape(6, n, TILE))
    return pl.pallas_call(
        functools.partial(backward_kernel, nz, chunks),
        out_shape=outs,
        in_specs=[VMEM] + [ANY] * len(arrays),
        out_specs=[ANY] * len(outs),
        scratch_shapes=[
            v((sizes["buf"], TILE), BF16), v((2, 2048, TILE), BF16), v((sizes["y_recv"], TILE), BF16),
            v((sizes["x_recv"], TILE), BF16), v((nz - 1, sizes["z_recv"], TILE), BF16), v((n, D), F32), v((n, D), F32), v((n, D), BF16),
            v((10, 8, D), F32), v((8, TILE), F32), v((16, D), F32), v((8, 3 * D), F32), v((8, TILE), F32),
            v((4, 16, 256), F32), v((3, 16, 256), F32), v((16, 256), F32), v((2 * nz, 16, 256), F32),
            pltpu.SemaphoreType.DMA((2, len(chunks), 3 * nz)), pltpu.SemaphoreType.DMA((2, 8)),
            pltpu.SemaphoreType.DMA((2, 3)), pltpu.SemaphoreType.DMA((2, 2 * nz - 1)),
            pltpu.SemaphoreType.REGULAR, pltpu.SemaphoreType.DMA((12,)), pltpu.SemaphoreType.DMA((2, 4)),
            pltpu.SemaphoreType.DMA((2,)), pltpu.SemaphoreType.DMA((2,)), pltpu.SemaphoreType.DMA((2 * len(chunks),)),
        ],
        compiler_params=pltpu.CompilerParams(collective_id=1, has_side_effects=True, vmem_limit_bytes=LIMIT),
        cost_estimate=pl.CostEstimate(flops=66 * 2**30, bytes_accessed=128 * 2**20, transcendentals=8 * 2**20),
        name="layer_backward",
    )(vec, *arrays), chunks


def on_device(
    tokens, norm1_gain, norm1_shift, w_qkv, bias_qv, w_out, bias_out, scale_one, norm2_gain, norm2_shift, w_up, bias_up,
    w_down, bias_down, scale_two, cotangent,
):
    images, length, _ = tokens.shape
    nz = lax.axis_size("replica") // 2
    flatten = lambda a: jnp.transpose(a, (1, 0, 2)).reshape(images * length, D)
    restore = lambda a: jnp.transpose(a.reshape(length, images, D), (1, 0, 2))
    vectors = (norm1_gain, norm1_shift, bias_out, scale_one, norm2_gain, norm2_shift, bias_down, scale_two, bias_qv, bias_up)
    full_qkv, full_out, full_up, full_down, vec, *kept = forward(
        flatten(tokens), flatten(cotangent), vectors, w_qkv, w_out, w_up, w_down)
    (result, grad_tokens, sums, small, _), chunks = backward(nz, images, vec, full_qkv, full_out, full_up, full_down, *kept)
    result, grad_tokens, *gradients = convert(chunks, sums, small, result, grad_tokens)
    return (restore(result), restore(grad_tokens)) + tuple(gradients)


def solution(mesh):
    placed = (
        P(("shard", "replica"), None, None),
        P("shard"),
        P("shard"),
        P("shard", None),
        P("shard"),
        P("shard", None),
        P("shard"),
        P("shard"),
        P("shard"),
        P("shard"),
        P(None, "shard"),
        P("shard"),
        P("shard", None),
        P("shard"),
        P("shard"),
        P(("shard", "replica"), None, None),
    )
    return jax.shard_map(
        on_device,
        mesh=mesh,
        in_specs=placed,
        out_specs=(
            P(("shard", "replica"), None, None),
            P(("shard", "replica"), None, None),
            P("shard"),
            P("shard"),
            P("shard", None),
            P("shard"),
            P("shard", None),
            P("shard"),
            P("shard"),
            P("shard"),
            P("shard"),
            P(None, "shard"),
            P("shard"),
            P("shard", None),
            P("shard"),
            P("shard"),
        ),
        check_vma=False,
    )
```

```python
import functools

import jax
import jax.numpy as jnp
from jax import lax
from jax.experimental import pallas as pl
from jax.experimental.pallas import tpu as pltpu
from jax.sharding import PartitionSpec as P

F32 = jnp.float32
BF16 = jnp.bfloat16
D = 1024
FF = 4096
HEADS = 16
PATCH = 128
CLS = 16
TILE = 512
FACTOR = 0.125
MESH = pl.DeviceIdType.MESH


def dot(a, b):
    return jnp.dot(a, b, preferred_element_type=F32)


def dot_nt(a, b):
    return lax.dot_general(a, b, (((1,), (1,)), ((), ())), preferred_element_type=F32)


def dot_tn(a, b):
    return lax.dot_general(a, b, (((0,), (0,)), ((), ())), preferred_element_type=F32)


def at(index, size):
    return pl.ds(pl.multiple_of(index * size, size), size)


def head_mask():
    lane = lax.shift_right_logical(lax.broadcasted_iota(jnp.int32, (HEADS, D), 1), 6)
    return lane == lax.broadcasted_iota(jnp.int32, (HEADS, D), 0)


def split_pair(v):
    low = lax.broadcasted_iota(jnp.int32, v.shape, 1) < 64
    zero = jnp.zeros_like(v)
    return jnp.concatenate([jnp.where(low, v, zero), jnp.where(low, zero, v)], 0)


def merge_pair(v):
    n = v.shape[0] // 2
    low = lax.broadcasted_iota(jnp.int32, (n, v.shape[1]), 1) < 64
    return jnp.where(low, v[:n], v[n:])


def place():
    s = lax.axis_index("shard")
    r = lax.axis_index("replica")
    x = lax.rem(r, 2)
    z = lax.div(r, 2)
    return s, r, x, z


def peers(s, r):
    sib = s + 1 - 2 * lax.rem(s, 2)
    across = lax.rem(s + 2, 4)
    side = r + 1 - 2 * lax.rem(r, 2)
    return sib, across, side


def rows_loop(n, step, body):
    lax.fori_loop(0, n // step, lambda k, c: (body(at(k, step)), c)[1], 0, unroll=13)


def unpack_vectors(vec, vecf, bias_qkv):
    for v in range(8):
        for s in range(4):
            vecf[v : v + 1, s * 256 : (s + 1) * 256] = vec[s, v : v + 1, :].astype(F32)
    bias_qkv[...] = jnp.zeros_like(bias_qkv)
    for s in range(4):
        for t in range(2):
            col = (s * 2 + t) * 256 + (D if s >= 2 else 0)
            bias_qkv[0:1, col : col + 256] = vec[s, 8 + t : 9 + t, :].astype(F32)


def layer_norm(v, gain, shift):
    c = v - jnp.mean(v, axis=-1, keepdims=True)
    inv = lax.rsqrt(jnp.mean(c * c, axis=-1, keepdims=True) + 1e-06)
    return c * inv * gain + shift


def to_images(src, dst, turn):
    images = (src.shape[0]) // (PATCH + 1)
    main = images * PATCH

    def lane_block(l, carry):
        cols = at(l, 128)
        slot = lax.rem(l, 2)
        turn[slot] = src[0:main, cols].astype(F32)
        for i in range(images):
            dst[i * PATCH : (i + 1) * PATCH, cols] = turn[slot, pl.ds(i, PATCH, stride=images), :].astype(BF16)
        return carry

    lax.fori_loop(0, D // 128, lane_block, 0)
    last = src[main : main + images, :].astype(F32)
    dst[main:, :] = jnp.concatenate([last, jnp.zeros((CLS - images, D), F32)], 0).astype(BF16)


def pack_vectors(vectors, dst):
    row = 0
    for v in vectors:
        count = v.shape[0] // 256
        wide = v[...].astype(F32)
        for k in range(count):
            dst[row : row + 1, :] = wide[k * 256 : (k + 1) * 256].reshape(1, 256)
            row += 1


def attend(i, qkv, qkv_cls, scores, probs, mix, probs_cls, att, att_cls, lse, lse_cls):
    rows = at(i, PATCH)
    mask = head_mask()
    own = qkv_cls[pl.ds(i, 1), :]
    q_c, k_c, v_c = own[:, :D] * FACTOR, own[:, D : 2 * D], own[:, 2 * D :]
    q_bd = jnp.where(mask, q_c, 0.0)
    k_bd = jnp.where(mask, k_c, 0.0).astype(BF16)
    v_bd = jnp.where(mask, v_c, 0.0).astype(BF16)
    to_cls = dot_nt(k_bd, qkv[rows, 0:D]) * FACTOR
    of_cls = dot_nt(q_bd.astype(BF16), qkv[rows, D : 2 * D])
    corner = jnp.sum(q_bd * k_c, axis=1, keepdims=True)
    top = jnp.maximum(jnp.max(of_cls, axis=1, keepdims=True), corner)
    e_row = jnp.exp(of_cls - top)
    e_cor = jnp.exp(corner - top)
    total = jnp.sum(e_row, axis=1, keepdims=True) + e_cor
    inv = 1.0 / total
    row = dot((e_row * inv).astype(BF16), qkv[rows, 2 * D : 3 * D])
    row = row + (e_cor * inv).astype(BF16).astype(F32) * v_c
    att_cls[pl.ds(i, 1), :] = jnp.sum(jnp.where(mask, row, 0.0), axis=0, keepdims=True)
    lse_cls[i] = jnp.broadcast_to(top + jnp.log(total), (HEADS, PATCH))
    for g in range(HEADS // 2):
        q2 = qkv[rows, g * 128 : g * 128 + 128] * jnp.asarray(FACTOR, BF16)
        scores[g] = dot_nt(split_pair(qkv[rows, g * 128 + D : g * 128 + D + 128]), q2)
    for g in range(HEADS // 2):
        for u in range(2):
            h = 2 * g + u
            part = scores[g, u * PATCH : (u + 1) * PATCH, :]
            extra = to_cls[h : h + 1, :]
            top = jnp.maximum(jnp.max(part, axis=0, keepdims=True), extra)
            e_part = jnp.exp(part - top)
            e_extra = jnp.exp(extra - top)
            total = jnp.sum(e_part, axis=0, keepdims=True) + e_extra
            inv = 1.0 / total
            probs[g, u * PATCH : (u + 1) * PATCH, :] = (e_part * inv).astype(BF16)
            probs_cls[h : h + 1, :] = e_extra * inv
            lse[i, h : h + 1, :] = top + jnp.log(total)
    for g in range(HEADS // 2):
        v2 = split_pair(qkv[rows, g * 128 + 2 * D : g * 128 + 2 * D + 128])
        mix[:, g * 128 : g * 128 + 128] = dot_tn(probs[g], v2)
    att[rows, :] = (mix[...] + dot_tn(probs_cls[...].astype(BF16), v_bd)).astype(BF16)


class Gather:
    KINDS = ("own", "far", "x1", "z1", "x2", "z2", "p0", "p1", "p2", "p3", "p4")

    def __init__(self, number, rows, src, dst, sems, local):
        s, r, x, z = place()
        sib, across, side = peers(s, r)
        self.number, self.sems = number, sems
        near = lax.rem(z, 2)
        level = {"replica": (z + 1 - 2 * near) * 2 + x}
        side, sib = {"replica": side}, {"shard": sib}
        size = rows // 4
        half = size // 2

        def start(zz, xx):
            return pl.multiple_of((2 * zz + xx) * size, 16)

        def same(first, count, to):
            ref = dst(across, pl.multiple_of(first, 16), count)
            return ref, ref, to

        mine, by_x, by_z, by_both = start(near, x), start(near, 1 - x), start(1 - near, x), start(1 - near, 1 - x)
        self.parts = {
            "own": (dst(s, 0, rows), dst(s, 0, rows), sib),
            "far": (dst(s, mine, size), dst(s, mine, size), {"shard": across}),
            "x1": same(mine, size, side),
            "z1": same(mine, size, level),
            "x2": same(by_z, half, side),
            "z2": same(by_x + half, half, level),
            "p0": same(mine, size, sib),
            "p1": same(by_x, size, sib),
            "p2": same(by_z, size, sib),
            "p3": same(by_both, half, sib),
            "p4": same(by_both + half, half, sib),
        }
        self.local = pltpu.make_async_copy(src(0, rows), dst(s, 0, rows), local.at[number])

    def copy(self, kind):
        a, b, to = self.parts[kind]
        k = self.KINDS.index(kind)
        return pltpu.make_async_remote_copy(
            a, b, self.sems.at[0, self.number, k], self.sems.at[1, self.number, k], device_id=to, device_id_type=MESH
        )

    def load(self):
        self.local.start()

    def begin(self):
        self.local.wait()
        self.copy("far").start()

    def share(self):
        self.copy("own").start()

    def on_far(self):
        self.copy("far").wait_recv()
        for kind in ("x1", "z1", "p0"):
            self.copy(kind).start()

    def on_near(self):
        self.copy("x1").wait_recv()
        self.copy("z2").start()
        self.copy("p1").start()
        self.copy("z1").wait_recv()
        self.copy("x2").start()
        self.copy("p2").start()

    def on_last(self):
        self.copy("x2").wait_recv()
        self.copy("p3").start()
        self.copy("z2").wait_recv()
        self.copy("p4").start()

    def ready(self):
        for kind in ("own", "p0", "p1", "p2", "p3", "p4"):
            self.copy(kind).wait_recv()

    def drain(self):
        for kind in self.KINDS:
            self.copy(kind).wait_send()


def relative_piece(s, rel):
    low, high = lax.rem(rel, 2), lax.div(rel, 2)
    return s + low * (1 - 2 * lax.rem(s, 2)) + high * (2 - 4 * lax.div(s, 2))


def unpack_bias_up(vec, bias_up):
    for p in range(4):
        for t in range(2):
            for k in range(2):
                row = 10 + 2 * t + k
                bias_up[2 * p + t : 2 * p + t + 1, k * 256 : (k + 1) * 256] = vec[p, row : row + 1, :].astype(F32)


def ffn_tile(act2, dr, dr_t, act2_t, w_up, w_down, bias, hid, br, gmid, fresh, on_back, on_hidden, put):
    n = act2.shape[0]
    cut = 16 * (n // 32)
    first, second = slice(0, cut), slice(cut, n)

    def both(rows, before, grad):
        hidden, step = gelu_both(before)
        hid[rows, :] = hidden.astype(BF16)
        grad = grad * step
        br[rows, :] = grad.astype(BF16)
        return jnp.sum(grad, axis=0, keepdims=True)

    def back(rows):
        out = dot_nt(br[rows, :], w_up())
        if fresh:
            gmid[rows, :] = out
        else:
            gmid[rows, :] += out

    before0 = dot(act2[first, :], w_up()) + bias
    grad0 = dot_nt(dr[first, :], w_down())
    before1 = dot(act2[second, :], w_up()) + bias
    column = both(first, before0, grad0)
    grad1 = dot_nt(dr[second, :], w_down())
    on_back()
    back(first)
    column = column + both(second, before1, grad1)
    back(second)
    on_hidden()
    put(0, dot(dr_t[...], hid[...]).astype(BF16))
    put(1, dot(act2_t[...], br[...]).astype(BF16))
    return column


def gather_kernel(
    tokens, cot, v0, v1, v2, v3, v4, v5, v6, v7, v8, v9, w_qkv, w_out, w_up, w_down,
    qkv_w_o, out_w_o, up_w_o, down_w_o, vec_all, qkv_o, act_t_o, x_o, att_t_o, mid_o, branch_o, act2_o, act2_t_o, up_o,
    dr_o, dr_t_o, lse_o, lsec_o, parts_o, hid_o, gact_o, column_o,
    full_qkv, full_out, full_up, full_down, x_s, qkv, act, att, mid, branch, act2, turned_a, turned_b, lse, lsec,
    scores, probs, mix, probs_cls, cls, qkv_cls, turn, vec32, vec_own_s, vec, vecf, bias_qkv,
    bias_up, column,
    sems, local, vsem, osem,
):
    s, r, x, z = place()
    sib, across, side = peers(s, r)
    n = x_s.shape[0]
    images = lse.shape[0]
    main = images * PATCH

    vec32[...] = jnp.zeros_like(vec32)
    pack_vectors((v0, v1, v2, v3, v4, v5, v6, v7, v8, v9), vec32)
    vec_own_s[...] = vec32[...].astype(BF16)
    barrier = pltpu.get_barrier_semaphore()
    level = (z + 1 - 2 * lax.rem(z, 2)) * 2 + x
    for to in ({"shard": sib}, {"shard": across}, {"replica": side}, {"replica": level}):
        pl.semaphore_signal(barrier, inc=1, device_id=to, device_id_type=MESH)

    def unit(number, rows, src, dst):
        return Gather(number, rows, src, dst, sems, local)

    def qkv_unit(number, t):
        cols = pl.ds(t * 3 * TILE, 3 * TILE)
        return unit(number, 256, lambda a, k: w_qkv.at[pl.ds(a, k), cols],
                    lambda p, a, k: full_qkv.at[pl.ds(pl.multiple_of(p * 256 + a, 16), k), cols])

    g_qa, g_qb = qkv_unit(0, 0), qkv_unit(6, 1)
    g_out = unit(1, 256, lambda a, k: w_out.at[pl.ds(a, k), :],
                 lambda p, a, k: full_out.at[pl.ds(pl.multiple_of(p * 256 + a, 16), k), :])

    def up_unit(number, t):
        cols = pl.ds(t * TILE, TILE)
        return unit(number, D, lambda a, k: w_up.at[pl.ds(a, k), cols],
                    lambda p, a, k: full_up.at[p, pl.ds(pl.multiple_of(a, 16), k), cols])

    def down_unit(number, t):
        return unit(number, TILE, lambda a, k: w_down.at[pl.ds(a + t * TILE, k), :],
                    lambda p, a, k: full_down.at[p, pl.ds(pl.multiple_of(a + t * TILE, 16), k), :])

    g_up0, g_down0, g_up1, g_down1 = up_unit(2, 0), down_unit(3, 0), up_unit(4, 1), down_unit(5, 1)

    for g in (g_qa, g_qb, g_out, g_up0, g_down0, g_up1, g_down1):
        g.load()
    pl.semaphore_wait(barrier, 4)

    def vec_copy(k, src, slot, to):
        return pltpu.make_async_remote_copy(src, vec.at[slot], vsem.at[0, k], vsem.at[1, k], device_id=to,
                                            device_id_type=MESH)

    vec_own = vec_copy(0, vec_own_s, s, {"shard": sib})
    vec_far = vec_copy(1, vec_own_s, s, {"shard": across})
    vec_pass = vec_copy(2, vec.at[across], across, {"shard": sib})
    vec_own.start()
    vec_far.start()
    for g in (g_qa, g_qb):
        g.begin()
        g.share()
    g_out.begin()
    vec[s] = vec_own_s[...]

    to_images(tokens, x_s, turn)
    outs = {}

    def send_out(k, src, dst):
        outs[k] = pltpu.make_async_copy(src, dst, osem.at[k])
        outs[k].start()

    send_out(0, x_s, x_o)
    vec_far.wait_recv()
    vec_pass.start()
    vec_own.wait_recv()
    vec_pass.wait_recv()
    unpack_vectors(vec, vecf, bias_qkv)
    g_qa.on_far()

    def first_norm(rows):
        act[rows, :] = layer_norm(x_s[rows, :].astype(F32), vecf[0:1, :], vecf[1:2, :]).astype(BF16)

    rows_loop(n, 16, first_norm)
    g_qa.on_near()
    g_qb.on_far()
    for g in (g_up0, g_down0, g_up1, g_down1):
        g.begin()
    transpose_into(act, turned_b)
    send_out(1, turned_b, act_t_o)
    to_images(cot, branch, turn)
    g_qa.on_last()
    g_qb.on_near()

    def down_rows(rows):
        act2[rows, :] = (branch[rows, :].astype(F32) * vecf[7:8, :]).astype(BF16)

    rows_loop(n, 16, down_rows)
    send_out(14, branch, up_o)
    send_out(15, act2, dr_o)
    transpose_into(act2, turned_a)
    send_out(16, turned_a, dr_t_o)
    g_qb.on_last()
    g_out.on_far()
    g_qa.ready()

    def qkv_tile(j, carry):
        cols = at(j, TILE)
        low = (dot(act[...], full_qkv[:, cols]) + bias_qkv[0:1, cols]).astype(BF16)
        qkv[:, cols] = low
        qkv_cls[:, cols] = low[main:].astype(F32)
        return carry

    lax.fori_loop(0, 3, qkv_tile, 0)
    g_out.on_near()
    g_qb.ready()
    send_out(4, full_qkv, qkv_w_o)
    for g in (g_out, g_up0, g_down0):
        g.share()
    lax.fori_loop(3, 6, qkv_tile, 0)
    send_out(2, qkv, qkv_o)
    act[...] = act2[...]
    unpack_bias_up(vec, bias_up)
    column[...] = jnp.zeros_like(column)
    send_out(3, vec, vec_all)
    cls[...] = jnp.zeros_like(cls)
    g_out.on_last()
    g_up0.on_far()
    plan = {1: [g_up0.on_near], 2: [g_down0.on_far], 3: [g_up0.on_last, g_up1.share], 4: [g_down0.on_near, g_up1.on_far],
            6: [g_down0.on_last, g_down1.share], 7: [g_up1.on_near, g_down1.on_far]}

    def image(i, carry):
        for k, steps in plan.items():
            @pl.when(i == k)
            def _(steps=steps):
                for step in steps:
                    step()

        attend(i, qkv, qkv_cls, scores, probs, mix, probs_cls, att, cls, lse, lsec)
        return carry

    lax.fori_loop(0, images, image, 0)
    att[main:, :] = cls[...].astype(BF16)
    outs.pop(1).wait()
    transpose_into(att, turned_b)
    send_out(8, turned_b, att_t_o)
    send_out(9, lse, lse_o)
    send_out(10, lsec, lsec_o)
    g_out.ready()
    outs.pop(14).wait()
    for j in range(D // TILE):
        cols = slice(j * TILE, (j + 1) * TILE)
        out = dot(att[...], full_out[:, cols]) + vecf[2:3, cols]
        branch[:, cols] = out.astype(BF16)
        mid[:, cols] = x_s[:, cols].astype(F32) + vecf[3:4, cols] * out
    send_out(11, mid, mid_o)
    send_out(12, branch, branch_o)
    g_up1.on_last()
    g_down1.on_near()

    def second_norm(rows):
        act2[rows, :] = layer_norm(mid[rows, :], vecf[4:5, :], vecf[5:6, :]).astype(BF16)

    outs.pop(15).wait()
    rows_loop(n, 16, second_norm)
    send_out(13, act2, act2_o)
    outs.pop(8).wait()
    transpose_into(act2, turned_b)
    send_out(17, turned_b, act2_t_o)
    half = pl.ds(0, TILE)
    rest = pl.ds(TILE, TILE)
    send_out(5, full_out, out_w_o)
    g_up0.ready()
    send_out(18, full_up.at[:, :, half], up_w_o.at[:, :, half])
    g_down0.ready()
    send_out(19, full_down.at[:, half, :], down_w_o.at[:, half, :])
    for k in (2, 11):
        outs.pop(k).wait()
    hid, br = qkv.at[:, pl.ds(0, TILE)], qkv.at[:, pl.ds(TILE, TILE)]
    for k, rel in enumerate((3, 2)):
        piece = relative_piece(s, rel)

        def put(half_k, value, k=k):
            qkv[0:D, (2 + 2 * k + half_k) * TILE : (3 + 2 * k + half_k) * TILE] = value

        if k:
            outs.pop(22).wait()
        column[pl.ds(2 * piece, 1), :] = ffn_tile(
            act2, act, turned_a, turned_b, lambda: full_up[piece, :, 0:TILE], lambda: full_down[piece, 0:TILE, :],
            bias_up[pl.ds(2 * piece, 1), :], hid, br, mid, k == 0, lambda: None, lambda: send_out(22 + k, hid, hid_o.at[k]), put)
        for half_k in range(2):
            send_out(24 + 2 * k + half_k, qkv.at[pl.ds(0, D), pl.ds((2 + 2 * k + half_k) * TILE, TILE)],
                     parts_o.at[k, pl.ds(half_k * D, D), :])
        if k == 0:
            g_down1.on_last()
            g_up1.ready()
            send_out(20, full_up.at[:, :, rest], up_w_o.at[:, :, rest])
    send_out(28, mid, gact_o)
    send_out(29, column, column_o)
    g_down1.ready()
    send_out(21, full_down.at[:, rest, :], down_w_o.at[:, rest, :])
    for copy in outs.values():
        copy.wait()
    for g in (g_qa, g_qb, g_out, g_up0, g_down0, g_up1, g_down1):
        g.drain()
    for copy in (vec_own, vec_far, vec_pass):
        copy.wait_send()


class Chunk:
    def __init__(self, index, rows, mine, y_send, y_recv, x_recv, z_recv, far):
        self.index, self.rows, self.mine, self.y_send, self.far = index, rows, mine, y_send, far
        self.y_recv, self.x_recv, self.z_recv = y_recv, x_recv, z_recv


def chunk_layout(nz):
    sizes = [1024, 1024, 1024, 1024, 512, 512, 512, 512]
    y_base = 2048
    y_a = y_base
    y_b = y_a + 2048
    mine_base = y_b + 2048
    chunks = []
    mine = mine_base
    late = 0
    xr = zr = 0
    for k, rows in enumerate(sizes):
        if k < 2:
            ys, yr = y_a + 1024 * k, 1024 * k
        elif k < 4:
            ys, yr = y_b + 1024 * (k - 2), 2048 + 1024 * (k - 2)
        else:
            ys, yr = y_a + late, late
            late += rows
        far = mine_base + sum(sizes) + 512 * k if k < 2 else ys
        chunks.append(Chunk(k, rows, mine, ys, yr, xr, zr, far))
        mine += rows
        xr += rows // 2
        zr += rows // 2 // nz
    return chunks, dict(buf=mine + 1024, total=sum(sizes), mine=mine_base, y_recv=2 * 2048, x_recv=xr, z_recv=zr)


def add_rows(dst, d0, src, s0, rows):
    step = next(k for k in (128, 96, 64, 32, 16) if rows % k == 0)

    def body(k, carry):
        d = pl.ds(pl.multiple_of(d0 + k * step, 16), step)
        t = pl.ds(pl.multiple_of(s0 + k * step, 16), step)
        dst[d, :] = (dst[d, :].astype(F32) + src[t, :].astype(F32)).astype(BF16)
        return carry

    lax.fori_loop(0, rows // step, body, 0)


class Reduce:
    def __init__(self, nz, buf, core_recv, y_recv, x_recv, z_recv, sems, core_sems, credit):
        self.nz, self.buf, self.core_recv = nz, buf, core_recv
        self.y_recv, self.x_recv, self.z_recv = y_recv, x_recv, z_recv
        self.sems, self.core_sems, self.credit = sems, core_sems, credit
        self.s, self.r, self.x, self.z = place()
        self.sib, self.across, self.side = peers(self.s, self.r)

    def remote(self, src, dst, chunk, kind, to):
        return pltpu.make_async_remote_copy(
            src, dst, self.sems.at[0, chunk.index, kind], self.sems.at[1, chunk.index, kind], device_id=to,
            device_id_type=MESH)

    def peer(self, k):
        return {"replica": lax.rem(self.z + k, self.nz) * 2 + self.x}

    def core_copy(self, turn, rows):
        slot = turn % 2
        return pltpu.make_async_remote_copy(
            self.buf.at[pl.ds(slot * 1024 if turn > 3 else 0, rows), :], self.core_recv.at[slot, pl.ds(0, rows), :],
            self.core_sems.at[0, turn], self.core_sems.at[1, turn], device_id={"shard": self.sib}, device_id_type=MESH)

    def add_core(self, turn, first, dst, rows):
        add_rows(self.buf, dst, self.core_recv.at[turn % 2], first, rows)

    def y_copy(self, c):
        return self.remote(self.buf.at[pl.ds(c.y_send, c.rows), :], self.y_recv.at[pl.ds(c.y_recv, c.rows), :], c, 0,
                           {"shard": self.across})

    def x_copy(self, c):
        half = c.rows // 2
        return self.remote(self.buf.at[pl.ds(pl.multiple_of(c.mine + (1 - self.x) * half, 16), half), :],
                           self.x_recv.at[pl.ds(c.x_recv, half), :], c, 1, {"replica": self.side})

    def quarter(self, c, x, z):
        half = c.rows // 2
        size = half // self.nz
        return pl.ds(pl.multiple_of(c.mine + x * half + z * size, 16), size)

    def z_copy(self, c, k):
        size = c.rows // 2 // self.nz
        return self.remote(self.buf.at[self.quarter(c, self.x, lax.rem(self.z + k, self.nz)), :],
                           self.z_recv.at[k - 1, pl.ds(c.z_recv, size), :], c, 1 + k, self.peer(k))

    def done(self, first, c, z):
        size = c.rows // 2 // self.nz
        return pl.ds(pl.multiple_of(first + z * size, 16), size)

    def back_z(self, c, k):
        part = self.x_recv.at[self.done(c.x_recv, c, self.z), :]
        return self.remote(part, part, c, self.nz + k, self.peer(k))

    def back_x(self, c, k):
        z = lax.rem(self.z + self.nz - k, self.nz)
        return self.remote(self.x_recv.at[self.done(c.x_recv, c, z), :], self.buf.at[self.done(c.far, c, z), :], c,
                           2 * self.nz + k, {"replica": self.side})

    def on_y(self, c):
        self.y_copy(c).wait_recv()
        add_rows(self.buf, c.mine, self.y_recv, c.y_recv, c.rows)
        self.y_copy(c).wait_send()
        self.x_copy(c).start()

    def on_x(self, c):
        half = c.rows // 2
        self.x_copy(c).wait_recv()
        add_rows(self.buf, c.mine + self.x * half, self.x_recv, c.x_recv, half)
        for k in range(1, self.nz):
            self.z_copy(c, k).start()

    def on_z(self, c):
        size = c.rows // 2 // self.nz
        start = c.mine + self.x * (c.rows // 2) + self.z * size
        for k in range(1, self.nz):
            self.z_copy(c, k).wait_recv()
        step = next(k for k in (64, 48, 32, 16) if size % k == 0)

        def body(i, carry):
            d = pl.ds(pl.multiple_of(start + i * step, 16), step)
            total = self.buf[d, :].astype(F32)
            for k in range(1, self.nz):
                total = total + self.z_recv[k - 1, pl.ds(pl.multiple_of(c.z_recv + i * step, 16), step), :].astype(F32)
            to = pl.ds(pl.multiple_of(c.x_recv + self.z * size + i * step, 16), step)
            self.x_recv[to, :] = total.astype(BF16)
            return carry

        lax.fori_loop(0, size // step, body, 0)
        for k in range(1, self.nz):
            self.back_z(c, k).start()
        self.back_x(c, 0).start()

    def on_back(self, c):
        for k in range(1, self.nz):
            self.back_z(c, k).wait_recv()
            self.back_x(c, k).start()

    def finish(self, c):
        for k in range(self.nz):
            self.back_x(c, k).wait_recv()

    def drain(self, c):
        self.x_copy(c).wait_send()
        for k in range(1, self.nz):
            self.z_copy(c, k).wait_send()
            self.back_z(c, k).wait_send()
        for k in range(self.nz):
            self.back_x(c, k).wait_send()


def fold(v):
    return jnp.sum(v.reshape(v.shape[0] // 8, 8, v.shape[1]), axis=0)


def gelu_both(v):
    e = jnp.exp(-0.5 * v * v)
    t = 1.0 / (1.0 + 0.23164189 * jnp.abs(v))
    poly = ((((1.061405429 * t - 1.453152027) * t + 1.421413741) * t - 0.284496736) * t + 0.254829592) * t
    tail = 0.5 * poly * e
    phi = jnp.where(v >= 0.0, 1.0 - tail, tail)
    return v * phi, phi + v * e * 0.3989422804014327


def transpose_into(src, dst):
    for c in range(D // 128):
        dst[c * 128 : (c + 1) * 128, :] = src[:, c * 128 : (c + 1) * 128].T


def attend_back(
    i, qkv, qkv_cls, datt, datt_cls, lse, lsec, scores, dprobs, probs, dscores, cls_row, joint_cls, joint, extra, sum_q, sum_v
):
    rows = at(i, PATCH)
    mask = head_mask()
    own = qkv_cls[pl.ds(i, 1), :]
    do_c = datt_cls[pl.ds(i, 1), :]
    q_c, k_c, v_c = own[:, :D] * FACTOR, own[:, D : 2 * D], own[:, 2 * D :]
    pick = lambda v: jnp.where(mask, v, 0.0)
    q_w, k_w, v_w, do_w = pick(q_c), pick(k_c), pick(v_c), pick(do_c)
    q_bd, k_bd, v_bd, do_bd = (v.astype(BF16) for v in (q_w, k_w, v_w, do_w))
    queries, keys, values = (qkv[rows, k * D : (k + 1) * D] for k in range(3))
    grads = datt[rows, :]
    low = lambda v: v.astype(BF16)
    top = lsec[i][:, 0:1]
    p_row = jnp.exp(dot_nt(q_bd, keys) - top)
    p_cor = jnp.exp(jnp.sum(q_w * k_c, axis=1, keepdims=True) - top)
    dp_row = dot_nt(do_bd, values)
    dp_cor = jnp.sum(do_w * v_c, axis=1, keepdims=True)
    delta = jnp.sum(p_row * dp_row, axis=1, keepdims=True) + p_cor * dp_cor
    ds_row = low(p_row * (dp_row - delta))
    ds_cor = low(p_cor * (dp_cor - delta)).astype(F32)
    p_col = jnp.exp(dot_nt(k_bd, queries) * FACTOR - lse[i])
    dp_col = dot_nt(v_bd, grads)
    for g in range(HEADS // 2):
        lanes = slice(g * 128, (g + 1) * 128)
        q2 = qkv[rows, lanes] * jnp.asarray(FACTOR, BF16)
        scores[g] = dot_nt(split_pair(qkv[rows, g * 128 + D : g * 128 + D + 128]), q2)
        dprobs[g] = dot_nt(split_pair(qkv[rows, g * 128 + 2 * D : g * 128 + 2 * D + 128]), datt[rows, lanes])
    for g in range(HEADS // 2):
        for u in range(2):
            h = 2 * g + u
            half = slice(u * PATCH, (u + 1) * PATCH)
            part = jnp.exp(scores[g, half, :] - lse[i, h : h + 1, :])
            dpart = dprobs[g, half, :]
            p_h, dp_h = p_col[h : h + 1, :], dp_col[h : h + 1, :]
            delta = jnp.sum(part * dpart, axis=0, keepdims=True) + p_h * dp_h
            probs[g, half, :] = low(part)
            dscores[g, half, :] = low(part * (dpart - delta))
            cls_row[h : h + 1, :] = p_h * (dp_h - delta)
    ds_col = low(cls_row[...])
    total = lambda v: jnp.sum(jnp.where(mask, v, 0.0), axis=0, keepdims=True)
    joint_cls[pl.ds(i, 1), 0:D] = FACTOR * (total(dot(ds_row, keys)) + jnp.sum(ds_cor * k_w, axis=0, keepdims=True))
    joint_cls[pl.ds(i, 1), D : 2 * D] = FACTOR * total(dot(ds_col, queries)) + jnp.sum(ds_cor * q_w, axis=0, keepdims=True)
    joint_cls[pl.ds(i, 1), 2 * D : 3 * D] = total(dot(low(p_col), grads)) + jnp.sum(
        low(p_cor).astype(F32) * do_w, axis=0, keepdims=True)
    extra[0] = dot_tn(ds_col, k_bd) * FACTOR
    extra[1] = dot_tn(ds_row, q_bd)
    extra[2] = dot_tn(low(p_row), do_bd)
    for g in range(HEADS // 2):
        lanes = slice(g * 128, (g + 1) * 128)
        klanes = slice(g * 128 + D, g * 128 + D + 128)
        vlanes = slice(g * 128 + 2 * D, g * 128 + 2 * D + 128)
        q2 = qkv[rows, lanes] * jnp.asarray(FACTOR, BF16)
        dv = merge_pair(dot(probs[g], datt[rows, lanes])) + extra[2, :, lanes]
        dk = merge_pair(dot(dscores[g], q2)) + extra[1, :, lanes]
        dq = dot_tn(dscores[g], split_pair(qkv[rows, klanes])) * FACTOR + extra[0, :, lanes]
        joint[:, lanes] = low(dq)
        joint[:, klanes] = low(dk)
        joint[:, vlanes] = low(dv)
        sum_q[:, lanes] += fold(dq)
        sum_v[:, lanes] += fold(dv)
    qkv[rows, :] = joint[...]


def to_tokens(src, dst, turn):
    images = dst.shape[0] // (PATCH + 1)
    main = images * PATCH

    def lane_block(l, carry):
        cols = at(l, 128)
        slot = lax.rem(l, 2)
        for i in range(images):
            turn[slot, pl.ds(i, PATCH, stride=images), :] = src[i * PATCH : (i + 1) * PATCH, cols].astype(F32)
        dst[0:main, cols] = turn[slot].astype(BF16)
        return carry

    lax.fori_loop(0, D // 128, lane_block, 0)
    dst[main : main + images, :] = src[main:, :].astype(F32)[0:images].astype(BF16)


def backward_kernel(
    nz, chunks, vec, full_qkv, full_out, full_up, full_down, qkv_h, act_t_h, x_h, att_t_h, mid_h, branch_h, act2_h,
    act2_t_h, up_h, dr_h, dr_t_h, lse_h, lsec_h, parts_h, hid_h, gact_h, column_h,
    result_o, tokens_o, sums_o, small_o, hidden_o,
    buf, core_recv, y_recv, x_recv, z_recv, gmid, grad_mid, up_s, acc, sums_up, vecf, bias_qkv, bias_up, v_part, v_group, v_sum, v_all,
    sems, core_sems, group_sems, all_sems, credit, dsem, wsem, hsem, osem, fsem,
):
    images = lse_h.shape[0]
    n = gmid.shape[0]
    main = images * PATCH
    red = Reduce(nz, buf, core_recv, y_recv, x_recv, z_recv, sems, core_sems, credit)
    s = red.s
    cd0, cu0, cd1, cu1, co, *cq = chunks

    def load(k, src, dst):
        copy = pltpu.make_async_copy(src, dst, dsem.at[k])
        copy.start()
        return copy

    def relative(rel):
        return relative_piece(s, rel)

    def target(rel, chunk, base):
        low, high = lax.rem(rel, 2), lax.div(rel, 2)
        return low * (base + (1 - high) * chunk.rows) + (1 - low) * (high * chunk.y_send + (1 - high) * chunk.mine)

    def group_peer(k):
        return {"shard": lax.rem(s + k, 4)}

    def replica_peer(k):
        return {"replica": lax.rem(red.r + k, 2 * nz)}

    def group_copy(k):
        return pltpu.make_async_remote_copy(
            v_part.at[lax.rem(s + k, 4)], v_group.at[k - 1], group_sems.at[0, k - 1], group_sems.at[1, k - 1],
            device_id=group_peer(k), device_id_type=MESH)

    def all_copy(k):
        return pltpu.make_async_remote_copy(
            v_sum, v_all.at[red.r], all_sems.at[0, k - 1], all_sems.at[1, k - 1], device_id=replica_peer(k),
            device_id_type=MESH)

    got_up = load(7, up_h, up_s)

    def ffn(dr, dr_t, act2, act2_t, w_up, w_down, hid, br):
        def fetch(j, slot):
            piece, t = relative(3 - lax.rem(j, 4)), lax.div(j, 4)
            return (
                pltpu.make_async_copy(full_up.at[piece, :, at(t, TILE)], w_up.at[slot], wsem.at[0, slot]),
                pltpu.make_async_copy(full_down.at[piece, at(t, TILE), :], w_down.at[slot], wsem.at[1, slot]),
            )

        for copy in fetch(2, 0):
            copy.start()
        got_parts, got_act2, got_dr = (load(8, parts_h.at[0], buf.at[pl.ds(0, 2048), :]), load(0, act2_h, act2),
                                       load(1, dr_h, dr))
        got_gact, got_column = load(10, gact_h, gmid), load(11, column_h, sums_up)
        gots = [got_parts, load(9, parts_h.at[1], buf.at[pl.ds(cd0.y_send, 2048), :]), got_act2, got_dr,
                load(2, dr_t_h, dr_t), load(3, act2_t_h, act2_t), got_gact, got_column]

        def keep(j, slot):
            return pltpu.make_async_copy(hid.at[slot], hidden_o.at[j - 2], hsem.at[slot])

        barrier = pltpu.get_barrier_semaphore()
        partners = [group_peer(k) for k in range(1, 4)] + [replica_peer(k) for k in range(1, 2 * nz)]
        for to in partners:
            pl.semaphore_signal(barrier, inc=1, device_id=to, device_id_type=MESH)
        pl.semaphore_wait(barrier, len(partners))
        unpack_vectors(vec, vecf, bias_qkv)
        unpack_bias_up(vec, bias_up)
        acc[...] = jnp.zeros_like(acc)
        gots[0].wait()
        red.core_copy(0, 2048).start()
        late = gots[4:6]
        for copy in gots[2:4]:
            copy.wait()

        def tile(j, carry):
            slot = lax.rem(j, 2)
            rel, t = 3 - lax.rem(j, 4), lax.div(j, 4)
            piece = relative(rel)
            low, high = lax.rem(rel, 2), lax.div(rel, 2)
            place_at = pl.multiple_of(
                (1 - low) * (high * (cd0.y_send + t * (cd1.y_send - cd0.y_send)) + (1 - high) * (cd0.mine + t * 2048)), 16)
            for copy in fetch(j, slot):
                copy.wait()

            @pl.when(j < 7)
            def _():
                for copy in fetch(j + 1, 1 - slot):
                    copy.start()

            @pl.when(j >= 4)
            def _():
                keep(j - 2, slot).wait()

            for k in (2, 4, 6):
                @pl.when(j == k)
                def _(k=k):
                    red.core_copy(k // 2 - 1, 2048).wait_send()

            def on_back():
                @pl.when(j == 2)
                def _():
                    for copy in gots[1:2] + gots[6:]:
                        copy.wait()

            def on_hidden():
                keep(j, slot).start()

                @pl.when(j == 2)
                def _():
                    for copy in late:
                        copy.wait()

            def put(half, value):
                buf[pl.ds(pl.multiple_of(place_at + half * D, 16), D), :] = value

            sums_up[pl.ds(2 * piece + t, 1), :] = ffn_tile(
                act2, dr, dr_t, act2_t, lambda: w_up[slot], lambda: w_down[slot], bias_up[pl.ds(2 * piece + t, 1), :],
                hid.at[slot], br, gmid, False, on_back, on_hidden, put)

            def y_part(turn, chunk):
                red.core_copy(turn, 2048).wait_recv()
                for k, c in enumerate(chunk):
                    red.add_core(turn, k * 1024, c.y_send, c.rows)
                    red.y_copy(c).start()

            def own_part(turn, chunk):
                red.core_copy(turn, 2048).wait_recv()
                red.add_core(turn, 0, chunk[0].mine, 2048)

            steps = {
                2: [lambda: y_part(0, (cd0, cu0)), lambda: red.core_copy(1, 2048).start()],
                3: [lambda: own_part(1, (cd0, cu0))],
                4: [lambda: red.core_copy(2, 2048).start()],
                5: [lambda: y_part(2, (cd1, cu1)), lambda: red.on_y(cd0)],
                6: [lambda: red.core_copy(3, 2048).start(), lambda: red.on_x(cd0)],
                7: [lambda: own_part(3, (cd1, cu1)), lambda: red.on_y(cu0)],
            }
            for k, todo in steps.items():
                @pl.when(j == k)
                def _(todo=todo):
                    for step in todo:
                        step()
            return carry

        lax.fori_loop(2, 8, tile, 0)
        pl.semaphore_signal(credit, inc=1, device_id={"shard": red.across}, device_id_type=MESH)
        for j in (6, 7):
            keep(j, j % 2).wait()
        red.core_copy(3, 2048).wait_send()

    v = pltpu.VMEM
    pl.run_scoped(ffn, v((n, D), BF16), v((D, n), BF16), v((n, D), BF16), v((D, n), BF16), v((2, D, TILE), BF16),
                  v((2, TILE, D), BF16), v((2, n, TILE), BF16), v((n, TILE), BF16))
    got_up.wait()

    def spread(out, chunk, tile_rows, turn):
        for p in range(4):
            low = lax.rem(lax.rem(s, 2) + p % 2, 2)
            high = lax.rem(lax.div(s, 2) + p // 2, 2)
            start = pl.multiple_of(target(low + 2 * high, chunk, 1024 * (turn % 2)) + tile_rows, 16)
            buf[pl.ds(start, 256), :] = out[p * 256 : (p + 1) * 256].astype(BF16)

    def on_core(turn, chunk):
        red.core_copy(turn, 2 * chunk.rows).wait_recv()
        red.add_core(turn, 0, chunk.y_send, chunk.rows)
        red.y_copy(chunk).start()
        red.add_core(turn, chunk.rows, chunk.mine, chunk.rows)

    def attention(
        qkv, datt, brr, lse, lsec, scores, dprobs, probs, dscores, cls_row, qkv_cls, datt_cls, joint_cls, joint, extra
    ):
        got_qkv, got_lse, got_lsec = load(0, qkv_h, qkv), load(1, lse_h, lse), load(2, lsec_h, lsec)

        def middle(mid, branch, att_t, w_out):
            got_mid, got_branch = load(3, mid_h, mid), load(4, branch_h, branch)
            got_att, got_out = load(5, att_t_h, att_t), load(6, full_out, w_out)
            red.on_z(cd0)
            got_mid.wait()
            got_branch.wait()

            def norm_rows(rows):
                m = mid[rows, :]
                c = m - jnp.mean(m, axis=-1, keepdims=True)
                inv = lax.rsqrt(jnp.mean(c * c, axis=-1, keepdims=True) + 1e-06)
                hat = c * inv
                g = gmid[rows, :]
                acc[4] += fold(g * hat)
                acc[5] += fold(g)
                sc = g * vecf[4:5, :]
                back = inv * (sc - jnp.mean(sc, axis=-1, keepdims=True)
                              - hat * jnp.mean(sc * hat, axis=-1, keepdims=True))
                gm = up_s[rows, :].astype(F32) + back
                grad_mid[rows, :] = gm
                acc[3] += fold(gm * branch[rows, :].astype(F32))
                gb = gm * vecf[3:4, :]
                acc[2] += fold(gb)
                brr[rows, :] = gb.astype(BF16)

            rows_loop(n, 16, norm_rows)
            got_att.wait()
            for q in range(2):
                spread(dot(att_t[...], brr[:, q * TILE : (q + 1) * TILE]), co, q * 256, 4)
            red.core_copy(4, 2 * co.rows).start()
            got_out.wait()
            for q in range(2):
                datt[:, q * TILE : (q + 1) * TILE] = dot_nt(brr[...], w_out[q * TILE : (q + 1) * TILE, :]).astype(BF16)
            red.on_x(cu0)

        pl.run_scoped(middle, v((n, D), F32), v((n, D), BF16), v((D, n), BF16), v((D, D), BF16))
        got_qkv.wait()
        got_lse.wait()
        got_lsec.wait()
        qkv_cls[...] = qkv[main:, :].astype(F32)
        datt_cls[...] = datt[main:, :].astype(F32)
        joint_cls[...] = jnp.zeros_like(joint_cls)
        pl.semaphore_wait(credit, 1)
        on_core(4, co)
        plan = {0: [lambda: red.on_y(cd1), lambda: red.on_back(cd0)], 3: [lambda: red.on_z(cu0)], 5: [lambda: red.on_x(cd1)],
                6: [lambda: red.on_y(cu1), lambda: red.on_back(cu0)]}

        def image(i, carry):
            for k, steps in plan.items():
                @pl.when(i == k)
                def _(steps=steps):
                    for step in steps:
                        step()

            attend_back(i, qkv, qkv_cls, datt, datt_cls, lse, lsec, scores, dprobs, probs, dscores, cls_row, joint_cls,
                        joint, extra, acc.at[8], acc.at[9])
            return carry

        lax.fori_loop(0, images, image, 0)
        qkv[main:, :] = joint_cls[...].astype(BF16)
        acc[8] += fold(joint_cls[:, 0:D])
        acc[9] += fold(joint_cls[:, 2 * D : 3 * D])

        def tail(act_t, w_qkv, turn, flat):
            x_s, gact, new = brr, gmid, datt
            got_act, got_x = load(3, act_t_h, act_t), load(4, x_h, x_s)

            def fetch(j):
                return pltpu.make_async_copy(full_qkv.at[pl.ds(j * 256, 256), :], w_qkv.at[j % 2], wsem.at[0, j % 2])

            fetch(0).start()
            fetch(1).start()
            def weight_grad(k):
                for q in range(2):
                    cols = slice((2 * k + q) * TILE, (2 * k + q + 1) * TILE)
                    spread(dot(act_t[...], qkv[:, cols]), cq[k], q * 256, 5 + k)

            def input_grad(j):
                fetch(j).wait()
                gact[:, j * 256 : (j + 1) * 256] = dot_nt(qkv[...], w_qkv[j % 2])
                if j < 2:
                    fetch(j + 2).start()

            got_act.wait()
            weight_grad(0)
            red.core_copy(5, 1024).start()
            red.on_z(cd1)
            red.core_copy(4, 1024).wait_send()
            weight_grad(1)
            on_core(5, cq[0])
            red.core_copy(6, 1024).start()
            red.on_y(co)
            red.core_copy(5, 1024).wait_send()
            weight_grad(2)
            on_core(6, cq[1])
            red.core_copy(7, 1024).start()
            red.on_x(cu1)
            red.on_back(cd1)
            input_grad(0)
            input_grad(1)
            on_core(7, cq[2])
            red.on_x(co)
            input_grad(2)
            red.on_y(cq[0])
            input_grad(3)
            red.on_z(cu1)
            got_x.wait()

            def norm_rows(rows):
                m = x_s[rows, :].astype(F32)
                c = m - jnp.mean(m, axis=-1, keepdims=True)
                inv = lax.rsqrt(jnp.mean(c * c, axis=-1, keepdims=True) + 1e-06)
                hat = c * inv
                g = gact[rows, :]
                acc[0] += fold(g * hat)
                acc[1] += fold(g)
                sc = g * vecf[0:1, :]
                back = inv * (sc - jnp.mean(sc, axis=-1, keepdims=True)
                              - hat * jnp.mean(sc * hat, axis=-1, keepdims=True))
                new[rows, :] = (grad_mid[rows, :] + back).astype(BF16)

            rows_loop(n, 16, norm_rows)
            red.on_z(co)
            red.on_x(cq[0])
            to_tokens(new, flat, turn)
            copy = pltpu.make_async_copy(flat, tokens_o, osem.at[0])
            copy.start()
            red.on_back(cu1)
            red.on_back(co)
            red.on_y(cq[1])
            copy.wait()

        pl.run_scoped(tail, v((D, n), BF16), v((2, 256, 3 * D), BF16),
                      v((2, main, 128), F32), v((main + images, D), BF16))

    pl.run_scoped(attention, v((n, 3 * D), BF16), v((n, D), BF16), v((n, D), BF16), v((images, HEADS, PATCH), F32),
                  v((images, HEADS, PATCH), F32), v((8, 256, PATCH), F32), v((8, 256, PATCH), F32),
                  v((8, 256, PATCH), BF16), v((8, 256, PATCH), BF16), v((HEADS, PATCH), F32), v((CLS, 3 * D), F32),
                  v((CLS, D), F32), v((CLS, 3 * D), F32), v((PATCH, 3 * D), BF16), v((3, PATCH, D), F32))

    def outcome(mid, hid, w_down, turn, flat, res):
        got_mid = load(3, mid_h, mid)

        def fetch(pair):
            copies = []
            for k in range(2):
                j = 2 * pair + k
                slot = pair % 2
                piece, t = relative(3 - j % 4), j // 4
                src = hid_h.at[k] if pair == 0 else hidden_o.at[j - 2]
                copies.append(pltpu.make_async_copy(src, hid.at[slot, :, pl.ds(k * TILE, TILE)], wsem.at[0, 2 * slot + k]))
                copies.append(pltpu.make_async_copy(full_down.at[piece, pl.ds(t * TILE, TILE), :],
                                                    w_down.at[slot, pl.ds(k * TILE, TILE), :], wsem.at[1, 2 * slot + k]))
            return copies

        for copy in fetch(0):
            copy.start()
        steps = {0: [lambda: red.on_z(cq[0]), lambda: red.on_x(cq[1])], 1: [lambda: red.on_back(cq[0])],
                 2: [lambda: red.on_y(cq[2]), lambda: red.on_z(cq[1])], 3: [lambda: red.on_back(cq[1])]}
        for pair in range(4):
            if pair < 3:
                for copy in fetch(pair + 1):
                    copy.start()
            for copy in fetch(pair):
                copy.wait()
            for q in range(2):
                cols = slice(q * TILE, (q + 1) * TILE)
                out = dot(hid[pair % 2], w_down[pair % 2, :, cols])
                if pair:
                    gmid[:, cols] += out
                else:
                    gmid[:, cols] = out
            for step in steps.get(pair, []):
                step()
        got_mid.wait()

        def rows_of(rows):
            projected = gmid[rows, :] + vecf[6:7, :]
            upstream = up_s[rows, :].astype(F32)
            acc[6] += fold(upstream * vecf[7:8, :])
            acc[7] += fold(upstream * projected)
            res[rows, :] = (mid[rows, :] + vecf[7:8, :] * projected).astype(BF16)

        rows_loop(n, 16, rows_of)
        for p in range(4):
            for k in range(8):
                v_part[p, k : k + 1, :] = jnp.sum(acc[k, :, p * 256 : (p + 1) * 256], axis=0, keepdims=True)
            joint = acc.at[8 + p // 2]
            for k in range(2):
                start = (p % 2) * TILE + k * 256
                v_part[p, 8 + k : 9 + k, :] = jnp.sum(joint[:, start : start + 256], axis=0, keepdims=True)
            for k in range(4):
                v_part[p, 10 + k : 11 + k, :] = sums_up[2 * p + k // 2 : 2 * p + k // 2 + 1, (k % 2) * 256 : (k % 2 + 1) * 256]
            v_part[p, 14:16, :] = jnp.zeros((2, 256), F32)
        for k in range(1, 4):
            group_copy(k).start()
        red.on_x(cq[2])
        total = v_part[s]
        for k in range(1, 4):
            group_copy(k).wait_recv()
            total = total + v_group[k - 1]
        v_sum[...] = total
        v_all[red.r] = total
        for k in range(1, 2 * nz):
            all_copy(k).start()
        to_tokens(res, flat, turn)
        copy = pltpu.make_async_copy(flat, result_o, osem.at[0])
        copy.start()
        red.on_z(cq[2])
        for k in range(1, 2 * nz):
            all_copy(k).wait_recv()
        total = v_all[0]
        for k in range(1, 2 * nz):
            total = total + v_all[k]
        v_group[0] = total
        small = pltpu.make_async_copy(v_group.at[0], small_o, osem.at[1])
        small.start()
        red.on_back(cq[2])
        copy.wait()
        small.wait()

    pl.run_scoped(outcome, v((n, D), F32), v((2, n, D), BF16), v((2, D, D), BF16), v((2, main, 128), F32),
                  v((main + images, D), BF16), v((n, D), BF16))
    copies = []
    for c in chunks:
        red.finish(c)
        half = c.rows // 2
        for k, (src, first, where) in enumerate(((x_recv, c.x_recv, red.x), (buf, c.far, 1 - red.x))):
            copy = pltpu.make_async_copy(
                src.at[pl.ds(first, half), :],
                sums_o.at[pl.ds(pl.multiple_of(c.mine - cd0.mine + where * half, 16), half), :], fsem.at[2 * c.index + k])
            copy.start()
            copies.append(copy)
    red.core_copy(6, 1024).wait_send()
    red.core_copy(7, 1024).wait_send()
    for k in range(1, 4):
        group_copy(k).wait_send()
    for k in range(1, 2 * nz):
        all_copy(k).wait_send()
    for c in chunks:
        red.drain(c)
    for copy in copies:
        copy.wait()


def convert_kernel(
    chunks, sums, small, result, tokens, result_o, tokens_o, g1_o, s1_o, qkv_o, bqv_o, out_o, bo_o, l1_o, g2_o, s2_o, up_o, bup_o, down_o, bd_o, l2_o,
    low, qkv, out, up, down, moved, dsem, osem, msem,
):
    base = chunks[0].mine
    moves = [pltpu.make_async_copy(src, moved.at[k], msem.at[0, k]) for k, src in enumerate((result, tokens))]
    stores = [pltpu.make_async_copy(moved.at[k], dst, msem.at[1, k]) for k, dst in enumerate((result_o, tokens_o))]
    gots = []
    for c in chunks:
        rows = pl.ds(c.mine - base, c.rows)
        gots.append(pltpu.make_async_copy(sums.at[rows, :], low.at[rows, :], dsem.at[c.index]))
        gots[-1].start()
    for copy in moves:
        copy.start()
    outs = []

    def send_out(src, dst):
        copy = pltpu.make_async_copy(src, dst, osem.at[len(outs)])
        copy.start()
        outs.append(copy)

    def block(c, first, count):
        return low[c.mine - base + first : c.mine - base + first + count, :]

    for t in range(2):
        gots[2 * t].wait()
        for k in range(8):
            down[t * TILE : (t + 1) * TILE, k * 128 : (k + 1) * 128] = block(chunks[2 * t], k * 128, 128).T.astype(F32)
        send_out(down.at[pl.ds(t * TILE, TILE), :], down_o.at[pl.ds(t * TILE, TILE), :])
        moves[t].wait()
        stores[t].start()
        gots[2 * t + 1].wait()
        up[t] = block(chunks[2 * t + 1], 0, D).astype(F32)
        send_out(up.at[t], up_o.at[:, pl.ds(t * TILE, TILE)])
    gots[4].wait()
    for k in range(2):
        out[:, k * TILE : (k + 1) * TILE] = block(chunks[4], k * 256, 256).astype(F32)
    send_out(out, out_o)
    for k in range(5, 8):
        gots[k].wait()
    for k in range(6):
        qkv[:, k * TILE : (k + 1) * TILE] = block(chunks[5], k * 256, 256).astype(F32)
    send_out(qkv, qkv_o)
    vectors = (g1_o, s1_o, bo_o, l1_o, g2_o, s2_o, bd_o, l2_o, bqv_o, bup_o)
    row = 0
    for v in vectors:
        for k in range(v.shape[0] // 256):
            v[pl.ds(k * 256, 256)] = small[row : row + 1, :].reshape(256)
            row += 1
    for copy in outs + stores:
        copy.wait()


def convert(chunks, sums, small, result, tokens):
    one = lambda k: jax.ShapeDtypeStruct((k,), F32)
    outs = (
        low_shape(*result.shape), low_shape(*tokens.shape), one(256), one(256), wide_shape(256, 3 * D), one(512), wide_shape(256, D), one(256), one(256), one(256), one(256),
        wide_shape(D, D), one(1024), wide_shape(D, D), one(256), one(256),
    )
    v = pltpu.VMEM
    return pl.pallas_call(
        functools.partial(convert_kernel, chunks),
        out_shape=outs,
        in_specs=[ANY, VMEM, ANY, ANY],
        out_specs=[VMEM if len(o.shape) == 1 else ANY for o in outs],
        scratch_shapes=[v(sums.shape, BF16), v((256, 3 * D), F32), v((256, D), F32), v((2, D, TILE), F32),
                        v((D, D), F32), v((2,) + result.shape, BF16), pltpu.SemaphoreType.DMA((8,)),
                        pltpu.SemaphoreType.DMA((6,)), pltpu.SemaphoreType.DMA((2, 2))],
        compiler_params=pltpu.CompilerParams(vmem_limit_bytes=LIMIT),
        name="gradients_to_float32",
    )(sums, small, result, tokens)


def low_shape(*shape):
    return jax.ShapeDtypeStruct(shape, BF16)


def wide_shape(*shape):
    return jax.ShapeDtypeStruct(shape, F32)


ANY = pl.BlockSpec(memory_space=pl.ANY)
VMEM = pl.BlockSpec(memory_space=pltpu.VMEM)
LIMIT = 62 * 2**20


def forward(flat, cot, vectors, w_qkv, w_out, w_up, w_down):
    images = flat.shape[0] // (PATCH + 1)
    n = images * PATCH + CLS
    v = pltpu.VMEM
    outs = (
        low_shape(D, 3 * D), low_shape(D, D), low_shape(4, D, D), low_shape(4, D, D), low_shape(4, 16, 256),
        low_shape(n, 3 * D), low_shape(D, n), low_shape(n, D), low_shape(D, n), wide_shape(n, D), low_shape(n, D),
        low_shape(n, D), low_shape(D, n), low_shape(n, D), low_shape(n, D), low_shape(D, n),
        wide_shape(images, HEADS, PATCH), wide_shape(images, HEADS, PATCH),
        low_shape(2, 2048, TILE), low_shape(2, n, TILE), wide_shape(n, D), wide_shape(8, TILE),
    )
    return pl.pallas_call(
        gather_kernel,
        out_shape=outs,
        in_specs=[VMEM] * 12 + [ANY] * 4,
        out_specs=[ANY] * len(outs),
        scratch_shapes=[
            v((D, 3 * D), BF16), v((D, D), BF16), v((4, D, D), BF16), v((4, D, D), BF16),
            v((n, D), BF16), v((n, 3 * D), BF16), v((n, D), BF16), v((n, D), BF16), v((n, D), F32), v((n, D), BF16),
            v((n, D), BF16), v((D, n), BF16), v((D, n), BF16),
            v((images, HEADS, PATCH), F32), v((images, HEADS, PATCH), F32),
            v((8, 256, PATCH), F32), v((8, 256, PATCH), BF16), v((PATCH, D), F32), v((HEADS, PATCH), F32),
            v((CLS, D), F32), v((CLS, 3 * D), F32), v((2, images * PATCH, 128), F32), v((16, 256), F32),
            v((16, 256), BF16), v((4, 16, 256), BF16), v((16, D), F32), v((8, 3 * D), F32), v((8, TILE), F32),
            v((8, TILE), F32), pltpu.SemaphoreType.DMA((2, 7, 11)), pltpu.SemaphoreType.DMA((7,)), pltpu.SemaphoreType.DMA((2, 3)),
            pltpu.SemaphoreType.DMA((30,)),
        ],
        compiler_params=pltpu.CompilerParams(collective_id=0, has_side_effects=True, vmem_limit_bytes=LIMIT),
        cost_estimate=pl.CostEstimate(flops=18 * 2**30, bytes_accessed=64 * 2**20, transcendentals=3 * 2**20),
        name="gather_and_attention",
    )(flat, cot, *vectors, w_qkv, w_out, w_up, w_down)


def backward(nz, images, vec, *arrays):
    n = images * PATCH + CLS
    tokens = images * (PATCH + 1)
    v = pltpu.VMEM
    chunks, sizes = chunk_layout(nz)
    outs = (low_shape(tokens, D), low_shape(tokens, D), low_shape(sizes["total"], TILE), wide_shape(16, 256),
            low_shape(6, n, TILE))
    return pl.pallas_call(
        functools.partial(backward_kernel, nz, chunks),
        out_shape=outs,
        in_specs=[VMEM] + [ANY] * len(arrays),
        out_specs=[ANY] * len(outs),
        scratch_shapes=[
            v((sizes["buf"], TILE), BF16), v((2, 2048, TILE), BF16), v((sizes["y_recv"], TILE), BF16),
            v((sizes["x_recv"], TILE), BF16), v((nz - 1, sizes["z_recv"], TILE), BF16), v((n, D), F32), v((n, D), F32), v((n, D), BF16),
            v((10, 8, D), F32), v((8, TILE), F32), v((16, D), F32), v((8, 3 * D), F32), v((8, TILE), F32),
            v((4, 16, 256), F32), v((3, 16, 256), F32), v((16, 256), F32), v((2 * nz, 16, 256), F32),
            pltpu.SemaphoreType.DMA((2, len(chunks), 3 * nz)), pltpu.SemaphoreType.DMA((2, 8)),
            pltpu.SemaphoreType.DMA((2, 3)), pltpu.SemaphoreType.DMA((2, 2 * nz - 1)),
            pltpu.SemaphoreType.REGULAR, pltpu.SemaphoreType.DMA((12,)), pltpu.SemaphoreType.DMA((2, 4)),
            pltpu.SemaphoreType.DMA((2,)), pltpu.SemaphoreType.DMA((2,)), pltpu.SemaphoreType.DMA((2 * len(chunks),)),
        ],
        compiler_params=pltpu.CompilerParams(collective_id=1, has_side_effects=True, vmem_limit_bytes=LIMIT),
        cost_estimate=pl.CostEstimate(flops=66 * 2**30, bytes_accessed=128 * 2**20, transcendentals=8 * 2**20),
        name="layer_backward",
    )(vec, *arrays), chunks


def on_device(
    tokens, norm1_gain, norm1_shift, w_qkv, bias_qv, w_out, bias_out, scale_one, norm2_gain, norm2_shift, w_up, bias_up,
    w_down, bias_down, scale_two, cotangent,
):
    images, length, _ = tokens.shape
    nz = lax.axis_size("replica") // 2
    flatten = lambda a: jnp.transpose(a, (1, 0, 2)).reshape(images * length, D)
    restore = lambda a: jnp.transpose(a.reshape(length, images, D), (1, 0, 2))
    vectors = (norm1_gain, norm1_shift, bias_out, scale_one, norm2_gain, norm2_shift, bias_down, scale_two, bias_qv, bias_up)
    full_qkv, full_out, full_up, full_down, vec, *kept = forward(
        flatten(tokens), flatten(cotangent), vectors, w_qkv, w_out, w_up, w_down)
    (result, grad_tokens, sums, small, _), chunks = backward(nz, images, vec, full_qkv, full_out, full_up, full_down, *kept)
    result, grad_tokens, *gradients = convert(chunks, sums, small, result, grad_tokens)
    return (restore(result), restore(grad_tokens)) + tuple(gradients)


def solution(mesh):
    placed = (
        P(("shard", "replica"), None, None),
        P("shard"),
        P("shard"),
        P("shard", None),
        P("shard"),
        P("shard", None),
        P("shard"),
        P("shard"),
        P("shard"),
        P("shard"),
        P(None, "shard"),
        P("shard"),
        P("shard", None),
        P("shard"),
        P("shard"),
        P(("shard", "replica"), None, None),
    )
    return jax.shard_map(
        on_device,
        mesh=mesh,
        in_specs=placed,
        out_specs=(
            P(("shard", "replica"), None, None),
            P(("shard", "replica"), None, None),
            P("shard"),
            P("shard"),
            P("shard", None),
            P("shard"),
            P("shard", None),
            P("shard"),
            P("shard"),
            P("shard"),
            P("shard"),
            P(None, "shard"),
            P("shard"),
            P("shard", None),
            P("shard"),
            P("shard"),
        ),
        check_vma=False,
    )
```

```python
import functools

import jax
import jax.numpy as jnp
from jax import lax
from jax.experimental import pallas as pl
from jax.experimental.pallas import tpu as pltpu
from jax.sharding import PartitionSpec as P

F32 = jnp.float32
BF16 = jnp.bfloat16
D = 1024
FF = 4096
HEADS = 16
PATCH = 128
CLS = 16
TILE = 512
FACTOR = 0.125
MESH = pl.DeviceIdType.MESH


def dot(a, b):
    return jnp.dot(a, b, preferred_element_type=F32)


def dot_nt(a, b):
    return lax.dot_general(a, b, (((1,), (1,)), ((), ())), preferred_element_type=F32)


def dot_tn(a, b):
    return lax.dot_general(a, b, (((0,), (0,)), ((), ())), preferred_element_type=F32)


def at(index, size):
    return pl.ds(pl.multiple_of(index * size, size), size)


def head_mask():
    lane = lax.shift_right_logical(lax.broadcasted_iota(jnp.int32, (HEADS, D), 1), 6)
    return lane == lax.broadcasted_iota(jnp.int32, (HEADS, D), 0)


def split_pair(v):
    low = lax.broadcasted_iota(jnp.int32, v.shape, 1) < 64
    zero = jnp.zeros_like(v)
    return jnp.concatenate([jnp.where(low, v, zero), jnp.where(low, zero, v)], 0)


def merge_pair(v):
    n = v.shape[0] // 2
    low = lax.broadcasted_iota(jnp.int32, (n, v.shape[1]), 1) < 64
    return jnp.where(low, v[:n], v[n:])


def place():
    s = lax.axis_index("shard")
    r = lax.axis_index("replica")
    x = lax.rem(r, 2)
    z = lax.div(r, 2)
    return s, r, x, z


def peers(s, r):
    sib = s + 1 - 2 * lax.rem(s, 2)
    across = lax.rem(s + 2, 4)
    side = r + 1 - 2 * lax.rem(r, 2)
    return sib, across, side


def rows_loop(n, step, body):
    lax.fori_loop(0, n // step, lambda k, c: (body(at(k, step)), c)[1], 0, unroll=13)


def unpack_vectors(vec, vecf, bias_qkv):
    for v in range(8):
        for s in range(4):
            vecf[v : v + 1, s * 256 : (s + 1) * 256] = vec[s, v : v + 1, :].astype(F32)
    bias_qkv[...] = jnp.zeros_like(bias_qkv)
    for s in range(4):
        for t in range(2):
            col = (s * 2 + t) * 256 + (D if s >= 2 else 0)
            bias_qkv[0:1, col : col + 256] = vec[s, 8 + t : 9 + t, :].astype(F32)


def layer_norm(v, gain, shift):
    c = v - jnp.mean(v, axis=-1, keepdims=True)
    inv = lax.rsqrt(jnp.mean(c * c, axis=-1, keepdims=True) + 1e-06)
    return c * inv * gain + shift


def to_images(src, dst, turn):
    images = (src.shape[0]) // (PATCH + 1)
    main = images * PATCH

    def lane_block(l, carry):
        cols = at(l, 128)
        slot = lax.rem(l, 2)
        turn[slot] = src[0:main, cols].astype(F32)
        for i in range(images):
            dst[i * PATCH : (i + 1) * PATCH, cols] = turn[slot, pl.ds(i, PATCH, stride=images), :].astype(BF16)
        return carry

    lax.fori_loop(0, D // 128, lane_block, 0)
    last = src[main : main + images, :].astype(F32)
    dst[main:, :] = jnp.concatenate([last, jnp.zeros((CLS - images, D), F32)], 0).astype(BF16)


def pack_vectors(vectors, dst):
    row = 0
    for v in vectors:
        count = v.shape[0] // 256
        wide = v[...].astype(F32)
        for k in range(count):
            dst[row : row + 1, :] = wide[k * 256 : (k + 1) * 256].reshape(1, 256)
            row += 1


def attend(i, qkv, qkv_cls, scores, probs, mix, probs_cls, att, att_cls, lse, lse_cls):
    rows = at(i, PATCH)
    mask = head_mask()
    own = qkv_cls[pl.ds(i, 1), :]
    q_c, k_c, v_c = own[:, :D] * FACTOR, own[:, D : 2 * D], own[:, 2 * D :]
    q_bd = jnp.where(mask, q_c, 0.0)
    k_bd = jnp.where(mask, k_c, 0.0).astype(BF16)
    v_bd = jnp.where(mask, v_c, 0.0).astype(BF16)
    to_cls = dot_nt(k_bd, qkv[rows, 0:D]) * FACTOR
    of_cls = dot_nt(q_bd.astype(BF16), qkv[rows, D : 2 * D])
    corner = jnp.sum(q_bd * k_c, axis=1, keepdims=True)
    top = jnp.maximum(jnp.max(of_cls, axis=1, keepdims=True), corner)
    e_row = jnp.exp(of_cls - top)
    e_cor = jnp.exp(corner - top)
    total = jnp.sum(e_row, axis=1, keepdims=True) + e_cor
    inv = 1.0 / total
    row = dot((e_row * inv).astype(BF16), qkv[rows, 2 * D : 3 * D])
    row = row + (e_cor * inv).astype(BF16).astype(F32) * v_c
    att_cls[pl.ds(i, 1), :] = jnp.sum(jnp.where(mask, row, 0.0), axis=0, keepdims=True)
    lse_cls[i] = jnp.broadcast_to(top + jnp.log(total), (HEADS, PATCH))
    for g in range(HEADS // 2):
        q2 = qkv[rows, g * 128 : g * 128 + 128] * jnp.asarray(FACTOR, BF16)
        scores[g] = dot_nt(split_pair(qkv[rows, g * 128 + D : g * 128 + D + 128]), q2)
    for g in range(HEADS // 2):
        for u in range(2):
            h = 2 * g + u
            part = scores[g, u * PATCH : (u + 1) * PATCH, :]
            extra = to_cls[h : h + 1, :]
            top = jnp.maximum(jnp.max(part, axis=0, keepdims=True), extra)
            e_part = jnp.exp(part - top)
            e_extra = jnp.exp(extra - top)
            total = jnp.sum(e_part, axis=0, keepdims=True) + e_extra
            inv = 1.0 / total
            probs[g, u * PATCH : (u + 1) * PATCH, :] = (e_part * inv).astype(BF16)
            probs_cls[h : h + 1, :] = e_extra * inv
            lse[i, h : h + 1, :] = top + jnp.log(total)
    for g in range(HEADS // 2):
        v2 = split_pair(qkv[rows, g * 128 + 2 * D : g * 128 + 2 * D + 128])
        mix[:, g * 128 : g * 128 + 128] = dot_tn(probs[g], v2)
    att[rows, :] = (mix[...] + dot_tn(probs_cls[...].astype(BF16), v_bd)).astype(BF16)


class Gather:
    KINDS = ("own", "far", "x1", "z1", "x2", "z2", "p0", "p1", "p2", "p3", "p4")

    def __init__(self, number, rows, src, dst, sems, local):
        s, r, x, z = place()
        sib, across, side = peers(s, r)
        self.number, self.sems = number, sems
        near = lax.rem(z, 2)
        level = {"replica": (z + 1 - 2 * near) * 2 + x}
        side, sib = {"replica": side}, {"shard": sib}
        size = rows // 4
        half = size // 2

        def start(zz, xx):
            return pl.multiple_of((2 * zz + xx) * size, 16)

        def same(first, count, to):
            ref = dst(across, pl.multiple_of(first, 16), count)
            return ref, ref, to

        mine, by_x, by_z, by_both = start(near, x), start(near, 1 - x), start(1 - near, x), start(1 - near, 1 - x)
        self.parts = {
            "own": (dst(s, 0, rows), dst(s, 0, rows), sib),
            "far": (dst(s, mine, size), dst(s, mine, size), {"shard": across}),
            "x1": same(mine, size, side),
            "z1": same(mine, size, level),
            "x2": same(by_z, half, side),
            "z2": same(by_x + half, half, level),
            "p0": same(mine, size, sib),
            "p1": same(by_x, size, sib),
            "p2": same(by_z, size, sib),
            "p3": same(by_both, half, sib),
            "p4": same(by_both + half, half, sib),
        }
        self.local = pltpu.make_async_copy(src(0, rows), dst(s, 0, rows), local.at[number])

    def copy(self, kind):
        a, b, to = self.parts[kind]
        k = self.KINDS.index(kind)
        return pltpu.make_async_remote_copy(
            a, b, self.sems.at[0, self.number, k], self.sems.at[1, self.number, k], device_id=to, device_id_type=MESH
        )

    def load(self):
        self.local.start()

    def begin(self):
        self.local.wait()
        self.copy("far").start()

    def share(self):
        self.copy("own").start()

    def on_far(self):
        self.copy("far").wait_recv()
        for kind in ("x1", "z1", "p0"):
            self.copy(kind).start()

    def on_near(self):
        self.copy("x1").wait_recv()
        self.copy("z2").start()
        self.copy("p1").start()
        self.copy("z1").wait_recv()
        self.copy("x2").start()
        self.copy("p2").start()

    def on_last(self):
        self.copy("x2").wait_recv()
        self.copy("p3").start()
        self.copy("z2").wait_recv()
        self.copy("p4").start()

    def ready(self):
        for kind in ("own", "p0", "p1", "p2", "p3", "p4"):
            self.copy(kind).wait_recv()

    def drain(self):
        for kind in self.KINDS:
            self.copy(kind).wait_send()


def relative_piece(s, rel):
    low, high = lax.rem(rel, 2), lax.div(rel, 2)
    return s + low * (1 - 2 * lax.rem(s, 2)) + high * (2 - 4 * lax.div(s, 2))


def unpack_bias_up(vec, bias_up):
    for p in range(4):
        for t in range(2):
            for k in range(2):
                row = 10 + 2 * t + k
                bias_up[2 * p + t : 2 * p + t + 1, k * 256 : (k + 1) * 256] = vec[p, row : row + 1, :].astype(F32)


def ffn_tile(act2, dr, dr_t, act2_t, w_up, w_down, bias, hid, br, gmid, fresh, on_back, on_hidden, put):
    n = act2.shape[0]
    cut = 16 * (n // 32)
    first, second = slice(0, cut), slice(cut, n)

    def both(rows, before, grad):
        hidden, step = gelu_both(before)
        hid[rows, :] = hidden.astype(BF16)
        grad = grad * step
        br[rows, :] = grad.astype(BF16)
        return jnp.sum(grad, axis=0, keepdims=True)

    def back(rows):
        out = dot_nt(br[rows, :], w_up())
        if fresh:
            gmid[rows, :] = out
        else:
            gmid[rows, :] += out

    before0 = dot(act2[first, :], w_up()) + bias
    grad0 = dot_nt(dr[first, :], w_down())
    before1 = dot(act2[second, :], w_up()) + bias
    column = both(first, before0, grad0)
    grad1 = dot_nt(dr[second, :], w_down())
    on_back()
    back(first)
    column = column + both(second, before1, grad1)
    back(second)
    on_hidden()
    put(0, dot(dr_t[...], hid[...]).astype(BF16))
    put(1, dot(act2_t[...], br[...]).astype(BF16))
    return column


def gather_kernel(
    tokens_h, cot_h, v0, v1, v2, v3, v4, v5, v6, v7, v8, v9, w_qkv, w_out, w_up, w_down,
    qkv_w_o, out_w_o, up_w_o, down_w_o, vec_all, qkv_o, act_t_o, x_o, att_t_o, mid_o, branch_o, act2_o, act2_t_o, up_o,
    dr_o, dr_t_o, lse_o, lsec_o, parts_o, hid_o, gact_o, column_o,
    full_qkv, full_out, full_up, full_down, x_s, qkv, act, att, mid, branch, act2, turned_a, turned_b, lse, lsec,
    scores, probs, mix, probs_cls, cls, qkv_cls, turn, vec32, vec_own_s, vec, vecf, bias_qkv,
    bias_up, column, core_in, flat,
    sems, local, vsem, osem, csem, fsem,
):
    s, r, x, z = place()
    sib, across, side = peers(s, r)
    n = x_s.shape[0]
    images = lse.shape[0]
    main = images * PATCH

    def load(src):
        copy = pltpu.make_async_copy(src, flat, fsem.at[0])
        copy.start()
        return copy

    got_tokens = load(tokens_h)
    vec32[...] = jnp.zeros_like(vec32)
    pack_vectors((v0, v1, v2, v3, v4, v5, v6, v7, v8, v9), vec32)
    vec_own_s[...] = vec32[...].astype(BF16)
    barrier = pltpu.get_barrier_semaphore()
    level = (z + 1 - 2 * lax.rem(z, 2)) * 2 + x
    for to in ({"shard": sib}, {"shard": across}, {"replica": side}, {"replica": level}):
        pl.semaphore_signal(barrier, inc=1, device_id=to, device_id_type=MESH)

    def unit(number, rows, src, dst):
        return Gather(number, rows, src, dst, sems, local)

    def qkv_unit(number, t):
        cols = pl.ds(t * 3 * TILE, 3 * TILE)
        return unit(number, 256, lambda a, k: w_qkv.at[pl.ds(a, k), cols],
                    lambda p, a, k: full_qkv.at[pl.ds(pl.multiple_of(p * 256 + a, 16), k), cols])

    g_qa, g_qb = qkv_unit(0, 0), qkv_unit(6, 1)
    g_out = unit(1, 256, lambda a, k: w_out.at[pl.ds(a, k), :],
                 lambda p, a, k: full_out.at[pl.ds(pl.multiple_of(p * 256 + a, 16), k), :])

    def up_unit(number, t):
        cols = pl.ds(t * TILE, TILE)
        return unit(number, D, lambda a, k: w_up.at[pl.ds(a, k), cols],
                    lambda p, a, k: full_up.at[p, pl.ds(pl.multiple_of(a, 16), k), cols])

    def down_unit(number, t):
        return unit(number, TILE, lambda a, k: w_down.at[pl.ds(a + t * TILE, k), :],
                    lambda p, a, k: full_down.at[p, pl.ds(pl.multiple_of(a + t * TILE, 16), k), :])

    g_up0, g_down0, g_up1, g_down1 = up_unit(2, 0), down_unit(3, 0), up_unit(4, 1), down_unit(5, 1)

    for g in (g_qa, g_qb, g_out, g_up0, g_down0, g_up1, g_down1):
        g.load()
    pl.semaphore_wait(barrier, 4)

    def vec_copy(k, src, slot, to):
        return pltpu.make_async_remote_copy(src, vec.at[slot], vsem.at[0, k], vsem.at[1, k], device_id=to,
                                            device_id_type=MESH)

    vec_own = vec_copy(0, vec_own_s, s, {"shard": sib})
    vec_far = vec_copy(1, vec_own_s, s, {"shard": across})
    vec_pass = vec_copy(2, vec.at[across], across, {"shard": sib})
    vec_own.start()
    vec_far.start()
    for g in (g_qa, g_qb):
        g.begin()
        g.share()
    g_out.begin()
    vec[s] = vec_own_s[...]

    got_tokens.wait()
    to_images(flat, x_s, turn)
    got_cot = load(cot_h)
    outs = {}

    def send_out(k, src, dst):
        outs[k] = pltpu.make_async_copy(src, dst, osem.at[k])
        outs[k].start()

    send_out(0, x_s, x_o)
    vec_far.wait_recv()
    vec_pass.start()
    vec_own.wait_recv()
    vec_pass.wait_recv()
    unpack_vectors(vec, vecf, bias_qkv)
    g_qa.on_far()

    def first_norm(rows):
        act[rows, :] = layer_norm(x_s[rows, :].astype(F32), vecf[0:1, :], vecf[1:2, :]).astype(BF16)

    rows_loop(n, 16, first_norm)
    g_qa.on_near()
    g_qb.on_far()
    for g in (g_up0, g_down0, g_up1, g_down1):
        g.begin()
    transpose_into(act, turned_b)
    send_out(1, turned_b, act_t_o)
    got_cot.wait()
    to_images(flat, branch, turn)
    g_qa.on_last()
    g_qb.on_near()

    def down_rows(rows):
        act2[rows, :] = (branch[rows, :].astype(F32) * vecf[7:8, :]).astype(BF16)

    rows_loop(n, 16, down_rows)
    send_out(14, branch, up_o)
    send_out(15, act2, dr_o)
    transpose_into(act2, turned_a)
    send_out(16, turned_a, dr_t_o)
    g_qb.on_last()
    g_out.on_far()
    g_qa.ready()

    def qkv_tile(j, carry):
        cols = at(j, TILE)
        low = (dot(act[...], full_qkv[:, cols]) + bias_qkv[0:1, cols]).astype(BF16)
        qkv[:, cols] = low
        qkv_cls[:, cols] = low[main:].astype(F32)
        return carry

    lax.fori_loop(0, 3, qkv_tile, 0)
    g_out.on_near()
    g_qb.ready()
    send_out(4, full_qkv, qkv_w_o)
    for g in (g_out, g_up0, g_down0):
        g.share()
    lax.fori_loop(3, 6, qkv_tile, 0)
    send_out(2, qkv, qkv_o)
    act[...] = act2[...]
    unpack_bias_up(vec, bias_up)
    column[...] = jnp.zeros_like(column)
    send_out(3, vec, vec_all)
    cls[...] = jnp.zeros_like(cls)
    g_out.on_last()
    g_up0.on_far()
    plan = {1: [g_up0.on_near], 2: [g_down0.on_far], 3: [g_up0.on_last, g_up1.share], 4: [g_down0.on_near, g_up1.on_far],
            6: [g_down0.on_last, g_down1.share], 7: [g_up1.on_near, g_down1.on_far]}

    def image(i, carry):
        for k, steps in plan.items():
            @pl.when(i == k)
            def _(steps=steps):
                for step in steps:
                    step()

        attend(i, qkv, qkv_cls, scores, probs, mix, probs_cls, att, cls, lse, lsec)
        return carry

    lax.fori_loop(0, images, image, 0)
    att[main:, :] = cls[...].astype(BF16)
    outs.pop(1).wait()
    transpose_into(att, turned_b)
    send_out(8, turned_b, att_t_o)
    send_out(9, lse, lse_o)
    send_out(10, lsec, lsec_o)
    g_out.ready()
    outs.pop(14).wait()
    for j in range(D // TILE):
        cols = slice(j * TILE, (j + 1) * TILE)
        out = dot(att[...], full_out[:, cols]) + vecf[2:3, cols]
        branch[:, cols] = out.astype(BF16)
        mid[:, cols] = x_s[:, cols].astype(F32) + vecf[3:4, cols] * out
    send_out(11, mid, mid_o)
    send_out(12, branch, branch_o)
    g_up1.on_last()
    g_down1.on_near()

    def second_norm(rows):
        act2[rows, :] = layer_norm(mid[rows, :], vecf[4:5, :], vecf[5:6, :]).astype(BF16)

    outs.pop(15).wait()
    rows_loop(n, 16, second_norm)
    send_out(13, act2, act2_o)
    outs.pop(8).wait()
    transpose_into(act2, turned_b)
    send_out(17, turned_b, act2_t_o)
    half = pl.ds(0, TILE)
    rest = pl.ds(TILE, TILE)
    send_out(5, full_out, out_w_o)
    g_up0.ready()
    send_out(18, full_up.at[:, :, half], up_w_o.at[:, :, half])
    g_down0.ready()
    send_out(19, full_down.at[:, half, :], down_w_o.at[:, half, :])
    for k in (2, 11):
        outs.pop(k).wait()
    hid, br = qkv.at[:, pl.ds(0, TILE)], qkv.at[:, pl.ds(TILE, TILE)]
    def core_copy(half_k):
        return pltpu.make_async_remote_copy(
            qkv.at[pl.ds(0, D), pl.ds((2 + half_k) * TILE, TILE)], core_in.at[half_k], csem.at[0, half_k],
            csem.at[1, half_k], device_id={"shard": sib}, device_id_type=MESH)

    for k, rel in enumerate((3, 2)):
        piece = relative_piece(s, rel)

        def put(half_k, value, k=k):
            qkv[0:D, (2 + 2 * k + half_k) * TILE : (3 + 2 * k + half_k) * TILE] = value

        if k:
            outs.pop(22).wait()
        column[pl.ds(2 * piece, 1), :] = ffn_tile(
            act2, act, turned_a, turned_b, lambda: full_up[piece, :, 0:TILE], lambda: full_down[piece, 0:TILE, :],
            bias_up[pl.ds(2 * piece, 1), :], hid, br, mid, k == 0, lambda: None, lambda: send_out(22 + k, hid, hid_o.at[k]), put)
        if k == 0:
            for half_k in range(2):
                core_copy(half_k).start()
            g_down1.on_last()
            g_up1.ready()
            send_out(20, full_up.at[:, :, rest], up_w_o.at[:, :, rest])
    send_out(28, mid, gact_o)
    for half_k in range(2):
        core_copy(half_k).wait_recv()
        cols = slice((4 + half_k) * TILE, (5 + half_k) * TILE)

        def join(k, carry, half_k=half_k, cols=cols):
            rows = at(k, 128)
            qkv[rows, cols] = (qkv[rows, cols].astype(F32) + core_in[half_k, rows, :].astype(F32)).astype(BF16)
            return carry

        lax.fori_loop(0, D // 128, join, 0)
        send_out(24 + half_k, qkv.at[pl.ds(0, D), pl.ds((4 + half_k) * TILE, TILE)], parts_o.at[pl.ds(half_k * D, D), :])
    send_out(29, column, column_o)
    g_down1.ready()
    send_out(21, full_down.at[:, rest, :], down_w_o.at[:, rest, :])
    for half_k in range(2):
        core_copy(half_k).wait_send()
    for copy in outs.values():
        copy.wait()
    for g in (g_qa, g_qb, g_out, g_up0, g_down0, g_up1, g_down1):
        g.drain()
    for copy in (vec_own, vec_far, vec_pass):
        copy.wait_send()


class Chunk:
    def __init__(self, index, rows, mine, y_send, y_recv, x_recv, z_recv, far):
        self.index, self.rows, self.mine, self.y_send, self.far = index, rows, mine, y_send, far
        self.y_recv, self.x_recv, self.z_recv = y_recv, x_recv, z_recv


def chunk_layout(nz):
    sizes = [1024, 1024, 1024, 1024, 512, 512, 512, 512]
    y_base = 2048
    y_a = y_base
    y_b = y_a + 2048
    mine_base = y_b + 2048
    chunks = []
    mine = mine_base
    late = 0
    xr = zr = 0
    for k, rows in enumerate(sizes):
        if k < 2:
            ys, yr = y_a + 1024 * k, 1024 * k
        elif k < 4:
            ys, yr = y_b + 1024 * (k - 2), 2048 + 1024 * (k - 2)
        else:
            ys, yr = y_a + late, late
            late += rows
        far = mine_base + sum(sizes) + 512 * k if k < 2 else ys
        chunks.append(Chunk(k, rows, mine, ys, yr, xr, zr, far))
        mine += rows
        xr += rows // 2
        zr += rows // 2 // nz
    return chunks, dict(buf=mine + 1024, total=sum(sizes), mine=mine_base, y_recv=2 * 2048, x_recv=xr, z_recv=zr)


def add_rows(dst, d0, src, s0, rows):
    step = next(k for k in (128, 96, 64, 32, 16) if rows % k == 0)

    def body(k, carry):
        d = pl.ds(pl.multiple_of(d0 + k * step, 16), step)
        t = pl.ds(pl.multiple_of(s0 + k * step, 16), step)
        dst[d, :] = (dst[d, :].astype(F32) + src[t, :].astype(F32)).astype(BF16)
        return carry

    lax.fori_loop(0, rows // step, body, 0)


class Reduce:
    def __init__(self, nz, buf, core_recv, y_recv, x_recv, z_recv, sems, core_sems, credit):
        self.nz, self.buf, self.core_recv = nz, buf, core_recv
        self.y_recv, self.x_recv, self.z_recv = y_recv, x_recv, z_recv
        self.sems, self.core_sems, self.credit = sems, core_sems, credit
        self.s, self.r, self.x, self.z = place()
        self.sib, self.across, self.side = peers(self.s, self.r)

    def remote(self, src, dst, chunk, kind, to):
        return pltpu.make_async_remote_copy(
            src, dst, self.sems.at[0, chunk.index, kind], self.sems.at[1, chunk.index, kind], device_id=to,
            device_id_type=MESH)

    def peer(self, k):
        return {"replica": lax.rem(self.z + k, self.nz) * 2 + self.x}

    def core_copy(self, turn, rows):
        slot = turn % 2
        return pltpu.make_async_remote_copy(
            self.buf.at[pl.ds(slot * 1024 if turn > 3 else 0, rows), :], self.core_recv.at[slot, pl.ds(0, rows), :],
            self.core_sems.at[0, turn], self.core_sems.at[1, turn], device_id={"shard": self.sib}, device_id_type=MESH)

    def add_core(self, turn, first, dst, rows):
        add_rows(self.buf, dst, self.core_recv.at[turn % 2], first, rows)

    def y_copy(self, c):
        return self.remote(self.buf.at[pl.ds(c.y_send, c.rows), :], self.y_recv.at[pl.ds(c.y_recv, c.rows), :], c, 0,
                           {"shard": self.across})

    def x_copy(self, c):
        half = c.rows // 2
        return self.remote(self.buf.at[pl.ds(pl.multiple_of(c.mine + (1 - self.x) * half, 16), half), :],
                           self.x_recv.at[pl.ds(c.x_recv, half), :], c, 1, {"replica": self.side})

    def quarter(self, c, x, z):
        half = c.rows // 2
        size = half // self.nz
        return pl.ds(pl.multiple_of(c.mine + x * half + z * size, 16), size)

    def z_copy(self, c, k):
        size = c.rows // 2 // self.nz
        return self.remote(self.buf.at[self.quarter(c, self.x, lax.rem(self.z + k, self.nz)), :],
                           self.z_recv.at[k - 1, pl.ds(c.z_recv, size), :], c, 1 + k, self.peer(k))

    def done(self, first, c, z):
        size = c.rows // 2 // self.nz
        return pl.ds(pl.multiple_of(first + z * size, 16), size)

    def back_z(self, c, k):
        part = self.x_recv.at[self.done(c.x_recv, c, self.z), :]
        return self.remote(part, part, c, self.nz + k, self.peer(k))

    def back_x(self, c, k):
        z = lax.rem(self.z + self.nz - k, self.nz)
        return self.remote(self.x_recv.at[self.done(c.x_recv, c, z), :], self.buf.at[self.done(c.far, c, z), :], c,
                           2 * self.nz + k, {"replica": self.side})

    def on_y(self, c):
        self.y_copy(c).wait_recv()
        add_rows(self.buf, c.mine, self.y_recv, c.y_recv, c.rows)
        self.y_copy(c).wait_send()
        self.x_copy(c).start()

    def on_x(self, c):
        half = c.rows // 2
        self.x_copy(c).wait_recv()
        add_rows(self.buf, c.mine + self.x * half, self.x_recv, c.x_recv, half)
        for k in range(1, self.nz):
            self.z_copy(c, k).start()

    def on_z(self, c):
        size = c.rows // 2 // self.nz
        start = c.mine + self.x * (c.rows // 2) + self.z * size
        for k in range(1, self.nz):
            self.z_copy(c, k).wait_recv()
        step = next(k for k in (64, 48, 32, 16) if size % k == 0)

        def body(i, carry):
            d = pl.ds(pl.multiple_of(start + i * step, 16), step)
            total = self.buf[d, :].astype(F32)
            for k in range(1, self.nz):
                total = total + self.z_recv[k - 1, pl.ds(pl.multiple_of(c.z_recv + i * step, 16), step), :].astype(F32)
            to = pl.ds(pl.multiple_of(c.x_recv + self.z * size + i * step, 16), step)
            self.x_recv[to, :] = total.astype(BF16)
            return carry

        lax.fori_loop(0, size // step, body, 0)
        for k in range(1, self.nz):
            self.back_z(c, k).start()
        self.back_x(c, 0).start()

    def on_back(self, c):
        for k in range(1, self.nz):
            self.back_z(c, k).wait_recv()
            self.back_x(c, k).start()

    def finish(self, c):
        for k in range(self.nz):
            self.back_x(c, k).wait_recv()

    def drain(self, c):
        self.x_copy(c).wait_send()
        for k in range(1, self.nz):
            self.z_copy(c, k).wait_send()
            self.back_z(c, k).wait_send()
        for k in range(self.nz):
            self.back_x(c, k).wait_send()


def fold(v):
    return jnp.sum(v.reshape(v.shape[0] // 8, 8, v.shape[1]), axis=0)


def gelu_both(v):
    e = jnp.exp(-0.5 * v * v)
    t = 1.0 / (1.0 + 0.23164189 * jnp.abs(v))
    poly = ((((1.061405429 * t - 1.453152027) * t + 1.421413741) * t - 0.284496736) * t + 0.254829592) * t
    tail = 0.5 * poly * e
    phi = jnp.where(v >= 0.0, 1.0 - tail, tail)
    return v * phi, phi + v * e * 0.3989422804014327


def transpose_into(src, dst):
    for c in range(D // 128):
        dst[c * 128 : (c + 1) * 128, :] = src[:, c * 128 : (c + 1) * 128].T


def attend_back(
    i, qkv, qkv_cls, datt, datt_cls, lse, lsec, scores, dprobs, probs, dscores, cls_row, joint_cls, joint, extra, sum_q, sum_v
):
    rows = at(i, PATCH)
    mask = head_mask()
    own = qkv_cls[pl.ds(i, 1), :]
    do_c = datt_cls[pl.ds(i, 1), :]
    q_c, k_c, v_c = own[:, :D] * FACTOR, own[:, D : 2 * D], own[:, 2 * D :]
    pick = lambda v: jnp.where(mask, v, 0.0)
    q_w, k_w, v_w, do_w = pick(q_c), pick(k_c), pick(v_c), pick(do_c)
    q_bd, k_bd, v_bd, do_bd = (v.astype(BF16) for v in (q_w, k_w, v_w, do_w))
    queries, keys, values = (qkv[rows, k * D : (k + 1) * D] for k in range(3))
    grads = datt[rows, :]
    low = lambda v: v.astype(BF16)
    top = lsec[i][:, 0:1]
    p_row = jnp.exp(dot_nt(q_bd, keys) - top)
    p_cor = jnp.exp(jnp.sum(q_w * k_c, axis=1, keepdims=True) - top)
    dp_row = dot_nt(do_bd, values)
    dp_cor = jnp.sum(do_w * v_c, axis=1, keepdims=True)
    delta = jnp.sum(p_row * dp_row, axis=1, keepdims=True) + p_cor * dp_cor
    ds_row = low(p_row * (dp_row - delta))
    ds_cor = low(p_cor * (dp_cor - delta)).astype(F32)
    p_col = jnp.exp(dot_nt(k_bd, queries) * FACTOR - lse[i])
    dp_col = dot_nt(v_bd, grads)
    for g in range(HEADS // 2):
        lanes = slice(g * 128, (g + 1) * 128)
        q2 = qkv[rows, lanes] * jnp.asarray(FACTOR, BF16)
        scores[g] = dot_nt(split_pair(qkv[rows, g * 128 + D : g * 128 + D + 128]), q2)
        dprobs[g] = dot_nt(split_pair(qkv[rows, g * 128 + 2 * D : g * 128 + 2 * D + 128]), datt[rows, lanes])
    for g in range(HEADS // 2):
        for u in range(2):
            h = 2 * g + u
            half = slice(u * PATCH, (u + 1) * PATCH)
            part = jnp.exp(scores[g, half, :] - lse[i, h : h + 1, :])
            dpart = dprobs[g, half, :]
            p_h, dp_h = p_col[h : h + 1, :], dp_col[h : h + 1, :]
            delta = jnp.sum(part * dpart, axis=0, keepdims=True) + p_h * dp_h
            probs[g, half, :] = low(part)
            dscores[g, half, :] = low(part * (dpart - delta))
            cls_row[h : h + 1, :] = p_h * (dp_h - delta)
    ds_col = low(cls_row[...])
    total = lambda v: jnp.sum(jnp.where(mask, v, 0.0), axis=0, keepdims=True)
    joint_cls[pl.ds(i, 1), 0:D] = FACTOR * (total(dot(ds_row, keys)) + jnp.sum(ds_cor * k_w, axis=0, keepdims=True))
    joint_cls[pl.ds(i, 1), D : 2 * D] = FACTOR * total(dot(ds_col, queries)) + jnp.sum(ds_cor * q_w, axis=0, keepdims=True)
    joint_cls[pl.ds(i, 1), 2 * D : 3 * D] = total(dot(low(p_col), grads)) + jnp.sum(
        low(p_cor).astype(F32) * do_w, axis=0, keepdims=True)
    extra[0] = dot_tn(ds_col, k_bd) * FACTOR
    extra[1] = dot_tn(ds_row, q_bd)
    extra[2] = dot_tn(low(p_row), do_bd)
    for g in range(HEADS // 2):
        lanes = slice(g * 128, (g + 1) * 128)
        klanes = slice(g * 128 + D, g * 128 + D + 128)
        vlanes = slice(g * 128 + 2 * D, g * 128 + 2 * D + 128)
        q2 = qkv[rows, lanes] * jnp.asarray(FACTOR, BF16)
        dv = merge_pair(dot(probs[g], datt[rows, lanes])) + extra[2, :, lanes]
        dk = merge_pair(dot(dscores[g], q2)) + extra[1, :, lanes]
        dq = dot_tn(dscores[g], split_pair(qkv[rows, klanes])) * FACTOR + extra[0, :, lanes]
        joint[:, lanes] = low(dq)
        joint[:, klanes] = low(dk)
        joint[:, vlanes] = low(dv)
        sum_q[:, lanes] += fold(dq)
        sum_v[:, lanes] += fold(dv)
    qkv[rows, :] = joint[...]


def to_tokens(src, dst, turn):
    images = dst.shape[0] // (PATCH + 1)
    main = images * PATCH

    def lane_block(l, carry):
        cols = at(l, 128)
        slot = lax.rem(l, 2)
        for i in range(images):
            turn[slot, pl.ds(i, PATCH, stride=images), :] = src[i * PATCH : (i + 1) * PATCH, cols].astype(F32)
        dst[0:main, cols] = turn[slot].astype(BF16)
        return carry

    lax.fori_loop(0, D // 128, lane_block, 0)
    dst[main : main + images, :] = src[main:, :].astype(F32)[0:images].astype(BF16)


def backward_kernel(
    nz, chunks, vec, full_qkv, full_out, full_up, full_down, qkv_h, act_t_h, x_h, att_t_h, mid_h, branch_h, act2_h,
    act2_t_h, up_h, dr_h, dr_t_h, lse_h, lsec_h, parts_h, hid_h, gact_h, column_h,
    result_o, tokens_o, sums_o, small_o, hidden_o,
    buf, core_recv, y_recv, x_recv, z_recv, gmid, grad_mid, up_s, acc, sums_up, vecf, bias_qkv, bias_up, v_part, v_group, v_sum, v_all,
    sems, core_sems, group_sems, all_sems, credit, dsem, wsem, hsem, osem, fsem,
):
    images = lse_h.shape[0]
    n = gmid.shape[0]
    main = images * PATCH
    red = Reduce(nz, buf, core_recv, y_recv, x_recv, z_recv, sems, core_sems, credit)
    s = red.s
    cd0, cu0, cd1, cu1, co, *cq = chunks

    def load(k, src, dst):
        copy = pltpu.make_async_copy(src, dst, dsem.at[k])
        copy.start()
        return copy

    def relative(rel):
        return relative_piece(s, rel)

    def target(rel, chunk, base):
        low, high = lax.rem(rel, 2), lax.div(rel, 2)
        return low * (base + (1 - high) * chunk.rows) + (1 - low) * (high * chunk.y_send + (1 - high) * chunk.mine)

    def group_peer(k):
        return {"shard": lax.rem(s + k, 4)}

    def replica_peer(k):
        return {"replica": lax.rem(red.r + k, 2 * nz)}

    def group_copy(k):
        return pltpu.make_async_remote_copy(
            v_part.at[lax.rem(s + k, 4)], v_group.at[k - 1], group_sems.at[0, k - 1], group_sems.at[1, k - 1],
            device_id=group_peer(k), device_id_type=MESH)

    def all_copy(k):
        return pltpu.make_async_remote_copy(
            v_sum, v_all.at[red.r], all_sems.at[0, k - 1], all_sems.at[1, k - 1], device_id=replica_peer(k),
            device_id_type=MESH)

    got_up = load(7, up_h, up_s)

    def ffn(dr, dr_t, act2, act2_t, w_up, w_down, hid, br):
        def fetch(j, slot):
            piece, t = relative(3 - lax.rem(j, 4)), lax.div(j, 4)
            return (
                pltpu.make_async_copy(full_up.at[piece, :, at(t, TILE)], w_up.at[slot], wsem.at[0, slot]),
                pltpu.make_async_copy(full_down.at[piece, at(t, TILE), :], w_down.at[slot], wsem.at[1, slot]),
            )

        for copy in fetch(2, 0):
            copy.start()
        got_parts, got_act2, got_dr = (load(8, parts_h, buf.at[pl.ds(cd0.y_send, 2048), :]), load(0, act2_h, act2),
                                       load(1, dr_h, dr))
        got_gact, got_column = load(10, gact_h, gmid), load(11, column_h, sums_up)
        late = [load(2, dr_t_h, dr_t), load(3, act2_t_h, act2_t)]

        def keep(j, slot):
            return pltpu.make_async_copy(hid.at[slot], hidden_o.at[j - 2], hsem.at[slot])

        barrier = pltpu.get_barrier_semaphore()
        partners = [group_peer(k) for k in range(1, 4)] + [replica_peer(k) for k in range(1, 2 * nz)]
        for to in partners:
            pl.semaphore_signal(barrier, inc=1, device_id=to, device_id_type=MESH)
        pl.semaphore_wait(barrier, len(partners))
        unpack_vectors(vec, vecf, bias_qkv)
        unpack_bias_up(vec, bias_up)
        acc[...] = jnp.zeros_like(acc)
        got_parts.wait()
        red.y_copy(cd0).start()
        red.y_copy(cu0).start()
        got_act2.wait()
        got_dr.wait()

        def tile(j, carry):
            slot = lax.rem(j, 2)
            rel, t = 3 - lax.rem(j, 4), lax.div(j, 4)
            piece = relative(rel)
            low, high = lax.rem(rel, 2), lax.div(rel, 2)
            place_at = pl.multiple_of(
                (1 - low) * (high * (cd0.y_send + t * (cd1.y_send - cd0.y_send)) + (1 - high) * (cd0.mine + t * 2048)), 16)
            for copy in fetch(j, slot):
                copy.wait()

            @pl.when(j < 7)
            def _():
                for copy in fetch(j + 1, 1 - slot):
                    copy.start()

            @pl.when(j >= 4)
            def _():
                keep(j - 2, slot).wait()

            for k in (4, 6):
                @pl.when(j == k)
                def _(k=k):
                    red.core_copy(k // 2 - 1, 2048).wait_send()

            def on_back():
                @pl.when(j == 2)
                def _():
                    for copy in (got_gact, got_column):
                        copy.wait()

            def on_hidden():
                keep(j, slot).start()

                @pl.when(j == 2)
                def _():
                    for copy in late:
                        copy.wait()

            def put(half, value):
                buf[pl.ds(pl.multiple_of(place_at + half * D, 16), D), :] = value

            sums_up[pl.ds(2 * piece + t, 1), :] = ffn_tile(
                act2, dr, dr_t, act2_t, lambda: w_up[slot], lambda: w_down[slot], bias_up[pl.ds(2 * piece + t, 1), :],
                hid.at[slot], br, gmid, False, on_back, on_hidden, put)

            def y_part(turn, chunk):
                red.core_copy(turn, 2048).wait_recv()
                for k, c in enumerate(chunk):
                    red.add_core(turn, k * 1024, c.y_send, c.rows)
                    red.y_copy(c).start()

            def own_part(turn, chunk):
                red.core_copy(turn, 2048).wait_recv()
                red.add_core(turn, 0, chunk[0].mine, 2048)

            steps = {
                2: [lambda: red.core_copy(1, 2048).start()],
                3: [lambda: own_part(1, (cd0, cu0))],
                4: [lambda: red.core_copy(2, 2048).start(), lambda: red.on_y(cd0)],
                5: [lambda: y_part(2, (cd1, cu1))],
                6: [lambda: red.core_copy(3, 2048).start(), lambda: red.on_x(cd0), lambda: red.on_y(cu0)],
                7: [lambda: own_part(3, (cd1, cu1))],
            }
            for k, todo in steps.items():
                @pl.when(j == k)
                def _(todo=todo):
                    for step in todo:
                        step()
            return carry

        lax.fori_loop(2, 8, tile, 0)
        pl.semaphore_signal(credit, inc=1, device_id={"shard": red.across}, device_id_type=MESH)
        for j in (6, 7):
            keep(j, j % 2).wait()
        red.core_copy(3, 2048).wait_send()

    v = pltpu.VMEM
    pl.run_scoped(ffn, v((n, D), BF16), v((D, n), BF16), v((n, D), BF16), v((D, n), BF16), v((2, D, TILE), BF16),
                  v((2, TILE, D), BF16), v((2, n, TILE), BF16), v((n, TILE), BF16))
    got_up.wait()

    def spread(out, chunk, tile_rows, turn):
        for p in range(4):
            low = lax.rem(lax.rem(s, 2) + p % 2, 2)
            high = lax.rem(lax.div(s, 2) + p // 2, 2)
            start = pl.multiple_of(target(low + 2 * high, chunk, 1024 * (turn % 2)) + tile_rows, 16)
            buf[pl.ds(start, 256), :] = out[p * 256 : (p + 1) * 256].astype(BF16)

    def on_core(turn, chunk):
        red.core_copy(turn, 2 * chunk.rows).wait_recv()
        red.add_core(turn, 0, chunk.y_send, chunk.rows)
        red.y_copy(chunk).start()
        red.add_core(turn, chunk.rows, chunk.mine, chunk.rows)

    def attention(
        qkv, datt, brr, lse, lsec, scores, dprobs, probs, dscores, cls_row, qkv_cls, datt_cls, joint_cls, joint, extra
    ):
        got_qkv, got_lse, got_lsec = load(0, qkv_h, qkv), load(1, lse_h, lse), load(2, lsec_h, lsec)

        def middle(mid, branch, att_t, w_out):
            got_mid, got_branch = load(3, mid_h, mid), load(4, branch_h, branch)
            got_att, got_out = load(5, att_t_h, att_t), load(6, full_out, w_out)
            red.on_z(cd0)
            got_mid.wait()
            got_branch.wait()

            def norm_rows(rows):
                m = mid[rows, :]
                c = m - jnp.mean(m, axis=-1, keepdims=True)
                inv = lax.rsqrt(jnp.mean(c * c, axis=-1, keepdims=True) + 1e-06)
                hat = c * inv
                g = gmid[rows, :]
                acc[4] += fold(g * hat)
                acc[5] += fold(g)
                sc = g * vecf[4:5, :]
                back = inv * (sc - jnp.mean(sc, axis=-1, keepdims=True)
                              - hat * jnp.mean(sc * hat, axis=-1, keepdims=True))
                gm = up_s[rows, :].astype(F32) + back
                grad_mid[rows, :] = gm
                acc[3] += fold(gm * branch[rows, :].astype(F32))
                gb = gm * vecf[3:4, :]
                acc[2] += fold(gb)
                brr[rows, :] = gb.astype(BF16)

            rows_loop(n, 16, norm_rows)
            red.on_x(cu0)
            got_att.wait()
            for q in range(2):
                spread(dot(att_t[...], brr[:, q * TILE : (q + 1) * TILE]), co, q * 256, 4)
            red.core_copy(4, 2 * co.rows).start()
            got_out.wait()
            for q in range(2):
                datt[:, q * TILE : (q + 1) * TILE] = dot_nt(brr[...], w_out[q * TILE : (q + 1) * TILE, :]).astype(BF16)

        pl.run_scoped(middle, v((n, D), F32), v((n, D), BF16), v((D, n), BF16), v((D, D), BF16))
        got_qkv.wait()
        got_lse.wait()
        got_lsec.wait()
        qkv_cls[...] = qkv[main:, :].astype(F32)
        datt_cls[...] = datt[main:, :].astype(F32)
        joint_cls[...] = jnp.zeros_like(joint_cls)
        pl.semaphore_wait(credit, 1)
        on_core(4, co)
        plan = {0: [lambda: red.on_y(cd1), lambda: red.on_back(cd0)], 1: [lambda: red.on_z(cu0)],
                3: [lambda: red.on_x(cd1), lambda: red.on_back(cu0)], 5: [lambda: red.on_y(cu1)], 6: [lambda: red.on_z(cd1)]}

        def image(i, carry):
            for k, steps in plan.items():
                @pl.when(i == k)
                def _(steps=steps):
                    for step in steps:
                        step()

            attend_back(i, qkv, qkv_cls, datt, datt_cls, lse, lsec, scores, dprobs, probs, dscores, cls_row, joint_cls,
                        joint, extra, acc.at[8], acc.at[9])
            return carry

        lax.fori_loop(0, images, image, 0)
        qkv[main:, :] = joint_cls[...].astype(BF16)
        acc[8] += fold(joint_cls[:, 0:D])
        acc[9] += fold(joint_cls[:, 2 * D : 3 * D])

        def tail(act_t, w_qkv, turn, flat):
            x_s, gact, new = brr, gmid, datt
            got_act, got_x = load(3, act_t_h, act_t), load(4, x_h, x_s)

            def fetch(j):
                return pltpu.make_async_copy(full_qkv.at[pl.ds(j * 256, 256), :], w_qkv.at[j % 2], wsem.at[0, j % 2])

            fetch(0).start()
            fetch(1).start()
            def weight_grad(k):
                for q in range(2):
                    cols = slice((2 * k + q) * TILE, (2 * k + q + 1) * TILE)
                    spread(dot(act_t[...], qkv[:, cols]), cq[k], q * 256, 5 + k)

            def input_grad(j):
                fetch(j).wait()
                gact[:, j * 256 : (j + 1) * 256] = dot_nt(qkv[...], w_qkv[j % 2])
                if j < 2:
                    fetch(j + 2).start()

            got_act.wait()
            weight_grad(0)
            red.core_copy(5, 1024).start()
            red.on_x(cu1)
            red.core_copy(4, 1024).wait_send()
            weight_grad(1)
            on_core(5, cq[0])
            red.core_copy(6, 1024).start()
            red.on_y(co)
            red.core_copy(5, 1024).wait_send()
            weight_grad(2)
            on_core(6, cq[1])
            red.core_copy(7, 1024).start()
            red.on_back(cd1)
            input_grad(0)
            red.on_z(cu1)
            input_grad(1)
            on_core(7, cq[2])
            red.on_x(co)
            input_grad(2)
            red.on_y(cq[0])
            input_grad(3)
            got_x.wait()

            def norm_rows(rows):
                m = x_s[rows, :].astype(F32)
                c = m - jnp.mean(m, axis=-1, keepdims=True)
                inv = lax.rsqrt(jnp.mean(c * c, axis=-1, keepdims=True) + 1e-06)
                hat = c * inv
                g = gact[rows, :]
                acc[0] += fold(g * hat)
                acc[1] += fold(g)
                sc = g * vecf[0:1, :]
                back = inv * (sc - jnp.mean(sc, axis=-1, keepdims=True)
                              - hat * jnp.mean(sc * hat, axis=-1, keepdims=True))
                new[rows, :] = (grad_mid[rows, :] + back).astype(BF16)

            rows_loop(n, 16, norm_rows)
            red.on_z(co)
            red.on_x(cq[0])
            to_tokens(new, flat, turn)
            copy = pltpu.make_async_copy(flat, tokens_o, osem.at[0])
            copy.start()
            red.on_back(cu1)
            red.on_back(co)
            red.on_y(cq[1])
            copy.wait()

        pl.run_scoped(tail, v((D, n), BF16), v((2, 256, 3 * D), BF16),
                      v((2, main, 128), F32), v((main + images, D), BF16))

    pl.run_scoped(attention, v((n, 3 * D), BF16), v((n, D), BF16), v((n, D), BF16), v((images, HEADS, PATCH), F32),
                  v((images, HEADS, PATCH), F32), v((8, 256, PATCH), F32), v((8, 256, PATCH), F32),
                  v((8, 256, PATCH), BF16), v((8, 256, PATCH), BF16), v((HEADS, PATCH), F32), v((CLS, 3 * D), F32),
                  v((CLS, D), F32), v((CLS, 3 * D), F32), v((PATCH, 3 * D), BF16), v((3, PATCH, D), F32))

    def outcome(mid, hid, w_down, turn, flat, res):
        got_mid = load(3, mid_h, mid)

        def fetch(pair):
            copies = []
            for k in range(2):
                j = 2 * pair + k
                slot = pair % 2
                piece, t = relative(3 - j % 4), j // 4
                src = hid_h.at[k] if pair == 0 else hidden_o.at[j - 2]
                copies.append(pltpu.make_async_copy(src, hid.at[slot, :, pl.ds(k * TILE, TILE)], wsem.at[0, 2 * slot + k]))
                copies.append(pltpu.make_async_copy(full_down.at[piece, pl.ds(t * TILE, TILE), :],
                                                    w_down.at[slot, pl.ds(k * TILE, TILE), :], wsem.at[1, 2 * slot + k]))
            return copies

        for copy in fetch(0):
            copy.start()
        steps = {0: [lambda: red.on_z(cq[0]), lambda: red.on_x(cq[1])], 1: [lambda: red.on_back(cq[0])],
                 2: [lambda: red.on_y(cq[2]), lambda: red.on_z(cq[1])], 3: [lambda: red.on_back(cq[1])]}
        for pair in range(4):
            if pair < 3:
                for copy in fetch(pair + 1):
                    copy.start()
            for copy in fetch(pair):
                copy.wait()
            for q in range(2):
                cols = slice(q * TILE, (q + 1) * TILE)
                out = dot(hid[pair % 2], w_down[pair % 2, :, cols])
                if pair:
                    gmid[:, cols] += out
                else:
                    gmid[:, cols] = out
            for step in steps.get(pair, []):
                step()
        got_mid.wait()

        def rows_of(rows):
            projected = gmid[rows, :] + vecf[6:7, :]
            upstream = up_s[rows, :].astype(F32)
            acc[6] += fold(upstream * vecf[7:8, :])
            acc[7] += fold(upstream * projected)
            res[rows, :] = (mid[rows, :] + vecf[7:8, :] * projected).astype(BF16)

        rows_loop(n, 16, rows_of)
        for p in range(4):
            for k in range(8):
                v_part[p, k : k + 1, :] = jnp.sum(acc[k, :, p * 256 : (p + 1) * 256], axis=0, keepdims=True)
            joint = acc.at[8 + p // 2]
            for k in range(2):
                start = (p % 2) * TILE + k * 256
                v_part[p, 8 + k : 9 + k, :] = jnp.sum(joint[:, start : start + 256], axis=0, keepdims=True)
            for k in range(4):
                v_part[p, 10 + k : 11 + k, :] = sums_up[2 * p + k // 2 : 2 * p + k // 2 + 1, (k % 2) * 256 : (k % 2 + 1) * 256]
            v_part[p, 14:16, :] = jnp.zeros((2, 256), F32)
        for k in range(1, 4):
            group_copy(k).start()
        red.on_x(cq[2])
        total = v_part[s]
        for k in range(1, 4):
            group_copy(k).wait_recv()
            total = total + v_group[k - 1]
        v_sum[...] = total
        v_all[red.r] = total
        for k in range(1, 2 * nz):
            all_copy(k).start()
        to_tokens(res, flat, turn)
        copy = pltpu.make_async_copy(flat, result_o, osem.at[0])
        copy.start()
        red.on_z(cq[2])
        for k in range(1, 2 * nz):
            all_copy(k).wait_recv()
        total = v_all[0]
        for k in range(1, 2 * nz):
            total = total + v_all[k]
        v_group[0] = total
        small = pltpu.make_async_copy(v_group.at[0], small_o, osem.at[1])
        small.start()
        red.on_back(cq[2])
        copy.wait()
        small.wait()

    pl.run_scoped(outcome, v((n, D), F32), v((2, n, D), BF16), v((2, D, D), BF16), v((2, main, 128), F32),
                  v((main + images, D), BF16), v((n, D), BF16))
    copies = []
    for c in chunks:
        red.finish(c)
        half = c.rows // 2
        for k, (src, first, where) in enumerate(((x_recv, c.x_recv, red.x), (buf, c.far, 1 - red.x))):
            copy = pltpu.make_async_copy(
                src.at[pl.ds(first, half), :],
                sums_o.at[pl.ds(pl.multiple_of(c.mine - cd0.mine + where * half, 16), half), :], fsem.at[2 * c.index + k])
            copy.start()
            copies.append(copy)
    red.core_copy(6, 1024).wait_send()
    red.core_copy(7, 1024).wait_send()
    for k in range(1, 4):
        group_copy(k).wait_send()
    for k in range(1, 2 * nz):
        all_copy(k).wait_send()
    for c in chunks:
        red.drain(c)
    for copy in copies:
        copy.wait()


def convert_kernel(
    chunks, sums, small, result, tokens, result_o, tokens_o, g1_o, s1_o, qkv_o, bqv_o, out_o, bo_o, l1_o, g2_o, s2_o, up_o, bup_o, down_o, bd_o, l2_o,
    low, qkv, out, up, down, moved, dsem, osem, msem,
):
    base = chunks[0].mine
    moves = [pltpu.make_async_copy(src, moved.at[k], msem.at[0, k]) for k, src in enumerate((result, tokens))]
    stores = [pltpu.make_async_copy(moved.at[k], dst, msem.at[1, k]) for k, dst in enumerate((result_o, tokens_o))]
    gots = []
    for c in chunks:
        rows = pl.ds(c.mine - base, c.rows)
        gots.append(pltpu.make_async_copy(sums.at[rows, :], low.at[rows, :], dsem.at[c.index]))
        gots[-1].start()
    for copy in moves:
        copy.start()
    outs = []

    def send_out(src, dst):
        copy = pltpu.make_async_copy(src, dst, osem.at[len(outs)])
        copy.start()
        outs.append(copy)

    def block(c, first, count):
        return low[c.mine - base + first : c.mine - base + first + count, :]

    for t in range(2):
        gots[2 * t].wait()
        for k in range(8):
            down[t * TILE : (t + 1) * TILE, k * 128 : (k + 1) * 128] = block(chunks[2 * t], k * 128, 128).T.astype(F32)
        send_out(down.at[pl.ds(t * TILE, TILE), :], down_o.at[pl.ds(t * TILE, TILE), :])
        moves[t].wait()
        stores[t].start()
        gots[2 * t + 1].wait()
        up[t] = block(chunks[2 * t + 1], 0, D).astype(F32)
        send_out(up.at[t], up_o.at[:, pl.ds(t * TILE, TILE)])
    gots[4].wait()
    for k in range(2):
        out[:, k * TILE : (k + 1) * TILE] = block(chunks[4], k * 256, 256).astype(F32)
    send_out(out, out_o)
    for k in range(5, 8):
        gots[k].wait()
    for k in range(6):
        qkv[:, k * TILE : (k + 1) * TILE] = block(chunks[5], k * 256, 256).astype(F32)
    send_out(qkv, qkv_o)
    vectors = (g1_o, s1_o, bo_o, l1_o, g2_o, s2_o, bd_o, l2_o, bqv_o, bup_o)
    row = 0
    for v in vectors:
        for k in range(v.shape[0] // 256):
            v[pl.ds(k * 256, 256)] = small[row : row + 1, :].reshape(256)
            row += 1
    for copy in outs + stores:
        copy.wait()


def convert(chunks, sums, small, result, tokens):
    one = lambda k: jax.ShapeDtypeStruct((k,), F32)
    outs = (
        low_shape(*result.shape), low_shape(*tokens.shape), one(256), one(256), wide_shape(256, 3 * D), one(512), wide_shape(256, D), one(256), one(256), one(256), one(256),
        wide_shape(D, D), one(1024), wide_shape(D, D), one(256), one(256),
    )
    v = pltpu.VMEM
    return pl.pallas_call(
        functools.partial(convert_kernel, chunks),
        out_shape=outs,
        in_specs=[ANY, VMEM, ANY, ANY],
        out_specs=[VMEM if len(o.shape) == 1 else ANY for o in outs],
        scratch_shapes=[v(sums.shape, BF16), v((256, 3 * D), F32), v((256, D), F32), v((2, D, TILE), F32),
                        v((D, D), F32), v((2,) + result.shape, BF16), pltpu.SemaphoreType.DMA((8,)),
                        pltpu.SemaphoreType.DMA((6,)), pltpu.SemaphoreType.DMA((2, 2))],
        compiler_params=pltpu.CompilerParams(vmem_limit_bytes=LIMIT),
        name="gradients_to_float32",
    )(sums, small, result, tokens)


def low_shape(*shape):
    return jax.ShapeDtypeStruct(shape, BF16)


def wide_shape(*shape):
    return jax.ShapeDtypeStruct(shape, F32)


ANY = pl.BlockSpec(memory_space=pl.ANY)
VMEM = pl.BlockSpec(memory_space=pltpu.VMEM)
LIMIT = 62 * 2**20


def forward(flat, cot, vectors, w_qkv, w_out, w_up, w_down):
    images = flat.shape[0] // (PATCH + 1)
    n = images * PATCH + CLS
    v = pltpu.VMEM
    outs = (
        low_shape(D, 3 * D), low_shape(D, D), low_shape(4, D, D), low_shape(4, D, D), low_shape(4, 16, 256),
        low_shape(n, 3 * D), low_shape(D, n), low_shape(n, D), low_shape(D, n), wide_shape(n, D), low_shape(n, D),
        low_shape(n, D), low_shape(D, n), low_shape(n, D), low_shape(n, D), low_shape(D, n),
        wide_shape(images, HEADS, PATCH), wide_shape(images, HEADS, PATCH),
        low_shape(2048, TILE), low_shape(2, n, TILE), wide_shape(n, D), wide_shape(8, TILE),
    )
    return pl.pallas_call(
        gather_kernel,
        out_shape=outs,
        in_specs=[ANY] * 2 + [VMEM] * 10 + [ANY] * 4,
        out_specs=[ANY] * len(outs),
        scratch_shapes=[
            v((D, 3 * D), BF16), v((D, D), BF16), v((4, D, D), BF16), v((4, D, D), BF16),
            v((n, D), BF16), v((n, 3 * D), BF16), v((n, D), BF16), v((n, D), BF16), v((n, D), F32), v((n, D), BF16),
            v((n, D), BF16), v((D, n), BF16), v((D, n), BF16),
            v((images, HEADS, PATCH), F32), v((images, HEADS, PATCH), F32),
            v((8, 256, PATCH), F32), v((8, 256, PATCH), BF16), v((PATCH, D), F32), v((HEADS, PATCH), F32),
            v((CLS, D), F32), v((CLS, 3 * D), F32), v((2, images * PATCH, 128), F32), v((16, 256), F32),
            v((16, 256), BF16), v((4, 16, 256), BF16), v((16, D), F32), v((8, 3 * D), F32), v((8, TILE), F32),
            v((8, TILE), F32), v((2, D, TILE), BF16), v(flat.shape, BF16), pltpu.SemaphoreType.DMA((2, 7, 11)), pltpu.SemaphoreType.DMA((7,)), pltpu.SemaphoreType.DMA((2, 3)),
            pltpu.SemaphoreType.DMA((30,)), pltpu.SemaphoreType.DMA((2, 2)),
            pltpu.SemaphoreType.DMA((1,)),
        ],
        compiler_params=pltpu.CompilerParams(collective_id=0, has_side_effects=True, vmem_limit_bytes=LIMIT),
        cost_estimate=pl.CostEstimate(flops=18 * 2**30, bytes_accessed=64 * 2**20, transcendentals=3 * 2**20),
        name="gather_and_attention",
    )(flat, cot, *vectors, w_qkv, w_out, w_up, w_down)


def backward(nz, images, vec, *arrays):
    n = images * PATCH + CLS
    tokens = images * (PATCH + 1)
    v = pltpu.VMEM
    chunks, sizes = chunk_layout(nz)
    outs = (low_shape(tokens, D), low_shape(tokens, D), low_shape(sizes["total"], TILE), wide_shape(16, 256),
            low_shape(6, n, TILE))
    return pl.pallas_call(
        functools.partial(backward_kernel, nz, chunks),
        out_shape=outs,
        in_specs=[VMEM] + [ANY] * len(arrays),
        out_specs=[ANY] * len(outs),
        scratch_shapes=[
            v((sizes["buf"], TILE), BF16), v((2, 2048, TILE), BF16), v((sizes["y_recv"], TILE), BF16),
            v((sizes["x_recv"], TILE), BF16), v((nz - 1, sizes["z_recv"], TILE), BF16), v((n, D), F32), v((n, D), F32), v((n, D), BF16),
            v((10, 8, D), F32), v((8, TILE), F32), v((16, D), F32), v((8, 3 * D), F32), v((8, TILE), F32),
            v((4, 16, 256), F32), v((3, 16, 256), F32), v((16, 256), F32), v((2 * nz, 16, 256), F32),
            pltpu.SemaphoreType.DMA((2, len(chunks), 3 * nz)), pltpu.SemaphoreType.DMA((2, 8)),
            pltpu.SemaphoreType.DMA((2, 3)), pltpu.SemaphoreType.DMA((2, 2 * nz - 1)),
            pltpu.SemaphoreType.REGULAR, pltpu.SemaphoreType.DMA((12,)), pltpu.SemaphoreType.DMA((2, 4)),
            pltpu.SemaphoreType.DMA((2,)), pltpu.SemaphoreType.DMA((2,)), pltpu.SemaphoreType.DMA((2 * len(chunks),)),
        ],
        compiler_params=pltpu.CompilerParams(collective_id=1, has_side_effects=True, vmem_limit_bytes=LIMIT),
        cost_estimate=pl.CostEstimate(flops=66 * 2**30, bytes_accessed=128 * 2**20, transcendentals=8 * 2**20),
        name="layer_backward",
    )(vec, *arrays), chunks


def on_device(
    tokens, norm1_gain, norm1_shift, w_qkv, bias_qv, w_out, bias_out, scale_one, norm2_gain, norm2_shift, w_up, bias_up,
    w_down, bias_down, scale_two, cotangent,
):
    images, length, _ = tokens.shape
    nz = lax.axis_size("replica") // 2
    flatten = lambda a: jnp.transpose(a, (1, 0, 2)).reshape(images * length, D)
    restore = lambda a: jnp.transpose(a.reshape(length, images, D), (1, 0, 2))
    vectors = (norm1_gain, norm1_shift, bias_out, scale_one, norm2_gain, norm2_shift, bias_down, scale_two, bias_qv, bias_up)
    full_qkv, full_out, full_up, full_down, vec, *kept = forward(
        flatten(tokens), flatten(cotangent), vectors, w_qkv, w_out, w_up, w_down)
    (result, grad_tokens, sums, small, _), chunks = backward(nz, images, vec, full_qkv, full_out, full_up, full_down, *kept)
    result, grad_tokens, *gradients = convert(chunks, sums, small, result, grad_tokens)
    return (restore(result), restore(grad_tokens)) + tuple(gradients)


def solution(mesh):
    placed = (
        P(("shard", "replica"), None, None),
        P("shard"),
        P("shard"),
        P("shard", None),
        P("shard"),
        P("shard", None),
        P("shard"),
        P("shard"),
        P("shard"),
        P("shard"),
        P(None, "shard"),
        P("shard"),
        P("shard", None),
        P("shard"),
        P("shard"),
        P(("shard", "replica"), None, None),
    )
    return jax.shard_map(
        on_device,
        mesh=mesh,
        in_specs=placed,
        out_specs=(
            P(("shard", "replica"), None, None),
            P(("shard", "replica"), None, None),
            P("shard"),
            P("shard"),
            P("shard", None),
            P("shard"),
            P("shard", None),
            P("shard"),
            P("shard"),
            P("shard"),
            P("shard"),
            P(None, "shard"),
            P("shard"),
            P("shard", None),
            P("shard"),
            P("shard"),
        ),
        check_vma=False,
    )
```

```python
import functools

import jax
import jax.numpy as jnp
from jax import lax
from jax.experimental import pallas as pl
from jax.experimental.pallas import tpu as pltpu
from jax.sharding import PartitionSpec as P

F32 = jnp.float32
BF16 = jnp.bfloat16
D = 1024
FF = 4096
HEADS = 16
PATCH = 128
CLS = 16
TILE = 512
FACTOR = 0.125
MESH = pl.DeviceIdType.MESH


def dot(a, b):
    return jnp.dot(a, b, preferred_element_type=F32)


def dot_nt(a, b):
    return lax.dot_general(a, b, (((1,), (1,)), ((), ())), preferred_element_type=F32)


def dot_tn(a, b):
    return lax.dot_general(a, b, (((0,), (0,)), ((), ())), preferred_element_type=F32)


def at(index, size):
    return pl.ds(pl.multiple_of(index * size, size), size)


def head_mask():
    lane = lax.shift_right_logical(lax.broadcasted_iota(jnp.int32, (HEADS, D), 1), 6)
    return lane == lax.broadcasted_iota(jnp.int32, (HEADS, D), 0)


def split_pair(v):
    low = lax.broadcasted_iota(jnp.int32, v.shape, 1) < 64
    zero = jnp.zeros_like(v)
    return jnp.concatenate([jnp.where(low, v, zero), jnp.where(low, zero, v)], 0)


def merge_pair(v):
    n = v.shape[0] // 2
    low = lax.broadcasted_iota(jnp.int32, (n, v.shape[1]), 1) < 64
    return jnp.where(low, v[:n], v[n:])


def place():
    s = lax.axis_index("shard")
    r = lax.axis_index("replica")
    x = lax.rem(r, 2)
    z = lax.div(r, 2)
    return s, r, x, z


def peers(s, r):
    sib = s + 1 - 2 * lax.rem(s, 2)
    across = lax.rem(s + 2, 4)
    side = r + 1 - 2 * lax.rem(r, 2)
    return sib, across, side


def rows_loop(n, step, body):
    lax.fori_loop(0, n // step, lambda k, c: (body(at(k, step)), c)[1], 0, unroll=13)


def unpack_vectors(vec, vecf, bias_qkv):
    for v in range(8):
        for s in range(4):
            vecf[v : v + 1, s * 256 : (s + 1) * 256] = vec[s, v : v + 1, :].astype(F32)
    bias_qkv[...] = jnp.zeros_like(bias_qkv)
    for s in range(4):
        for t in range(2):
            col = (s * 2 + t) * 256 + (D if s >= 2 else 0)
            bias_qkv[0:1, col : col + 256] = vec[s, 8 + t : 9 + t, :].astype(F32)


def layer_norm(v, gain, shift):
    c = v - jnp.mean(v, axis=-1, keepdims=True)
    inv = lax.rsqrt(jnp.mean(c * c, axis=-1, keepdims=True) + 1e-06)
    return c * inv * gain + shift


def to_images(src, dst, turn):
    images = (src.shape[0]) // (PATCH + 1)
    main = images * PATCH

    def lane_block(l, carry):
        cols = at(l, 128)
        slot = lax.rem(l, 2)
        turn[slot] = src[0:main, cols].astype(F32)
        for i in range(images):
            dst[i * PATCH : (i + 1) * PATCH, cols] = turn[slot, pl.ds(i, PATCH, stride=images), :].astype(BF16)
        return carry

    lax.fori_loop(0, D // 128, lane_block, 0)
    last = src[main : main + images, :].astype(F32)
    dst[main:, :] = jnp.concatenate([last, jnp.zeros((CLS - images, D), F32)], 0).astype(BF16)


def pack_vectors(vectors, dst):
    row = 0
    for v in vectors:
        count = v.shape[0] // 256
        wide = v[...].astype(F32)
        for k in range(count):
            dst[row : row + 1, :] = wide[k * 256 : (k + 1) * 256].reshape(1, 256)
            row += 1


def attend(i, qkv, qkv_cls, scores, probs, mix, probs_cls, att, att_cls, lse, lse_cls):
    rows = at(i, PATCH)
    mask = head_mask()
    own = qkv_cls[pl.ds(i, 1), :]
    q_c, k_c, v_c = own[:, :D] * FACTOR, own[:, D : 2 * D], own[:, 2 * D :]
    q_bd = jnp.where(mask, q_c, 0.0)
    k_bd = jnp.where(mask, k_c, 0.0).astype(BF16)
    v_bd = jnp.where(mask, v_c, 0.0).astype(BF16)
    to_cls = dot_nt(k_bd, qkv[rows, 0:D]) * FACTOR
    of_cls = dot_nt(q_bd.astype(BF16), qkv[rows, D : 2 * D])
    corner = jnp.sum(q_bd * k_c, axis=1, keepdims=True)
    top = jnp.maximum(jnp.max(of_cls, axis=1, keepdims=True), corner)
    e_row = jnp.exp(of_cls - top)
    e_cor = jnp.exp(corner - top)
    total = jnp.sum(e_row, axis=1, keepdims=True) + e_cor
    inv = 1.0 / total
    row = dot((e_row * inv).astype(BF16), qkv[rows, 2 * D : 3 * D])
    row = row + (e_cor * inv).astype(BF16).astype(F32) * v_c
    att_cls[pl.ds(i, 1), :] = jnp.sum(jnp.where(mask, row, 0.0), axis=0, keepdims=True)
    lse_cls[i] = jnp.broadcast_to(top + jnp.log(total), (HEADS, PATCH))
    for g in range(HEADS // 2):
        q2 = qkv[rows, g * 128 : g * 128 + 128] * jnp.asarray(FACTOR, BF16)
        scores[g] = dot_nt(split_pair(qkv[rows, g * 128 + D : g * 128 + D + 128]), q2)
    for g in range(HEADS // 2):
        for u in range(2):
            h = 2 * g + u
            part = scores[g, u * PATCH : (u + 1) * PATCH, :]
            extra = to_cls[h : h + 1, :]
            top = jnp.maximum(jnp.max(part, axis=0, keepdims=True), extra)
            e_part = jnp.exp(part - top)
            e_extra = jnp.exp(extra - top)
            total = jnp.sum(e_part, axis=0, keepdims=True) + e_extra
            inv = 1.0 / total
            probs[g, u * PATCH : (u + 1) * PATCH, :] = (e_part * inv).astype(BF16)
            probs_cls[h : h + 1, :] = e_extra * inv
            lse[i, h : h + 1, :] = top + jnp.log(total)
    for g in range(HEADS // 2):
        v2 = split_pair(qkv[rows, g * 128 + 2 * D : g * 128 + 2 * D + 128])
        mix[:, g * 128 : g * 128 + 128] = dot_tn(probs[g], v2)
    att[rows, :] = (mix[...] + dot_tn(probs_cls[...].astype(BF16), v_bd)).astype(BF16)


class Gather:
    KINDS = ("own", "far", "x1", "z1", "x2", "z2", "p0", "p1", "p2", "p3", "p4")

    def __init__(self, number, rows, src, dst, sems, local):
        s, r, x, z = place()
        sib, across, side = peers(s, r)
        self.number, self.sems = number, sems
        near = lax.rem(z, 2)
        level = {"replica": (z + 1 - 2 * near) * 2 + x}
        side, sib = {"replica": side}, {"shard": sib}
        size = rows // 4
        half = size // 2

        def start(zz, xx):
            return pl.multiple_of((2 * zz + xx) * size, 16)

        def same(first, count, to):
            ref = dst(across, pl.multiple_of(first, 16), count)
            return ref, ref, to

        mine, by_x, by_z, by_both = start(near, x), start(near, 1 - x), start(1 - near, x), start(1 - near, 1 - x)
        self.parts = {
            "own": (dst(s, 0, rows), dst(s, 0, rows), sib),
            "far": (dst(s, mine, size), dst(s, mine, size), {"shard": across}),
            "x1": same(mine, size, side),
            "z1": same(mine, size, level),
            "x2": same(by_z, half, side),
            "z2": same(by_x + half, half, level),
            "p0": same(mine, size, sib),
            "p1": same(by_x, size, sib),
            "p2": same(by_z, size, sib),
            "p3": same(by_both, half, sib),
            "p4": same(by_both + half, half, sib),
        }
        self.local = pltpu.make_async_copy(src(0, rows), dst(s, 0, rows), local.at[number])

    def copy(self, kind):
        a, b, to = self.parts[kind]
        k = self.KINDS.index(kind)
        return pltpu.make_async_remote_copy(
            a, b, self.sems.at[0, self.number, k], self.sems.at[1, self.number, k], device_id=to, device_id_type=MESH
        )

    def load(self):
        self.local.start()

    def begin(self):
        self.local.wait()
        self.copy("far").start()

    def share(self):
        self.copy("own").start()

    def on_far(self):
        self.copy("far").wait_recv()
        for kind in ("x1", "z1", "p0"):
            self.copy(kind).start()

    def on_near(self):
        self.copy("x1").wait_recv()
        self.copy("z2").start()
        self.copy("p1").start()
        self.copy("z1").wait_recv()
        self.copy("x2").start()
        self.copy("p2").start()

    def on_last(self):
        self.copy("x2").wait_recv()
        self.copy("p3").start()
        self.copy("z2").wait_recv()
        self.copy("p4").start()

    def ready(self):
        for kind in ("own", "p0", "p1", "p2", "p3", "p4"):
            self.copy(kind).wait_recv()

    def drain(self):
        for kind in self.KINDS:
            self.copy(kind).wait_send()


def relative_piece(s, rel):
    low, high = lax.rem(rel, 2), lax.div(rel, 2)
    return s + low * (1 - 2 * lax.rem(s, 2)) + high * (2 - 4 * lax.div(s, 2))


def unpack_bias_up(vec, bias_up):
    for p in range(4):
        for t in range(2):
            for k in range(2):
                row = 10 + 2 * t + k
                bias_up[2 * p + t : 2 * p + t + 1, k * 256 : (k + 1) * 256] = vec[p, row : row + 1, :].astype(F32)


def ffn_tile(act2, dr, dr_t, act2_t, w_up, w_down, bias, hid, br, gmid, fresh, on_back, on_hidden, put):
    n = act2.shape[0]
    cut = 16 * (n // 32)
    first, second = slice(0, cut), slice(cut, n)

    def both(rows, before, grad):
        hidden, step = gelu_both(before)
        hid[rows, :] = hidden.astype(BF16)
        grad = grad * step
        br[rows, :] = grad.astype(BF16)
        return jnp.sum(grad, axis=0, keepdims=True)

    def back(rows):
        out = dot_nt(br[rows, :], w_up())
        if fresh:
            gmid[rows, :] = out
        else:
            gmid[rows, :] += out

    before0 = dot(act2[first, :], w_up()) + bias
    grad0 = dot_nt(dr[first, :], w_down())
    before1 = dot(act2[second, :], w_up()) + bias
    column = both(first, before0, grad0)
    grad1 = dot_nt(dr[second, :], w_down())
    on_back()
    back(first)
    column = column + both(second, before1, grad1)
    back(second)
    on_hidden()
    put(0, dot(dr_t[...], hid[...]).astype(BF16))
    put(1, dot(act2_t[...], br[...]).astype(BF16))
    return column


def gather_kernel(
    tokens_h, cot_h, v0, v1, v2, v3, v4, v5, v6, v7, v8, v9, w_qkv, w_out, w_up, w_down,
    qkv_w_o, out_w_o, up_w_o, down_w_o, vec_all, qkv_o, act_t_o, x_o, att_t_o, mid_o, branch_o, act2_o, act2_t_o, up_o,
    dr_o, dr_t_o, lse_o, lsec_o, parts_o, hid_o, gact_o, column_o,
    full_qkv, full_out, full_up, full_down, x_s, qkv, act, att, mid, branch, act2, turned_a, turned_b, lse, lsec,
    scores, probs, mix, probs_cls, cls, qkv_cls, turn, vec32, vec_own_s, vec, vecf, bias_qkv,
    bias_up, column, core_in, flat,
    sems, local, vsem, osem, csem, fsem,
):
    s, r, x, z = place()
    sib, across, side = peers(s, r)
    n = x_s.shape[0]
    images = lse.shape[0]
    main = images * PATCH

    def load(src):
        copy = pltpu.make_async_copy(src, flat, fsem.at[0])
        copy.start()
        return copy

    got_tokens = load(tokens_h)
    vec32[...] = jnp.zeros_like(vec32)
    pack_vectors((v0, v1, v2, v3, v4, v5, v6, v7, v8, v9), vec32)
    vec_own_s[...] = vec32[...].astype(BF16)
    barrier = pltpu.get_barrier_semaphore()
    level = (z + 1 - 2 * lax.rem(z, 2)) * 2 + x
    for to in ({"shard": sib}, {"shard": across}, {"replica": side}, {"replica": level}):
        pl.semaphore_signal(barrier, inc=1, device_id=to, device_id_type=MESH)

    def unit(number, rows, src, dst):
        return Gather(number, rows, src, dst, sems, local)

    def qkv_unit(number, t):
        cols = pl.ds(t * 3 * TILE, 3 * TILE)
        return unit(number, 256, lambda a, k: w_qkv.at[pl.ds(a, k), cols],
                    lambda p, a, k: full_qkv.at[pl.ds(pl.multiple_of(p * 256 + a, 16), k), cols])

    g_qa, g_qb = qkv_unit(0, 0), qkv_unit(6, 1)
    g_out = unit(1, 256, lambda a, k: w_out.at[pl.ds(a, k), :],
                 lambda p, a, k: full_out.at[pl.ds(pl.multiple_of(p * 256 + a, 16), k), :])

    def up_unit(number, t):
        cols = pl.ds(t * TILE, TILE)
        return unit(number, D, lambda a, k: w_up.at[pl.ds(a, k), cols],
                    lambda p, a, k: full_up.at[p, pl.ds(pl.multiple_of(a, 16), k), cols])

    def down_unit(number, t):
        return unit(number, TILE, lambda a, k: w_down.at[pl.ds(a + t * TILE, k), :],
                    lambda p, a, k: full_down.at[p, pl.ds(pl.multiple_of(a + t * TILE, 16), k), :])

    g_up0, g_down0, g_up1, g_down1 = up_unit(2, 0), down_unit(3, 0), up_unit(4, 1), down_unit(5, 1)

    for g in (g_qa, g_qb, g_out, g_up0, g_down0, g_up1, g_down1):
        g.load()
    pl.semaphore_wait(barrier, 4)

    def vec_copy(k, src, slot, to):
        return pltpu.make_async_remote_copy(src, vec.at[slot], vsem.at[0, k], vsem.at[1, k], device_id=to,
                                            device_id_type=MESH)

    vec_own = vec_copy(0, vec_own_s, s, {"shard": sib})
    vec_far = vec_copy(1, vec_own_s, s, {"shard": across})
    vec_pass = vec_copy(2, vec.at[across], across, {"shard": sib})
    vec_own.start()
    vec_far.start()
    for g in (g_qa, g_qb):
        g.begin()
        g.share()
    g_out.begin()
    vec[s] = vec_own_s[...]

    got_tokens.wait()
    to_images(flat, x_s, turn)
    got_cot = load(cot_h)
    outs = {}

    def send_out(k, src, dst):
        outs[k] = pltpu.make_async_copy(src, dst, osem.at[k])
        outs[k].start()

    send_out(0, x_s, x_o)
    vec_far.wait_recv()
    vec_pass.start()
    vec_own.wait_recv()
    vec_pass.wait_recv()
    unpack_vectors(vec, vecf, bias_qkv)
    g_qa.on_far()

    def first_norm(rows):
        act[rows, :] = layer_norm(x_s[rows, :].astype(F32), vecf[0:1, :], vecf[1:2, :]).astype(BF16)

    rows_loop(n, 16, first_norm)
    g_qa.on_near()
    g_qb.on_far()
    for g in (g_up0, g_down0, g_up1, g_down1):
        g.begin()
    transpose_into(act, turned_b)
    send_out(1, turned_b, act_t_o)
    got_cot.wait()
    to_images(flat, branch, turn)
    g_qa.on_last()
    g_qb.on_near()

    def down_rows(rows):
        act2[rows, :] = (branch[rows, :].astype(F32) * vecf[7:8, :]).astype(BF16)

    rows_loop(n, 16, down_rows)
    send_out(14, branch, up_o)
    send_out(15, act2, dr_o)
    transpose_into(act2, turned_a)
    send_out(16, turned_a, dr_t_o)
    g_qb.on_last()
    g_out.on_far()
    g_qa.ready()

    def qkv_tile(j, carry):
        cols = at(j, TILE)
        low = (dot(act[...], full_qkv[:, cols]) + bias_qkv[0:1, cols]).astype(BF16)
        qkv[:, cols] = low
        qkv_cls[:, cols] = low[main:].astype(F32)
        return carry

    lax.fori_loop(0, 3, qkv_tile, 0)
    g_out.on_near()
    g_qb.ready()
    send_out(4, full_qkv, qkv_w_o)
    for g in (g_out, g_up0, g_down0):
        g.share()
    lax.fori_loop(3, 6, qkv_tile, 0)
    send_out(2, qkv, qkv_o)
    act[...] = act2[...]
    unpack_bias_up(vec, bias_up)
    column[...] = jnp.zeros_like(column)
    send_out(3, vec, vec_all)
    cls[...] = jnp.zeros_like(cls)
    g_out.on_last()
    g_up0.on_far()
    plan = {1: [g_up0.on_near], 2: [g_down0.on_far], 3: [g_up0.on_last, g_up1.share], 4: [g_down0.on_near, g_up1.on_far],
            6: [g_down0.on_last, g_down1.share], 7: [g_up1.on_near, g_down1.on_far]}

    def image(i, carry):
        for k, steps in plan.items():
            @pl.when(i == k)
            def _(steps=steps):
                for step in steps:
                    step()

        attend(i, qkv, qkv_cls, scores, probs, mix, probs_cls, att, cls, lse, lsec)
        return carry

    lax.fori_loop(0, images, image, 0)
    att[main:, :] = cls[...].astype(BF16)
    outs.pop(1).wait()
    transpose_into(att, turned_b)
    send_out(8, turned_b, att_t_o)
    send_out(9, lse, lse_o)
    send_out(10, lsec, lsec_o)
    g_out.ready()
    outs.pop(14).wait()
    for j in range(D // TILE):
        cols = slice(j * TILE, (j + 1) * TILE)
        out = dot(att[...], full_out[:, cols]) + vecf[2:3, cols]
        branch[:, cols] = out.astype(BF16)
        mid[:, cols] = x_s[:, cols].astype(F32) + vecf[3:4, cols] * out
    send_out(11, mid, mid_o)
    send_out(12, branch, branch_o)
    g_up1.on_last()
    g_down1.on_near()

    def second_norm(rows):
        act2[rows, :] = layer_norm(mid[rows, :], vecf[4:5, :], vecf[5:6, :]).astype(BF16)

    outs.pop(15).wait()
    rows_loop(n, 16, second_norm)
    send_out(13, act2, act2_o)
    outs.pop(8).wait()
    transpose_into(act2, turned_b)
    send_out(17, turned_b, act2_t_o)
    half = pl.ds(0, TILE)
    rest = pl.ds(TILE, TILE)
    send_out(5, full_out, out_w_o)
    g_up0.ready()
    send_out(18, full_up.at[:, :, half], up_w_o.at[:, :, half])
    g_down0.ready()
    send_out(19, full_down.at[:, half, :], down_w_o.at[:, half, :])
    for k in (2, 11):
        outs.pop(k).wait()
    hid, br = qkv.at[:, pl.ds(0, TILE)], qkv.at[:, pl.ds(TILE, TILE)]
    def core_copy(half_k):
        return pltpu.make_async_remote_copy(
            qkv.at[pl.ds(0, D), pl.ds((2 + half_k) * TILE, TILE)], core_in.at[half_k], csem.at[0, half_k],
            csem.at[1, half_k], device_id={"shard": sib}, device_id_type=MESH)

    for k, rel in enumerate((3, 2)):
        piece = relative_piece(s, rel)

        def put(half_k, value, k=k):
            qkv[0:D, (2 + 2 * k + half_k) * TILE : (3 + 2 * k + half_k) * TILE] = value

        if k:
            outs.pop(22).wait()
        column[pl.ds(2 * piece, 1), :] = ffn_tile(
            act2, act, turned_a, turned_b, lambda: full_up[piece, :, 0:TILE], lambda: full_down[piece, 0:TILE, :],
            bias_up[pl.ds(2 * piece, 1), :], hid, br, mid, k == 0, lambda: None, lambda: send_out(22 + k, hid, hid_o.at[k]), put)
        if k == 0:
            for half_k in range(2):
                core_copy(half_k).start()
            g_down1.on_last()
            g_up1.ready()
            send_out(20, full_up.at[:, :, rest], up_w_o.at[:, :, rest])
    send_out(28, mid, gact_o)
    for half_k in range(2):
        core_copy(half_k).wait_recv()
        cols = slice((4 + half_k) * TILE, (5 + half_k) * TILE)

        def join(k, carry, half_k=half_k, cols=cols):
            rows = at(k, 128)
            qkv[rows, cols] = (qkv[rows, cols].astype(F32) + core_in[half_k, rows, :].astype(F32)).astype(BF16)
            return carry

        lax.fori_loop(0, D // 128, join, 0)
        send_out(24 + half_k, qkv.at[pl.ds(0, D), pl.ds((4 + half_k) * TILE, TILE)], parts_o.at[pl.ds(half_k * D, D), :])
    send_out(29, column, column_o)
    g_down1.ready()
    send_out(21, full_down.at[:, rest, :], down_w_o.at[:, rest, :])
    for half_k in range(2):
        core_copy(half_k).wait_send()
    for copy in outs.values():
        copy.wait()
    for g in (g_qa, g_qb, g_out, g_up0, g_down0, g_up1, g_down1):
        g.drain()
    for copy in (vec_own, vec_far, vec_pass):
        copy.wait_send()


class Chunk:
    def __init__(self, index, rows, mine, y_send, y_recv, x_recv, z_recv, far):
        self.index, self.rows, self.mine, self.y_send, self.far = index, rows, mine, y_send, far
        self.y_recv, self.x_recv, self.z_recv = y_recv, x_recv, z_recv


def chunk_layout(nz):
    sizes = [1024, 1024, 1024, 1024, 512, 512, 512, 512]
    y_base = 2048
    y_a = y_base
    y_b = y_a + 2048
    mine_base = y_b + 2048
    chunks = []
    mine = mine_base
    late = 0
    xr = zr = 0
    for k, rows in enumerate(sizes):
        if k < 2:
            ys, yr = y_a + 1024 * k, 1024 * k
        elif k < 4:
            ys, yr = y_b + 1024 * (k - 2), 2048 + 1024 * (k - 2)
        else:
            ys, yr = y_a + late, late
            late += rows
        far = mine_base + sum(sizes) + 512 * k if k < 2 else ys
        chunks.append(Chunk(k, rows, mine, ys, yr, xr, zr, far))
        mine += rows
        xr += rows // 2
        zr += rows // 2 // nz
    return chunks, dict(buf=mine + 1024, total=sum(sizes), mine=mine_base, y_recv=2 * 2048, x_recv=xr, z_recv=zr)


def add_rows(dst, d0, src, s0, rows):
    step = next(k for k in (128, 96, 64, 32, 16) if rows % k == 0)

    def body(k, carry):
        d = pl.ds(pl.multiple_of(d0 + k * step, 16), step)
        t = pl.ds(pl.multiple_of(s0 + k * step, 16), step)
        dst[d, :] = (dst[d, :].astype(F32) + src[t, :].astype(F32)).astype(BF16)
        return carry

    lax.fori_loop(0, rows // step, body, 0)


class Reduce:
    def __init__(self, nz, buf, core_recv, y_recv, x_recv, z_recv, sems, core_sems, credit):
        self.nz, self.buf, self.core_recv = nz, buf, core_recv
        self.y_recv, self.x_recv, self.z_recv = y_recv, x_recv, z_recv
        self.sems, self.core_sems, self.credit = sems, core_sems, credit
        self.s, self.r, self.x, self.z = place()
        self.sib, self.across, self.side = peers(self.s, self.r)

    def remote(self, src, dst, chunk, kind, to):
        return pltpu.make_async_remote_copy(
            src, dst, self.sems.at[0, chunk.index, kind], self.sems.at[1, chunk.index, kind], device_id=to,
            device_id_type=MESH)

    def peer(self, k):
        return {"replica": lax.rem(self.z + k, self.nz) * 2 + self.x}

    def core_copy(self, turn, rows):
        slot = turn % 2
        return pltpu.make_async_remote_copy(
            self.buf.at[pl.ds(slot * 1024 if turn > 3 else 0, rows), :], self.core_recv.at[slot, pl.ds(0, rows), :],
            self.core_sems.at[0, turn], self.core_sems.at[1, turn], device_id={"shard": self.sib}, device_id_type=MESH)

    def add_core(self, turn, first, dst, rows):
        add_rows(self.buf, dst, self.core_recv.at[turn % 2], first, rows)

    def y_copy(self, c):
        return self.remote(self.buf.at[pl.ds(c.y_send, c.rows), :], self.y_recv.at[pl.ds(c.y_recv, c.rows), :], c, 0,
                           {"shard": self.across})

    def x_copy(self, c):
        half = c.rows // 2
        return self.remote(self.buf.at[pl.ds(pl.multiple_of(c.mine + (1 - self.x) * half, 16), half), :],
                           self.x_recv.at[pl.ds(c.x_recv, half), :], c, 1, {"replica": self.side})

    def quarter(self, c, x, z):
        half = c.rows // 2
        size = half // self.nz
        return pl.ds(pl.multiple_of(c.mine + x * half + z * size, 16), size)

    def z_copy(self, c, k):
        size = c.rows // 2 // self.nz
        return self.remote(self.buf.at[self.quarter(c, self.x, lax.rem(self.z + k, self.nz)), :],
                           self.z_recv.at[k - 1, pl.ds(c.z_recv, size), :], c, 1 + k, self.peer(k))

    def done(self, first, c, z):
        size = c.rows // 2 // self.nz
        return pl.ds(pl.multiple_of(first + z * size, 16), size)

    def back_z(self, c, k):
        part = self.x_recv.at[self.done(c.x_recv, c, self.z), :]
        return self.remote(part, part, c, self.nz + k, self.peer(k))

    def back_x(self, c, k):
        z = lax.rem(self.z + self.nz - k, self.nz)
        return self.remote(self.x_recv.at[self.done(c.x_recv, c, z), :], self.buf.at[self.done(c.far, c, z), :], c,
                           2 * self.nz + k, {"replica": self.side})

    def on_y(self, c):
        self.y_copy(c).wait_recv()
        add_rows(self.buf, c.mine, self.y_recv, c.y_recv, c.rows)
        self.y_copy(c).wait_send()
        self.x_copy(c).start()

    def on_x(self, c):
        half = c.rows // 2
        self.x_copy(c).wait_recv()
        add_rows(self.buf, c.mine + self.x * half, self.x_recv, c.x_recv, half)
        for k in range(1, self.nz):
            self.z_copy(c, k).start()

    def on_z(self, c):
        size = c.rows // 2 // self.nz
        start = c.mine + self.x * (c.rows // 2) + self.z * size
        for k in range(1, self.nz):
            self.z_copy(c, k).wait_recv()
        step = next(k for k in (64, 48, 32, 16) if size % k == 0)

        def body(i, carry):
            d = pl.ds(pl.multiple_of(start + i * step, 16), step)
            total = self.buf[d, :].astype(F32)
            for k in range(1, self.nz):
                total = total + self.z_recv[k - 1, pl.ds(pl.multiple_of(c.z_recv + i * step, 16), step), :].astype(F32)
            to = pl.ds(pl.multiple_of(c.x_recv + self.z * size + i * step, 16), step)
            self.x_recv[to, :] = total.astype(BF16)
            return carry

        lax.fori_loop(0, size // step, body, 0)
        for k in range(1, self.nz):
            self.back_z(c, k).start()
        self.back_x(c, 0).start()

    def on_back(self, c):
        for k in range(1, self.nz):
            self.back_z(c, k).wait_recv()
            self.back_x(c, k).start()

    def finish(self, c):
        for k in range(self.nz):
            self.back_x(c, k).wait_recv()

    def drain(self, c):
        self.x_copy(c).wait_send()
        for k in range(1, self.nz):
            self.z_copy(c, k).wait_send()
            self.back_z(c, k).wait_send()
        for k in range(self.nz):
            self.back_x(c, k).wait_send()


def fold(v):
    return jnp.sum(v.reshape(v.shape[0] // 8, 8, v.shape[1]), axis=0)


def gelu_both(v):
    e = jnp.exp(-0.5 * v * v)
    t = 1.0 / (1.0 + 0.23164189 * jnp.abs(v))
    poly = ((((1.061405429 * t - 1.453152027) * t + 1.421413741) * t - 0.284496736) * t + 0.254829592) * t
    tail = 0.5 * poly * e
    phi = jnp.where(v >= 0.0, 1.0 - tail, tail)
    return v * phi, phi + v * e * 0.3989422804014327


def transpose_into(src, dst):
    for c in range(D // 128):
        dst[c * 128 : (c + 1) * 128, :] = src[:, c * 128 : (c + 1) * 128].T


def attend_back(
    i, qkv, qkv_cls, datt, datt_cls, lse, lsec, scores, dprobs, probs, dscores, cls_row, joint_cls, joint, extra, sum_q, sum_v
):
    rows = at(i, PATCH)
    mask = head_mask()
    own = qkv_cls[pl.ds(i, 1), :]
    do_c = datt_cls[pl.ds(i, 1), :]
    q_c, k_c, v_c = own[:, :D] * FACTOR, own[:, D : 2 * D], own[:, 2 * D :]
    pick = lambda v: jnp.where(mask, v, 0.0)
    q_w, k_w, v_w, do_w = pick(q_c), pick(k_c), pick(v_c), pick(do_c)
    q_bd, k_bd, v_bd, do_bd = (v.astype(BF16) for v in (q_w, k_w, v_w, do_w))
    queries, keys, values = (qkv[rows, k * D : (k + 1) * D] for k in range(3))
    grads = datt[rows, :]
    low = lambda v: v.astype(BF16)
    top = lsec[i][:, 0:1]
    p_row = jnp.exp(dot_nt(q_bd, keys) - top)
    p_cor = jnp.exp(jnp.sum(q_w * k_c, axis=1, keepdims=True) - top)
    dp_row = dot_nt(do_bd, values)
    dp_cor = jnp.sum(do_w * v_c, axis=1, keepdims=True)
    delta = jnp.sum(p_row * dp_row, axis=1, keepdims=True) + p_cor * dp_cor
    ds_row = low(p_row * (dp_row - delta))
    ds_cor = low(p_cor * (dp_cor - delta)).astype(F32)
    p_col = jnp.exp(dot_nt(k_bd, queries) * FACTOR - lse[i])
    dp_col = dot_nt(v_bd, grads)
    for g in range(HEADS // 2):
        lanes = slice(g * 128, (g + 1) * 128)
        q2 = qkv[rows, lanes] * jnp.asarray(FACTOR, BF16)
        scores[g] = dot_nt(split_pair(qkv[rows, g * 128 + D : g * 128 + D + 128]), q2)
        dprobs[g] = dot_nt(split_pair(qkv[rows, g * 128 + 2 * D : g * 128 + 2 * D + 128]), datt[rows, lanes])
    for g in range(HEADS // 2):
        for u in range(2):
            h = 2 * g + u
            half = slice(u * PATCH, (u + 1) * PATCH)
            part = jnp.exp(scores[g, half, :] - lse[i, h : h + 1, :])
            dpart = dprobs[g, half, :]
            p_h, dp_h = p_col[h : h + 1, :], dp_col[h : h + 1, :]
            delta = jnp.sum(part * dpart, axis=0, keepdims=True) + p_h * dp_h
            probs[g, half, :] = low(part)
            dscores[g, half, :] = low(part * (dpart - delta))
            cls_row[h : h + 1, :] = p_h * (dp_h - delta)
    ds_col = low(cls_row[...])
    total = lambda v: jnp.sum(jnp.where(mask, v, 0.0), axis=0, keepdims=True)
    joint_cls[pl.ds(i, 1), 0:D] = FACTOR * (total(dot(ds_row, keys)) + jnp.sum(ds_cor * k_w, axis=0, keepdims=True))
    joint_cls[pl.ds(i, 1), D : 2 * D] = FACTOR * total(dot(ds_col, queries)) + jnp.sum(ds_cor * q_w, axis=0, keepdims=True)
    joint_cls[pl.ds(i, 1), 2 * D : 3 * D] = total(dot(low(p_col), grads)) + jnp.sum(
        low(p_cor).astype(F32) * do_w, axis=0, keepdims=True)
    extra[0] = dot_tn(ds_col, k_bd) * FACTOR
    extra[1] = dot_tn(ds_row, q_bd)
    extra[2] = dot_tn(low(p_row), do_bd)
    for g in range(HEADS // 2):
        lanes = slice(g * 128, (g + 1) * 128)
        klanes = slice(g * 128 + D, g * 128 + D + 128)
        vlanes = slice(g * 128 + 2 * D, g * 128 + 2 * D + 128)
        q2 = qkv[rows, lanes] * jnp.asarray(FACTOR, BF16)
        dv = merge_pair(dot(probs[g], datt[rows, lanes])) + extra[2, :, lanes]
        dk = merge_pair(dot(dscores[g], q2)) + extra[1, :, lanes]
        dq = dot_tn(dscores[g], split_pair(qkv[rows, klanes])) * FACTOR + extra[0, :, lanes]
        joint[:, lanes] = low(dq)
        joint[:, klanes] = low(dk)
        joint[:, vlanes] = low(dv)
        sum_q[:, lanes] += fold(dq)
        sum_v[:, lanes] += fold(dv)
    qkv[rows, :] = joint[...]


def to_tokens(src, dst, turn):
    images = dst.shape[0] // (PATCH + 1)
    main = images * PATCH

    def lane_block(l, carry):
        cols = at(l, 128)
        slot = lax.rem(l, 2)
        for i in range(images):
            turn[slot, pl.ds(i, PATCH, stride=images), :] = src[i * PATCH : (i + 1) * PATCH, cols].astype(F32)
        dst[0:main, cols] = turn[slot].astype(BF16)
        return carry

    lax.fori_loop(0, D // 128, lane_block, 0)
    dst[main : main + images, :] = src[main:, :].astype(F32)[0:images].astype(BF16)


def backward_kernel(
    nz, chunks, vec, full_qkv, full_out, full_up, full_down, qkv_h, act_t_h, x_h, att_t_h, mid_h, branch_h, act2_h,
    act2_t_h, up_h, dr_h, dr_t_h, lse_h, lsec_h, parts_h, hid_h, gact_h, column_h,
    result_o, tokens_o, sums_o, small_o, hidden_o,
    buf, core_recv, y_recv, x_recv, z_recv, gmid, grad_mid, up_s, acc, sums_up, vecf, bias_qkv, bias_up, v_part, v_group, v_sum, v_all,
    sems, core_sems, group_sems, all_sems, credit, dsem, wsem, hsem, osem, fsem,
):
    images = lse_h.shape[0]
    n = gmid.shape[0]
    main = images * PATCH
    red = Reduce(nz, buf, core_recv, y_recv, x_recv, z_recv, sems, core_sems, credit)
    s = red.s
    cd0, cu0, cd1, cu1, co, *cq = chunks

    def load(k, src, dst):
        copy = pltpu.make_async_copy(src, dst, dsem.at[k])
        copy.start()
        return copy

    def relative(rel):
        return relative_piece(s, rel)

    def target(rel, chunk, base):
        low, high = lax.rem(rel, 2), lax.div(rel, 2)
        return low * (base + (1 - high) * chunk.rows) + (1 - low) * (high * chunk.y_send + (1 - high) * chunk.mine)

    def group_peer(k):
        return {"shard": lax.rem(s + k, 4)}

    def replica_peer(k):
        return {"replica": lax.rem(red.r + k, 2 * nz)}

    def group_copy(k):
        return pltpu.make_async_remote_copy(
            v_part.at[lax.rem(s + k, 4)], v_group.at[k - 1], group_sems.at[0, k - 1], group_sems.at[1, k - 1],
            device_id=group_peer(k), device_id_type=MESH)

    def all_copy(k):
        return pltpu.make_async_remote_copy(
            v_sum, v_all.at[red.r], all_sems.at[0, k - 1], all_sems.at[1, k - 1], device_id=replica_peer(k),
            device_id_type=MESH)

    got_up = load(7, up_h, up_s)

    def ffn(dr, dr_t, act2, act2_t, w_up, w_down, hid, br):
        def fetch(j, slot):
            piece, t = relative(3 - lax.rem(j, 4)), lax.div(j, 4)
            return (
                pltpu.make_async_copy(full_up.at[piece, :, at(t, TILE)], w_up.at[slot], wsem.at[0, slot]),
                pltpu.make_async_copy(full_down.at[piece, at(t, TILE), :], w_down.at[slot], wsem.at[1, slot]),
            )

        for copy in fetch(2, 0):
            copy.start()
        got_parts, got_act2, got_dr = (load(8, parts_h, buf.at[pl.ds(cd0.y_send, 2048), :]), load(0, act2_h, act2),
                                       load(1, dr_h, dr))
        got_gact, got_column = load(10, gact_h, gmid), load(11, column_h, sums_up)
        late = [load(2, dr_t_h, dr_t), load(3, act2_t_h, act2_t)]

        def keep(j, slot):
            return pltpu.make_async_copy(hid.at[slot], hidden_o.at[j - 2], hsem.at[slot])

        barrier = pltpu.get_barrier_semaphore()
        partners = [group_peer(k) for k in range(1, 4)] + [replica_peer(k) for k in range(1, 2 * nz)]
        for to in partners:
            pl.semaphore_signal(barrier, inc=1, device_id=to, device_id_type=MESH)
        pl.semaphore_wait(barrier, len(partners))
        unpack_vectors(vec, vecf, bias_qkv)
        unpack_bias_up(vec, bias_up)
        acc[...] = jnp.zeros_like(acc)
        got_parts.wait()
        red.y_copy(cd0).start()
        red.y_copy(cu0).start()
        got_act2.wait()
        got_dr.wait()

        def tile(j, carry):
            slot = lax.rem(j, 2)
            rel, t = 3 - lax.rem(j, 4), lax.div(j, 4)
            piece = relative(rel)
            low, high = lax.rem(rel, 2), lax.div(rel, 2)
            place_at = pl.multiple_of(
                (1 - low) * (high * (cd0.y_send + t * (cd1.y_send - cd0.y_send)) + (1 - high) * (cd0.mine + t * 2048)), 16)
            for copy in fetch(j, slot):
                copy.wait()

            @pl.when(j < 7)
            def _():
                for copy in fetch(j + 1, 1 - slot):
                    copy.start()

            @pl.when(j >= 4)
            def _():
                keep(j - 2, slot).wait()

            for k in (4, 6):
                @pl.when(j == k)
                def _(k=k):
                    red.core_copy(k // 2 - 1, 2048).wait_send()

            def on_back():
                @pl.when(j == 2)
                def _():
                    for copy in (got_gact, got_column):
                        copy.wait()

                for k, chunk in ((4, cd0), (6, cu0)):
                    @pl.when(j == k)
                    def _(chunk=chunk):
                        red.on_y(chunk)

            def on_hidden():
                keep(j, slot).start()

                @pl.when(j == 2)
                def _():
                    for copy in late:
                        copy.wait()

            def put(half, value):
                buf[pl.ds(pl.multiple_of(place_at + half * D, 16), D), :] = value

            sums_up[pl.ds(2 * piece + t, 1), :] = ffn_tile(
                act2, dr, dr_t, act2_t, lambda: w_up[slot], lambda: w_down[slot], bias_up[pl.ds(2 * piece + t, 1), :],
                hid.at[slot], br, gmid, False, on_back, on_hidden, put)

            def y_part(turn, chunk):
                red.core_copy(turn, 2048).wait_recv()
                for k, c in enumerate(chunk):
                    red.add_core(turn, k * 1024, c.y_send, c.rows)
                    red.y_copy(c).start()

            def own_part(turn, chunk):
                red.core_copy(turn, 2048).wait_recv()
                red.add_core(turn, 0, chunk[0].mine, 2048)

            steps = {
                2: [lambda: red.core_copy(1, 2048).start()],
                3: [lambda: own_part(1, (cd0, cu0))],
                4: [lambda: red.core_copy(2, 2048).start()],
                5: [lambda: y_part(2, (cd1, cu1)), lambda: red.on_x(cd0)],
                6: [lambda: red.core_copy(3, 2048).start()],
                7: [lambda: own_part(3, (cd1, cu1))],
            }
            for k, todo in steps.items():
                @pl.when(j == k)
                def _(todo=todo):
                    for step in todo:
                        step()
            return carry

        lax.fori_loop(2, 8, tile, 0)
        pl.semaphore_signal(credit, inc=1, device_id={"shard": red.across}, device_id_type=MESH)
        for j in (6, 7):
            keep(j, j % 2).wait()
        red.core_copy(3, 2048).wait_send()

    v = pltpu.VMEM
    pl.run_scoped(ffn, v((n, D), BF16), v((D, n), BF16), v((n, D), BF16), v((D, n), BF16), v((2, D, TILE), BF16),
                  v((2, TILE, D), BF16), v((2, n, TILE), BF16), v((n, TILE), BF16))
    got_up.wait()

    def spread(out, chunk, tile_rows, turn):
        for p in range(4):
            low = lax.rem(lax.rem(s, 2) + p % 2, 2)
            high = lax.rem(lax.div(s, 2) + p // 2, 2)
            start = pl.multiple_of(target(low + 2 * high, chunk, 1024 * (turn % 2)) + tile_rows, 16)
            buf[pl.ds(start, 256), :] = out[p * 256 : (p + 1) * 256].astype(BF16)

    def on_core(turn, chunk):
        red.core_copy(turn, 2 * chunk.rows).wait_recv()
        red.add_core(turn, 0, chunk.y_send, chunk.rows)
        red.y_copy(chunk).start()
        red.add_core(turn, chunk.rows, chunk.mine, chunk.rows)

    def attention(
        qkv, datt, brr, lse, lsec, scores, dprobs, probs, dscores, cls_row, qkv_cls, datt_cls, joint_cls, joint, extra
    ):
        got_qkv, got_lse, got_lsec = load(0, qkv_h, qkv), load(1, lse_h, lse), load(2, lsec_h, lsec)

        def middle(mid, branch, att_t, w_out):
            got_mid, got_branch = load(3, mid_h, mid), load(4, branch_h, branch)
            got_att, got_out = load(5, att_t_h, att_t), load(6, full_out, w_out)
            red.on_z(cd0)
            red.on_x(cu0)
            got_mid.wait()
            got_branch.wait()

            def norm_rows(rows):
                m = mid[rows, :]
                c = m - jnp.mean(m, axis=-1, keepdims=True)
                inv = lax.rsqrt(jnp.mean(c * c, axis=-1, keepdims=True) + 1e-06)
                hat = c * inv
                g = gmid[rows, :]
                acc[4] += fold(g * hat)
                acc[5] += fold(g)
                sc = g * vecf[4:5, :]
                back = inv * (sc - jnp.mean(sc, axis=-1, keepdims=True)
                              - hat * jnp.mean(sc * hat, axis=-1, keepdims=True))
                gm = up_s[rows, :].astype(F32) + back
                grad_mid[rows, :] = gm
                acc[3] += fold(gm * branch[rows, :].astype(F32))
                gb = gm * vecf[3:4, :]
                acc[2] += fold(gb)
                brr[rows, :] = gb.astype(BF16)

            rows_loop(n, 16, norm_rows)
            got_att.wait()
            for q in range(2):
                spread(dot(att_t[...], brr[:, q * TILE : (q + 1) * TILE]), co, q * 256, 4)
            red.core_copy(4, 2 * co.rows).start()
            got_out.wait()
            for q in range(2):
                datt[:, q * TILE : (q + 1) * TILE] = dot_nt(brr[...], w_out[q * TILE : (q + 1) * TILE, :]).astype(BF16)

        pl.run_scoped(middle, v((n, D), F32), v((n, D), BF16), v((D, n), BF16), v((D, D), BF16))
        got_qkv.wait()
        got_lse.wait()
        got_lsec.wait()
        qkv_cls[...] = qkv[main:, :].astype(F32)
        datt_cls[...] = datt[main:, :].astype(F32)
        joint_cls[...] = jnp.zeros_like(joint_cls)
        pl.semaphore_wait(credit, 1)
        on_core(4, co)
        plan = {0: [lambda: red.on_y(cd1)], 1: [lambda: red.on_back(cd0)], 2: [lambda: red.on_z(cu0)],
                3: [lambda: red.on_x(cd1), lambda: red.on_back(cu0)], 5: [lambda: red.on_y(cu1)], 6: [lambda: red.on_z(cd1)]}

        def image(i, carry):
            for k, steps in plan.items():
                @pl.when(i == k)
                def _(steps=steps):
                    for step in steps:
                        step()

            attend_back(i, qkv, qkv_cls, datt, datt_cls, lse, lsec, scores, dprobs, probs, dscores, cls_row, joint_cls,
                        joint, extra, acc.at[8], acc.at[9])
            return carry

        lax.fori_loop(0, images, image, 0)
        qkv[main:, :] = joint_cls[...].astype(BF16)
        acc[8] += fold(joint_cls[:, 0:D])
        acc[9] += fold(joint_cls[:, 2 * D : 3 * D])

        def tail(act_t, w_qkv, turn, flat):
            x_s, gact, new = brr, gmid, datt
            got_act, got_x = load(3, act_t_h, act_t), load(4, x_h, x_s)

            def fetch(j):
                return pltpu.make_async_copy(full_qkv.at[pl.ds(j * 256, 256), :], w_qkv.at[j % 2], wsem.at[0, j % 2])

            fetch(0).start()
            fetch(1).start()
            def weight_grad(k):
                for q in range(2):
                    cols = slice((2 * k + q) * TILE, (2 * k + q + 1) * TILE)
                    spread(dot(act_t[...], qkv[:, cols]), cq[k], q * 256, 5 + k)

            def input_grad(j):
                fetch(j).wait()
                gact[:, j * 256 : (j + 1) * 256] = dot_nt(qkv[...], w_qkv[j % 2])
                if j < 2:
                    fetch(j + 2).start()

            got_act.wait()
            weight_grad(0)
            red.core_copy(5, 1024).start()
            red.on_x(cu1)
            red.core_copy(4, 1024).wait_send()
            weight_grad(1)
            on_core(5, cq[0])
            red.core_copy(6, 1024).start()
            red.on_y(co)
            red.core_copy(5, 1024).wait_send()
            weight_grad(2)
            on_core(6, cq[1])
            red.core_copy(7, 1024).start()
            red.on_back(cd1)
            input_grad(0)
            red.on_z(cu1)
            input_grad(1)
            on_core(7, cq[2])
            red.on_x(co)
            input_grad(2)
            red.on_y(cq[0])
            input_grad(3)
            got_x.wait()

            def norm_rows(rows):
                m = x_s[rows, :].astype(F32)
                c = m - jnp.mean(m, axis=-1, keepdims=True)
                inv = lax.rsqrt(jnp.mean(c * c, axis=-1, keepdims=True) + 1e-06)
                hat = c * inv
                g = gact[rows, :]
                acc[0] += fold(g * hat)
                acc[1] += fold(g)
                sc = g * vecf[0:1, :]
                back = inv * (sc - jnp.mean(sc, axis=-1, keepdims=True)
                              - hat * jnp.mean(sc * hat, axis=-1, keepdims=True))
                new[rows, :] = (grad_mid[rows, :] + back).astype(BF16)

            rows_loop(n, 16, norm_rows)
            red.on_z(co)
            red.on_x(cq[0])
            to_tokens(new, flat, turn)
            copy = pltpu.make_async_copy(flat, tokens_o, osem.at[0])
            copy.start()
            red.on_back(cu1)
            red.on_back(co)
            red.on_y(cq[1])
            copy.wait()

        pl.run_scoped(tail, v((D, n), BF16), v((2, 256, 3 * D), BF16),
                      v((2, main, 128), F32), v((main + images, D), BF16))

    pl.run_scoped(attention, v((n, 3 * D), BF16), v((n, D), BF16), v((n, D), BF16), v((images, HEADS, PATCH), F32),
                  v((images, HEADS, PATCH), F32), v((8, 256, PATCH), F32), v((8, 256, PATCH), F32),
                  v((8, 256, PATCH), BF16), v((8, 256, PATCH), BF16), v((HEADS, PATCH), F32), v((CLS, 3 * D), F32),
                  v((CLS, D), F32), v((CLS, 3 * D), F32), v((PATCH, 3 * D), BF16), v((3, PATCH, D), F32))

    def outcome(mid, hid, w_down, turn, flat, res):
        got_mid = load(3, mid_h, mid)

        def fetch(pair):
            copies = []
            for k in range(2):
                j = 2 * pair + k
                slot = pair % 2
                piece, t = relative(3 - j % 4), j // 4
                src = hid_h.at[k] if pair == 0 else hidden_o.at[j - 2]
                copies.append(pltpu.make_async_copy(src, hid.at[slot, :, pl.ds(k * TILE, TILE)], wsem.at[0, 2 * slot + k]))
                copies.append(pltpu.make_async_copy(full_down.at[piece, pl.ds(t * TILE, TILE), :],
                                                    w_down.at[slot, pl.ds(k * TILE, TILE), :], wsem.at[1, 2 * slot + k]))
            return copies

        for copy in fetch(0):
            copy.start()
        steps = {0: [lambda: red.on_z(cq[0]), lambda: red.on_x(cq[1])], 1: [lambda: red.on_back(cq[0])],
                 2: [lambda: red.on_y(cq[2]), lambda: red.on_z(cq[1])], 3: [lambda: red.on_back(cq[1])]}
        for pair in range(4):
            if pair < 3:
                for copy in fetch(pair + 1):
                    copy.start()
            for copy in fetch(pair):
                copy.wait()
            for q in range(2):
                cols = slice(q * TILE, (q + 1) * TILE)
                out = dot(hid[pair % 2], w_down[pair % 2, :, cols])
                if pair:
                    gmid[:, cols] += out
                else:
                    gmid[:, cols] = out
            for step in steps.get(pair, []):
                step()
        got_mid.wait()

        def rows_of(rows):
            projected = gmid[rows, :] + vecf[6:7, :]
            upstream = up_s[rows, :].astype(F32)
            acc[6] += fold(upstream * vecf[7:8, :])
            acc[7] += fold(upstream * projected)
            res[rows, :] = (mid[rows, :] + vecf[7:8, :] * projected).astype(BF16)

        rows_loop(n, 16, rows_of)
        for p in range(4):
            for k in range(8):
                v_part[p, k : k + 1, :] = jnp.sum(acc[k, :, p * 256 : (p + 1) * 256], axis=0, keepdims=True)
            joint = acc.at[8 + p // 2]
            for k in range(2):
                start = (p % 2) * TILE + k * 256
                v_part[p, 8 + k : 9 + k, :] = jnp.sum(joint[:, start : start + 256], axis=0, keepdims=True)
            for k in range(4):
                v_part[p, 10 + k : 11 + k, :] = sums_up[2 * p + k // 2 : 2 * p + k // 2 + 1, (k % 2) * 256 : (k % 2 + 1) * 256]
            v_part[p, 14:16, :] = jnp.zeros((2, 256), F32)
        for k in range(1, 4):
            group_copy(k).start()
        red.on_x(cq[2])
        total = v_part[s]
        for k in range(1, 4):
            group_copy(k).wait_recv()
            total = total + v_group[k - 1]
        v_sum[...] = total
        v_all[red.r] = total
        for k in range(1, 2 * nz):
            all_copy(k).start()
        to_tokens(res, flat, turn)
        copy = pltpu.make_async_copy(flat, result_o, osem.at[0])
        copy.start()
        red.on_z(cq[2])
        for k in range(1, 2 * nz):
            all_copy(k).wait_recv()
        total = v_all[0]
        for k in range(1, 2 * nz):
            total = total + v_all[k]
        v_group[0] = total
        small = pltpu.make_async_copy(v_group.at[0], small_o, osem.at[1])
        small.start()
        red.on_back(cq[2])
        copy.wait()
        small.wait()

    pl.run_scoped(outcome, v((n, D), F32), v((2, n, D), BF16), v((2, D, D), BF16), v((2, main, 128), F32),
                  v((main + images, D), BF16), v((n, D), BF16))
    copies = []
    for c in chunks:
        red.finish(c)
        half = c.rows // 2
        for k, (src, first, where) in enumerate(((x_recv, c.x_recv, red.x), (buf, c.far, 1 - red.x))):
            copy = pltpu.make_async_copy(
                src.at[pl.ds(first, half), :],
                sums_o.at[pl.ds(pl.multiple_of(c.mine - cd0.mine + where * half, 16), half), :], fsem.at[2 * c.index + k])
            copy.start()
            copies.append(copy)
    red.core_copy(6, 1024).wait_send()
    red.core_copy(7, 1024).wait_send()
    for k in range(1, 4):
        group_copy(k).wait_send()
    for k in range(1, 2 * nz):
        all_copy(k).wait_send()
    for c in chunks:
        red.drain(c)
    for copy in copies:
        copy.wait()


def convert_kernel(
    chunks, sums, small, result, tokens, result_o, tokens_o, g1_o, s1_o, qkv_o, bqv_o, out_o, bo_o, l1_o, g2_o, s2_o, up_o, bup_o, down_o, bd_o, l2_o,
    low, qkv, out, up, down, moved, dsem, osem, msem,
):
    base = chunks[0].mine
    moves = [pltpu.make_async_copy(src, moved.at[k], msem.at[0, k]) for k, src in enumerate((result, tokens))]
    stores = [pltpu.make_async_copy(moved.at[k], dst, msem.at[1, k]) for k, dst in enumerate((result_o, tokens_o))]
    gots = []
    for c in chunks:
        rows = pl.ds(c.mine - base, c.rows)
        gots.append(pltpu.make_async_copy(sums.at[rows, :], low.at[rows, :], dsem.at[c.index]))
        gots[-1].start()
    for copy in moves:
        copy.start()
    outs = []

    def send_out(src, dst):
        copy = pltpu.make_async_copy(src, dst, osem.at[len(outs)])
        copy.start()
        outs.append(copy)

    def block(c, first, count):
        return low[c.mine - base + first : c.mine - base + first + count, :]

    for t in range(2):
        gots[2 * t].wait()
        for k in range(8):
            down[t * TILE : (t + 1) * TILE, k * 128 : (k + 1) * 128] = block(chunks[2 * t], k * 128, 128).T.astype(F32)
        send_out(down.at[pl.ds(t * TILE, TILE), :], down_o.at[pl.ds(t * TILE, TILE), :])
        moves[t].wait()
        stores[t].start()
        gots[2 * t + 1].wait()
        up[t] = block(chunks[2 * t + 1], 0, D).astype(F32)
        send_out(up.at[t], up_o.at[:, pl.ds(t * TILE, TILE)])
    gots[4].wait()
    for k in range(2):
        out[:, k * TILE : (k + 1) * TILE] = block(chunks[4], k * 256, 256).astype(F32)
    send_out(out, out_o)
    for k in range(5, 8):
        gots[k].wait()
    for k in range(6):
        qkv[:, k * TILE : (k + 1) * TILE] = block(chunks[5], k * 256, 256).astype(F32)
    send_out(qkv, qkv_o)
    vectors = (g1_o, s1_o, bo_o, l1_o, g2_o, s2_o, bd_o, l2_o, bqv_o, bup_o)
    row = 0
    for v in vectors:
        for k in range(v.shape[0] // 256):
            v[pl.ds(k * 256, 256)] = small[row : row + 1, :].reshape(256)
            row += 1
    for copy in outs + stores:
        copy.wait()


def convert(chunks, sums, small, result, tokens):
    one = lambda k: jax.ShapeDtypeStruct((k,), F32)
    outs = (
        low_shape(*result.shape), low_shape(*tokens.shape), one(256), one(256), wide_shape(256, 3 * D), one(512), wide_shape(256, D), one(256), one(256), one(256), one(256),
        wide_shape(D, D), one(1024), wide_shape(D, D), one(256), one(256),
    )
    v = pltpu.VMEM
    return pl.pallas_call(
        functools.partial(convert_kernel, chunks),
        out_shape=outs,
        in_specs=[ANY, VMEM, ANY, ANY],
        out_specs=[VMEM if len(o.shape) == 1 else ANY for o in outs],
        scratch_shapes=[v(sums.shape, BF16), v((256, 3 * D), F32), v((256, D), F32), v((2, D, TILE), F32),
                        v((D, D), F32), v((2,) + result.shape, BF16), pltpu.SemaphoreType.DMA((8,)),
                        pltpu.SemaphoreType.DMA((6,)), pltpu.SemaphoreType.DMA((2, 2))],
        compiler_params=pltpu.CompilerParams(vmem_limit_bytes=LIMIT),
        name="gradients_to_float32",
    )(sums, small, result, tokens)


def low_shape(*shape):
    return jax.ShapeDtypeStruct(shape, BF16)


def wide_shape(*shape):
    return jax.ShapeDtypeStruct(shape, F32)


ANY = pl.BlockSpec(memory_space=pl.ANY)
VMEM = pl.BlockSpec(memory_space=pltpu.VMEM)
LIMIT = 62 * 2**20


def forward(flat, cot, vectors, w_qkv, w_out, w_up, w_down):
    images = flat.shape[0] // (PATCH + 1)
    n = images * PATCH + CLS
    v = pltpu.VMEM
    outs = (
        low_shape(D, 3 * D), low_shape(D, D), low_shape(4, D, D), low_shape(4, D, D), low_shape(4, 16, 256),
        low_shape(n, 3 * D), low_shape(D, n), low_shape(n, D), low_shape(D, n), wide_shape(n, D), low_shape(n, D),
        low_shape(n, D), low_shape(D, n), low_shape(n, D), low_shape(n, D), low_shape(D, n),
        wide_shape(images, HEADS, PATCH), wide_shape(images, HEADS, PATCH),
        low_shape(2048, TILE), low_shape(2, n, TILE), wide_shape(n, D), wide_shape(8, TILE),
    )
    return pl.pallas_call(
        gather_kernel,
        out_shape=outs,
        in_specs=[ANY] * 2 + [VMEM] * 10 + [ANY] * 4,
        out_specs=[ANY] * len(outs),
        scratch_shapes=[
            v((D, 3 * D), BF16), v((D, D), BF16), v((4, D, D), BF16), v((4, D, D), BF16),
            v((n, D), BF16), v((n, 3 * D), BF16), v((n, D), BF16), v((n, D), BF16), v((n, D), F32), v((n, D), BF16),
            v((n, D), BF16), v((D, n), BF16), v((D, n), BF16),
            v((images, HEADS, PATCH), F32), v((images, HEADS, PATCH), F32),
            v((8, 256, PATCH), F32), v((8, 256, PATCH), BF16), v((PATCH, D), F32), v((HEADS, PATCH), F32),
            v((CLS, D), F32), v((CLS, 3 * D), F32), v((2, images * PATCH, 128), F32), v((16, 256), F32),
            v((16, 256), BF16), v((4, 16, 256), BF16), v((16, D), F32), v((8, 3 * D), F32), v((8, TILE), F32),
            v((8, TILE), F32), v((2, D, TILE), BF16), v(flat.shape, BF16), pltpu.SemaphoreType.DMA((2, 7, 11)), pltpu.SemaphoreType.DMA((7,)), pltpu.SemaphoreType.DMA((2, 3)),
            pltpu.SemaphoreType.DMA((30,)), pltpu.SemaphoreType.DMA((2, 2)),
            pltpu.SemaphoreType.DMA((1,)),
        ],
        compiler_params=pltpu.CompilerParams(collective_id=0, has_side_effects=True, vmem_limit_bytes=LIMIT),
        cost_estimate=pl.CostEstimate(flops=18 * 2**30, bytes_accessed=64 * 2**20, transcendentals=3 * 2**20),
        name="gather_and_attention",
    )(flat, cot, *vectors, w_qkv, w_out, w_up, w_down)


def backward(nz, images, vec, *arrays):
    n = images * PATCH + CLS
    tokens = images * (PATCH + 1)
    v = pltpu.VMEM
    chunks, sizes = chunk_layout(nz)
    outs = (low_shape(tokens, D), low_shape(tokens, D), low_shape(sizes["total"], TILE), wide_shape(16, 256),
            low_shape(6, n, TILE))
    return pl.pallas_call(
        functools.partial(backward_kernel, nz, chunks),
        out_shape=outs,
        in_specs=[VMEM] + [ANY] * len(arrays),
        out_specs=[ANY] * len(outs),
        scratch_shapes=[
            v((sizes["buf"], TILE), BF16), v((2, 2048, TILE), BF16), v((sizes["y_recv"], TILE), BF16),
            v((sizes["x_recv"], TILE), BF16), v((nz - 1, sizes["z_recv"], TILE), BF16), v((n, D), F32), v((n, D), F32), v((n, D), BF16),
            v((10, 8, D), F32), v((8, TILE), F32), v((16, D), F32), v((8, 3 * D), F32), v((8, TILE), F32),
            v((4, 16, 256), F32), v((3, 16, 256), F32), v((16, 256), F32), v((2 * nz, 16, 256), F32),
            pltpu.SemaphoreType.DMA((2, len(chunks), 3 * nz)), pltpu.SemaphoreType.DMA((2, 8)),
            pltpu.SemaphoreType.DMA((2, 3)), pltpu.SemaphoreType.DMA((2, 2 * nz - 1)),
            pltpu.SemaphoreType.REGULAR, pltpu.SemaphoreType.DMA((12,)), pltpu.SemaphoreType.DMA((2, 4)),
            pltpu.SemaphoreType.DMA((2,)), pltpu.SemaphoreType.DMA((2,)), pltpu.SemaphoreType.DMA((2 * len(chunks),)),
        ],
        compiler_params=pltpu.CompilerParams(collective_id=1, has_side_effects=True, vmem_limit_bytes=LIMIT),
        cost_estimate=pl.CostEstimate(flops=66 * 2**30, bytes_accessed=128 * 2**20, transcendentals=8 * 2**20),
        name="layer_backward",
    )(vec, *arrays), chunks


def on_device(
    tokens, norm1_gain, norm1_shift, w_qkv, bias_qv, w_out, bias_out, scale_one, norm2_gain, norm2_shift, w_up, bias_up,
    w_down, bias_down, scale_two, cotangent,
):
    images, length, _ = tokens.shape
    nz = lax.axis_size("replica") // 2
    flatten = lambda a: jnp.transpose(a, (1, 0, 2)).reshape(images * length, D)
    restore = lambda a: jnp.transpose(a.reshape(length, images, D), (1, 0, 2))
    vectors = (norm1_gain, norm1_shift, bias_out, scale_one, norm2_gain, norm2_shift, bias_down, scale_two, bias_qv, bias_up)
    full_qkv, full_out, full_up, full_down, vec, *kept = forward(
        flatten(tokens), flatten(cotangent), vectors, w_qkv, w_out, w_up, w_down)
    (result, grad_tokens, sums, small, _), chunks = backward(nz, images, vec, full_qkv, full_out, full_up, full_down, *kept)
    result, grad_tokens, *gradients = convert(chunks, sums, small, result, grad_tokens)
    return (restore(result), restore(grad_tokens)) + tuple(gradients)


def solution(mesh):
    placed = (
        P(("shard", "replica"), None, None),
        P("shard"),
        P("shard"),
        P("shard", None),
        P("shard"),
        P("shard", None),
        P("shard"),
        P("shard"),
        P("shard"),
        P("shard"),
        P(None, "shard"),
        P("shard"),
        P("shard", None),
        P("shard"),
        P("shard"),
        P(("shard", "replica"), None, None),
    )
    return jax.shard_map(
        on_device,
        mesh=mesh,
        in_specs=placed,
        out_specs=(
            P(("shard", "replica"), None, None),
            P(("shard", "replica"), None, None),
            P("shard"),
            P("shard"),
            P("shard", None),
            P("shard"),
            P("shard", None),
            P("shard"),
            P("shard"),
            P("shard"),
            P("shard"),
            P(None, "shard"),
            P("shard"),
            P("shard", None),
            P("shard"),
            P("shard"),
        ),
        check_vma=False,
    )
```
